128 devices in a mesh: ctx: 8 (over z, core), heads: 16 (over y, x).
Axes of the slice: x: 4, y: 4, z: 4, core: 2. Of those that a mesh axis runs over, the one named last changes fastest.
Arguments:
- context: bfloat16 [4096, 8192], P('ctx', 'heads'), may hold values from -12 to 12
- question: bfloat16 [8, 256, 8192], P('ctx', None, 'heads'), may hold values from -12 to 12
- w_query: bfloat16 [8192, 8192], P(None, 'heads')
- w_key: bfloat16 [8192, 1024], P(None, 'heads')
- w_value: bfloat16 [8192, 1024], P(None, 'heads'), may hold values from -0.0625 to 0.0625
- lengths: int32 [8], replicated, may hold values from 1 to 512, 3072 in all
- owner: int32 [8], replicated, may hold values from 0 to 7, each once
Outputs:
- context_attn: bfloat16 [4096, 8192], P('ctx', 'heads')
- question_attn: bfloat16 [256, 8192], P('ctx', 'heads')
The draws below stay inside these ranges and needn't reach their ends.
All inputs are finite; a program needn't handle non-finite values.
Results may differ from the reference program's by a relative error of at most 0.01005.
The reference program's roundings to bfloat16 on the way count: a program that leaves them out, or rounds other values in their place, can miss the bound.
Values may be sent and summed in bfloat16 or wider, within the bound.
No kernel may reach another device: no remote copies, remote signals or barrier semaphores. Data moves between devices by JAX's collectives and lax.ppermute only.
A program may use at most 128 MiB of HBM per device.

```python
import math
import jax
import jax.numpy as jnp
import numpy as np
from jax import lax

D = 8192
HD = 128
QH = 64
KVH = 8
CTX_DEV = 512
QTOK = 256
TOKENS = 4096
N_CTX = 8


def shared_query(key):
    entries = jax.random.normal(jax.random.fold_in(key, 11), (D, QH * HD), jnp.float32)
    return jnp.clip(entries, -6.0, 6.0) * D ** (-0.5)


def context_rows(key):
    entries = jax.random.normal(jax.random.fold_in(key, 21), (TOKENS, D), jnp.float32)
    return jnp.clip(entries, -12.0, 12.0)


def draw_w_query(key, part):
    return shared_query(key).astype(jnp.bfloat16)


def draw_w_key(key, part):
    key = jax.random.fold_in(key, 2)
    entries = jnp.clip(jax.random.normal(key, (D, KVH * HD), jnp.float32), -6.0, 6.0) * D ** (-0.5)
    return entries.astype(jnp.bfloat16)


def draw_context(key, part):
    entries = context_rows(key)
    return entries.astype(jnp.bfloat16)


def draw_question(key, part):
    own_key = jax.random.fold_in(key, 4)
    entries = jnp.clip(jax.random.normal(own_key, (N_CTX, QTOK, D), jnp.float32), -12.0, 12.0)
    return entries.astype(jnp.bfloat16)


def levels(key, shape, shards, low, high):
    factor_of, own = 1.0, jax.random.fold_in(key, 6)
    for dim, parts in shards:
        draws = jnp.exp(jax.random.uniform(jax.random.fold_in(own, dim), (parts,), jnp.float32, low / len(shards), high / len(shards)))
        factor_of = factor_of * jnp.repeat(draws, shape[dim] // parts).reshape([-1 if axis == dim else 1 for axis in range(len(shape))])
    return factor_of


def profile(count, total, bound, skew):
    weights = [(1 << 20) // math.isqrt(grade ** skew) + 1 for grade in range(2, count + 1)]
    surplus, given = total - bound - (count - 1), [1] * (count - 1)
    while surplus > 0:
        candidates = [i for i in range(count - 1) if given[i] < bound]
        pool, budget = sum([weights[i] for i in candidates]), surplus
        for i in candidates:
            extra = min(bound - given[i], max(1, budget * weights[i] // pool), surplus)
            given[i] = given[i] + extra
            surplus = surplus - extra
    return np.array([bound] + given)


def uneven_parts(rng, number_of, total, limit, slope):
    if number_of == 2:
        one = jax.random.randint(rng, (), max(1, total - limit), min(limit, total - 1) + 1)
        return jnp.stack([one, total - one])
    sizes = jnp.asarray(profile(number_of, total, limit, slope), jnp.int32)
    pairs = (number_of - 1) // 2
    source_of, taker = sizes[1:1 + 2 * pairs:2], sizes[2:2 + 2 * pairs:2]
    room = jnp.minimum(source_of - 1, limit - taker)
    passed = jax.random.randint(jax.random.fold_in(rng, 1), (pairs,), 0, 1 << 20) % (room + 1)
    sizes = sizes.at[1:1 + 2 * pairs:2].set(source_of - passed).at[2:2 + 2 * pairs:2].set(taker + passed)
    return sizes[jax.random.permutation(jax.random.fold_in(rng, 2), number_of)]


def bell_draw(key, shape, width, most, pieces=(), kind=jnp.bfloat16):
    gain = levels(key, shape, pieces, -0.22, 0.18) if pieces else 1.0
    array = jax.random.normal(key, shape, jnp.float32) * width * gain
    return jnp.minimum(jnp.maximum(array, -most), most).astype(kind)


def setup_inputs(seed: int = 0) -> dict:
    seeds = jax.random.split(jax.random.key(seed), 8)
    context = draw_context(jax.random.fold_in(seeds[7], 71), 0)
    question = draw_question(jax.random.fold_in(seeds[7], 71), 0)
    w_query = draw_w_query(jax.random.fold_in(seeds[7], 71), 0)
    w_key = draw_w_key(jax.random.fold_in(seeds[7], 71), 0)
    w_value = bell_draw(seeds[4], (D, KVH * HD), D ** -0.5, 0.0625, ((1, 16),))
    lengths = uneven_parts(seeds[5], N_CTX, N_CTX * CTX_DEV * 3 // 4, CTX_DEV, 2).astype(jnp.int32)
    owner = jax.random.permutation(seeds[6], N_CTX).astype(jnp.int32)
    return {"context": context, "question": question, "w_query": w_query, "w_key": w_key, "w_value": w_value, "lengths": lengths, "owner": owner}


rope_base = 500000.0


def angles(positions):
    inverse_freq = rope_base ** (-(jnp.arange(HD // 2, dtype=jnp.float32) * 2.0 / HD))
    phases = positions.astype(jnp.float32)[:, None] * inverse_freq[None, :]
    return jnp.cos(phases), jnp.sin(phases)


def rotate(vectors, cos_part, sin_part):
    half_width = HD // 2
    low_half = vectors[..., :half_width]
    high_half = vectors[..., half_width:]
    cos_wide = cos_part[:, None, :]
    sin_wide = sin_part[:, None, :]
    return jnp.concatenate([low_half * cos_wide - high_half * sin_wide, high_half * cos_wide + low_half * sin_wide], axis=-1)


def project(tokens, positions, w_query, w_key, w_value):
    row_count = tokens.shape[0]
    cos_part, sin_part = angles(positions)
    queries = jnp.dot(tokens, w_query, preferred_element_type=jnp.float32).reshape(row_count, QH, HD)
    queries = rotate(queries, cos_part, sin_part).astype(jnp.bfloat16)
    key_raw = jnp.dot(tokens, w_key, preferred_element_type=jnp.float32).astype(jnp.bfloat16)
    key_raw = lax.optimization_barrier(key_raw)
    key_rows = rotate(key_raw.astype(jnp.float32).reshape(row_count, KVH, HD), cos_part, sin_part).astype(jnp.bfloat16)
    value_rows = jnp.dot(tokens, w_value, preferred_element_type=jnp.float32).astype(jnp.bfloat16).reshape(row_count, KVH, HD)
    return queries, key_rows, value_rows


def attend(queries, key_rows, value_rows, allowed):
    row_count = queries.shape[0]
    group_size = QH // KVH
    grouped = queries.astype(jnp.float32).reshape(row_count, KVH, group_size, HD)
    scores = jnp.einsum('ngqd,mgd->ngqm', grouped, key_rows.astype(jnp.float32)) * (HD ** -0.5)
    scores = jnp.where(allowed[:, None, None, :], scores, -jnp.inf)
    highest = jnp.max(scores, axis=-1)
    exp_scores = jnp.exp(scores - highest[..., None])
    weight_sum = jnp.sum(exp_scores, axis=-1)
    rounded = lax.optimization_barrier(exp_scores.astype(jnp.bfloat16))
    weighted = jnp.einsum('ngqm,mgd->ngqd', rounded.astype(jnp.float32), value_rows.astype(jnp.float32))
    return highest, weight_sum, weighted


def reference(context, question, w_query, w_key, w_value, lengths, owner):
    offsets = jnp.cumsum(lengths) - lengths
    filled = jnp.sum(lengths)
    slot_ids = jnp.arange(CTX_DEV, dtype=jnp.int32)
    positions = (offsets[:, None] + slot_ids[None, :]).reshape(TOKENS)
    queries, key_rows, value_rows = project(context, positions, w_query, w_key, w_value)
    queries = queries.reshape(N_CTX, CTX_DEV, QH, HD)
    key_rows = key_rows.reshape(N_CTX, CTX_DEV, KVH, HD)
    value_rows = value_rows.reshape(N_CTX, CTX_DEV, KVH, HD)

    def block_attend(index):
        anchor_ok = (slot_ids < lengths[0]) & (index > 0)
        own_ok = (slot_ids[None, :] <= slot_ids[:, None]) & (slot_ids[None, :] < lengths[index])
        allowed = jnp.concatenate([jnp.broadcast_to(anchor_ok[None, :], (CTX_DEV, CTX_DEV)), own_ok], axis=1)
        block_keys = jnp.concatenate([key_rows[0], key_rows[index]], axis=0)
        block_values = jnp.concatenate([value_rows[0], value_rows[index]], axis=0)
        highest, weight_sum, weighted = attend(queries[index], block_keys, block_values, allowed)
        result = weighted / weight_sum[..., None]
        result = jnp.where((slot_ids < lengths[index])[:, None, None, None], result, 0.0)
        return result.reshape(CTX_DEV, QH * HD).astype(jnp.bfloat16)

    context_attn = lax.map(block_attend, jnp.arange(N_CTX, dtype=jnp.int32)).reshape(TOKENS, QH * HD)

    question_rows = lax.dynamic_index_in_dim(question, owner[0], 0, keepdims=False)
    row_ids = jnp.arange(QTOK, dtype=jnp.int32)
    q_queries, q_keys, q_values = project(question_rows, filled + row_ids, w_query, w_key, w_value)

    def cache_part(index):
        allowed = jnp.broadcast_to((slot_ids < lengths[index])[None, :], (QTOK, CTX_DEV))
        return attend(q_queries, key_rows[index], value_rows[index], allowed)

    block_max, block_sum, block_weighted = lax.map(cache_part, jnp.arange(N_CTX, dtype=jnp.int32))
    self_max, self_sum, self_weighted = attend(q_queries, q_keys, q_values, row_ids[None, :] <= row_ids[:, None])
    overall_max = jnp.maximum(jnp.max(block_max, axis=0), self_max)
    block_scale = jnp.exp(block_max - overall_max[None])
    self_scale = jnp.exp(self_max - overall_max)
    denominator = jnp.sum(block_sum * block_scale, axis=0) + self_sum * self_scale
    numerator = jnp.sum(block_weighted * block_scale[..., None], axis=0) + self_weighted * self_scale[..., None]
    question_attn = (numerator / denominator[..., None]).reshape(QTOK, QH * HD).astype(jnp.bfloat16)
    return context_attn, question_attn
```

```python
import functools

import jax
import jax.numpy as jnp
from jax import lax
from jax.experimental import pallas as pl
from jax.experimental.pallas import tpu as pltpu
from jax.sharding import PartitionSpec as P

HD = 128
ROPE_BASE = 500000.0
BF = jnp.bfloat16
F32 = jnp.float32
VMEM_LIMIT = 40 * 1024 * 1024
NEG = -1e30
SCALE = HD ** (-0.5)

ANY = pl.BlockSpec(memory_space=pl.ANY)
VM = pl.BlockSpec(memory_space=pltpu.VMEM)
SM = pl.BlockSpec(memory_space=pltpu.SMEM)


def shift_heads(array, dy, dx):
    pairs = [(i, ((i // 4 + dy) % 4) * 4 + (i % 4 + dx) % 4) for i in range(16)]
    return lax.ppermute(array, "heads", pairs)


def swap_heads(array, my, mx):
    pairs = [(i, ((i // 4) ^ my) * 4 + ((i % 4) ^ mx)) for i in range(16)]
    return lax.ppermute(array, "heads", pairs)


def swap_ctx(array, mz, mc):
    pairs = [(i, ((i // 2) ^ mz) * 2 + ((i % 2) ^ mc)) for i in range(8)]
    return lax.ppermute(array, "ctx", pairs)


def project_kernel(plan, n_x, with_q, with_kv, has_acc, finish, *refs):
    refs = list(refs)
    take = lambda count: [refs.pop(0) for _ in range(count)]
    (widx,) = take(1)
    xs = take(n_x)
    wq = take(1)[0] if with_q else None
    wk, wv = take(2) if with_kv else (None, None)
    acc_q_in = take(1)[0] if has_acc and with_q else None
    acc_kv_in = take(1)[0] if has_acc and with_kv else None
    cos, sin = take(2) if finish and with_q else (None, None)
    q_out = take(1)[0] if with_q else None
    kv_out = take(1)[0] if with_kv else None
    x_buf = take(n_x)
    q_buf = take(1)[0] if with_q else None
    kv_buf = take(1)[0] if with_kv else None
    q_acc = take(1)[0] if finish and with_q else q_out
    kv_acc = take(1)[0] if finish and with_kv else kv_out
    x_sem, w_sem = take(2)

    x_copies = [pltpu.make_async_copy(xs[i], x_buf[i], x_sem.at[i]) for i in range(n_x)]
    w_copies = []
    started = set()
    for slot, uses in enumerate(plan):
        base = pl.multiple_of(widx[slot] * 512, 512)
        copies = []
        if with_q:
            copies.append(pltpu.make_async_copy(wq.at[pl.ds(base, 512), :], q_buf.at[slot], w_sem.at[slot, 0]))
        if with_kv:
            copies.append(
                pltpu.make_async_copy(wk.at[:, pl.ds(base, 512)], kv_buf.at[slot, pl.ds(0, 64), :], w_sem.at[slot, 1])
            )
            copies.append(
                pltpu.make_async_copy(wv.at[:, pl.ds(base, 512)], kv_buf.at[slot, pl.ds(64, 64), :], w_sem.at[slot, 2])
            )
        for use in uses:
            if use[0] not in started:
                x_copies[use[0]].start()
                started.add(use[0])
        for copy in copies:
            copy.start()
        w_copies.append(copies)

    if with_q:
        q_acc[...] = acc_q_in[...] if has_acc else jnp.zeros_like(q_acc)
    if with_kv:
        kv_acc[...] = acc_kv_in[...] if has_acc else jnp.zeros_like(kv_acc)
    arrived = set()
    for slot, uses in enumerate(plan):
        for copy in w_copies[slot]:
            copy.wait()
        for operand, row, count, target in uses:
            if operand not in arrived:
                x_copies[operand].wait()
                arrived.add(operand)
            piece = x_buf[operand][pl.ds(row, count), :]
            if with_kv:
                kv_acc[pl.ds(target, count), :] += lax.dot_general(
                    piece, kv_buf[slot], (((1,), (1,)), ((), ())), preferred_element_type=F32
                )
            if with_q:
                q_acc[pl.ds(target, count), :] += jnp.dot(piece, q_buf[slot], preferred_element_type=F32)
    if finish:
        if with_kv:
            kv_out[...] = kv_acc[...].astype(BF)
        if with_q:
            for head in range(q_out.shape[1] // HD):
                cols = slice(head * HD, (head + 1) * HD)
                part = q_acc[:, cols]
                q_out[:, cols] = (part * cos[...] + pltpu.roll(part, HD // 2, 1) * sin[...]).astype(BF)


def project(widx, xs, plan, weights, accs, with_q, with_kv, finish=False, tables=None):
    wq, wk, wv = weights
    rows = 512
    slots = len(plan)
    operands, specs = [widx], [SM]
    operands += xs
    specs += [ANY] * len(xs)
    if with_q:
        operands.append(wq)
        specs.append(ANY)
    if with_kv:
        operands += [wk, wv]
        specs += [ANY, ANY]
    has_acc = accs is not None
    if has_acc:
        if with_q:
            operands.append(accs[0])
            specs.append(VM)
        if with_kv:
            operands.append(accs[1])
            specs.append(VM)
    if finish and with_q:
        operands += list(tables)
        specs += [VM, VM]
    kind = BF if finish else F32
    outs, scratch = [], [pltpu.VMEM(x.shape, BF) for x in xs]
    if with_q:
        outs.append(jax.ShapeDtypeStruct((rows, 512), kind))
        scratch.append(pltpu.VMEM((slots, 512, 512), BF))
    if with_kv:
        outs.append(jax.ShapeDtypeStruct((rows, 128), kind))
        scratch.append(pltpu.VMEM((slots, 128, 512), BF))
    if finish and with_q:
        scratch.append(pltpu.VMEM((rows, 512), F32))
    if finish and with_kv:
        scratch.append(pltpu.VMEM((rows, 128), F32))
    scratch += [pltpu.SemaphoreType.DMA((len(xs),)), pltpu.SemaphoreType.DMA((slots, 3))]
    columns = (512 if with_q else 0) + (128 if with_kv else 0)
    used = sum(use[2] for uses in plan for use in uses)
    return pl.pallas_call(
        functools.partial(project_kernel, plan, len(xs), with_q, with_kv, has_acc, finish),
        out_shape=outs,
        in_specs=specs,
        out_specs=[VM] * len(outs),
        scratch_shapes=scratch,
        compiler_params=pltpu.CompilerParams(vmem_limit_bytes=VMEM_LIMIT),
        cost_estimate=pl.CostEstimate(
            flops=2 * used * 512 * columns, bytes_accessed=slots * 512 * columns * 2, transcendentals=0
        ),
    )(*operands)


def question_project_kernel(widx, x, wq, wk, wv, cos, sin, out, q_acc, kv_acc):
    step = pl.program_id(0)

    @pl.when(step == 0)
    def _():
        q_acc[...] = jnp.zeros_like(q_acc)
        kv_acc[...] = jnp.zeros_like(kv_acc)

    piece = x[...]
    turned = (((1,), (1,)), ((), ()))
    q_acc[...] += jnp.dot(piece, wq[...], preferred_element_type=F32)
    both = jnp.concatenate([wk[...], wv[...]], axis=0)
    kv_acc[...] += lax.dot_general(piece, both, turned, preferred_element_type=F32)

    @pl.when(step == pl.num_programs(0) - 1)
    def _():
        for head in range(4):
            cols = slice(head * HD, (head + 1) * HD)
            part = q_acc[:, cols]
            out[:, cols] = (part * cos[...] + pltpu.roll(part, HD // 2, 1) * sin[...]).astype(BF)
        out[:, 512:640] = kv_acc[...].astype(BF)


def question_project(widx, x, weights, cos, sin):
    wq, wk, wv = weights
    whole = lambda s, w: (0, 0)
    return pl.pallas_call(
        question_project_kernel,
        out_shape=jax.ShapeDtypeStruct((32, 640), BF),
        grid_spec=pltpu.PrefetchScalarGridSpec(
            num_scalar_prefetch=1,
            grid=(16,),
            in_specs=[
                pl.BlockSpec((32, 512), lambda s, w: (s, 0)),
                pl.BlockSpec((512, 512), lambda s, w: (w[s], 0)),
                pl.BlockSpec((64, 512), lambda s, w: (0, w[s])),
                pl.BlockSpec((64, 512), lambda s, w: (0, w[s])),
                pl.BlockSpec((32, HD), whole),
                pl.BlockSpec((32, HD), whole),
            ],
            out_specs=pl.BlockSpec((32, 640), whole),
            scratch_shapes=[pltpu.VMEM((32, 512), F32), pltpu.VMEM((32, 128), F32)],
        ),
        compiler_params=pltpu.CompilerParams(vmem_limit_bytes=VMEM_LIMIT),
        cost_estimate=pl.CostEstimate(flops=2 * 256 * 8192 * 640, bytes_accessed=8192 * 640 * 2, transcendentals=0),
    )(widx, x, wq, wk, wv, cos, sin)


def key_value_kernel(lower, own, partner, cos, sin, out):
    is_lower = lower[0] > 0
    mine, other = own[...].astype(F32), partner[...].astype(F32)
    low = jnp.where(is_lower, mine, other)
    high = jnp.where(is_lower, other, mine)
    lane = lax.broadcasted_iota(jnp.int32, low.shape, 1)
    keys = jnp.where(lane < 64, low, pltpu.roll(high, 64, 1))
    values = jnp.where(lane < 64, pltpu.roll(low, 64, 1), high)
    out[:, :HD] = (keys * cos[...] + pltpu.roll(keys, 64, 1) * sin[...]).astype(BF)
    out[:, HD:] = values.astype(BF)


def key_value(lower, own, partner, cos, sin):
    return pl.pallas_call(
        key_value_kernel,
        out_shape=jax.ShapeDtypeStruct((own.shape[0], 2 * HD), BF),
        in_specs=[SM, VM, VM, VM, VM],
        out_specs=VM,
        compiler_params=pltpu.CompilerParams(vmem_limit_bytes=VMEM_LIMIT),
    )(lower, own, partner, cos, sin)


def scores_of(queries, keys):
    return lax.dot_general(queries, keys, (((1,), (1,)), ((), ())), preferred_element_type=F32) * SCALE


def put_lane(ref, rows, lane_index, column):
    block = ref[rows, :]
    lane = lax.broadcasted_iota(jnp.int32, block.shape, 1)
    ref[rows, :] = jnp.where(lane == lane_index, column, block)


def own_kernel(limits, q, kv, weighted, stats):
    head = pl.program_id(0)
    length = limits[0]

    @pl.when(head == 0)
    def _():
        stats[...] = jnp.zeros_like(stats)

    for tile in range(2):
        rows = slice(tile * 256, tile * 256 + 256)
        width = 256 * (tile + 1)
        s = scores_of(q[rows, :], kv[:width, :HD])
        row = tile * 256 + lax.broadcasted_iota(jnp.int32, s.shape, 0)
        key = lax.broadcasted_iota(jnp.int32, s.shape, 1)
        s = jnp.where((key <= row) & (key < length), s, NEG)
        top = jnp.max(s, axis=1, keepdims=True)
        e = jnp.exp(s - top)
        total = jnp.sum(e, axis=1, keepdims=True)
        weighted[rows, :] = jnp.dot(e.astype(BF), kv[:width, HD:], preferred_element_type=F32)
        put_lane(stats, rows, head, top)
        put_lane(stats, rows, head + 4, total)


def own_attention(limits, q, kv):
    return pl.pallas_call(
        own_kernel,
        out_shape=[jax.ShapeDtypeStruct((512, 512), F32), jax.ShapeDtypeStruct((512, 128), F32)],
        grid=(4,),
        in_specs=[SM, pl.BlockSpec((512, HD), lambda h: (0, h)), pl.BlockSpec((512, 2 * HD), lambda h: (0, 0))],
        out_specs=[pl.BlockSpec((512, HD), lambda h: (0, h)), pl.BlockSpec((512, 128), lambda h: (0, 0))],
        compiler_params=pltpu.CompilerParams(vmem_limit_bytes=VMEM_LIMIT),
        cost_estimate=pl.CostEstimate(flops=4 * 4 * 512 * 512 * 128, bytes_accessed=3 << 20, transcendentals=1 << 20),
    )(limits, q, kv)


def lane_of(block, lane_index):
    lane = lax.broadcasted_iota(jnp.int32, block.shape, 1)
    return jnp.sum(jnp.where(lane == lane_index, block, 0.0), axis=1, keepdims=True)


def anchor_kernel(limits, q, kv, weighted, stats, out):
    head = pl.program_id(0)
    length, anchor_length = limits[0], limits[1]
    for tile in range(2):
        rows = slice(tile * 256, tile * 256 + 256)
        s = scores_of(q[rows, :], kv[:, :HD])
        key = lax.broadcasted_iota(jnp.int32, s.shape, 1)
        s = jnp.where(key < anchor_length, s, NEG)
        block = stats[rows, :]
        own_top, own_sum = lane_of(block, head), lane_of(block, head + 4)
        top = jnp.maximum(own_top, jnp.max(s, axis=1, keepdims=True))
        e = jnp.exp(s - top)
        factor = jnp.exp(own_top - top)
        total = own_sum * factor + jnp.sum(e, axis=1, keepdims=True)
        both = weighted[rows, :] * factor + jnp.dot(e.astype(BF), kv[:, HD:], preferred_element_type=F32)
        row = tile * 256 + lax.broadcasted_iota(jnp.int32, both.shape, 0)
        out[rows, :] = jnp.where(row < length, both / total, 0.0).astype(BF)


def anchor_attention(limits, q, kv, weighted, stats):
    return pl.pallas_call(
        anchor_kernel,
        out_shape=jax.ShapeDtypeStruct((512, 512), BF),
        grid=(4,),
        in_specs=[
            SM,
            pl.BlockSpec((512, HD), lambda h: (0, h)),
            pl.BlockSpec((512, 2 * HD), lambda h: (0, 0)),
            pl.BlockSpec((512, HD), lambda h: (0, h)),
            pl.BlockSpec((512, 128), lambda h: (0, 0)),
        ],
        out_specs=pl.BlockSpec((512, HD), lambda h: (0, h)),
        compiler_params=pltpu.CompilerParams(vmem_limit_bytes=VMEM_LIMIT),
        cost_estimate=pl.CostEstimate(flops=4 * 4 * 512 * 512 * 128, bytes_accessed=3 << 20, transcendentals=1 << 20),
    )(limits, q, kv, weighted, stats)


def question_kernel(limits, key_ids, q, kv, out):
    head = pl.program_id(0)
    length, first_row = limits[0], limits[2]

    @pl.when(head == 0)
    def _():
        out[:, 512:640] = jnp.zeros((256, 128), F32)

    s = scores_of(q[...], kv[:512, :HD])
    key = lax.broadcasted_iota(jnp.int32, s.shape, 1)
    s = jnp.where(key < length, s, NEG)
    top = jnp.max(s, axis=1, keepdims=True)
    e = jnp.exp(s - top)
    total = jnp.sum(e, axis=1, keepdims=True)
    both = jnp.dot(e.astype(BF), kv[:512, HD:], preferred_element_type=F32)

    s_self = scores_of(q[:32, :], kv[512:, :HD])
    row = first_row + lax.broadcasted_iota(jnp.int32, s_self.shape, 0)
    s_self = jnp.where(key_ids[...] <= row, s_self, NEG)
    top_self = jnp.maximum(top[:32], jnp.max(s_self, axis=1, keepdims=True))
    e_self = jnp.exp(s_self - top_self)
    factor = jnp.exp(top[:32] - top_self)
    total_self = total[:32] * factor + jnp.sum(e_self, axis=1, keepdims=True)
    both_self = both[:32] * factor + jnp.dot(e_self.astype(BF), kv[512:, HD:], preferred_element_type=F32)

    top = jnp.concatenate([top_self, top[32:]], axis=0)
    total = jnp.concatenate([total_self, total[32:]], axis=0)
    cols = pl.ds(pl.multiple_of(head * HD, HD), HD)
    out[:32, cols] = both_self
    out[32:, cols] = both[32:]
    block = out[:, 512:640]
    lane = lax.broadcasted_iota(jnp.int32, block.shape, 1)
    block = jnp.where(lane == head, top, block)
    out[:, 512:640] = jnp.where(lane == head + 4, total, block)


def question_attention(limits, key_ids, q, kv):
    return pl.pallas_call(
        question_kernel,
        out_shape=jax.ShapeDtypeStruct((256, 640), F32),
        grid=(4,),
        in_specs=[
            SM,
            pl.BlockSpec((1, 256), lambda h: (0, 0)),
            pl.BlockSpec((256, HD), lambda h: (0, h)),
            pl.BlockSpec((768, 2 * HD), lambda h: (0, 0)),
        ],
        out_specs=pl.BlockSpec((256, 640), lambda h: (0, 0)),
        compiler_params=pltpu.CompilerParams(vmem_limit_bytes=VMEM_LIMIT),
        cost_estimate=pl.CostEstimate(flops=4 * 4 * 256 * 512 * 128, bytes_accessed=2 << 20, transcendentals=1 << 19),
    )(limits, key_ids, q, kv)


def merge_kernel(finish, a, b, out):
    stat_a, stat_b = a[:, 512:640], b[:, 512:640]
    lane = lax.broadcasted_iota(jnp.int32, stat_a.shape, 1)
    stat = jnp.zeros_like(stat_a)
    for head in range(4):
        cols = slice(head * HD, (head + 1) * HD)
        top_a, top_b = stat_a[:, head : head + 1], stat_b[:, head : head + 1]
        top = jnp.maximum(top_a, top_b)
        factor_a, factor_b = jnp.exp(top_a - top), jnp.exp(top_b - top)
        total = stat_a[:, head + 4 : head + 5] * factor_a + stat_b[:, head + 4 : head + 5] * factor_b
        both = a[:, cols] * factor_a + b[:, cols] * factor_b
        if finish:
            out[:, cols] = (both / total).astype(BF)
        else:
            out[:, cols] = both
            stat = jnp.where(lane == head, top, stat)
            stat = jnp.where(lane == head + 4, total, stat)
    if not finish:
        out[:, 512:640] = stat


def merge(a, b, finish=False):
    rows = a.shape[0]
    return pl.pallas_call(
        functools.partial(merge_kernel, finish),
        out_shape=jax.ShapeDtypeStruct((rows, 512), BF) if finish else jax.ShapeDtypeStruct((rows, 640), F32),
        in_specs=[VM, VM],
        out_specs=VM,
        compiler_params=pltpu.CompilerParams(vmem_limit_bytes=VMEM_LIMIT),
    )(a, b)


def tables_of(positions):
    inverse_freq = ROPE_BASE ** (-(jnp.arange(HD // 2, dtype=jnp.float32) * 2.0 / HD))
    phases = positions.astype(jnp.float32)[:, None] * inverse_freq[None, :]
    cos, sin = jnp.cos(phases), jnp.sin(phases)
    return jnp.concatenate([cos, cos], axis=1), jnp.concatenate([-sin, sin], axis=1)


def rows_of(array, start, count):
    return lax.slice_in_dim(array, start, start + count, axis=0)


def per_device(context, question, w_query, w_key, w_value, lengths, owner):
    ctx = lax.axis_index("ctx")
    z, core = ctx // 2, ctx % 2
    heads = lax.axis_index("heads")
    y, x = heads // 4, heads % 4
    weights = (w_query, w_key.T, w_value.T)
    offsets = jnp.cumsum(lengths) - lengths
    filled = jnp.sum(lengths)
    own_length = lax.dynamic_index_in_dim(lengths, ctx, 0, keepdims=False)
    own_offset = lax.dynamic_index_in_dim(offsets, ctx, 0, keepdims=False)
    anchor_length = jnp.where(ctx > 0, lengths[0], 0)
    limits = jnp.stack([own_length, anchor_length, ctx * 32, ctx]).astype(jnp.int32)

    def block_index(dy, dx):
        return ((y + dy) % 4) * 4 + (x + dx) % 4

    def indices(places):
        return jnp.stack([block_index(dy, dx) for dy, dx in places]).astype(jnp.int32)

    low, high = rows_of(context, 0, 256), rows_of(context, 256, 256)
    up = shift_heads(context, 1, 0)
    down = shift_heads(context, -1, 0)
    right = shift_heads(context, 0, 1)
    left = shift_heads(context, 0, -1)
    far_y = shift_heads(low, 2, 0)
    far_x = shift_heads(high, 0, 2)

    z_order = (0, 1, 3, 2)
    asked = jnp.where(ctx == owner[0], question[0], jnp.zeros_like(question[0]))
    block_ids = [(z ^ mz) * 2 + (core ^ mc) for mz in z_order for mc in (0, 1)]

    def asked_block(place):
        return lax.dynamic_slice_in_dim(asked, block_ids[place] * 32, 32, 0)

    keep = jnp.concatenate([asked_block(p) for p in (0, 2, 4, 6)], axis=0)
    send = jnp.concatenate([asked_block(p) for p in (1, 3, 5, 7)], axis=0)
    share = keep + swap_ctx(send, 0, 1)
    blocks = share.reshape(4, 32, 512)
    share = jnp.concatenate([blocks[0], blocks[2]], axis=0) + swap_ctx(
        jnp.concatenate([blocks[1], blocks[3]], axis=0), 1, 0
    )
    share = rows_of(share, 0, 32) + swap_ctx(rows_of(share, 32, 32), 3, 0)
    share = jnp.concatenate([share, swap_heads(share, 1, 0)], axis=0)
    share = jnp.concatenate([share, swap_heads(share, 3, 0)], axis=0)
    share = jnp.concatenate([share, swap_heads(share, 0, 1)], axis=0)
    share = jnp.concatenate([share, swap_heads(share, 0, 3)], axis=0)
    question_index = jnp.stack([(y ^ my) * 4 + (x ^ mx) for mx in z_order for my in z_order]).astype(jnp.int32)

    slot_ids = jnp.arange(512, dtype=jnp.int32)
    key_ids = jnp.concatenate([block * 32 + jnp.arange(32, dtype=jnp.int32) for block in block_ids])
    cos, sin = tables_of(jnp.concatenate([own_offset + slot_ids, filled + key_ids]))

    plan_1 = [[(i, 0, 512, 0)] for i in range(5)] + [[(5, 0, 256, 0)], [(6, 0, 256, 256)]]
    places_1 = [(0, 0), (-1, 0), (1, 0), (0, -1), (0, 1), (2, 0), (0, 2)]
    accs = project(
        indices(places_1), [context, up, down, right, left, far_y, far_x], plan_1, weights, None, True, True
    )

    near_y = [rows_of(up, 0, 256), rows_of(down, 0, 256), far_y]
    near_x = [rows_of(right, 256, 256), rows_of(left, 256, 256), far_x]
    a_right = shift_heads(jnp.concatenate(near_y + [rows_of(right, 0, 128)], axis=0), 0, 1)
    a_left = shift_heads(jnp.concatenate(near_y + [rows_of(left, 128, 128)], axis=0), 0, -1)
    b_up = shift_heads(jnp.concatenate(near_x + [rows_of(up, 256, 128)], axis=0), 1, 0)
    b_down = shift_heads(jnp.concatenate(near_x + [rows_of(down, 384, 128)], axis=0), -1, 0)
    places_2 = [(-1, -1), (1, -1), (-1, 1), (1, 1), (2, -1), (2, 1), (-1, 2), (1, 2), (0, 2), (2, 0)]
    plan_2 = [
        [(0, 0, 256, 0), (2, 0, 256, 256)],
        [(0, 256, 256, 0), (3, 0, 256, 256)],
        [(1, 0, 256, 0), (2, 256, 256, 256)],
        [(1, 256, 256, 0), (3, 256, 256, 256)],
        [(0, 512, 256, 0)],
        [(1, 512, 256, 0)],
        [(2, 512, 256, 256)],
        [(3, 512, 256, 256)],
        [(0, 768, 128, 0), (1, 768, 128, 128)],
        [(2, 768, 128, 256), (3, 768, 128, 384)],
    ]
    accs = project(indices(places_2), [a_right, a_left, b_up, b_down], plan_2, weights, accs, True, True)

    c_right = shift_heads(rows_of(a_right, 0, 384), 0, 1)
    c_left = shift_heads(rows_of(a_left, 384, 384), 0, -1)
    d_up = shift_heads(rows_of(b_up, 0, 384), 1, 0)
    d_down = shift_heads(rows_of(b_down, 384, 384), -1, 0)
    places_3 = [(-1, 2), (1, 2), (2, 2), (2, -1), (2, 1)]
    plan_3 = [
        [(0, 0, 256, 0)],
        [(0, 256, 128, 0), (1, 0, 128, 128)],
        [(1, 128, 256, 0), (3, 128, 256, 256)],
        [(2, 0, 256, 256)],
        [(2, 256, 128, 256), (3, 0, 128, 384)],
    ]
    last = [c_right, c_left, d_up, d_down]
    index_3 = indices(places_3)
    (halves,) = project(index_3, last, plan_3, weights, accs, False, True, True)
    (queries,) = project(index_3, last, plan_3, weights, accs, True, False, True, (cos[:512], sin[:512]))

    q_share = question_project(question_index, share, weights, cos[512:544], sin[512:544])
    q_all = jnp.concatenate([q_share, swap_ctx(q_share, 0, 1)], axis=0)
    q_all = jnp.concatenate([q_all, swap_ctx(q_all, 1, 0)], axis=0)
    q_all = jnp.concatenate([q_all, swap_ctx(q_all, 3, 0)], axis=0)

    own_halves = jnp.concatenate([halves, q_all[:, 512:640]], axis=0)
    partner_halves = swap_heads(own_halves, 0, 1)
    lower = (1 - x % 2).astype(jnp.int32).reshape(1)
    kv_all = key_value(lower, own_halves, partner_halves, cos, sin)
    kv = rows_of(kv_all, 0, 512)
    to_1 = lax.ppermute(kv, "ctx", [(0, 2)])
    to_2 = lax.ppermute(kv, "ctx", [(0, 4)])
    to_3 = lax.ppermute(kv, "ctx", [(0, 6)])
    anchor = jnp.where(z == 0, kv, jnp.where(z == 1, to_1, jnp.where(z == 2, to_2, to_3)))
    across = lax.ppermute(anchor, "ctx", [(0, 1), (2, 3), (4, 5), (6, 7)])
    anchor = jnp.where(core == 0, anchor, across)

    part = question_attention(limits, key_ids[None, :], q_all, kv_all)
    blocks = part.reshape(4, 2, 32, 640)
    part = merge(blocks[:, 0].reshape(128, 640), swap_ctx(blocks[:, 1].reshape(128, 640), 0, 1))
    blocks = part.reshape(4, 32, 640)
    part = merge(
        jnp.concatenate([blocks[0], blocks[2]], axis=0),
        swap_ctx(jnp.concatenate([blocks[1], blocks[3]], axis=0), 1, 0),
    )
    question_attn = merge(rows_of(part, 0, 32), swap_ctx(rows_of(part, 32, 32), 3, 0), True)

    weighted, stats = own_attention(limits, queries, kv)
    context_attn = anchor_attention(limits, queries, anchor, weighted, stats)
    return (context_attn, question_attn)


def solution(mesh):
    in_specs = (
        P("ctx", "heads"),
        P("ctx", None, "heads"),
        P(None, "heads"),
        P(None, "heads"),
        P(None, "heads"),
        P(),
        P(),
    )
    out_specs = (P("ctx", "heads"), P("ctx", "heads"))
    return jax.shard_map(
        per_device, mesh=mesh, in_specs=in_specs, out_specs=out_specs, check_vma=False
    )
```

```python
import functools

import jax
import jax.numpy as jnp
from jax import lax
from jax.experimental import pallas as pl
from jax.experimental.pallas import tpu as pltpu
from jax.sharding import PartitionSpec as P

HD = 128
ROPE_BASE = 500000.0
BF = jnp.bfloat16
F32 = jnp.float32
VMEM_LIMIT = 24 * 1024 * 1024
NEG = -1e30
SCALE2 = HD ** (-0.5) * 1.4426950408889634
ROWS = 544

ANY = pl.BlockSpec(memory_space=pl.ANY)
VM = pl.BlockSpec(memory_space=pltpu.VMEM)
SM = pl.BlockSpec(memory_space=pltpu.SMEM)


def shift_heads(array, dy, dx):
    pairs = [(i, ((i // 4 + dy) % 4) * 4 + (i % 4 + dx) % 4) for i in range(16)]
    return lax.ppermute(array, "heads", pairs)


def swap_heads(array, my, mx):
    pairs = [(i, ((i // 4) ^ my) * 4 + ((i % 4) ^ mx)) for i in range(16)]
    return lax.ppermute(array, "heads", pairs)


def swap_ctx(array, mz, mc):
    pairs = [(i, ((i // 2) ^ mz) * 2 + ((i % 2) ^ mc)) for i in range(8)]
    return lax.ppermute(array, "ctx", pairs)


def pack_kernel(plan, n_in, *refs):
    ins, outs, sem = refs[:n_in], refs[n_in:-1], refs[-1]
    copies = []
    for out, pieces in zip(outs, plan):
        row = 0
        for operand, start, count in pieces:
            source = ins[operand].at[pl.ds(start, count), :]
            copies.append(pltpu.make_async_copy(source, out.at[pl.ds(row, count), :], sem.at[len(copies)]))
            row += count
    for copy in copies:
        copy.start()
    for copy in copies:
        copy.wait()


def pack(plan, ins):
    outs = [jax.ShapeDtypeStruct((sum(p[2] for p in pieces), 512), BF) for pieces in plan]
    return pl.pallas_call(
        functools.partial(pack_kernel, plan, len(ins)),
        out_shape=outs,
        in_specs=[ANY] * len(ins),
        out_specs=[ANY] * len(outs),
        scratch_shapes=[pltpu.SemaphoreType.DMA((sum(len(p) for p in plan),))],
        compiler_params=pltpu.CompilerParams(vmem_limit_bytes=1 << 20),
        cost_estimate=pl.CostEstimate(flops=0, bytes_accessed=4 << 20, transcendentals=0),
    )(*ins)


def project_kernel(plan, n_x, with_q, with_kv, has_acc, finish, *refs):
    refs = list(refs)
    take = lambda count: [refs.pop(0) for _ in range(count)]
    (info,) = take(1)
    xs = take(n_x)
    wq = take(1)[0] if with_q else None
    wk, wv = take(2) if with_kv else (None, None)
    acc_q = take(1)[0] if has_acc and with_q else None
    acc_kv = take(1)[0] if has_acc and with_kv else None
    cos, sin = take(2) if finish and with_q else (None, None)
    if finish and with_q:
        question_out, context_out = take(2)
        q_out = None
    else:
        q_out = take(1)[0] if with_q else None
    kv_out = take(1)[0] if with_kv else None
    q_sum = take(1)[0] if finish and with_q else q_out
    kv_sum = take(1)[0] if finish and with_kv else kv_out
    y, x = info[0], info[1]
    odd = y % 2 == 1

    def load(use):
        if use[0] == "row":
            start = pl.multiple_of(jnp.where(odd, use[2], use[3]), 16)
            return xs[use[1]][pl.ds(start, 32), :]
        if use[0] == "pick":
            (one, row_one), (two, row_two) = use[1:]
            return jnp.where(odd, xs[one][pl.ds(row_one, 32), :], xs[two][pl.ds(row_two, 32), :])
        return xs[use[0]][pl.ds(use[1], use[2]), :]

    if has_acc:
        if with_q:
            q_sum[...] = acc_q[...]
        if with_kv:
            kv_sum[...] = acc_kv[...]
    for slot, ((dy, dx), low, high, uses) in enumerate(plan):
        base = pl.multiple_of((((y + dy + 4) % 4) * 4 + (x + dx + 4) % 4) * 512, 512)
        parts = [load(use) for use in uses]
        piece = parts[0] if len(parts) == 1 else jnp.concatenate(parts, axis=0)
        fresh = slot == 0 and not has_acc
        if with_kv:
            both = jnp.concatenate([wk[:, pl.ds(base, 512)], wv[:, pl.ds(base, 512)]], axis=0)
            term = lax.dot_general(piece, both, (((1,), (1,)), ((), ())), preferred_element_type=F32)
            kv_sum[low:high, :] = term if fresh else kv_sum[low:high, :] + term
        if with_q:
            term = jnp.dot(piece, wq[pl.ds(base, 512), :], preferred_element_type=F32)
            q_sum[low:high, :] = term if fresh else q_sum[low:high, :] + term
    if finish and with_kv:
        kv_out[...] = kv_sum[...].astype(BF)
    if finish and with_q:
        for head in range(4):
            cols = slice(head * HD, (head + 1) * HD)
            part = q_sum[:, cols]
            turned = (part * cos[...] + pltpu.roll(part, HD // 2, 1) * sin[...]).astype(BF)
            question_out[:, cols] = turned[:32]
            context_out[:, cols] = turned[32:]


def project(info, xs, plan, weights, accs, with_q, with_kv, finish=False, tables=None):
    wq, wk, wv = weights
    operands, specs = [info] + list(xs), [SM] + [VM] * len(xs)
    if with_q:
        operands.append(wq)
        specs.append(VM)
    if with_kv:
        operands += [wk, wv]
        specs += [VM, VM]
    has_acc = accs is not None
    if has_acc:
        if with_q:
            operands.append(accs[0])
            specs.append(VM)
        if with_kv:
            operands.append(accs[1])
            specs.append(VM)
    if finish and with_q:
        operands += list(tables)
        specs += [VM, VM]
    outs, scratch = [], []
    if with_q and finish:
        outs += [jax.ShapeDtypeStruct((32, 512), BF), jax.ShapeDtypeStruct((512, 512), BF)]
        scratch.append(pltpu.VMEM((ROWS, 512), F32))
    elif with_q:
        outs.append(jax.ShapeDtypeStruct((ROWS, 512), F32))
    if with_kv:
        outs.append(jax.ShapeDtypeStruct((ROWS, 128), BF if finish else F32))
        if finish:
            scratch.append(pltpu.VMEM((ROWS, 128), F32))
    columns = (512 if with_q else 0) + (128 if with_kv else 0)
    used = sum(high - low for _, low, high, _ in plan)
    return pl.pallas_call(
        functools.partial(project_kernel, plan, len(xs), with_q, with_kv, has_acc, finish),
        out_shape=outs,
        in_specs=specs,
        out_specs=[VM] * len(outs),
        scratch_shapes=scratch,
        compiler_params=pltpu.CompilerParams(vmem_limit_bytes=VMEM_LIMIT),
        cost_estimate=pl.CostEstimate(
            flops=2 * used * 512 * columns, bytes_accessed=len(plan) * 512 * columns * 2, transcendentals=0
        ),
    )(*operands)


def key_value_kernel(info, own, partner, cos, sin, out):
    is_lower = info[1] % 2 == 0
    mine, other = own[...].astype(F32), partner[...].astype(F32)
    low = jnp.where(is_lower, mine, other)
    high = jnp.where(is_lower, other, mine)
    lane = lax.broadcasted_iota(jnp.int32, low.shape, 1)
    keys = jnp.where(lane < 64, low, pltpu.roll(high, 64, 1))
    values = jnp.where(lane < 64, pltpu.roll(low, 64, 1), high)
    out[:, :HD] = (keys * cos[...] + pltpu.roll(keys, 64, 1) * sin[...]).astype(BF)
    out[:, HD:] = values.astype(BF)


def key_value(info, own, partner, cos, sin):
    return pl.pallas_call(
        key_value_kernel,
        out_shape=jax.ShapeDtypeStruct((ROWS, 2 * HD), BF),
        in_specs=[SM, VM, VM, VM, VM],
        out_specs=VM,
        compiler_params=pltpu.CompilerParams(vmem_limit_bytes=VMEM_LIMIT),
    )(info, own, partner, cos, sin)


def scores_of(queries, keys):
    return lax.dot_general(queries, keys, (((1,), (1,)), ((), ())), preferred_element_type=F32)


def weights_of(scores, top):
    return jnp.exp2(scores * SCALE2 - top * SCALE2)


def columns_to_stats(columns):
    rows = columns[0].shape[0]
    lane = lax.broadcasted_iota(jnp.int32, (rows, 128), 1)
    stats = jnp.zeros((rows, 128), F32)
    for index, column in enumerate(columns):
        stats = jnp.where(lane == index, column, stats)
    return stats


def own_kernel(info, q, kv, weighted, stats):
    length = info[5]
    for tile in range(2):
        rows = slice(tile * 256, tile * 256 + 256)
        width = 256 * (tile + 1)
        row = tile * 256 + lax.broadcasted_iota(jnp.int32, (256, width), 0)
        key = lax.broadcasted_iota(jnp.int32, (256, width), 1)
        bias = jnp.where((key <= row) & (key < length), 0.0, NEG)
        tops, totals = [], []
        for head in range(4):
            cols = slice(head * HD, (head + 1) * HD)
            s = scores_of(q[rows, cols], kv[32 : 32 + width, :HD]) + bias
            top = jnp.max(s, axis=1, keepdims=True)
            e = weights_of(s, top)
            totals.append(jnp.sum(e, axis=1, keepdims=True))
            tops.append(top)
            weighted[rows, cols] = jnp.dot(e.astype(BF), kv[32 : 32 + width, HD:], preferred_element_type=F32)
        stats[rows, :] = columns_to_stats(tops + totals)


def own_attention(info, q, kv):
    return pl.pallas_call(
        own_kernel,
        out_shape=[jax.ShapeDtypeStruct((512, 512), F32), jax.ShapeDtypeStruct((512, 128), F32)],
        in_specs=[SM, VM, VM],
        out_specs=[VM, VM],
        compiler_params=pltpu.CompilerParams(vmem_limit_bytes=VMEM_LIMIT),
        cost_estimate=pl.CostEstimate(flops=4 * 4 * 512 * 512 * 128, bytes_accessed=3 << 20, transcendentals=1 << 20),
    )(info, q, kv)


def anchor_kernel(info, q, kv_zero, kv_one, weighted, stats, out):
    length, anchor_length = info[5], info[6]
    first_core = info[3] == 0
    kv = jnp.where(first_core, kv_zero[...], kv_one[...])
    keys, values = kv[:, :HD], kv[:, HD:]
    key = lax.broadcasted_iota(jnp.int32, (1, 512), 1)
    bias = jnp.where(key < anchor_length, 0.0, NEG)
    for tile in range(2):
        rows = slice(tile * 256, tile * 256 + 256)
        block = stats[rows, :]
        row = tile * 256 + lax.broadcasted_iota(jnp.int32, (256, HD), 0)
        for head in range(4):
            cols = slice(head * HD, (head + 1) * HD)
            s = scores_of(q[rows, cols], keys) + bias
            own_top, own_sum = block[:, head : head + 1], block[:, head + 4 : head + 5]
            top = jnp.maximum(own_top, jnp.max(s, axis=1, keepdims=True))
            e = weights_of(s, top)
            factor = weights_of(own_top, top)
            total = own_sum * factor + jnp.sum(e, axis=1, keepdims=True)
            both = weighted[rows, cols] * factor + jnp.dot(e.astype(BF), values, preferred_element_type=F32)
            out[rows, cols] = jnp.where(row < length, both / total, 0.0).astype(BF)


def anchor_attention(info, q, kv_zero, kv_one, weighted, stats):
    return pl.pallas_call(
        anchor_kernel,
        out_shape=jax.ShapeDtypeStruct((512, 512), BF),
        in_specs=[SM, VM, VM, VM, VM, VM],
        out_specs=VM,
        compiler_params=pltpu.CompilerParams(vmem_limit_bytes=VMEM_LIMIT),
        cost_estimate=pl.CostEstimate(flops=4 * 4 * 512 * 512 * 128, bytes_accessed=3 << 20, transcendentals=1 << 20),
    )(info, q, kv_zero, kv_one, weighted, stats)


def question_kernel(info, q_own, q_other, kv_0, kv_1, kv_2, kv_3, out_own, out_other):
    kvs = (kv_0, kv_1, kv_2, kv_3)
    z, core, ctx = info[2], info[3], info[4]
    lengths = [info[5], info[7], info[8], info[9]]
    places = [z, (z + 3) % 4, (z + 1) % 4, (z + 2) % 4]
    stacked = [q_own[:, h * HD : (h + 1) * HD] for h in range(4)]
    stacked += [q_other[:, h * HD : (h + 1) * HD] for h in range(4)]
    q = jnp.concatenate(stacked, axis=0)
    scores = []
    key = lax.broadcasted_iota(jnp.int32, (1, 512), 1)
    for kv, length in zip(kvs, lengths):
        scores.append(scores_of(q, kv[32:, :HD]) + jnp.where(key < length, 0.0, NEG))
    row = lax.broadcasted_iota(jnp.int32, (256, 128), 0)
    lane = lax.broadcasted_iota(jnp.int32, (256, 128), 1)
    row_id = row % 32 + 32 * jnp.where(row < 128, ctx, ctx + 1 - 2 * core)
    block = jnp.where(lane < 64, jnp.where(lane < 32, places[0], places[1]), jnp.where(lane < 96, places[2], places[3]))
    key_id = lane % 32 + 32 * (2 * block + core)
    asked_keys = jnp.concatenate([kv[:32, :HD] for kv in kvs], axis=0)
    asked_values = jnp.concatenate([kv[:32, HD:] for kv in kvs], axis=0)
    scores.append(jnp.where(key_id <= row_id, scores_of(q, asked_keys), NEG))
    top = jnp.max(scores[-1], axis=1, keepdims=True)
    for s in scores[:-1]:
        top = jnp.maximum(top, jnp.max(s, axis=1, keepdims=True))
    values = [kv[32:, HD:] for kv in kvs] + [asked_values]
    total = jnp.zeros((256, 1), F32)
    both = jnp.zeros((256, HD), F32)
    for s, value in zip(scores, values):
        e = weights_of(s, top)
        total = total + jnp.sum(e, axis=1, keepdims=True)
        both = both + jnp.dot(e.astype(BF), value, preferred_element_type=F32)
    for out, start in ((out_own, 0), (out_other, 128)):
        tops, totals = [], []
        for head in range(4):
            rows = slice(start + head * 32, start + head * 32 + 32)
            out[:, head * HD : (head + 1) * HD] = both[rows]
            tops.append(top[rows])
            totals.append(total[rows])
        out[:, 512:640] = columns_to_stats(tops + totals)


def question_attention(info, q_own, q_other, kvs):
    part = jax.ShapeDtypeStruct((32, 640), F32)
    return pl.pallas_call(
        question_kernel,
        out_shape=[part, part],
        in_specs=[SM] + [VM] * 6,
        out_specs=[VM, VM],
        compiler_params=pltpu.CompilerParams(vmem_limit_bytes=VMEM_LIMIT),
        cost_estimate=pl.CostEstimate(flops=4 * 256 * 2176 * 128, bytes_accessed=2 << 20, transcendentals=1 << 19),
    )(info, q_own, q_other, *kvs)


def merge_kernel(a, b, out):
    stat_a, stat_b = a[:, 512:640], b[:, 512:640]
    for head in range(4):
        cols = slice(head * HD, (head + 1) * HD)
        top_a, top_b = stat_a[:, head : head + 1], stat_b[:, head : head + 1]
        top = jnp.maximum(top_a, top_b)
        factor_a, factor_b = weights_of(top_a, top), weights_of(top_b, top)
        total = stat_a[:, head + 4 : head + 5] * factor_a + stat_b[:, head + 4 : head + 5] * factor_b
        out[:, cols] = ((a[:, cols] * factor_a + b[:, cols] * factor_b) / total).astype(BF)


def merge(a, b):
    return pl.pallas_call(
        merge_kernel,
        out_shape=jax.ShapeDtypeStruct((32, 512), BF),
        in_specs=[VM, VM],
        out_specs=VM,
        compiler_params=pltpu.CompilerParams(vmem_limit_bytes=VMEM_LIMIT),
    )(a, b)


PLAN_1 = [
    ((0, 0), 0, 544, [(7, 0, 32), (0, 0, 512)]),
    ((-1, 0), 0, 544, [("row", 7, 32, 64), (1, 0, 512)]),
    ((1, 0), 0, 544, [("row", 7, 64, 32), (2, 0, 512)]),
    ((2, 0), 0, 256, [(7, 96, 32), (5, 0, 224)]),
    ((0, -1), 32, 544, [(3, 0, 512)]),
    ((0, 1), 32, 544, [(4, 0, 512)]),
    ((0, 2), 256, 544, [(6, 0, 288)]),
]
PLAN_2 = [
    ((-1, -1), 0, 544, [("row", 0, 368, 736), (0, 0, 224), (2, 0, 288)]),
    ((1, -1), 0, 544, [("row", 0, 736, 368), (0, 224, 112), (0, 400, 112), (3, 0, 288)]),
    ((2, -1), 0, 256, [(0, 768, 32), (0, 512, 224)]),
    ((0, -1), 0, 32, [(0, 336, 32)]),
    ((-1, 1), 0, 544, [("row", 1, 368, 736), (1, 0, 224), (2, 288, 288)]),
    ((1, 1), 0, 544, [("row", 1, 736, 368), (1, 224, 112), (1, 400, 112), (3, 288, 288)]),
    ((2, 1), 0, 256, [(1, 768, 32), (1, 512, 224)]),
    ((0, 1), 0, 32, [(1, 336, 32)]),
    ((-1, 2), 256, 544, [(2, 576, 288)]),
    ((1, 2), 256, 544, [(3, 576, 288)]),
    ((0, 2), 32, 256, [(0, 800, 112), (1, 800, 112)]),
    ((2, 0), 256, 544, [(2, 864, 144), (3, 864, 144)]),
]
PLAN_3 = [
    ((2, 2), 0, 544, [(1, 368, 32), (1, 112, 224), (3, 144, 288)]),
    ((-1, 2), 0, 256, [("pick", (0, 368), (1, 336)), (0, 0, 224)]),
    ((1, 2), 0, 256, [("pick", (1, 336), (0, 368)), (0, 224, 112), (1, 0, 112)]),
    ((0, 2), 0, 32, [(0, 336, 32)]),
    ((2, -1), 256, 544, [(2, 0, 288)]),
    ((2, 1), 256, 544, [(2, 288, 144), (3, 0, 144)]),
]
NEAR_Y = [(0, 0, 224), (1, 0, 112), (6, 0, 64), (1, 112, 112), (4, 0, 224), (6, 64, 64)]
NEAR_X = [(2, 224, 288), (3, 224, 288), (5, 0, 288)]
PACK_2 = [
    NEAR_Y + [(2, 0, 112)],
    NEAR_Y + [(3, 112, 112)],
    NEAR_X + [(0, 224, 144)],
    NEAR_X + [(1, 368, 144)],
]
PACK_3 = [[(0, 0, 400)], [(1, 400, 400)], [(2, 0, 432)], [(3, 432, 432)]]


def tables_of(positions):
    exponents = -(jnp.arange(HD // 2, dtype=jnp.float32) * 2.0 / HD)
    inverse_freq = ROPE_BASE ** jnp.concatenate([exponents, exponents])
    phases = positions.astype(jnp.float32)[:, None] * inverse_freq[None, :]
    signs = jnp.where(jnp.arange(HD) < HD // 2, -1.0, 1.0).astype(jnp.float32)
    return jnp.cos(phases), jnp.sin(phases) * signs[None, :]


def shift_z(array, dz):
    pairs = [(i, ((i // 2 + dz) % 4) * 2 + i % 2) for i in range(8)]
    return lax.ppermute(array, "ctx", pairs)


def per_device(context, question, w_query, w_key, w_value, lengths, owner):
    ctx = lax.axis_index("ctx")
    z, core = ctx // 2, ctx % 2
    heads = lax.axis_index("heads")
    y, x = heads // 4, heads % 4
    weights = (w_query, w_key.T, w_value.T)
    ids = jnp.arange(8, dtype=jnp.int32)
    own_offset = jnp.sum(jnp.where(ids < ctx, lengths, 0))
    filled = jnp.sum(lengths)

    def length_of(dz):
        return jnp.sum(jnp.where(ids == ((z + dz) % 4) * 2 + core, lengths, 0))

    anchor_length = jnp.where(ctx > 0, lengths[0], 0)
    info = jnp.stack(
        [y, x, z, core, ctx, length_of(0), anchor_length, length_of(3), length_of(1), length_of(2)]
    ).astype(jnp.int32)

    up = shift_heads(context, 1, 0)
    down = shift_heads(context, -1, 0)
    right = shift_heads(context, 0, 1)
    left = shift_heads(context, 0, -1)
    far_y = shift_heads(lax.slice_in_dim(context, 0, 224, axis=0), 2, 0)
    far_x = shift_heads(lax.slice_in_dim(context, 224, 512, axis=0), 0, 2)

    rows = question[0].reshape(4, 2, 32, 512)
    mine = ctx == owner[0]
    keep = jnp.where(mine, lax.dynamic_index_in_dim(rows, core, 1, False), 0)
    send = jnp.where(mine, lax.dynamic_index_in_dim(rows, 1 - core, 1, False), 0)
    share = keep + swap_ctx(send, 0, 1)
    outer = jnp.concatenate([share[0], share[3]], axis=0)
    inner = jnp.concatenate([share[1], share[2]], axis=0)
    is_outer = (z == 0) | (z == 3)
    share = jnp.where(is_outer, outer, inner) + swap_ctx(jnp.where(is_outer, inner, outer), 1, 0)
    share = jnp.where(z < 2, share[:32], share[32:]) + swap_ctx(jnp.where(z < 2, share[32:], share[:32]), 3, 0)
    share = jnp.concatenate([share, swap_heads(share, 1, 0)], axis=0)
    share = jnp.concatenate([share, swap_heads(share, 3, 0)], axis=0)

    cos, sin = tables_of(
        jnp.concatenate(
            [filled + 32 * ctx + jnp.arange(32, dtype=jnp.int32), own_offset + jnp.arange(512, dtype=jnp.int32)]
        )
    )

    to_right, to_left, to_up, to_down = pack(PACK_2, [up, down, right, left, far_y, far_x, share])
    a_right = shift_heads(to_right, 0, 1)
    a_left = shift_heads(to_left, 0, -1)
    b_up = shift_heads(to_up, 1, 0)
    b_down = shift_heads(to_down, -1, 0)
    accs = project(info, [context, up, down, right, left, far_y, far_x, share], PLAN_1, weights, None, True, True)

    to_right, to_left, to_up, to_down = pack(PACK_3, [a_right, a_left, b_up, b_down])
    c_right = shift_heads(to_right, 0, 1)
    c_left = shift_heads(to_left, 0, -1)
    d_up = shift_heads(to_up, 1, 0)
    d_down = shift_heads(to_down, -1, 0)
    accs = project(info, [a_right, a_left, b_up, b_down], PLAN_2, weights, accs, True, True)

    last = [c_right, c_left, d_up, d_down]
    (halves,) = project(info, last, PLAN_3, weights, accs, False, True, True)
    q_asked, queries = project(info, last, PLAN_3, weights, accs, True, False, True, (cos, sin))

    kv = key_value(info, halves, swap_heads(halves, 0, 1), cos, sin)
    below = shift_z(kv, 1)
    above = shift_z(kv, -1)
    across = shift_z(kv, 2)
    weighted, stats = own_attention(info, queries, kv)
    nearer = jnp.where(z == 0, kv[32:], jnp.where(z == 1, below[32:], jnp.where(z == 2, across[32:], above[32:])))
    from_zero = lax.ppermute(nearer, "ctx", [(0, 1), (2, 3), (4, 5), (6, 7)])
    q_other = swap_ctx(q_asked, 0, 1)
    part, part_other = question_attention(info, q_asked, q_other, [kv, below, above, across])
    context_attn = anchor_attention(info, queries, nearer, from_zero, weighted, stats)
    question_attn = merge(part, swap_ctx(part_other, 0, 1))
    return (context_attn, question_attn)


def solution(mesh):
    in_specs = (
        P("ctx", "heads"),
        P("ctx", None, "heads"),
        P(None, "heads"),
        P(None, "heads"),
        P(None, "heads"),
        P(),
        P(),
    )
    out_specs = (P("ctx", "heads"), P("ctx", "heads"))
    return jax.shard_map(
        per_device, mesh=mesh, in_specs=in_specs, out_specs=out_specs, check_vma=False
    )
```

```python
import functools

import jax
import jax.numpy as jnp
from jax import lax
from jax.experimental import pallas as pl
from jax.experimental.pallas import tpu as pltpu
from jax.sharding import PartitionSpec as P

HD = 128
ROPE_BASE = 500000.0
BF = jnp.bfloat16
F32 = jnp.float32
VMEM_LIMIT = 24 * 1024 * 1024
NEG = -1e30
SCALE2 = HD ** (-0.5) * 1.4426950408889634
ROWS = 512
ASKED = 256
ALL = ROWS + ASKED
Z_ORDER = (0, 1, 3, 2)

ANY = pl.BlockSpec(memory_space=pl.ANY)
VM = pl.BlockSpec(memory_space=pltpu.VMEM)
SM = pl.BlockSpec(memory_space=pltpu.SMEM)


def shift_heads(array, dy, dx):
    pairs = [(i, ((i // 4 + dy) % 4) * 4 + (i % 4 + dx) % 4) for i in range(16)]
    return lax.ppermute(array, "heads", pairs)


def swap_heads(array, my, mx):
    pairs = [(i, ((i // 4) ^ my) * 4 + ((i % 4) ^ mx)) for i in range(16)]
    return lax.ppermute(array, "heads", pairs)


def swap_ctx(array, mz, mc):
    pairs = [(i, ((i // 2) ^ mz) * 2 + ((i % 2) ^ mc)) for i in range(8)]
    return lax.ppermute(array, "ctx", pairs)


def pack_kernel(plan, n_in, *refs):
    ins, outs, sem = refs[:n_in], refs[n_in:-1], refs[-1]
    copies = []
    for out, pieces in zip(outs, plan):
        row = 0
        for operand, start, count in pieces:
            source = ins[operand].at[pl.ds(start, count), :]
            copies.append(pltpu.make_async_copy(source, out.at[pl.ds(row, count), :], sem.at[len(copies)]))
            row += count
    for copy in copies:
        copy.start()
    for copy in copies:
        copy.wait()


def pack(plan, ins):
    outs = [jax.ShapeDtypeStruct((sum(p[2] for p in pieces), 512), BF) for pieces in plan]
    return pl.pallas_call(
        functools.partial(pack_kernel, plan, len(ins)),
        out_shape=outs,
        in_specs=[ANY] * len(ins),
        out_specs=[ANY] * len(outs),
        scratch_shapes=[pltpu.SemaphoreType.DMA((sum(len(p) for p in plan),))],
        compiler_params=pltpu.CompilerParams(vmem_limit_bytes=1 << 20),
        cost_estimate=pl.CostEstimate(flops=0, bytes_accessed=4 << 20, transcendentals=0),
    )(*ins)


def turn(part, cos, sin):
    return (part * cos + pltpu.roll(part, HD // 2, 1) * sin).astype(BF)


def project_kernel(plan, n_x, with_q, with_kv, has_acc, finish, *refs):
    refs = list(refs)
    take = lambda count: [refs.pop(0) for _ in range(count)]
    (info,) = take(1)
    xs = take(n_x)
    wq = take(1)[0] if with_q else None
    wk, wv = take(2) if with_kv else (None, None)
    acc_q = take(1)[0] if has_acc and with_q else None
    acc_kv = take(1)[0] if has_acc and with_kv else None
    cos, sin = take(2) if finish and with_q else (None, None)
    asked = take(1)[0] if finish and with_kv else None
    q_out = take(1)[0] if with_q else None
    kv_out = take(1)[0] if with_kv else None
    q_sum = take(1)[0] if finish and with_q else q_out
    kv_sum = take(1)[0] if finish and with_kv else kv_out
    y, x = info[0], info[1]
    if has_acc:
        if with_q:
            q_sum[...] = acc_q[...]
        if with_kv:
            kv_sum[...] = acc_kv[...]
    for slot, ((dy, dx), low, high, uses) in enumerate(plan):
        base = pl.multiple_of((((y + dy + 4) % 4) * 4 + (x + dx + 4) % 4) * 512, 512)
        parts = [xs[operand][pl.ds(start, count), :] for operand, start, count in uses]
        piece = parts[0] if len(parts) == 1 else jnp.concatenate(parts, axis=0)
        fresh = slot == 0 and not has_acc
        if with_kv:
            both = jnp.concatenate([wk[:, pl.ds(base, 512)], wv[:, pl.ds(base, 512)]], axis=0)
            term = lax.dot_general(piece, both, (((1,), (1,)), ((), ())), preferred_element_type=F32)
            kv_sum[low:high, :] = term if fresh else kv_sum[low:high, :] + term
        if with_q:
            term = jnp.dot(piece, wq[pl.ds(base, 512), :], preferred_element_type=F32)
            q_sum[low:high, :] = term if fresh else q_sum[low:high, :] + term
    if finish and with_kv:
        kv_out[:ROWS, :] = kv_sum[...].astype(BF)
        kv_out[ROWS:, :] = asked[:, 512:640]
    if finish and with_q:
        for head in range(4):
            cols = slice(head * HD, (head + 1) * HD)
            q_out[:, cols] = turn(q_sum[:, cols], cos[:ROWS, :], sin[:ROWS, :])


def project(info, xs, plan, weights, accs, with_q, with_kv, finish=False, tables=None, asked=None):
    wq, wk, wv = weights
    operands, specs = [info] + list(xs), [SM] + [VM] * len(xs)
    if with_q:
        operands.append(wq)
        specs.append(VM)
    if with_kv:
        operands += [wk, wv]
        specs += [VM, VM]
    has_acc = accs is not None
    if has_acc:
        if with_q:
            operands.append(accs[0])
            specs.append(VM)
        if with_kv:
            operands.append(accs[1])
            specs.append(VM)
    if finish and with_q:
        operands += list(tables)
        specs += [VM, VM]
    if finish and with_kv:
        operands.append(asked)
        specs.append(VM)
    outs, scratch = [], []
    if with_q:
        outs.append(jax.ShapeDtypeStruct((ROWS, 512), BF if finish else F32))
        if finish:
            scratch.append(pltpu.VMEM((ROWS, 512), F32))
    if with_kv:
        outs.append(jax.ShapeDtypeStruct((ALL, 128), BF) if finish else jax.ShapeDtypeStruct((ROWS, 128), F32))
        if finish:
            scratch.append(pltpu.VMEM((ROWS, 128), F32))
    columns = (512 if with_q else 0) + (128 if with_kv else 0)
    used = sum(high - low for _, low, high, _ in plan)
    return pl.pallas_call(
        functools.partial(project_kernel, plan, len(xs), with_q, with_kv, has_acc, finish),
        out_shape=outs,
        in_specs=specs,
        out_specs=[VM] * len(outs),
        scratch_shapes=scratch,
        compiler_params=pltpu.CompilerParams(vmem_limit_bytes=VMEM_LIMIT),
        cost_estimate=pl.CostEstimate(
            flops=2 * used * 512 * columns, bytes_accessed=len(plan) * 512 * columns * 2, transcendentals=0
        ),
    )(*operands)


def question_project_kernel(info, pieces, wq, wk, wv, cos, sin, out):
    y, x = info[0], info[1]
    q_sum, kv_sum = None, None
    for place in range(16):
        mx, my = Z_ORDER[place // 4], Z_ORDER[place % 4]
        base = pl.multiple_of(((y ^ my) * 4 + (x ^ mx)) * 512, 512)
        piece = pieces[pl.ds(place * 32, 32), :]
        both = jnp.concatenate([wk[:, pl.ds(base, 512)], wv[:, pl.ds(base, 512)]], axis=0)
        kv_term = lax.dot_general(piece, both, (((1,), (1,)), ((), ())), preferred_element_type=F32)
        q_term = jnp.dot(piece, wq[pl.ds(base, 512), :], preferred_element_type=F32)
        q_sum = q_term if q_sum is None else q_sum + q_term
        kv_sum = kv_term if kv_sum is None else kv_sum + kv_term
    for head in range(4):
        cols = slice(head * HD, (head + 1) * HD)
        out[:, cols] = turn(q_sum[:, cols], cos[ROWS : ROWS + 32, :], sin[ROWS : ROWS + 32, :])
    out[:, 512:640] = kv_sum.astype(BF)


def question_project(info, pieces, weights, tables):
    return pl.pallas_call(
        question_project_kernel,
        out_shape=jax.ShapeDtypeStruct((32, 640), BF),
        in_specs=[SM] + [VM] * 6,
        out_specs=VM,
        compiler_params=pltpu.CompilerParams(vmem_limit_bytes=VMEM_LIMIT),
        cost_estimate=pl.CostEstimate(flops=2 * 256 * 8192 * 640, bytes_accessed=8192 * 640 * 2, transcendentals=0),
    )(info, pieces, *weights, *tables)


def key_value_kernel(info, own, partner, cos, sin, out):
    is_lower = info[1] % 2 == 0
    mine, other = own[...].astype(F32), partner[...].astype(F32)
    low = jnp.where(is_lower, mine, other)
    high = jnp.where(is_lower, other, mine)
    lane = lax.broadcasted_iota(jnp.int32, low.shape, 1)
    keys = jnp.where(lane < 64, low, pltpu.roll(high, 64, 1))
    values = jnp.where(lane < 64, pltpu.roll(low, 64, 1), high)
    out[:, :HD] = (keys * cos[...] + pltpu.roll(keys, 64, 1) * sin[...]).astype(BF)
    out[:, HD:] = values.astype(BF)


def key_value(info, own, partner, cos, sin):
    return pl.pallas_call(
        key_value_kernel,
        out_shape=jax.ShapeDtypeStruct((ALL, 2 * HD), BF),
        in_specs=[SM, VM, VM, VM, VM],
        out_specs=VM,
        compiler_params=pltpu.CompilerParams(vmem_limit_bytes=VMEM_LIMIT),
    )(info, own, partner, cos, sin)


def scores_of(queries, keys):
    return lax.dot_general(queries, keys, (((1,), (1,)), ((), ())), preferred_element_type=F32)


def weights_of(scores, top):
    return jnp.exp2(scores * SCALE2 - top * SCALE2)


def columns_to_stats(columns):
    rows = columns[0].shape[0]
    lane = lax.broadcasted_iota(jnp.int32, (rows, 128), 1)
    stats = jnp.zeros((rows, 128), F32)
    for index, column in enumerate(columns):
        stats = jnp.where(lane == index, column, stats)
    return stats


def own_kernel(info, q, kv, weighted, stats):
    length = info[5]
    for tile in range(2):
        rows = slice(tile * 256, tile * 256 + 256)
        width = 256 * (tile + 1)
        row = tile * 256 + lax.broadcasted_iota(jnp.int32, (256, width), 0)
        key = lax.broadcasted_iota(jnp.int32, (256, width), 1)
        bias = jnp.where((key <= row) & (key < length), 0.0, NEG)
        tops, totals = [], []
        for head in range(4):
            cols = slice(head * HD, (head + 1) * HD)
            s = scores_of(q[rows, cols], kv[:width, :HD]) + bias
            top = jnp.max(s, axis=1, keepdims=True)
            e = weights_of(s, top)
            totals.append(jnp.sum(e, axis=1, keepdims=True))
            tops.append(top)
            weighted[rows, cols] = jnp.dot(e.astype(BF), kv[:width, HD:], preferred_element_type=F32)
        stats[rows, :] = columns_to_stats(tops + totals)


def own_attention(info, q, kv):
    return pl.pallas_call(
        own_kernel,
        out_shape=[jax.ShapeDtypeStruct((512, 512), F32), jax.ShapeDtypeStruct((512, 128), F32)],
        in_specs=[SM, VM, VM],
        out_specs=[VM, VM],
        compiler_params=pltpu.CompilerParams(vmem_limit_bytes=VMEM_LIMIT),
        cost_estimate=pl.CostEstimate(flops=4 * 4 * 512 * 512 * 128, bytes_accessed=3 << 20, transcendentals=1 << 20),
    )(info, q, kv)


def anchor_kernel(info, q, kv_zero, kv_one, weighted, stats, out):
    length, anchor_length = info[5], info[6]
    first_core = info[3] == 0
    kv = jnp.where(first_core, kv_zero[...], kv_one[...])
    keys, values = kv[:, :HD], kv[:, HD:]
    key = lax.broadcasted_iota(jnp.int32, (1, 512), 1)
    bias = jnp.where(key < anchor_length, 0.0, NEG)
    for tile in range(2):
        rows = slice(tile * 256, tile * 256 + 256)
        block = stats[rows, :]
        row = tile * 256 + lax.broadcasted_iota(jnp.int32, (256, HD), 0)
        for head in range(4):
            cols = slice(head * HD, (head + 1) * HD)
            s = scores_of(q[rows, cols], keys) + bias
            own_top, own_sum = block[:, head : head + 1], block[:, head + 4 : head + 5]
            top = jnp.maximum(own_top, jnp.max(s, axis=1, keepdims=True))
            e = weights_of(s, top)
            factor = weights_of(own_top, top)
            total = own_sum * factor + jnp.sum(e, axis=1, keepdims=True)
            both = weighted[rows, cols] * factor + jnp.dot(e.astype(BF), values, preferred_element_type=F32)
            out[rows, cols] = jnp.where(row < length, both / total, 0.0).astype(BF)


def anchor_attention(info, q, kv_zero, kv_one, weighted, stats):
    return pl.pallas_call(
        anchor_kernel,
        out_shape=jax.ShapeDtypeStruct((512, 512), BF),
        in_specs=[SM, VM, VM, VM, VM, VM],
        out_specs=VM,
        compiler_params=pltpu.CompilerParams(vmem_limit_bytes=VMEM_LIMIT),
        cost_estimate=pl.CostEstimate(flops=4 * 4 * 512 * 512 * 128, bytes_accessed=3 << 20, transcendentals=1 << 20),
    )(info, q, kv_zero, kv_one, weighted, stats)


def question_kernel(info, q, kv, *outs):
    length, z, core, ctx = info[5], info[2], info[3], info[4]
    stacked = jnp.concatenate([q[:, h * HD : (h + 1) * HD] for h in range(4)], axis=0)
    key = lax.broadcasted_iota(jnp.int32, (1, ROWS), 1)
    s = scores_of(stacked, kv[:ROWS, :HD]) + jnp.where(key < length, 0.0, NEG)
    top = jnp.max(s, axis=1, keepdims=True)
    share = jnp.concatenate([q[:32, h * HD : (h + 1) * HD] for h in range(4)], axis=0)
    s_self = scores_of(share, kv[ROWS:, :HD])
    row_id = 32 * ctx + lax.broadcasted_iota(jnp.int32, s_self.shape, 0) % 32
    place = lax.broadcasted_iota(jnp.int32, s_self.shape, 1)
    z_place = place // 64
    z_mask = jnp.where(z_place == 2, 3, jnp.where(z_place == 3, 2, z_place))
    key_id = 64 * (z ^ z_mask) + 32 * (core ^ ((place // 32) % 2)) + place % 32
    s_self = jnp.where(key_id <= row_id, s_self, NEG)
    top_self = jnp.max(s_self, axis=1, keepdims=True)
    pieces = []
    for head in range(4):
        first = jnp.maximum(top[head * 256 : head * 256 + 32], top_self[head * 32 : head * 32 + 32])
        pieces += [first, top[head * 256 + 32 : head * 256 + 256]]
    top = jnp.concatenate(pieces, axis=0)
    top_share = jnp.concatenate([pieces[2 * head] for head in range(4)], axis=0)
    e = weights_of(s, top)
    e_self = weights_of(s_self, top_share)
    total = jnp.sum(e, axis=1, keepdims=True)
    total_self = jnp.sum(e_self, axis=1, keepdims=True)
    both = jnp.dot(e.astype(BF), kv[:ROWS, HD:], preferred_element_type=F32)
    both_self = jnp.dot(e_self.astype(BF), kv[ROWS:, HD:], preferred_element_type=F32)
    for index, out in enumerate(outs):
        tops, totals = [], []
        for head in range(4):
            start = head * 256 + index * 64
            cols = slice(head * HD, (head + 1) * HD)
            rows = slice(start, start + 64)
            sums, weighted = total[rows], both[rows]
            if index == 0:
                mine = slice(head * 32, head * 32 + 32)
                sums = jnp.concatenate([sums[:32] + total_self[mine], sums[32:]], axis=0)
                weighted = jnp.concatenate([weighted[:32] + both_self[mine], weighted[32:]], axis=0)
            out[:, cols] = weighted
            tops.append(top[rows])
            totals.append(sums)
        out[:, 512:640] = columns_to_stats(tops + totals)


def question_attention(info, q, kv):
    part = jax.ShapeDtypeStruct((64, 640), F32)
    return pl.pallas_call(
        question_kernel,
        out_shape=[part] * 4,
        in_specs=[SM, VM, VM],
        out_specs=[VM] * 4,
        compiler_params=pltpu.CompilerParams(vmem_limit_bytes=VMEM_LIMIT),
        cost_estimate=pl.CostEstimate(flops=4 * 1024 * 512 * 128, bytes_accessed=2 << 20, transcendentals=1 << 19),
    )(info, q, kv)


def merge_kernel(last, n_in, *refs):
    ins, outs = refs[:n_in], refs[n_in:]
    stats = [a[:, 512:640] for a in ins]
    tops, totals = [], []
    for head in range(4):
        cols = slice(head * HD, (head + 1) * HD)
        each = [stat[:, head : head + 1] for stat in stats]
        top = functools.reduce(jnp.maximum, each)
        factors = [weights_of(one, top) for one in each]
        total = sum(stat[:, head + 4 : head + 5] * factor for stat, factor in zip(stats, factors))
        both = sum(a[:, cols] * factor for a, factor in zip(ins, factors))
        if last:
            outs[0][:, cols] = (both / total).astype(BF)
        else:
            outs[0][:, cols] = both[:32]
            outs[1][:, cols] = both[32:]
        tops.append(top)
        totals.append(total)
    if not last:
        stat = columns_to_stats(tops + totals)
        outs[0][:, 512:640] = stat[:32]
        outs[1][:, 512:640] = stat[32:]


def merge(parts, last):
    half = jax.ShapeDtypeStruct((32, 640), F32)
    return pl.pallas_call(
        functools.partial(merge_kernel, last, len(parts)),
        out_shape=[jax.ShapeDtypeStruct((32, 512), BF)] if last else [half, half],
        in_specs=[VM] * len(parts),
        out_specs=[VM] if last else [VM, VM],
        compiler_params=pltpu.CompilerParams(vmem_limit_bytes=VMEM_LIMIT),
    )(*parts)


PLAN_1 = [
    ((0, 0), 0, 512, [(0, 0, 512)]),
    ((-1, 0), 0, 512, [(1, 0, 512)]),
    ((1, 0), 0, 512, [(2, 0, 512)]),
    ((0, -1), 0, 512, [(3, 0, 512)]),
    ((0, 1), 0, 512, [(4, 0, 512)]),
    ((2, 0), 0, 256, [(5, 0, 256)]),
    ((0, 2), 256, 512, [(6, 0, 256)]),
]
PLAN_2 = [
    ((-1, -1), 0, 512, [(0, 0, 256), (4, 0, 256)]),
    ((1, -1), 0, 512, [(0, 256, 128), (1, 0, 128), (7, 0, 256)]),
    ((-1, 1), 0, 512, [(3, 0, 256), (4, 256, 128), (5, 0, 128)]),
    ((1, 1), 0, 512, [(3, 256, 128), (2, 0, 128), (7, 256, 128), (6, 0, 128)]),
    ((2, -1), 0, 256, [(1, 128, 256)]),
    ((2, 1), 0, 256, [(2, 128, 256)]),
    ((-1, 2), 256, 512, [(5, 128, 256)]),
    ((1, 2), 256, 512, [(6, 128, 256)]),
    ((0, 2), 0, 256, [(1, 384, 128), (3, 384, 128)]),
    ((2, 0), 256, 512, [(5, 384, 128), (7, 384, 128)]),
]
PLAN_3 = [
    ((2, 2), 0, 512, [(1, 128, 256), (3, 128, 256)]),
    ((-1, 2), 0, 256, [(0, 0, 256)]),
    ((1, 2), 0, 256, [(0, 256, 128), (1, 0, 128)]),
    ((2, -1), 256, 512, [(2, 0, 256)]),
    ((2, 1), 256, 512, [(2, 256, 128), (3, 0, 128)]),
]
Y_ONE = [(0, 0, 256), (1, 0, 128)]
Y_TWO = [(1, 128, 128), (4, 0, 256)]
X_ONE = [(2, 256, 256), (3, 256, 128)]
X_TWO = [(3, 384, 128), (5, 0, 256)]
PACK = [
    Y_ONE,
    Y_TWO,
    X_ONE,
    X_TWO,
    Y_TWO + [(2, 0, 128)],
    Y_ONE + [(3, 128, 128)],
    X_TWO + [(0, 256, 128)],
    X_ONE + [(1, 384, 128)],
]


def tables_of(positions):
    inverse_freq = ROPE_BASE ** (-(jnp.arange(HD // 2, dtype=jnp.float32) * 2.0 / HD))
    inverse_freq = jnp.concatenate([inverse_freq, inverse_freq])
    phases = positions.astype(jnp.float32)[:, None] * inverse_freq[None, :]
    signs = jnp.where(jnp.arange(HD) < HD // 2, -1.0, 1.0).astype(jnp.float32)
    return jnp.cos(phases), jnp.sin(phases) * signs[None, :]


def per_device(context, question, w_query, w_key, w_value, lengths, owner):
    ctx = lax.axis_index("ctx")
    z, core = ctx // 2, ctx % 2
    heads = lax.axis_index("heads")
    y, x = heads // 4, heads % 4
    weights = (w_query, w_key.T, w_value.T)
    ids = jnp.arange(8, dtype=jnp.int32)
    own_offset = jnp.sum(jnp.where(ids < ctx, lengths, 0))
    own_length = jnp.sum(jnp.where(ids == ctx, lengths, 0))
    filled = jnp.sum(lengths)
    anchor_length = jnp.where(ctx > 0, lengths[0], 0)
    info = jnp.stack([y, x, z, core, ctx, own_length, anchor_length]).astype(jnp.int32)

    up = shift_heads(context, 1, 0)
    down = shift_heads(context, -1, 0)
    right = shift_heads(context, 0, 1)
    left = shift_heads(context, 0, -1)
    far_y = shift_heads(lax.slice_in_dim(context, 0, 256, axis=0), 2, 0)
    far_x = shift_heads(lax.slice_in_dim(context, 256, 512, axis=0), 0, 2)

    asked = jnp.where(ctx == owner[0], question[0], jnp.zeros_like(question[0]))
    share = lax.psum_scatter(asked, "ctx", scatter_dimension=0, tiled=True)

    r1, l1, u1, d1, r2, l2, u2, d2 = pack(PACK, [up, down, right, left, far_y, far_x])
    r1, l1, u1, d1 = shift_heads(r1, 0, 1), shift_heads(l1, 0, -1), shift_heads(u1, 1, 0), shift_heads(d1, -1, 0)
    r2, l2, u2, d2 = shift_heads(r2, 0, 1), shift_heads(l2, 0, -1), shift_heads(u2, 1, 0), shift_heads(d2, -1, 0)
    accs = project(info, [context, up, down, right, left, far_y, far_x], PLAN_1, weights, None, True, True)

    r1, l1, u1, d1, accs = lax.optimization_barrier((r1, l1, u1, d1, accs))
    last = [shift_heads(r1, 0, 1), shift_heads(l1, 0, -1), shift_heads(u1, 1, 0), shift_heads(d1, -1, 0)]
    accs = project(info, [r1, r2, l1, l2, u1, u2, d1, d2], PLAN_2, weights, accs, True, True)

    z_masks = jnp.array([m for m in Z_ORDER for _ in range(64)], jnp.int32)
    c_masks = jnp.array([m for _ in Z_ORDER for m in (0, 1) for _ in range(32)], jnp.int32)
    key_ids = 64 * (z ^ z_masks) + 32 * (core ^ c_masks) + jnp.arange(ASKED, dtype=jnp.int32) % 32
    tables = tables_of(jnp.concatenate([own_offset + jnp.arange(ROWS, dtype=jnp.int32), filled + key_ids]))
    for my, mx in ((1, 0), (3, 0), (0, 1), (0, 3)):
        share = jnp.concatenate([share, swap_heads(share, my, mx)], axis=0)
    q_all = question_project(info, share, weights, tables)
    for mz, mc in ((0, 1), (1, 0), (3, 0)):
        q_all = jnp.concatenate([q_all, swap_ctx(q_all, mz, mc)], axis=0)

    (halves,) = project(info, last, PLAN_3, weights, accs, False, True, True, asked=q_all)
    (queries,) = project(info, last, PLAN_3, weights, accs, True, False, True, tables)
    partner = swap_heads(halves, 0, 1)
    partner, queries = lax.optimization_barrier((partner, queries))
    kv = key_value(info, halves, partner, *tables)

    anchor = kv[:ROWS]
    to_1 = lax.ppermute(anchor, "ctx", [(0, 2)])
    to_2 = lax.ppermute(anchor, "ctx", [(0, 4)])
    to_3 = lax.ppermute(anchor, "ctx", [(0, 6)])
    parts = question_attention(info, q_all, kv)
    others = [swap_ctx(part, m, 0) for part, m in zip(parts[1:], Z_ORDER[1:])]
    to_1, to_2, to_3, kv = lax.optimization_barrier((to_1, to_2, to_3, kv))
    nearer = jnp.where(z == 0, anchor, jnp.where(z == 1, to_1, jnp.where(z == 2, to_2, to_3)))
    from_zero = lax.ppermute(nearer, "ctx", [(0, 1), (2, 3), (4, 5), (6, 7)])
    weighted, stats = own_attention(info, queries, kv)
    from_zero, weighted = lax.optimization_barrier((from_zero, weighted))
    mine, theirs = merge([parts[0]] + others, False)
    context_attn = anchor_attention(info, queries, nearer, from_zero, weighted, stats)
    (question_attn,) = merge([mine, swap_ctx(theirs, 0, 1)], True)
    return (context_attn, question_attn)


def solution(mesh):
    in_specs = (
        P("ctx", "heads"),
        P("ctx", None, "heads"),
        P(None, "heads"),
        P(None, "heads"),
        P(None, "heads"),
        P(),
        P(),
    )
    out_specs = (P("ctx", "heads"), P("ctx", "heads"))
    return jax.shard_map(
        per_device, mesh=mesh, in_specs=in_specs, out_specs=out_specs, check_vma=False
    )
```

```python
import functools

import jax
import jax.numpy as jnp
from jax import lax
from jax.experimental import pallas as pl
from jax.experimental.pallas import tpu as pltpu
from jax.sharding import PartitionSpec as P

HD = 128
ROPE_BASE = 500000.0
BF = jnp.bfloat16
F32 = jnp.float32
VMEM_LIMIT = 24 * 1024 * 1024
NEG = -1e30
SCALE2 = HD ** (-0.5) * 1.4426950408889634
ROWS = 512
ASKED = 32
ALL = ROWS + ASKED
Z_ORDER = (0, 1, 3, 2)

ANY = pl.BlockSpec(memory_space=pl.ANY)
VM = pl.BlockSpec(memory_space=pltpu.VMEM)
SM = pl.BlockSpec(memory_space=pltpu.SMEM)


def shift_heads(array, dy, dx):
    pairs = [(i, ((i // 4 + dy) % 4) * 4 + (i % 4 + dx) % 4) for i in range(16)]
    return lax.ppermute(array, "heads", pairs)


def swap_heads(array, my, mx):
    pairs = [(i, ((i // 4) ^ my) * 4 + ((i % 4) ^ mx)) for i in range(16)]
    return lax.ppermute(array, "heads", pairs)


def swap_ctx(array, mz, mc):
    pairs = [(i, ((i // 2) ^ mz) * 2 + ((i % 2) ^ mc)) for i in range(8)]
    return lax.ppermute(array, "ctx", pairs)


def pack_kernel(plan, n_in, *refs):
    ins, outs = refs[:n_in], refs[n_in:]
    for out, pieces in zip(outs, plan):
        row = 0
        for operand, start, count in pieces:
            out[row : row + count, :] = ins[operand][start : start + count, :]
            row += count


def pack(plan, ins):
    return pl.pallas_call(
        functools.partial(pack_kernel, plan, len(ins)),
        out_shape=[jax.ShapeDtypeStruct((sum(p[2] for p in pieces), 512), BF) for pieces in plan],
        in_specs=[VM] * len(ins),
        out_specs=[VM] * len(plan),
        compiler_params=pltpu.CompilerParams(vmem_limit_bytes=VMEM_LIMIT),
        cost_estimate=pl.CostEstimate(flops=0, bytes_accessed=1 << 20, transcendentals=0),
    )(*ins)


def turn(part, cos, sin):
    return (part * cos + pltpu.roll(part, HD // 2, 1) * sin).astype(BF)


def project_kernel(plan, n_x, with_q, with_kv, has_acc, finish, *refs):
    refs = list(refs)
    take = lambda count: [refs.pop(0) for _ in range(count)]
    (info,) = take(1)
    xs = take(n_x)
    wq = take(1)[0] if with_q else None
    wk, wv = take(2) if with_kv else (None, None)
    acc_q = take(1)[0] if has_acc and with_q else None
    acc_kv = take(1)[0] if has_acc and with_kv else None
    cos, sin = take(2) if finish and with_q else (None, None)
    asked = take(1)[0] if finish and with_kv else None
    q_out = take(1)[0] if with_q else None
    kv_out = take(1)[0] if with_kv else None
    q_sum = take(1)[0] if finish and with_q else q_out
    kv_sum = take(1)[0] if finish and with_kv else kv_out
    y, x = info[0], info[1]
    if has_acc:
        if with_q:
            q_sum[...] = acc_q[...]
        if with_kv:
            kv_sum[...] = acc_kv[...]
    for slot, ((dy, dx), low, high, uses) in enumerate(plan):
        base = pl.multiple_of((((y + dy + 4) % 4) * 4 + (x + dx + 4) % 4) * 512, 512)
        parts = [xs[operand][pl.ds(start, count), :] for operand, start, count in uses]
        piece = parts[0] if len(parts) == 1 else jnp.concatenate(parts, axis=0)
        fresh = slot == 0 and not has_acc
        if with_kv:
            both = jnp.concatenate([wk[:, pl.ds(base, 512)], wv[:, pl.ds(base, 512)]], axis=0)
            term = lax.dot_general(piece, both, (((1,), (1,)), ((), ())), preferred_element_type=F32)
            kv_sum[low:high, :] = term if fresh else kv_sum[low:high, :] + term
        if with_q:
            term = jnp.dot(piece, wq[pl.ds(base, 512), :], preferred_element_type=F32)
            q_sum[low:high, :] = term if fresh else q_sum[low:high, :] + term
    if finish and with_kv:
        kv_out[:ROWS, :] = kv_sum[...].astype(BF)
        kv_out[ROWS:, :] = asked[:, 512:640]
    if finish and with_q:
        for head in range(4):
            cols = slice(head * HD, (head + 1) * HD)
            q_out[:, cols] = turn(q_sum[:, cols], cos[:ROWS, :], sin[:ROWS, :])


def project(info, xs, plan, weights, accs, with_q, with_kv, finish=False, tables=None, asked=None):
    wq, wk, wv = weights
    operands, specs = [info] + list(xs), [SM] + [VM] * len(xs)
    if with_q:
        operands.append(wq)
        specs.append(VM)
    if with_kv:
        operands += [wk, wv]
        specs += [VM, VM]
    has_acc = accs is not None
    if has_acc:
        if with_q:
            operands.append(accs[0])
            specs.append(VM)
        if with_kv:
            operands.append(accs[1])
            specs.append(VM)
    if finish and with_q:
        operands += list(tables)
        specs += [VM, VM]
    if finish and with_kv:
        operands.append(asked)
        specs.append(VM)
    outs, scratch = [], []
    if with_q:
        outs.append(jax.ShapeDtypeStruct((ROWS, 512), BF if finish else F32))
        if finish:
            scratch.append(pltpu.VMEM((ROWS, 512), F32))
    if with_kv:
        outs.append(jax.ShapeDtypeStruct((ALL, 128), BF) if finish else jax.ShapeDtypeStruct((ROWS, 128), F32))
        if finish:
            scratch.append(pltpu.VMEM((ROWS, 128), F32))
    columns = (512 if with_q else 0) + (128 if with_kv else 0)
    used = sum(high - low for _, low, high, _ in plan)
    return pl.pallas_call(
        functools.partial(project_kernel, plan, len(xs), with_q, with_kv, has_acc, finish),
        out_shape=outs,
        in_specs=specs,
        out_specs=[VM] * len(outs),
        scratch_shapes=scratch,
        compiler_params=pltpu.CompilerParams(vmem_limit_bytes=VMEM_LIMIT),
        cost_estimate=pl.CostEstimate(
            flops=2 * used * 512 * columns, bytes_accessed=len(plan) * 512 * columns * 2, transcendentals=0
        ),
    )(*operands)


def question_project_kernel(info, pieces, wq, wk, wv, cos, sin, out):
    y, x = info[0], info[1]
    q_sum, kv_sum = None, None
    for place in range(16):
        mx, my = Z_ORDER[place // 4], Z_ORDER[place % 4]
        base = pl.multiple_of(((y ^ my) * 4 + (x ^ mx)) * 512, 512)
        piece = pieces[pl.ds(place * 32, 32), :]
        both = jnp.concatenate([wk[:, pl.ds(base, 512)], wv[:, pl.ds(base, 512)]], axis=0)
        kv_term = lax.dot_general(piece, both, (((1,), (1,)), ((), ())), preferred_element_type=F32)
        q_term = jnp.dot(piece, wq[pl.ds(base, 512), :], preferred_element_type=F32)
        q_sum = q_term if q_sum is None else q_sum + q_term
        kv_sum = kv_term if kv_sum is None else kv_sum + kv_term
    for head in range(4):
        cols = slice(head * HD, (head + 1) * HD)
        out[:, cols] = turn(q_sum[:, cols], cos[ROWS : ROWS + 32, :], sin[ROWS : ROWS + 32, :])
    out[:, 512:640] = kv_sum.astype(BF)


def question_project(info, pieces, weights, tables):
    return pl.pallas_call(
        question_project_kernel,
        out_shape=jax.ShapeDtypeStruct((32, 640), BF),
        in_specs=[SM] + [VM] * 6,
        out_specs=VM,
        compiler_params=pltpu.CompilerParams(vmem_limit_bytes=VMEM_LIMIT),
        cost_estimate=pl.CostEstimate(flops=2 * 256 * 8192 * 640, bytes_accessed=8192 * 640 * 2, transcendentals=0),
    )(info, pieces, *weights, *tables)


def key_value_kernel(info, own, partner, cos, sin, out):
    is_lower = info[1] % 2 == 0
    mine, other = own[...].astype(F32), partner[...].astype(F32)
    low = jnp.where(is_lower, mine, other)
    high = jnp.where(is_lower, other, mine)
    lane = lax.broadcasted_iota(jnp.int32, low.shape, 1)
    keys = jnp.where(lane < 64, low, pltpu.roll(high, 64, 1))
    values = jnp.where(lane < 64, pltpu.roll(low, 64, 1), high)
    out[:, :HD] = (keys * cos[...] + pltpu.roll(keys, 64, 1) * sin[...]).astype(BF)
    out[:, HD:] = values.astype(BF)


def key_value(info, own, partner, cos, sin):
    return pl.pallas_call(
        key_value_kernel,
        out_shape=jax.ShapeDtypeStruct((ALL, 2 * HD), BF),
        in_specs=[SM, VM, VM, VM, VM],
        out_specs=VM,
        compiler_params=pltpu.CompilerParams(vmem_limit_bytes=VMEM_LIMIT),
    )(info, own, partner, cos, sin)


def scores_of(queries, keys):
    return lax.dot_general(queries, keys, (((1,), (1,)), ((), ())), preferred_element_type=F32)


def weights_of(scores, top):
    return jnp.exp2(scores * SCALE2 - top * SCALE2)


def columns_to_stats(columns):
    rows = columns[0].shape[0]
    lane = lax.broadcasted_iota(jnp.int32, (rows, 128), 1)
    stats = jnp.zeros((rows, 128), F32)
    for index, column in enumerate(columns):
        stats = jnp.where(lane == index, column, stats)
    return stats


def own_kernel(info, q, kv, weighted, stats):
    length = info[5]
    for tile in range(2):
        rows = slice(tile * 256, tile * 256 + 256)
        width = 256 * (tile + 1)
        row = tile * 256 + lax.broadcasted_iota(jnp.int32, (256, width), 0)
        key = lax.broadcasted_iota(jnp.int32, (256, width), 1)
        bias = jnp.where((key <= row) & (key < length), 0.0, NEG)
        tops, totals = [], []
        for head in range(4):
            cols = slice(head * HD, (head + 1) * HD)
            s = scores_of(q[rows, cols], kv[:width, :HD]) + bias
            top = jnp.max(s, axis=1, keepdims=True)
            e = weights_of(s, top)
            totals.append(jnp.sum(e, axis=1, keepdims=True))
            tops.append(top)
            weighted[rows, cols] = jnp.dot(e.astype(BF), kv[:width, HD:], preferred_element_type=F32)
        stats[rows, :] = columns_to_stats(tops + totals)


def own_attention(info, q, kv):
    return pl.pallas_call(
        own_kernel,
        out_shape=[jax.ShapeDtypeStruct((512, 512), F32), jax.ShapeDtypeStruct((512, 128), F32)],
        in_specs=[SM, VM, VM],
        out_specs=[VM, VM],
        compiler_params=pltpu.CompilerParams(vmem_limit_bytes=VMEM_LIMIT),
        cost_estimate=pl.CostEstimate(flops=4 * 4 * 512 * 512 * 128, bytes_accessed=3 << 20, transcendentals=1 << 20),
    )(info, q, kv)


def anchor_kernel(info, q, kv_zero, kv_one, weighted, stats, out):
    length, anchor_length = info[5], info[6]
    first_core = info[3] == 0
    kv = jnp.where(first_core, kv_zero[...], kv_one[...])
    keys, values = kv[:, :HD], kv[:, HD:]
    key = lax.broadcasted_iota(jnp.int32, (1, 512), 1)
    bias = jnp.where(key < anchor_length, 0.0, NEG)
    for tile in range(2):
        rows = slice(tile * 256, tile * 256 + 256)
        block = stats[rows, :]
        row = tile * 256 + lax.broadcasted_iota(jnp.int32, (256, HD), 0)
        for head in range(4):
            cols = slice(head * HD, (head + 1) * HD)
            s = scores_of(q[rows, cols], keys) + bias
            own_top, own_sum = block[:, head : head + 1], block[:, head + 4 : head + 5]
            top = jnp.maximum(own_top, jnp.max(s, axis=1, keepdims=True))
            e = weights_of(s, top)
            factor = weights_of(own_top, top)
            total = own_sum * factor + jnp.sum(e, axis=1, keepdims=True)
            both = weighted[rows, cols] * factor + jnp.dot(e.astype(BF), values, preferred_element_type=F32)
            out[rows, cols] = jnp.where(row < length, both / total, 0.0).astype(BF)


def anchor_attention(info, q, kv_zero, kv_one, weighted, stats):
    return pl.pallas_call(
        anchor_kernel,
        out_shape=jax.ShapeDtypeStruct((512, 512), BF),
        in_specs=[SM, VM, VM, VM, VM, VM],
        out_specs=VM,
        compiler_params=pltpu.CompilerParams(vmem_limit_bytes=VMEM_LIMIT),
        cost_estimate=pl.CostEstimate(flops=4 * 4 * 512 * 512 * 128, bytes_accessed=3 << 20, transcendentals=1 << 20),
    )(info, q, kv_zero, kv_one, weighted, stats)


def question_kernel(info, q_own, q_other, kv_0, kv_1, kv_2, kv_3, out_own, out_other):
    kvs = (kv_0, kv_1, kv_2, kv_3)
    z, core, ctx = info[2], info[3], info[4]
    lengths = [info[5], info[7], info[8], info[9]]
    places = [z, (z + 3) % 4, (z + 1) % 4, (z + 2) % 4]
    stacked = [q_own[:, h * HD : (h + 1) * HD] for h in range(4)]
    stacked += [q_other[:, h * HD : (h + 1) * HD] for h in range(4)]
    q = jnp.concatenate(stacked, axis=0)
    scores = []
    key = lax.broadcasted_iota(jnp.int32, (1, 512), 1)
    for kv, length in zip(kvs, lengths):
        scores.append(scores_of(q, kv[:ROWS, :HD]) + jnp.where(key < length, 0.0, NEG))
    row = lax.broadcasted_iota(jnp.int32, (256, 128), 0)
    lane = lax.broadcasted_iota(jnp.int32, (256, 128), 1)
    row_id = row % 32 + 32 * jnp.where(row < 128, ctx, ctx + 1 - 2 * core)
    block = jnp.where(lane < 64, jnp.where(lane < 32, places[0], places[1]), jnp.where(lane < 96, places[2], places[3]))
    key_id = lane % 32 + 32 * (2 * block + core)
    asked_keys = jnp.concatenate([kv[ROWS:, :HD] for kv in kvs], axis=0)
    asked_values = jnp.concatenate([kv[ROWS:, HD:] for kv in kvs], axis=0)
    scores.append(jnp.where(key_id <= row_id, scores_of(q, asked_keys), NEG))
    top = jnp.max(scores[-1], axis=1, keepdims=True)
    for s in scores[:-1]:
        top = jnp.maximum(top, jnp.max(s, axis=1, keepdims=True))
    values = [kv[:ROWS, HD:] for kv in kvs] + [asked_values]
    total = jnp.zeros((256, 1), F32)
    both = jnp.zeros((256, HD), F32)
    for s, value in zip(scores, values):
        e = weights_of(s, top)
        total = total + jnp.sum(e, axis=1, keepdims=True)
        both = both + jnp.dot(e.astype(BF), value, preferred_element_type=F32)
    for out, start in ((out_own, 0), (out_other, 128)):
        tops, totals = [], []
        for head in range(4):
            rows = slice(start + head * 32, start + head * 32 + 32)
            out[:, head * HD : (head + 1) * HD] = both[rows]
            tops.append(top[rows])
            totals.append(total[rows])
        out[:, 512:640] = columns_to_stats(tops + totals)


def question_attention(info, q_own, q_other, kvs):
    part = jax.ShapeDtypeStruct((32, 640), F32)
    return pl.pallas_call(
        question_kernel,
        out_shape=[part, part],
        in_specs=[SM] + [VM] * 6,
        out_specs=[VM, VM],
        compiler_params=pltpu.CompilerParams(vmem_limit_bytes=VMEM_LIMIT),
        cost_estimate=pl.CostEstimate(flops=4 * 256 * 2176 * 128, bytes_accessed=2 << 20, transcendentals=1 << 19),
    )(info, q_own, q_other, *kvs)


def merge_kernel(a, b, out):
    stat_a, stat_b = a[:, 512:640], b[:, 512:640]
    for head in range(4):
        cols = slice(head * HD, (head + 1) * HD)
        top_a, top_b = stat_a[:, head : head + 1], stat_b[:, head : head + 1]
        top = jnp.maximum(top_a, top_b)
        factor_a, factor_b = weights_of(top_a, top), weights_of(top_b, top)
        total = stat_a[:, head + 4 : head + 5] * factor_a + stat_b[:, head + 4 : head + 5] * factor_b
        out[:, cols] = ((a[:, cols] * factor_a + b[:, cols] * factor_b) / total).astype(BF)


def merge(a, b):
    return pl.pallas_call(
        merge_kernel,
        out_shape=jax.ShapeDtypeStruct((32, 512), BF),
        in_specs=[VM, VM],
        out_specs=VM,
        compiler_params=pltpu.CompilerParams(vmem_limit_bytes=VMEM_LIMIT),
    )(a, b)


PLAN_1 = [
    ((0, 0), 0, 512, [(0, 0, 512)]),
    ((-1, 0), 0, 512, [(1, 0, 512)]),
    ((1, 0), 0, 512, [(2, 0, 512)]),
    ((0, -1), 0, 512, [(3, 0, 512)]),
    ((0, 1), 0, 512, [(4, 0, 512)]),
    ((2, 0), 0, 256, [(5, 0, 256)]),
    ((0, 2), 256, 512, [(6, 0, 256)]),
]
PLAN_2 = [
    ((-1, -1), 0, 512, [(0, 0, 256), (2, 0, 256)]),
    ((1, -1), 0, 512, [(0, 256, 256), (3, 0, 256)]),
    ((-1, 1), 0, 512, [(1, 0, 256), (2, 256, 256)]),
    ((1, 1), 0, 512, [(1, 256, 256), (3, 256, 256)]),
    ((2, -1), 0, 256, [(0, 512, 256)]),
    ((2, 1), 0, 256, [(1, 512, 256)]),
    ((-1, 2), 256, 512, [(2, 512, 256)]),
    ((1, 2), 256, 512, [(3, 512, 256)]),
    ((0, 2), 0, 256, [(0, 768, 128), (1, 768, 128)]),
    ((2, 0), 256, 512, [(2, 768, 128), (3, 768, 128)]),
]
PLAN_3 = [
    ((2, 2), 0, 512, [(1, 128, 256), (3, 128, 256)]),
    ((-1, 2), 0, 256, [(0, 0, 256)]),
    ((1, 2), 0, 256, [(0, 256, 128), (1, 0, 128)]),
    ((2, -1), 256, 512, [(2, 0, 256)]),
    ((2, 1), 256, 512, [(2, 256, 128), (3, 0, 128)]),
]
NEAR_Y = [(0, 0, 256), (1, 0, 256), (4, 0, 256)]
NEAR_X = [(2, 256, 256), (3, 256, 256), (5, 0, 256)]
PACK_2 = [NEAR_Y + [(2, 0, 128)], NEAR_Y + [(3, 128, 128)], NEAR_X + [(0, 256, 128)], NEAR_X + [(1, 384, 128)]]
PACK_3 = [[(0, 0, 384)], [(1, 384, 384)], [(2, 0, 384)], [(3, 384, 384)]]


def tables_of(positions):
    inverse_freq = ROPE_BASE ** (-(jnp.arange(HD // 2, dtype=jnp.float32) * 2.0 / HD))
    inverse_freq = jnp.concatenate([inverse_freq, inverse_freq])
    phases = positions.astype(jnp.float32)[:, None] * inverse_freq[None, :]
    signs = jnp.where(jnp.arange(HD) < HD // 2, -1.0, 1.0).astype(jnp.float32)
    return jnp.cos(phases), jnp.sin(phases) * signs[None, :]


def shift_z(array, dz):
    pairs = [(i, ((i // 2 + dz) % 4) * 2 + i % 2) for i in range(8)]
    return lax.ppermute(array, "ctx", pairs)


def per_device(context, question, w_query, w_key, w_value, lengths, owner):
    ctx = lax.axis_index("ctx")
    z, core = ctx // 2, ctx % 2
    heads = lax.axis_index("heads")
    y, x = heads // 4, heads % 4
    weights = (w_query, w_key.T, w_value.T)
    ids = jnp.arange(8, dtype=jnp.int32)
    own_offset = jnp.sum(jnp.where(ids < ctx, lengths, 0))
    own_length = jnp.sum(jnp.where(ids == ctx, lengths, 0))
    filled = jnp.sum(lengths)
    anchor_length = jnp.where(ctx > 0, lengths[0], 0)

    def length_of(dz):
        return jnp.sum(jnp.where(ids == ((z + dz) % 4) * 2 + core, lengths, 0))

    info = jnp.stack(
        [y, x, z, core, ctx, own_length, anchor_length, length_of(3), length_of(1), length_of(2)]
    ).astype(jnp.int32)

    up = shift_heads(context, 1, 0)
    down = shift_heads(context, -1, 0)
    right = shift_heads(context, 0, 1)
    left = shift_heads(context, 0, -1)
    far_y = shift_heads(lax.slice_in_dim(context, 0, 256, axis=0), 2, 0)
    far_x = shift_heads(lax.slice_in_dim(context, 256, 512, axis=0), 0, 2)

    share = lax.all_to_all(question[0].reshape(8, 32, 512), "ctx", 0, 0)
    share = lax.dynamic_index_in_dim(share, owner[0], 0, False)

    to_right, to_left, to_up, to_down = pack(PACK_2, [up, down, right, left, far_y, far_x])
    share, to_right = lax.optimization_barrier((share, to_right))
    a_right, a_left = shift_heads(to_right, 0, 1), shift_heads(to_left, 0, -1)
    b_up, b_down = shift_heads(to_up, 1, 0), shift_heads(to_down, -1, 0)
    accs = project(info, [context, up, down, right, left, far_y, far_x], PLAN_1, weights, None, True, True)
    for my, mx in ((1, 0), (3, 0)):
        share = jnp.concatenate([share, swap_heads(share, my, mx)], axis=0)
    share, accs = lax.optimization_barrier((share, accs))
    share = jnp.concatenate([share, swap_heads(share, 0, 1)], axis=0)

    a_right, a_left, b_up, b_down, share = lax.optimization_barrier((a_right, a_left, b_up, b_down, share))
    to_right, to_left, to_up, to_down = pack(PACK_3, [a_right, a_left, b_up, b_down])
    last = [
        shift_heads(to_right, 0, 1),
        shift_heads(to_left, 0, -1),
        shift_heads(to_up, 1, 0),
        shift_heads(to_down, -1, 0),
    ]
    share = jnp.concatenate([share, swap_heads(share, 0, 3)], axis=0)
    accs = project(info, [a_right, a_left, b_up, b_down], PLAN_2, weights, accs, True, True)

    tables = tables_of(
        jnp.concatenate(
            [own_offset + jnp.arange(ROWS, dtype=jnp.int32), filled + 32 * ctx + jnp.arange(ASKED, dtype=jnp.int32)]
        )
    )
    q_share = question_project(info, share, weights, tables)

    (halves,) = project(info, last, PLAN_3, weights, accs, False, True, True, asked=q_share)
    (queries,) = project(info, last, PLAN_3, weights, accs, True, False, True, tables)
    partner = swap_heads(halves, 0, 1)
    q_asked = q_share[:, :512]
    q_other = swap_ctx(q_asked, 0, 1)
    partner, queries, q_other = lax.optimization_barrier((partner, queries, q_other))
    kv = key_value(info, halves, partner, *tables)

    below, above, across = shift_z(kv, 1), shift_z(kv, -1), shift_z(kv, 2)
    weighted, stats = own_attention(info, queries, kv)
    below, above, across, weighted = lax.optimization_barrier((below, above, across, weighted))
    nearer = jnp.where(z == 0, kv[:ROWS], jnp.where(z == 1, below[:ROWS], jnp.where(z == 2, across[:ROWS], above[:ROWS])))
    from_zero = lax.ppermute(nearer, "ctx", [(0, 1), (2, 3), (4, 5), (6, 7)])
    part, part_other = question_attention(info, q_asked, q_other, [kv, below, above, across])
    from_zero, part = lax.optimization_barrier((from_zero, part))
    context_attn = anchor_attention(info, queries, nearer, from_zero, weighted, stats)
    question_attn = merge(part, swap_ctx(part_other, 0, 1))
    return (context_attn, question_attn)


def solution(mesh):
    in_specs = (
        P("ctx", "heads"),
        P("ctx", None, "heads"),
        P(None, "heads"),
        P(None, "heads"),
        P(None, "heads"),
        P(),
        P(),
    )
    out_specs = (P("ctx", "heads"), P("ctx", "heads"))
    return jax.shard_map(
        per_device, mesh=mesh, in_specs=in_specs, out_specs=out_specs, check_vma=False
    )
```

```python
import functools

import jax
import jax.numpy as jnp
from jax import lax
from jax.experimental import pallas as pl
from jax.experimental.pallas import tpu as pltpu
from jax.sharding import PartitionSpec as P

HD = 128
ROPE_BASE = 500000.0
BF = jnp.bfloat16
F32 = jnp.float32
VMEM_LIMIT = 24 * 1024 * 1024
NEG = -1e30
SCALE2 = HD ** (-0.5) * 1.4426950408889634
ROWS = 512
ASKED = 32
ALL = ROWS + ASKED

ANY = pl.BlockSpec(memory_space=pl.ANY)
VM = pl.BlockSpec(memory_space=pltpu.VMEM)
SM = pl.BlockSpec(memory_space=pltpu.SMEM)


def shift_heads(array, dy, dx):
    pairs = [(i, ((i // 4 + dy) % 4) * 4 + (i % 4 + dx) % 4) for i in range(16)]
    return lax.ppermute(array, "heads", pairs)


def swap_heads(array, my, mx):
    pairs = [(i, ((i // 4) ^ my) * 4 + ((i % 4) ^ mx)) for i in range(16)]
    return lax.ppermute(array, "heads", pairs)


def swap_ctx(array, mz, mc):
    pairs = [(i, ((i // 2) ^ mz) * 2 + ((i % 2) ^ mc)) for i in range(8)]
    return lax.ppermute(array, "ctx", pairs)


def pack_kernel(plan, n_in, *refs):
    ins, outs = refs[:n_in], refs[n_in:]
    for out, pieces in zip(outs, plan):
        row = 0
        for operand, start, count in pieces:
            out[row : row + count, :] = ins[operand][start : start + count, :]
            row += count


def pack(plan, ins):
    return pl.pallas_call(
        functools.partial(pack_kernel, plan, len(ins)),
        out_shape=[jax.ShapeDtypeStruct((sum(p[2] for p in pieces), 512), BF) for pieces in plan],
        in_specs=[VM] * len(ins),
        out_specs=[VM] * len(plan),
        compiler_params=pltpu.CompilerParams(vmem_limit_bytes=VMEM_LIMIT),
        cost_estimate=pl.CostEstimate(flops=0, bytes_accessed=1 << 20, transcendentals=0),
    )(*ins)


def turn(part, cos, sin):
    return (part * cos + pltpu.roll(part, HD // 2, 1) * sin).astype(BF)


def project_kernel(plan, n_x, with_q, with_kv, has_acc, finish, fetch, *refs):
    refs = list(refs)
    take = lambda count: [refs.pop(0) for _ in range(count)]
    (info,) = take(1)
    xs = take(n_x)
    wq = take(1)[0] if with_q else None
    wk, wv = take(2) if with_kv else (None, None)
    acc_q = take(1)[0] if has_acc and with_q else None
    acc_kv = take(1)[0] if has_acc and with_kv else None
    cos, sin = take(2) if finish and with_q else (None, None)
    asked = take(1)[0] if finish and with_kv else None
    q_out = take(1)[0] if with_q else None
    kv_out = take(1)[0] if with_kv else None
    q_sum = take(1)[0] if finish and with_q else q_out
    kv_sum = take(1)[0] if finish and with_kv else kv_out
    q_buf, kv_buf, sem = take(3) if fetch else (None, None, None)
    y, x = info[0], info[1]
    bases = [pl.multiple_of((((y + dy + 4) % 4) * 4 + (x + dx + 4) % 4) * 512, 512) for (dy, dx), *_ in plan]
    copies = []
    if fetch:
        for slot, base in enumerate(bases):
            copies.append(
                [
                    pltpu.make_async_copy(wk.at[:, pl.ds(base, 512)], kv_buf.at[slot, pl.ds(0, 64), :], sem.at[slot, 0]),
                    pltpu.make_async_copy(wv.at[:, pl.ds(base, 512)], kv_buf.at[slot, pl.ds(64, 64), :], sem.at[slot, 1]),
                    pltpu.make_async_copy(wq.at[pl.ds(base, 512), :], q_buf.at[slot], sem.at[slot, 2]),
                ]
            )
            for copy in copies[-1]:
                copy.start()
    if has_acc:
        if with_q:
            q_sum[...] = acc_q[...]
        if with_kv:
            kv_sum[...] = acc_kv[...]
    for slot, (_, low, high, uses) in enumerate(plan):
        base = bases[slot]
        if fetch:
            for copy in copies[slot]:
                copy.wait()
        parts = [xs[operand][pl.ds(start, count), :] for operand, start, count in uses]
        piece = parts[0] if len(parts) == 1 else jnp.concatenate(parts, axis=0)
        fresh = slot == 0 and not has_acc
        if with_kv:
            if fetch:
                both = kv_buf[slot]
            else:
                both = jnp.concatenate([wk[:, pl.ds(base, 512)], wv[:, pl.ds(base, 512)]], axis=0)
            term = lax.dot_general(piece, both, (((1,), (1,)), ((), ())), preferred_element_type=F32)
            kv_sum[low:high, :] = term if fresh else kv_sum[low:high, :] + term
        if with_q:
            block = q_buf[slot] if fetch else wq[pl.ds(base, 512), :]
            term = jnp.dot(piece, block, preferred_element_type=F32)
            q_sum[low:high, :] = term if fresh else q_sum[low:high, :] + term
    if finish and with_kv:
        kv_out[:ROWS, :] = kv_sum[...].astype(BF)
        kv_out[ROWS:, :] = asked[:, 512:640]
    if finish and with_q:
        for head in range(4):
            cols = slice(head * HD, (head + 1) * HD)
            q_out[:, cols] = turn(q_sum[:, cols], cos[:ROWS, :], sin[:ROWS, :])


def project(info, xs, plan, weights, accs, with_q, with_kv, finish=False, tables=None, asked=None, fetch=False):
    wq, wk, wv = weights
    operands, specs = [info] + list(xs), [SM] + [VM] * len(xs)
    if with_q:
        operands.append(wq)
        specs.append(ANY if fetch else VM)
    if with_kv:
        operands += [wk, wv]
        specs += [ANY, ANY] if fetch else [VM, VM]
    has_acc = accs is not None
    if has_acc:
        if with_q:
            operands.append(accs[0])
            specs.append(VM)
        if with_kv:
            operands.append(accs[1])
            specs.append(VM)
    if finish and with_q:
        operands += list(tables)
        specs += [VM, VM]
    if finish and with_kv:
        operands.append(asked)
        specs.append(VM)
    outs, scratch = [], []
    if with_q:
        outs.append(jax.ShapeDtypeStruct((ROWS, 512), BF if finish else F32))
        if finish:
            scratch.append(pltpu.VMEM((ROWS, 512), F32))
    if with_kv:
        outs.append(jax.ShapeDtypeStruct((ALL, 128), BF) if finish else jax.ShapeDtypeStruct((ROWS, 128), F32))
        if finish:
            scratch.append(pltpu.VMEM((ROWS, 128), F32))
    if fetch:
        scratch += [
            pltpu.VMEM((len(plan), 512, 512), BF),
            pltpu.VMEM((len(plan), 128, 512), BF),
            pltpu.SemaphoreType.DMA((len(plan), 3)),
        ]
    columns = (512 if with_q else 0) + (128 if with_kv else 0)
    used = sum(high - low for _, low, high, _ in plan)
    return pl.pallas_call(
        functools.partial(project_kernel, plan, len(xs), with_q, with_kv, has_acc, finish, fetch),
        out_shape=outs,
        in_specs=specs,
        out_specs=[VM] * len(outs),
        scratch_shapes=scratch,
        compiler_params=pltpu.CompilerParams(vmem_limit_bytes=VMEM_LIMIT),
        cost_estimate=pl.CostEstimate(
            flops=2 * used * 512 * columns, bytes_accessed=len(plan) * 512 * columns * 2, transcendentals=0
        ),
    )(*operands)


def question_project_kernel(pieces, wq, wk, wv, cos, sin, out):
    q_sum, kv_sum = None, None
    for place in range(16):
        base = place * 512
        piece = pieces[place]
        both = jnp.concatenate([wk[:, pl.ds(base, 512)], wv[:, pl.ds(base, 512)]], axis=0)
        kv_term = lax.dot_general(piece, both, (((1,), (1,)), ((), ())), preferred_element_type=F32)
        q_term = jnp.dot(piece, wq[pl.ds(base, 512), :], preferred_element_type=F32)
        q_sum = q_term if q_sum is None else q_sum + q_term
        kv_sum = kv_term if kv_sum is None else kv_sum + kv_term
    for head in range(4):
        cols = slice(head * HD, (head + 1) * HD)
        out[:, cols] = turn(q_sum[:, cols], cos[ROWS : ROWS + 32, :], sin[ROWS : ROWS + 32, :])
    out[:, 512:640] = kv_sum.astype(BF)


def question_project(pieces, weights, tables):
    return pl.pallas_call(
        question_project_kernel,
        out_shape=jax.ShapeDtypeStruct((32, 640), BF),
        in_specs=[VM] * 6,
        out_specs=VM,
        compiler_params=pltpu.CompilerParams(vmem_limit_bytes=VMEM_LIMIT),
        cost_estimate=pl.CostEstimate(flops=2 * 256 * 8192 * 640, bytes_accessed=8192 * 640 * 2, transcendentals=0),
    )(pieces, *weights, *tables)


def key_value_kernel(info, own, partner, cos, sin, out):
    is_lower = info[1] % 2 == 0
    mine, other = own[...].astype(F32), partner[...].astype(F32)
    low = jnp.where(is_lower, mine, other)
    high = jnp.where(is_lower, other, mine)
    lane = lax.broadcasted_iota(jnp.int32, low.shape, 1)
    keys = jnp.where(lane < 64, low, pltpu.roll(high, 64, 1))
    values = jnp.where(lane < 64, pltpu.roll(low, 64, 1), high)
    out[:, :HD] = (keys * cos[...] + pltpu.roll(keys, 64, 1) * sin[...]).astype(BF)
    out[:, HD:] = values.astype(BF)


def key_value(info, own, partner, cos, sin):
    return pl.pallas_call(
        key_value_kernel,
        out_shape=jax.ShapeDtypeStruct((ALL, 2 * HD), BF),
        in_specs=[SM, VM, VM, VM, VM],
        out_specs=VM,
        compiler_params=pltpu.CompilerParams(vmem_limit_bytes=VMEM_LIMIT),
    )(info, own, partner, cos, sin)


def scores_of(queries, keys):
    return lax.dot_general(queries, keys, (((1,), (1,)), ((), ())), preferred_element_type=F32)


def weights_of(scores, top):
    return jnp.exp2(scores * SCALE2 - top * SCALE2)


def columns_to_stats(columns):
    rows = columns[0].shape[0]
    lane = lax.broadcasted_iota(jnp.int32, (rows, 128), 1)
    stats = jnp.zeros((rows, 128), F32)
    for index, column in enumerate(columns):
        stats = jnp.where(lane == index, column, stats)
    return stats


def own_kernel(info, q, kv, weighted, stats):
    length = info[5]
    for tile in range(2):
        rows = slice(tile * 256, tile * 256 + 256)
        width = 256 * (tile + 1)
        row = tile * 256 + lax.broadcasted_iota(jnp.int32, (256, width), 0)
        key = lax.broadcasted_iota(jnp.int32, (256, width), 1)
        bias = jnp.where((key <= row) & (key < length), 0.0, NEG)
        tops, totals = [], []
        for head in range(4):
            cols = slice(head * HD, (head + 1) * HD)
            s = scores_of(q[rows, cols], kv[:width, :HD]) + bias
            top = jnp.max(s, axis=1, keepdims=True)
            e = weights_of(s, top)
            totals.append(jnp.sum(e, axis=1, keepdims=True))
            tops.append(top)
            weighted[rows, cols] = jnp.dot(e.astype(BF), kv[:width, HD:], preferred_element_type=F32)
        stats[rows, :] = columns_to_stats(tops + totals)


def own_attention(info, q, kv):
    return pl.pallas_call(
        own_kernel,
        out_shape=[jax.ShapeDtypeStruct((512, 512), F32), jax.ShapeDtypeStruct((512, 128), F32)],
        in_specs=[SM, VM, VM],
        out_specs=[VM, VM],
        compiler_params=pltpu.CompilerParams(vmem_limit_bytes=VMEM_LIMIT),
        cost_estimate=pl.CostEstimate(flops=4 * 4 * 512 * 512 * 128, bytes_accessed=3 << 20, transcendentals=1 << 20),
    )(info, q, kv)


def anchor_kernel(info, q, kv_zero, kv_one, weighted, stats, out):
    length, anchor_length = info[5], info[6]
    first_core = info[3] == 0
    kv = jnp.where(first_core, kv_zero[...], kv_one[...])
    keys, values = kv[:, :HD], kv[:, HD:]
    key = lax.broadcasted_iota(jnp.int32, (1, 512), 1)
    bias = jnp.where(key < anchor_length, 0.0, NEG)
    for tile in range(2):
        rows = slice(tile * 256, tile * 256 + 256)
        block = stats[rows, :]
        row = tile * 256 + lax.broadcasted_iota(jnp.int32, (256, HD), 0)
        for head in range(4):
            cols = slice(head * HD, (head + 1) * HD)
            s = scores_of(q[rows, cols], keys) + bias
            own_top, own_sum = block[:, head : head + 1], block[:, head + 4 : head + 5]
            top = jnp.maximum(own_top, jnp.max(s, axis=1, keepdims=True))
            e = weights_of(s, top)
            factor = weights_of(own_top, top)
            total = own_sum * factor + jnp.sum(e, axis=1, keepdims=True)
            both = weighted[rows, cols] * factor + jnp.dot(e.astype(BF), values, preferred_element_type=F32)
            out[rows, cols] = jnp.where(row < length, both / total, 0.0).astype(BF)


def anchor_attention(info, q, kv_zero, kv_one, weighted, stats):
    return pl.pallas_call(
        anchor_kernel,
        out_shape=jax.ShapeDtypeStruct((512, 512), BF),
        in_specs=[SM, VM, VM, VM, VM, VM],
        out_specs=VM,
        compiler_params=pltpu.CompilerParams(vmem_limit_bytes=VMEM_LIMIT),
        cost_estimate=pl.CostEstimate(flops=4 * 4 * 512 * 512 * 128, bytes_accessed=3 << 20, transcendentals=1 << 20),
    )(info, q, kv_zero, kv_one, weighted, stats)


def question_kernel(info, q_own, q_other, kv_0, kv_1, kv_2, kv_3, out_own, out_other):
    kvs = (kv_0, kv_1, kv_2, kv_3)
    z, core, ctx = info[2], info[3], info[4]
    lengths = [info[5], info[7], info[8], info[9]]
    places = [z, (z + 3) % 4, (z + 1) % 4, (z + 2) % 4]
    stacked = [q_own[:, h * HD : (h + 1) * HD] for h in range(4)]
    stacked += [q_other[:, h * HD : (h + 1) * HD] for h in range(4)]
    q = jnp.concatenate(stacked, axis=0)
    scores = []
    key = lax.broadcasted_iota(jnp.int32, (1, 512), 1)
    for kv, length in zip(kvs, lengths):
        scores.append(scores_of(q, kv[:ROWS, :HD]) + jnp.where(key < length, 0.0, NEG))
    row = lax.broadcasted_iota(jnp.int32, (256, 128), 0)
    lane = lax.broadcasted_iota(jnp.int32, (256, 128), 1)
    row_id = row % 32 + 32 * jnp.where(row < 128, ctx, ctx + 1 - 2 * core)
    block = jnp.where(lane < 64, jnp.where(lane < 32, places[0], places[1]), jnp.where(lane < 96, places[2], places[3]))
    key_id = lane % 32 + 32 * (2 * block + core)
    asked_keys = jnp.concatenate([kv[ROWS:, :HD] for kv in kvs], axis=0)
    asked_values = jnp.concatenate([kv[ROWS:, HD:] for kv in kvs], axis=0)
    scores.append(jnp.where(key_id <= row_id, scores_of(q, asked_keys), NEG))
    top = jnp.max(scores[-1], axis=1, keepdims=True)
    for s in scores[:-1]:
        top = jnp.maximum(top, jnp.max(s, axis=1, keepdims=True))
    values = [kv[:ROWS, HD:] for kv in kvs] + [asked_values]
    total = jnp.zeros((256, 1), F32)
    both = jnp.zeros((256, HD), F32)
    for s, value in zip(scores, values):
        e = weights_of(s, top)
        total = total + jnp.sum(e, axis=1, keepdims=True)
        both = both + jnp.dot(e.astype(BF), value, preferred_element_type=F32)
    for out, start in ((out_own, 0), (out_other, 128)):
        tops, totals = [], []
        for head in range(4):
            rows = slice(start + head * 32, start + head * 32 + 32)
            out[:, head * HD : (head + 1) * HD] = both[rows]
            tops.append(top[rows])
            totals.append(total[rows])
        out[:, 512:640] = columns_to_stats(tops + totals)


def question_attention(info, q_own, q_other, kvs):
    part = jax.ShapeDtypeStruct((32, 640), F32)
    return pl.pallas_call(
        question_kernel,
        out_shape=[part, part],
        in_specs=[SM] + [VM] * 6,
        out_specs=[VM, VM],
        compiler_params=pltpu.CompilerParams(vmem_limit_bytes=VMEM_LIMIT),
        cost_estimate=pl.CostEstimate(flops=4 * 256 * 2176 * 128, bytes_accessed=2 << 20, transcendentals=1 << 19),
    )(info, q_own, q_other, *kvs)


def merge_kernel(a, b, out):
    stat_a, stat_b = a[:, 512:640], b[:, 512:640]
    for head in range(4):
        cols = slice(head * HD, (head + 1) * HD)
        top_a, top_b = stat_a[:, head : head + 1], stat_b[:, head : head + 1]
        top = jnp.maximum(top_a, top_b)
        factor_a, factor_b = weights_of(top_a, top), weights_of(top_b, top)
        total = stat_a[:, head + 4 : head + 5] * factor_a + stat_b[:, head + 4 : head + 5] * factor_b
        out[:, cols] = ((a[:, cols] * factor_a + b[:, cols] * factor_b) / total).astype(BF)


def merge(a, b):
    return pl.pallas_call(
        merge_kernel,
        out_shape=jax.ShapeDtypeStruct((32, 512), BF),
        in_specs=[VM, VM],
        out_specs=VM,
        compiler_params=pltpu.CompilerParams(vmem_limit_bytes=VMEM_LIMIT),
    )(a, b)


PLAN_1 = [
    ((0, 0), 0, 512, [(0, 0, 512)]),
    ((-1, 0), 0, 512, [(1, 0, 512)]),
    ((1, 0), 0, 512, [(2, 0, 512)]),
    ((0, -1), 0, 512, [(3, 0, 512)]),
    ((0, 1), 0, 512, [(4, 0, 512)]),
    ((2, 0), 0, 256, [(5, 0, 256)]),
    ((0, 2), 256, 512, [(6, 0, 256)]),
]
PLAN_2 = [
    ((-1, -1), 0, 512, [(0, 0, 256), (2, 0, 256)]),
    ((1, -1), 0, 512, [(0, 256, 256), (3, 0, 256)]),
    ((-1, 1), 0, 512, [(1, 0, 256), (2, 256, 256)]),
    ((1, 1), 0, 512, [(1, 256, 256), (3, 256, 256)]),
    ((2, -1), 0, 256, [(0, 512, 256)]),
    ((2, 1), 0, 256, [(1, 512, 256)]),
    ((-1, 2), 256, 512, [(2, 512, 256)]),
    ((1, 2), 256, 512, [(3, 512, 256)]),
    ((0, 2), 0, 256, [(0, 768, 128), (1, 768, 128)]),
    ((2, 0), 256, 512, [(2, 768, 128), (3, 768, 128)]),
]
PLAN_3 = [
    ((2, 2), 0, 512, [(1, 128, 256), (3, 128, 256)]),
    ((-1, 2), 0, 256, [(0, 0, 256)]),
    ((1, 2), 0, 256, [(0, 256, 128), (1, 0, 128)]),
    ((2, -1), 256, 512, [(2, 0, 256)]),
    ((2, 1), 256, 512, [(2, 256, 128), (3, 0, 128)]),
]
NEAR_Y = [(0, 0, 256), (1, 0, 256), (4, 0, 256)]
NEAR_X = [(2, 256, 256), (3, 256, 256), (5, 0, 256)]
PACK_2 = [NEAR_Y + [(2, 0, 128)], NEAR_Y + [(3, 128, 128)], NEAR_X + [(0, 256, 128)], NEAR_X + [(1, 384, 128)]]
PACK_3 = [[(0, 0, 384)], [(1, 384, 384)], [(2, 0, 384)], [(3, 384, 384)]]


def tables_of(positions):
    inverse_freq = ROPE_BASE ** (-(jnp.arange(HD // 2, dtype=jnp.float32) * 2.0 / HD))
    inverse_freq = jnp.concatenate([inverse_freq, inverse_freq])
    phases = positions.astype(jnp.float32)[:, None] * inverse_freq[None, :]
    signs = jnp.where(jnp.arange(HD) < HD // 2, -1.0, 1.0).astype(jnp.float32)
    return jnp.cos(phases), jnp.sin(phases) * signs[None, :]


def shift_z(array, dz):
    pairs = [(i, ((i // 2 + dz) % 4) * 2 + i % 2) for i in range(8)]
    return lax.ppermute(array, "ctx", pairs)


def per_device(context, question, w_query, w_key, w_value, lengths, owner):
    ctx = lax.axis_index("ctx")
    z, core = ctx // 2, ctx % 2
    heads = lax.axis_index("heads")
    y, x = heads // 4, heads % 4
    weights = (w_query, w_key.T, w_value.T)
    ids = jnp.arange(8, dtype=jnp.int32)
    own_offset = jnp.sum(jnp.where(ids < ctx, lengths, 0))
    own_length = jnp.sum(jnp.where(ids == ctx, lengths, 0))
    filled = jnp.sum(lengths)
    anchor_length = jnp.where(ctx > 0, lengths[0], 0)

    def length_of(dz):
        return jnp.sum(jnp.where(ids == ((z + dz) % 4) * 2 + core, lengths, 0))

    info = jnp.stack(
        [y, x, z, core, ctx, own_length, anchor_length, length_of(3), length_of(1), length_of(2)]
    ).astype(jnp.int32)

    far_y = shift_heads(lax.slice_in_dim(context, 0, 256, axis=0), 2, 0)
    up = shift_heads(context, 1, 0)
    down = shift_heads(context, -1, 0)
    right = shift_heads(context, 0, 1)
    left = shift_heads(context, 0, -1)
    far_y, again = lax.optimization_barrier((far_y, context))
    far_x = shift_heads(lax.slice_in_dim(again, 256, 512, axis=0), 0, 2)

    share = lax.all_to_all(question[0].reshape(8, 32, 512), "ctx", 0, 0)
    share = lax.dynamic_index_in_dim(share, owner[0], 0, False)
    tables = tables_of(
        jnp.concatenate(
            [own_offset + jnp.arange(ROWS, dtype=jnp.int32), filled + 32 * ctx + jnp.arange(ASKED, dtype=jnp.int32)]
        )
    )
    up, share, tables = lax.optimization_barrier((up, share, tables))

    to_right, to_left, to_up, to_down = pack(PACK_2, [up, down, right, left, far_y, far_x])
    a_right, a_left = shift_heads(to_right, 0, 1), shift_heads(to_left, 0, -1)
    b_up, b_down = shift_heads(to_up, 1, 0), shift_heads(to_down, -1, 0)
    up, to_right = lax.optimization_barrier((up, to_right))
    accs = project(info, [context, up, down, right, left, far_y, far_x], PLAN_1, weights, None, True, True)
    share, accs = lax.optimization_barrier((share, accs))
    pieces = lax.all_to_all(jnp.broadcast_to(share[None], (16, 32, 512)), "heads", 0, 0)

    a_right, a_left, b_up, b_down, accs = lax.optimization_barrier((a_right, a_left, b_up, b_down, accs))
    to_right, to_left, to_up, to_down = pack(PACK_3, [a_right, a_left, b_up, b_down])
    last = [
        shift_heads(to_right, 0, 1),
        shift_heads(to_left, 0, -1),
        shift_heads(to_up, 1, 0),
        shift_heads(to_down, -1, 0),
    ]
    accs = project(info, [a_right, a_left, b_up, b_down], PLAN_2, weights, accs, True, True)
    q_share = question_project(pieces, weights, tables)

    (halves,) = project(info, last, PLAN_3, weights, accs, False, True, True, asked=q_share)
    (queries,) = project(info, last, PLAN_3, weights, accs, True, False, True, tables)
    partner = swap_heads(halves, 0, 1)
    q_asked = q_share[:, :512]
    q_other = swap_ctx(q_asked, 0, 1)
    partner, queries, q_other = lax.optimization_barrier((partner, queries, q_other))
    kv = key_value(info, halves, partner, *tables)

    below, above, across = shift_z(kv, 1), shift_z(kv, -1), shift_z(kv, 2)
    weighted, stats = own_attention(info, queries, kv)
    below, above, across, weighted = lax.optimization_barrier((below, above, across, weighted))
    nearer = jnp.where(z == 0, kv[:ROWS], jnp.where(z == 1, below[:ROWS], jnp.where(z == 2, across[:ROWS], above[:ROWS])))
    from_zero = lax.ppermute(nearer, "ctx", [(0, 1), (2, 3), (4, 5), (6, 7)])
    part, part_other = question_attention(info, q_asked, q_other, [kv, below, above, across])
    from_zero, part = lax.optimization_barrier((from_zero, part))
    context_attn = anchor_attention(info, queries, nearer, from_zero, weighted, stats)
    question_attn = merge(part, swap_ctx(part_other, 0, 1))
    return (context_attn, question_attn)


def solution(mesh):
    in_specs = (
        P("ctx", "heads"),
        P("ctx", None, "heads"),
        P(None, "heads"),
        P(None, "heads"),
        P(None, "heads"),
        P(),
        P(),
    )
    out_specs = (P("ctx", "heads"), P("ctx", "heads"))
    return jax.shard_map(
        per_device, mesh=mesh, in_specs=in_specs, out_specs=out_specs, check_vma=False
    )
```

```python
import functools

import jax
import jax.numpy as jnp
from jax import lax
from jax.experimental import pallas as pl
from jax.experimental.pallas import tpu as pltpu
from jax.sharding import PartitionSpec as P

HD = 128
ROPE_BASE = 500000.0
BF = jnp.bfloat16
F32 = jnp.float32
VMEM_LIMIT = 8 * 1024 * 1024
NEG = -1e30
SCALE2 = HD ** (-0.5) * 1.4426950408889634
ROWS = 512
ASKED = 32
ALL = ROWS + ASKED

ANY = pl.BlockSpec(memory_space=pl.ANY)
VM = pl.BlockSpec(memory_space=pltpu.VMEM)
SM = pl.BlockSpec(memory_space=pltpu.SMEM)


def shift_heads(array, dy, dx):
    pairs = [(i, ((i // 4 + dy) % 4) * 4 + (i % 4 + dx) % 4) for i in range(16)]
    return lax.ppermute(array, "heads", pairs)


def swap_heads(array, my, mx):
    pairs = [(i, ((i // 4) ^ my) * 4 + ((i % 4) ^ mx)) for i in range(16)]
    return lax.ppermute(array, "heads", pairs)


def swap_ctx(array, mz, mc):
    pairs = [(i, ((i // 2) ^ mz) * 2 + ((i % 2) ^ mc)) for i in range(8)]
    return lax.ppermute(array, "ctx", pairs)


def pack_kernel(plan, n_in, *refs):
    ins, outs = refs[:n_in], refs[n_in:]
    for out, pieces in zip(outs, plan):
        row = 0
        for operand, start, count in pieces:
            out[row : row + count, :] = ins[operand][start : start + count, :]
            row += count


def pack(plan, ins):
    return pl.pallas_call(
        functools.partial(pack_kernel, plan, len(ins)),
        out_shape=[jax.ShapeDtypeStruct((sum(p[2] for p in pieces), 512), BF) for pieces in plan],
        in_specs=[VM] * len(ins),
        out_specs=[VM] * len(plan),
        compiler_params=pltpu.CompilerParams(vmem_limit_bytes=VMEM_LIMIT),
        cost_estimate=pl.CostEstimate(flops=0, bytes_accessed=1 << 20, transcendentals=0),
    )(*ins)


def turn(part, cos, sin):
    return (part * cos + pltpu.roll(part, HD // 2, 1) * sin).astype(BF)


def project_kernel(plan, n_x, with_q, with_kv, has_acc, finish, fetch, *refs):
    refs = list(refs)
    take = lambda count: [refs.pop(0) for _ in range(count)]
    (info,) = take(1)
    xs = take(n_x)
    wq = take(1)[0] if with_q else None
    wk, wv = take(2) if with_kv else (None, None)
    acc_q = take(1)[0] if has_acc and with_q else None
    acc_kv = take(1)[0] if has_acc and with_kv else None
    cos, sin = take(2) if finish and with_q else (None, None)
    asked = take(1)[0] if finish and with_kv else None
    q_out = take(1)[0] if with_q else None
    kv_out = take(1)[0] if with_kv else None
    q_sum = take(1)[0] if finish and with_q else q_out
    kv_sum = take(1)[0] if finish and with_kv else kv_out
    q_buf, kv_buf, sem = take(3) if fetch else (None, None, None)
    y, x = info[0], info[1]
    bases = [pl.multiple_of((((y + dy + 4) % 4) * 4 + (x + dx + 4) % 4) * 512, 512) for (dy, dx), *_ in plan]
    copies = []
    if fetch:
        for slot, base in enumerate(bases):
            copies.append(
                [
                    pltpu.make_async_copy(wk.at[:, pl.ds(base, 512)], kv_buf.at[slot, pl.ds(0, 64), :], sem.at[slot, 0]),
                    pltpu.make_async_copy(wv.at[:, pl.ds(base, 512)], kv_buf.at[slot, pl.ds(64, 64), :], sem.at[slot, 1]),
                    pltpu.make_async_copy(wq.at[pl.ds(base, 512), :], q_buf.at[slot], sem.at[slot, 2]),
                ]
            )
            for copy in copies[-1]:
                copy.start()
    if has_acc:
        if with_q:
            q_sum[...] = acc_q[...]
        if with_kv:
            kv_sum[...] = acc_kv[...]
    for slot, (_, low, high, uses) in enumerate(plan):
        base = bases[slot]
        if fetch:
            for copy in copies[slot]:
                copy.wait()
        parts = [xs[operand][pl.ds(start, count), :] for operand, start, count in uses]
        piece = parts[0] if len(parts) == 1 else jnp.concatenate(parts, axis=0)
        fresh = slot == 0 and not has_acc
        if with_kv:
            if fetch:
                both = kv_buf[slot]
            else:
                both = jnp.concatenate([wk[:, pl.ds(base, 512)], wv[:, pl.ds(base, 512)]], axis=0)
            term = lax.dot_general(piece, both, (((1,), (1,)), ((), ())), preferred_element_type=F32)
            kv_sum[low:high, :] = term if fresh else kv_sum[low:high, :] + term
        if with_q:
            block = q_buf[slot] if fetch else wq[pl.ds(base, 512), :]
            term = jnp.dot(piece, block, preferred_element_type=F32)
            q_sum[low:high, :] = term if fresh else q_sum[low:high, :] + term
    if finish and with_kv:
        kv_out[:ROWS, :] = kv_sum[...].astype(BF)
        kv_out[ROWS:, :] = asked[:, 512:640]
    if finish and with_q:
        for head in range(4):
            cols = slice(head * HD, (head + 1) * HD)
            q_out[:, cols] = turn(q_sum[:, cols], cos[:ROWS, :], sin[:ROWS, :])


def project(info, xs, plan, weights, accs, with_q, with_kv, finish=False, tables=None, asked=None, fetch=False):
    wq, wk, wv = weights
    operands, specs = [info] + list(xs), [SM] + [VM] * len(xs)
    if with_q:
        operands.append(wq)
        specs.append(ANY if fetch else VM)
    if with_kv:
        operands += [wk, wv]
        specs += [ANY, ANY] if fetch else [VM, VM]
    has_acc = accs is not None
    if has_acc:
        if with_q:
            operands.append(accs[0])
            specs.append(VM)
        if with_kv:
            operands.append(accs[1])
            specs.append(VM)
    if finish and with_q:
        operands += list(tables)
        specs += [VM, VM]
    if finish and with_kv:
        operands.append(asked)
        specs.append(VM)
    outs, scratch = [], []
    if with_q:
        outs.append(jax.ShapeDtypeStruct((ROWS, 512), BF if finish else F32))
        if finish:
            scratch.append(pltpu.VMEM((ROWS, 512), F32))
    if with_kv:
        outs.append(jax.ShapeDtypeStruct((ALL, 128), BF) if finish else jax.ShapeDtypeStruct((ROWS, 128), F32))
        if finish:
            scratch.append(pltpu.VMEM((ROWS, 128), F32))
    if fetch:
        scratch += [
            pltpu.VMEM((len(plan), 512, 512), BF),
            pltpu.VMEM((len(plan), 128, 512), BF),
            pltpu.SemaphoreType.DMA((len(plan), 3)),
        ]
    columns = (512 if with_q else 0) + (128 if with_kv else 0)
    used = sum(high - low for _, low, high, _ in plan)
    return pl.pallas_call(
        functools.partial(project_kernel, plan, len(xs), with_q, with_kv, has_acc, finish, fetch),
        out_shape=outs,
        in_specs=specs,
        out_specs=[VM] * len(outs),
        scratch_shapes=scratch,
        compiler_params=pltpu.CompilerParams(vmem_limit_bytes=VMEM_LIMIT),
        cost_estimate=pl.CostEstimate(
            flops=2 * used * 512 * columns, bytes_accessed=len(plan) * 512 * columns * 2, transcendentals=0
        ),
    )(*operands)


def question_project_kernel(pieces, wq, wk, wv, cos, sin, out):
    q_sum, kv_sum = None, None
    for place in range(16):
        base = place * 512
        piece = pieces[place]
        both = jnp.concatenate([wk[:, pl.ds(base, 512)], wv[:, pl.ds(base, 512)]], axis=0)
        kv_term = lax.dot_general(piece, both, (((1,), (1,)), ((), ())), preferred_element_type=F32)
        q_term = jnp.dot(piece, wq[pl.ds(base, 512), :], preferred_element_type=F32)
        q_sum = q_term if q_sum is None else q_sum + q_term
        kv_sum = kv_term if kv_sum is None else kv_sum + kv_term
    for head in range(4):
        cols = slice(head * HD, (head + 1) * HD)
        out[:, cols] = turn(q_sum[:, cols], cos[ROWS : ROWS + 32, :], sin[ROWS : ROWS + 32, :])
    out[:, 512:640] = kv_sum.astype(BF)


def question_project(pieces, weights, tables):
    return pl.pallas_call(
        question_project_kernel,
        out_shape=jax.ShapeDtypeStruct((32, 640), BF),
        in_specs=[VM] * 6,
        out_specs=VM,
        compiler_params=pltpu.CompilerParams(vmem_limit_bytes=VMEM_LIMIT),
        cost_estimate=pl.CostEstimate(flops=2 * 256 * 8192 * 640, bytes_accessed=8192 * 640 * 2, transcendentals=0),
    )(pieces, *weights, *tables)


def key_value_kernel(info, own, partner, cos, sin, out):
    is_lower = info[1] % 2 == 0
    mine, other = own[...].astype(F32), partner[...].astype(F32)
    low = jnp.where(is_lower, mine, other)
    high = jnp.where(is_lower, other, mine)
    lane = lax.broadcasted_iota(jnp.int32, low.shape, 1)
    keys = jnp.where(lane < 64, low, pltpu.roll(high, 64, 1))
    values = jnp.where(lane < 64, pltpu.roll(low, 64, 1), high)
    out[:, :HD] = (keys * cos[...] + pltpu.roll(keys, 64, 1) * sin[...]).astype(BF)
    out[:, HD:] = values.astype(BF)


def key_value(info, own, partner, cos, sin):
    return pl.pallas_call(
        key_value_kernel,
        out_shape=jax.ShapeDtypeStruct((ALL, 2 * HD), BF),
        in_specs=[SM, VM, VM, VM, VM],
        out_specs=VM,
        compiler_params=pltpu.CompilerParams(vmem_limit_bytes=VMEM_LIMIT),
    )(info, own, partner, cos, sin)


def scores_of(queries, keys):
    return lax.dot_general(queries, keys, (((1,), (1,)), ((), ())), preferred_element_type=F32)


def weights_of(scores, top):
    return jnp.exp2(scores * SCALE2 - top * SCALE2)


def columns_to_stats(columns):
    rows = columns[0].shape[0]
    lane = lax.broadcasted_iota(jnp.int32, (rows, 128), 1)
    stats = jnp.zeros((rows, 128), F32)
    for index, column in enumerate(columns):
        stats = jnp.where(lane == index, column, stats)
    return stats


def own_kernel(info, q, kv, weighted, stats):
    length = info[5]
    for tile in range(2):
        rows = slice(tile * 256, tile * 256 + 256)
        width = 256 * (tile + 1)
        row = tile * 256 + lax.broadcasted_iota(jnp.int32, (256, width), 0)
        key = lax.broadcasted_iota(jnp.int32, (256, width), 1)
        bias = jnp.where((key <= row) & (key < length), 0.0, NEG)
        tops, totals = [], []
        for head in range(4):
            cols = slice(head * HD, (head + 1) * HD)
            s = scores_of(q[rows, cols], kv[:width, :HD]) + bias
            top = jnp.max(s, axis=1, keepdims=True)
            e = weights_of(s, top)
            totals.append(jnp.sum(e, axis=1, keepdims=True))
            tops.append(top)
            weighted[rows, cols] = jnp.dot(e.astype(BF), kv[:width, HD:], preferred_element_type=F32)
        stats[rows, :] = columns_to_stats(tops + totals)


def own_attention(info, q, kv):
    return pl.pallas_call(
        own_kernel,
        out_shape=[jax.ShapeDtypeStruct((512, 512), F32), jax.ShapeDtypeStruct((512, 128), F32)],
        in_specs=[SM, VM, VM],
        out_specs=[VM, VM],
        compiler_params=pltpu.CompilerParams(vmem_limit_bytes=VMEM_LIMIT),
        cost_estimate=pl.CostEstimate(flops=4 * 4 * 512 * 512 * 128, bytes_accessed=3 << 20, transcendentals=1 << 20),
    )(info, q, kv)


def anchor_kernel(info, q, kv_zero, kv_one, weighted, stats, out):
    length, anchor_length = info[5], info[6]
    first_core = info[3] == 0
    kv = jnp.where(first_core, kv_zero[...], kv_one[...])
    keys, values = kv[:, :HD], kv[:, HD:]
    key = lax.broadcasted_iota(jnp.int32, (1, 512), 1)
    bias = jnp.where(key < anchor_length, 0.0, NEG)
    for tile in range(2):
        rows = slice(tile * 256, tile * 256 + 256)
        block = stats[rows, :]
        row = tile * 256 + lax.broadcasted_iota(jnp.int32, (256, HD), 0)
        for head in range(4):
            cols = slice(head * HD, (head + 1) * HD)
            s = scores_of(q[rows, cols], keys) + bias
            own_top, own_sum = block[:, head : head + 1], block[:, head + 4 : head + 5]
            top = jnp.maximum(own_top, jnp.max(s, axis=1, keepdims=True))
            e = weights_of(s, top)
            factor = weights_of(own_top, top)
            total = own_sum * factor + jnp.sum(e, axis=1, keepdims=True)
            both = weighted[rows, cols] * factor + jnp.dot(e.astype(BF), values, preferred_element_type=F32)
            out[rows, cols] = jnp.where(row < length, both / total, 0.0).astype(BF)


def anchor_attention(info, q, kv_zero, kv_one, weighted, stats):
    return pl.pallas_call(
        anchor_kernel,
        out_shape=jax.ShapeDtypeStruct((512, 512), BF),
        in_specs=[SM, VM, VM, VM, VM, VM],
        out_specs=VM,
        compiler_params=pltpu.CompilerParams(vmem_limit_bytes=VMEM_LIMIT),
        cost_estimate=pl.CostEstimate(flops=4 * 4 * 512 * 512 * 128, bytes_accessed=3 << 20, transcendentals=1 << 20),
    )(info, q, kv_zero, kv_one, weighted, stats)


def question_kernel(info, q_own, q_other, kv_0, kv_1, kv_2, kv_3, out_own, out_other):
    kvs = (kv_0, kv_1, kv_2, kv_3)
    z, core, ctx = info[2], info[3], info[4]
    lengths = [info[5], info[7], info[8], info[9]]
    places = [z, (z + 3) % 4, (z + 1) % 4, (z + 2) % 4]
    stacked = [q_own[:, h * HD : (h + 1) * HD] for h in range(4)]
    stacked += [q_other[:, h * HD : (h + 1) * HD] for h in range(4)]
    q = jnp.concatenate(stacked, axis=0)
    scores = []
    key = lax.broadcasted_iota(jnp.int32, (1, 512), 1)
    for kv, length in zip(kvs, lengths):
        scores.append(scores_of(q, kv[:ROWS, :HD]) + jnp.where(key < length, 0.0, NEG))
    row = lax.broadcasted_iota(jnp.int32, (256, 128), 0)
    lane = lax.broadcasted_iota(jnp.int32, (256, 128), 1)
    row_id = row % 32 + 32 * jnp.where(row < 128, ctx, ctx + 1 - 2 * core)
    block = jnp.where(lane < 64, jnp.where(lane < 32, places[0], places[1]), jnp.where(lane < 96, places[2], places[3]))
    key_id = lane % 32 + 32 * (2 * block + core)
    asked_keys = jnp.concatenate([kv[ROWS:, :HD] for kv in kvs], axis=0)
    asked_values = jnp.concatenate([kv[ROWS:, HD:] for kv in kvs], axis=0)
    scores.append(jnp.where(key_id <= row_id, scores_of(q, asked_keys), NEG))
    top = jnp.max(scores[-1], axis=1, keepdims=True)
    for s in scores[:-1]:
        top = jnp.maximum(top, jnp.max(s, axis=1, keepdims=True))
    values = [kv[:ROWS, HD:] for kv in kvs] + [asked_values]
    total = jnp.zeros((256, 1), F32)
    both = jnp.zeros((256, HD), F32)
    for s, value in zip(scores, values):
        e = weights_of(s, top)
        total = total + jnp.sum(e, axis=1, keepdims=True)
        both = both + jnp.dot(e.astype(BF), value, preferred_element_type=F32)
    for out, start in ((out_own, 0), (out_other, 128)):
        tops, totals = [], []
        for head in range(4):
            rows = slice(start + head * 32, start + head * 32 + 32)
            out[:, head * HD : (head + 1) * HD] = both[rows]
            tops.append(top[rows])
            totals.append(total[rows])
        out[:, 512:640] = columns_to_stats(tops + totals)


def question_attention(info, q_own, q_other, kvs):
    part = jax.ShapeDtypeStruct((32, 640), F32)
    return pl.pallas_call(
        question_kernel,
        out_shape=[part, part],
        in_specs=[SM] + [VM] * 6,
        out_specs=[VM, VM],
        compiler_params=pltpu.CompilerParams(vmem_limit_bytes=VMEM_LIMIT),
        cost_estimate=pl.CostEstimate(flops=4 * 256 * 2176 * 128, bytes_accessed=2 << 20, transcendentals=1 << 19),
    )(info, q_own, q_other, *kvs)


def merge_kernel(a, b, out):
    stat_a, stat_b = a[:, 512:640], b[:, 512:640]
    for head in range(4):
        cols = slice(head * HD, (head + 1) * HD)
        top_a, top_b = stat_a[:, head : head + 1], stat_b[:, head : head + 1]
        top = jnp.maximum(top_a, top_b)
        factor_a, factor_b = weights_of(top_a, top), weights_of(top_b, top)
        total = stat_a[:, head + 4 : head + 5] * factor_a + stat_b[:, head + 4 : head + 5] * factor_b
        out[:, cols] = ((a[:, cols] * factor_a + b[:, cols] * factor_b) / total).astype(BF)


def merge(a, b):
    return pl.pallas_call(
        merge_kernel,
        out_shape=jax.ShapeDtypeStruct((32, 512), BF),
        in_specs=[VM, VM],
        out_specs=VM,
        compiler_params=pltpu.CompilerParams(vmem_limit_bytes=VMEM_LIMIT),
    )(a, b)


PLAN_0 = [((0, 0), 0, 512, [(0, 0, 512)])]
PLAN_1 = [
    ((-1, 0), 0, 512, [(0, 0, 512)]),
    ((1, 0), 0, 512, [(1, 0, 512)]),
    ((0, -1), 0, 512, [(2, 0, 512)]),
    ((0, 1), 0, 512, [(3, 0, 512)]),
    ((2, 0), 0, 256, [(4, 0, 256)]),
    ((0, 2), 256, 512, [(5, 0, 256)]),
]
PLAN_2 = [
    ((-1, -1), 0, 512, [(0, 0, 256), (2, 0, 256)]),
    ((1, -1), 0, 512, [(0, 256, 256), (3, 0, 256)]),
    ((-1, 1), 0, 512, [(1, 0, 256), (2, 256, 256)]),
    ((1, 1), 0, 512, [(1, 256, 256), (3, 256, 256)]),
    ((2, -1), 0, 256, [(0, 512, 256)]),
    ((2, 1), 0, 256, [(1, 512, 256)]),
    ((-1, 2), 256, 512, [(2, 512, 256)]),
    ((1, 2), 256, 512, [(3, 512, 256)]),
    ((0, 2), 0, 256, [(0, 768, 128), (1, 768, 128)]),
    ((2, 0), 256, 512, [(2, 768, 128), (3, 768, 128)]),
]
PLAN_3 = [
    ((2, 2), 0, 512, [(1, 128, 256), (3, 128, 256)]),
    ((-1, 2), 0, 256, [(0, 0, 256)]),
    ((1, 2), 0, 256, [(0, 256, 128), (1, 0, 128)]),
    ((2, -1), 256, 512, [(2, 0, 256)]),
    ((2, 1), 256, 512, [(2, 256, 128), (3, 0, 128)]),
]
NEAR_Y = [(0, 0, 256), (1, 0, 256), (4, 0, 256)]
NEAR_X = [(2, 256, 256), (3, 256, 256), (5, 0, 256)]
PACK_2 = [NEAR_Y + [(2, 0, 128)], NEAR_Y + [(3, 128, 128)], NEAR_X + [(0, 256, 128)], NEAR_X + [(1, 384, 128)]]
PACK_3 = [[(0, 0, 384)], [(1, 384, 384)], [(2, 0, 384)], [(3, 384, 384)]]


def tables_of(positions):
    inverse_freq = ROPE_BASE ** (-(jnp.arange(HD // 2, dtype=jnp.float32) * 2.0 / HD))
    inverse_freq = jnp.concatenate([inverse_freq, inverse_freq])
    phases = positions.astype(jnp.float32)[:, None] * inverse_freq[None, :]
    signs = jnp.where(jnp.arange(HD) < HD // 2, -1.0, 1.0).astype(jnp.float32)
    return jnp.cos(phases), jnp.sin(phases) * signs[None, :]


def shift_z(array, dz):
    pairs = [(i, ((i // 2 + dz) % 4) * 2 + i % 2) for i in range(8)]
    return lax.ppermute(array, "ctx", pairs)


def per_device(context, question, w_query, w_key, w_value, lengths, owner):
    ctx = lax.axis_index("ctx")
    z, core = ctx // 2, ctx % 2
    heads = lax.axis_index("heads")
    y, x = heads // 4, heads % 4
    weights = (w_query, w_key.T, w_value.T)
    ids = jnp.arange(8, dtype=jnp.int32)
    own_offset = jnp.sum(jnp.where(ids < ctx, lengths, 0))
    own_length = jnp.sum(jnp.where(ids == ctx, lengths, 0))
    filled = jnp.sum(lengths)
    anchor_length = jnp.where(ctx > 0, lengths[0], 0)

    def length_of(dz):
        return jnp.sum(jnp.where(ids == ((z + dz) % 4) * 2 + core, lengths, 0))

    info = jnp.stack(
        [y, x, z, core, ctx, own_length, anchor_length, length_of(3), length_of(1), length_of(2)]
    ).astype(jnp.int32)

    far_y = shift_heads(lax.slice_in_dim(context, 0, 256, axis=0), 2, 0)
    far_x = shift_heads(lax.slice_in_dim(context, 256, 512, axis=0), 0, 2)
    up = shift_heads(context, 1, 0)
    right = shift_heads(context, 0, 1)
    left = shift_heads(context, 0, -1)
    far_y, again, asked = lax.optimization_barrier((far_y, context, question))
    down = shift_heads(again, -1, 0)

    share = lax.all_to_all(asked[0].reshape(8, 32, 512), "ctx", 0, 0)
    share = lax.dynamic_index_in_dim(share, owner[0], 0, False)
    accs = project(info, [again], PLAN_0, weights, None, True, True)
    tables = tables_of(
        jnp.concatenate(
            [own_offset + jnp.arange(ROWS, dtype=jnp.int32), filled + 32 * ctx + jnp.arange(ASKED, dtype=jnp.int32)]
        )
    )
    up, accs, share = lax.optimization_barrier((up, accs, share))

    to_right, to_left, to_up, to_down = pack(PACK_2, [up, down, right, left, far_y, far_x])
    a_right, a_left = shift_heads(to_right, 0, 1), shift_heads(to_left, 0, -1)
    b_up, b_down = shift_heads(to_up, 1, 0), shift_heads(to_down, -1, 0)
    up, to_right = lax.optimization_barrier((up, to_right))
    accs = project(info, [up, down, right, left, far_y, far_x], PLAN_1, weights, accs, True, True)
    share, accs = lax.optimization_barrier((share, accs))
    pieces = lax.all_to_all(jnp.broadcast_to(share[None], (16, 32, 512)), "heads", 0, 0)

    a_right, a_left, b_up, b_down, accs = lax.optimization_barrier((a_right, a_left, b_up, b_down, accs))
    to_right, to_left, to_up, to_down = pack(PACK_3, [a_right, a_left, b_up, b_down])
    last = [
        shift_heads(to_right, 0, 1),
        shift_heads(to_left, 0, -1),
        shift_heads(to_up, 1, 0),
        shift_heads(to_down, -1, 0),
    ]
    accs = project(info, [a_right, a_left, b_up, b_down], PLAN_2, weights, accs, True, True)
    q_share = question_project(pieces, weights, tables)

    (halves,) = project(info, last, PLAN_3, weights, accs, False, True, True, asked=q_share)
    (queries,) = project(info, last, PLAN_3, weights, accs, True, False, True, tables)
    partner = swap_heads(halves, 0, 1)
    q_asked = q_share[:, :512]
    q_other = swap_ctx(q_asked, 0, 1)
    partner, queries, q_other = lax.optimization_barrier((partner, queries, q_other))
    kv = key_value(info, halves, partner, *tables)

    below, above, across = shift_z(kv, 1), shift_z(kv, -1), shift_z(kv, 2)
    weighted, stats = own_attention(info, queries, kv)
    below, above, across, weighted = lax.optimization_barrier((below, above, across, weighted))
    nearer = jnp.where(z == 0, kv[:ROWS], jnp.where(z == 1, below[:ROWS], jnp.where(z == 2, across[:ROWS], above[:ROWS])))
    from_zero = lax.ppermute(nearer, "ctx", [(0, 1), (2, 3), (4, 5), (6, 7)])
    part, part_other = question_attention(info, q_asked, q_other, [kv, below, above, across])
    from_zero, part = lax.optimization_barrier((from_zero, part))
    context_attn = anchor_attention(info, queries, nearer, from_zero, weighted, stats)
    question_attn = merge(part, swap_ctx(part_other, 0, 1))
    return (context_attn, question_attn)


def solution(mesh):
    in_specs = (
        P("ctx", "heads"),
        P("ctx", None, "heads"),
        P(None, "heads"),
        P(None, "heads"),
        P(None, "heads"),
        P(),
        P(),
    )
    out_specs = (P("ctx", "heads"), P("ctx", "heads"))
    return jax.shard_map(
        per_device, mesh=mesh, in_specs=in_specs, out_specs=out_specs, check_vma=False
    )
```

```python
import functools

import jax
import jax.numpy as jnp
from jax import lax
from jax.experimental import pallas as pl
from jax.experimental.pallas import tpu as pltpu
from jax.sharding import PartitionSpec as P

HD = 128
ROPE_BASE = 500000.0
BF = jnp.bfloat16
F32 = jnp.float32
VMEM_LIMIT = 8 * 1024 * 1024
WIDE_LIMIT = 49 * 1024 * 1024
AHEAD = 4
NEG = -1e30
SCALE2 = HD ** (-0.5) * 1.4426950408889634
ROWS = 512
ASKED = 32
ALL = ROWS + ASKED

HBM = pl.BlockSpec(memory_space=pltpu.HBM)
VM = pl.BlockSpec(memory_space=pltpu.VMEM)
SM = pl.BlockSpec(memory_space=pltpu.SMEM)


def shift_heads(array, dy, dx):
    pairs = [(i, ((i // 4 + dy) % 4) * 4 + (i % 4 + dx) % 4) for i in range(16)]
    return lax.ppermute(array, "heads", pairs)


def swap_heads(array, my, mx):
    pairs = [(i, ((i // 4) ^ my) * 4 + ((i % 4) ^ mx)) for i in range(16)]
    return lax.ppermute(array, "heads", pairs)


def swap_ctx(array, mz, mc):
    pairs = [(i, ((i // 2) ^ mz) * 2 + ((i % 2) ^ mc)) for i in range(8)]
    return lax.ppermute(array, "ctx", pairs)


def pack_kernel(plan, n_in, *refs):
    ins, outs = refs[:n_in], refs[n_in:]
    for out, pieces in zip(outs, plan):
        row = 0
        for operand, start, count in pieces:
            out[row : row + count, :] = ins[operand][start : start + count, :]
            row += count


def pack(plan, ins):
    return pl.pallas_call(
        functools.partial(pack_kernel, plan, len(ins)),
        out_shape=[jax.ShapeDtypeStruct((sum(p[2] for p in pieces), 512), BF) for pieces in plan],
        in_specs=[VM] * len(ins),
        out_specs=[VM] * len(plan),
        compiler_params=pltpu.CompilerParams(vmem_limit_bytes=VMEM_LIMIT),
        cost_estimate=pl.CostEstimate(flops=0, bytes_accessed=1 << 20, transcendentals=0),
    )(*ins)


def turn(part, cos, sin):
    return (part * cos + pltpu.roll(part, HD // 2, 1) * sin).astype(BF)


def fetcher(bases, weights, buffers, sem, with_q, with_kv):
    wq, wk, wv = weights
    q_buf, kv_buf = buffers
    copies = []
    for slot, base in enumerate(bases):
        each = []
        if with_kv:
            for part, source in enumerate((wk, wv)):
                target = kv_buf.at[slot, pl.ds(64 * part, 64), :]
                each.append(pltpu.make_async_copy(source.at[:, pl.ds(base, 512)], target, sem.at[slot, part]))
        if with_q:
            each.append(pltpu.make_async_copy(wq.at[pl.ds(base, 512), :], q_buf.at[slot], sem.at[slot, 2]))
        copies.append(each)
    for each in copies[:AHEAD]:
        for copy in each:
            copy.start()

    def ready(slot):
        for copy in copies[slot]:
            copy.wait()
        for copy in copies[slot + AHEAD] if slot + AHEAD < len(copies) else ():
            copy.start()

    return ready


def project_kernel(plan, n_x, with_q, with_kv, has_acc, finish, *refs):
    refs = list(refs)
    take = lambda count: [refs.pop(0) for _ in range(count)]
    (info,) = take(1)
    xs = take(n_x)
    wq = take(1)[0] if with_q else None
    wk, wv = take(2) if with_kv else (None, None)
    acc_q = take(1)[0] if has_acc and with_q else None
    acc_kv = take(1)[0] if has_acc and with_kv else None
    cos, sin = take(2) if finish and with_q else (None, None)
    asked = take(1)[0] if finish and with_kv else None
    q_out = take(1)[0] if with_q else None
    kv_out = take(1)[0] if with_kv else None
    q_buf = take(1)[0] if with_q else None
    kv_buf = take(1)[0] if with_kv else None
    q_sum = take(1)[0] if finish and with_q else q_out
    kv_sum = take(1)[0] if finish and with_kv else kv_out
    (sem,) = take(1)
    y, x = info[0], info[1]
    bases = [pl.multiple_of((((y + dy + 4) % 4) * 4 + (x + dx + 4) % 4) * 512, 512) for (dy, dx), *_ in plan]
    ready = fetcher(bases, (wq, wk, wv), (q_buf, kv_buf), sem, with_q, with_kv)
    if has_acc:
        if with_q:
            q_sum[...] = acc_q[...]
        if with_kv:
            kv_sum[...] = acc_kv[...]
    for slot, (_, low, high, uses) in enumerate(plan):
        ready(slot)
        parts = [xs[operand][pl.ds(start, count), :] for operand, start, count in uses]
        piece = parts[0] if len(parts) == 1 else jnp.concatenate(parts, axis=0)
        fresh = slot == 0 and not has_acc
        if with_kv:
            term = lax.dot_general(piece, kv_buf[slot], (((1,), (1,)), ((), ())), preferred_element_type=F32)
            kv_sum[low:high, :] = term if fresh else kv_sum[low:high, :] + term
        if with_q:
            term = jnp.dot(piece, q_buf[slot], preferred_element_type=F32)
            q_sum[low:high, :] = term if fresh else q_sum[low:high, :] + term
    if finish and with_kv:
        kv_out[:ROWS, :] = kv_sum[...].astype(BF)
        kv_out[ROWS:, :] = asked[:, 512:640]
    if finish and with_q:
        for head in range(4):
            cols = slice(head * HD, (head + 1) * HD)
            q_out[:, cols] = turn(q_sum[:, cols], cos[:ROWS, :], sin[:ROWS, :])


def project(info, xs, plan, weights, accs, with_q, with_kv, finish=False, tables=None, asked=None):
    wq, wk, wv = weights
    slots = len(plan)
    operands, specs = [info] + list(xs), [SM] + [VM] * len(xs)
    if with_q:
        operands.append(wq)
        specs.append(HBM)
    if with_kv:
        operands += [wk, wv]
        specs += [HBM, HBM]
    has_acc = accs is not None
    if has_acc:
        if with_q:
            operands.append(accs[0])
            specs.append(VM)
        if with_kv:
            operands.append(accs[1])
            specs.append(VM)
    if finish and with_q:
        operands += list(tables)
        specs += [VM, VM]
    if finish and with_kv:
        operands.append(asked)
        specs.append(VM)
    outs, scratch, sums = [], [], []
    if with_q:
        outs.append(jax.ShapeDtypeStruct((ROWS, 512), BF if finish else F32))
        scratch.append(pltpu.VMEM((slots, 512, 512), BF))
        if finish:
            sums.append(pltpu.VMEM((ROWS, 512), F32))
    if with_kv:
        outs.append(jax.ShapeDtypeStruct((ALL, 128), BF) if finish else jax.ShapeDtypeStruct((ROWS, 128), F32))
        scratch.append(pltpu.VMEM((slots, 128, 512), BF))
        if finish:
            sums.append(pltpu.VMEM((ROWS, 128), F32))
    scratch += sums + [pltpu.SemaphoreType.DMA((slots, 3))]
    columns = (512 if with_q else 0) + (128 if with_kv else 0)
    used = sum(high - low for _, low, high, _ in plan)
    return pl.pallas_call(
        functools.partial(project_kernel, plan, len(xs), with_q, with_kv, has_acc, finish),
        out_shape=outs,
        in_specs=specs,
        out_specs=[VM] * len(outs),
        scratch_shapes=scratch,
        compiler_params=pltpu.CompilerParams(vmem_limit_bytes=WIDE_LIMIT),
        cost_estimate=pl.CostEstimate(
            flops=2 * used * 512 * columns, bytes_accessed=slots * 512 * columns * 2, transcendentals=0
        ),
    )(*operands)


def question_project_kernel(pieces, wq, wk, wv, cos, sin, out, q_buf, kv_buf, sem):
    ready = fetcher([place * 512 for place in range(16)], (wq, wk, wv), (q_buf, kv_buf), sem, True, True)
    q_sum, kv_sum = None, None
    for place in range(16):
        ready(place)
        piece = pieces[place]
        kv_term = lax.dot_general(piece, kv_buf[place], (((1,), (1,)), ((), ())), preferred_element_type=F32)
        q_term = jnp.dot(piece, q_buf[place], preferred_element_type=F32)
        q_sum = q_term if q_sum is None else q_sum + q_term
        kv_sum = kv_term if kv_sum is None else kv_sum + kv_term
    for head in range(4):
        cols = slice(head * HD, (head + 1) * HD)
        out[:, cols] = turn(q_sum[:, cols], cos[ROWS : ROWS + 32, :], sin[ROWS : ROWS + 32, :])
    out[:, 512:640] = kv_sum.astype(BF)


def question_project(pieces, weights, tables):
    return pl.pallas_call(
        question_project_kernel,
        out_shape=jax.ShapeDtypeStruct((32, 640), BF),
        in_specs=[VM, HBM, HBM, HBM, VM, VM],
        out_specs=VM,
        scratch_shapes=[
            pltpu.VMEM((16, 512, 512), BF),
            pltpu.VMEM((16, 128, 512), BF),
            pltpu.SemaphoreType.DMA((16, 3)),
        ],
        compiler_params=pltpu.CompilerParams(vmem_limit_bytes=WIDE_LIMIT),
        cost_estimate=pl.CostEstimate(flops=2 * 256 * 8192 * 640, bytes_accessed=8192 * 640 * 2, transcendentals=0),
    )(pieces, *weights, *tables)


def key_value_kernel(info, own, partner, cos, sin, out):
    is_lower = info[1] % 2 == 0
    mine, other = own[...].astype(F32), partner[...].astype(F32)
    low = jnp.where(is_lower, mine, other)
    high = jnp.where(is_lower, other, mine)
    lane = lax.broadcasted_iota(jnp.int32, low.shape, 1)
    keys = jnp.where(lane < 64, low, pltpu.roll(high, 64, 1))
    values = jnp.where(lane < 64, pltpu.roll(low, 64, 1), high)
    out[:, :HD] = (keys * cos[...] + pltpu.roll(keys, 64, 1) * sin[...]).astype(BF)
    out[:, HD:] = values.astype(BF)


def key_value(info, own, partner, cos, sin):
    return pl.pallas_call(
        key_value_kernel,
        out_shape=jax.ShapeDtypeStruct((ALL, 2 * HD), BF),
        in_specs=[SM, VM, VM, VM, VM],
        out_specs=VM,
        compiler_params=pltpu.CompilerParams(vmem_limit_bytes=VMEM_LIMIT),
    )(info, own, partner, cos, sin)


def scores_of(queries, keys):
    return lax.dot_general(queries, keys, (((1,), (1,)), ((), ())), preferred_element_type=F32)


def weights_of(scores, top):
    return jnp.exp2(scores * SCALE2 - top * SCALE2)


def columns_to_stats(columns):
    rows = columns[0].shape[0]
    lane = lax.broadcasted_iota(jnp.int32, (rows, 128), 1)
    stats = jnp.zeros((rows, 128), F32)
    for index, column in enumerate(columns):
        stats = jnp.where(lane == index, column, stats)
    return stats


def own_kernel(info, q, kv, weighted, stats):
    length = info[5]
    for tile in range(2):
        rows = slice(tile * 256, tile * 256 + 256)
        width = 256 * (tile + 1)
        row = tile * 256 + lax.broadcasted_iota(jnp.int32, (256, width), 0)
        key = lax.broadcasted_iota(jnp.int32, (256, width), 1)
        bias = jnp.where((key <= row) & (key < length), 0.0, NEG)
        tops, totals = [], []
        for head in range(4):
            cols = slice(head * HD, (head + 1) * HD)
            s = scores_of(q[rows, cols], kv[:width, :HD]) + bias
            top = jnp.max(s, axis=1, keepdims=True)
            e = weights_of(s, top)
            totals.append(jnp.sum(e, axis=1, keepdims=True))
            tops.append(top)
            weighted[rows, cols] = jnp.dot(e.astype(BF), kv[:width, HD:], preferred_element_type=F32)
        stats[rows, :] = columns_to_stats(tops + totals)


def own_attention(info, q, kv):
    return pl.pallas_call(
        own_kernel,
        out_shape=[jax.ShapeDtypeStruct((512, 512), F32), jax.ShapeDtypeStruct((512, 128), F32)],
        in_specs=[SM, VM, VM],
        out_specs=[VM, VM],
        compiler_params=pltpu.CompilerParams(vmem_limit_bytes=VMEM_LIMIT),
        cost_estimate=pl.CostEstimate(flops=4 * 4 * 512 * 512 * 128, bytes_accessed=3 << 20, transcendentals=1 << 20),
    )(info, q, kv)


def anchor_kernel(info, q, kv_zero, kv_one, weighted, stats, out):
    length, anchor_length = info[5], info[6]
    first_core = info[3] == 0
    kv = jnp.where(first_core, kv_zero[...], kv_one[...])
    keys, values = kv[:, :HD], kv[:, HD:]
    key = lax.broadcasted_iota(jnp.int32, (1, 512), 1)
    bias = jnp.where(key < anchor_length, 0.0, NEG)
    for tile in range(2):
        rows = slice(tile * 256, tile * 256 + 256)
        block = stats[rows, :]
        row = tile * 256 + lax.broadcasted_iota(jnp.int32, (256, HD), 0)
        for head in range(4):
            cols = slice(head * HD, (head + 1) * HD)
            s = scores_of(q[rows, cols], keys) + bias
            own_top, own_sum = block[:, head : head + 1], block[:, head + 4 : head + 5]
            top = jnp.maximum(own_top, jnp.max(s, axis=1, keepdims=True))
            e = weights_of(s, top)
            factor = weights_of(own_top, top)
            total = own_sum * factor + jnp.sum(e, axis=1, keepdims=True)
            both = weighted[rows, cols] * factor + jnp.dot(e.astype(BF), values, preferred_element_type=F32)
            out[rows, cols] = jnp.where(row < length, both / total, 0.0).astype(BF)


def anchor_attention(info, q, kv_zero, kv_one, weighted, stats):
    return pl.pallas_call(
        anchor_kernel,
        out_shape=jax.ShapeDtypeStruct((512, 512), BF),
        in_specs=[SM, VM, VM, VM, VM, VM],
        out_specs=VM,
        compiler_params=pltpu.CompilerParams(vmem_limit_bytes=VMEM_LIMIT),
        cost_estimate=pl.CostEstimate(flops=4 * 4 * 512 * 512 * 128, bytes_accessed=3 << 20, transcendentals=1 << 20),
    )(info, q, kv_zero, kv_one, weighted, stats)


def question_kernel(info, q_own, q_other, kv_0, kv_1, kv_2, kv_3, out_own, out_other):
    kvs = (kv_0, kv_1, kv_2, kv_3)
    z, core, ctx = info[2], info[3], info[4]
    lengths = [info[5], info[7], info[8], info[9]]
    places = [z, (z + 3) % 4, (z + 1) % 4, (z + 2) % 4]
    stacked = [q_own[:, h * HD : (h + 1) * HD] for h in range(4)]
    stacked += [q_other[:, h * HD : (h + 1) * HD] for h in range(4)]
    q = jnp.concatenate(stacked, axis=0)
    scores = []
    key = lax.broadcasted_iota(jnp.int32, (1, 512), 1)
    for kv, length in zip(kvs, lengths):
        scores.append(scores_of(q, kv[:ROWS, :HD]) + jnp.where(key < length, 0.0, NEG))
    row = lax.broadcasted_iota(jnp.int32, (256, 128), 0)
    lane = lax.broadcasted_iota(jnp.int32, (256, 128), 1)
    row_id = row % 32 + 32 * jnp.where(row < 128, ctx, ctx + 1 - 2 * core)
    block = jnp.where(lane < 64, jnp.where(lane < 32, places[0], places[1]), jnp.where(lane < 96, places[2], places[3]))
    key_id = lane % 32 + 32 * (2 * block + core)
    asked_keys = jnp.concatenate([kv[ROWS:, :HD] for kv in kvs], axis=0)
    asked_values = jnp.concatenate([kv[ROWS:, HD:] for kv in kvs], axis=0)
    scores.append(jnp.where(key_id <= row_id, scores_of(q, asked_keys), NEG))
    top = jnp.max(scores[-1], axis=1, keepdims=True)
    for s in scores[:-1]:
        top = jnp.maximum(top, jnp.max(s, axis=1, keepdims=True))
    values = [kv[:ROWS, HD:] for kv in kvs] + [asked_values]
    total = jnp.zeros((256, 1), F32)
    both = jnp.zeros((256, HD), F32)
    for s, value in zip(scores, values):
        e = weights_of(s, top)
        total = total + jnp.sum(e, axis=1, keepdims=True)
        both = both + jnp.dot(e.astype(BF), value, preferred_element_type=F32)
    for out, start in ((out_own, 0), (out_other, 128)):
        tops, totals = [], []
        for head in range(4):
            rows = slice(start + head * 32, start + head * 32 + 32)
            out[:, head * HD : (head + 1) * HD] = both[rows]
            tops.append(top[rows])
            totals.append(total[rows])
        out[:, 512:640] = columns_to_stats(tops + totals)


def question_attention(info, q_own, q_other, kvs):
    part = jax.ShapeDtypeStruct((32, 640), F32)
    return pl.pallas_call(
        question_kernel,
        out_shape=[part, part],
        in_specs=[SM] + [VM] * 6,
        out_specs=[VM, VM],
        compiler_params=pltpu.CompilerParams(vmem_limit_bytes=VMEM_LIMIT),
        cost_estimate=pl.CostEstimate(flops=4 * 256 * 2176 * 128, bytes_accessed=2 << 20, transcendentals=1 << 19),
    )(info, q_own, q_other, *kvs)


def merge_kernel(a, b, out):
    stat_a, stat_b = a[:, 512:640], b[:, 512:640]
    for head in range(4):
        cols = slice(head * HD, (head + 1) * HD)
        top_a, top_b = stat_a[:, head : head + 1], stat_b[:, head : head + 1]
        top = jnp.maximum(top_a, top_b)
        factor_a, factor_b = weights_of(top_a, top), weights_of(top_b, top)
        total = stat_a[:, head + 4 : head + 5] * factor_a + stat_b[:, head + 4 : head + 5] * factor_b
        out[:, cols] = ((a[:, cols] * factor_a + b[:, cols] * factor_b) / total).astype(BF)


def merge(a, b):
    return pl.pallas_call(
        merge_kernel,
        out_shape=jax.ShapeDtypeStruct((32, 512), BF),
        in_specs=[VM, VM],
        out_specs=VM,
        compiler_params=pltpu.CompilerParams(vmem_limit_bytes=VMEM_LIMIT),
    )(a, b)


PLAN_1 = [
    ((0, 0), 0, 512, [(0, 0, 512)]),
    ((-1, 0), 0, 512, [(1, 0, 512)]),
    ((1, 0), 0, 512, [(2, 0, 512)]),
    ((0, -1), 0, 512, [(3, 0, 512)]),
    ((0, 1), 0, 512, [(4, 0, 512)]),
    ((2, 0), 0, 256, [(5, 0, 256)]),
    ((0, 2), 256, 512, [(6, 0, 256)]),
]
PLAN_2 = [
    ((-1, -1), 0, 512, [(0, 0, 256), (2, 0, 256)]),
    ((1, -1), 0, 512, [(0, 256, 256), (3, 0, 256)]),
    ((-1, 1), 0, 512, [(1, 0, 256), (2, 256, 256)]),
    ((1, 1), 0, 512, [(1, 256, 256), (3, 256, 256)]),
    ((2, -1), 0, 256, [(0, 512, 256)]),
    ((2, 1), 0, 256, [(1, 512, 256)]),
    ((-1, 2), 256, 512, [(2, 512, 256)]),
    ((1, 2), 256, 512, [(3, 512, 256)]),
    ((0, 2), 0, 256, [(0, 768, 128), (1, 768, 128)]),
    ((2, 0), 256, 512, [(2, 768, 128), (3, 768, 128)]),
]
PLAN_3 = [
    ((2, 2), 0, 512, [(1, 128, 256), (3, 128, 256)]),
    ((-1, 2), 0, 256, [(0, 0, 256)]),
    ((1, 2), 0, 256, [(0, 256, 128), (1, 0, 128)]),
    ((2, -1), 256, 512, [(2, 0, 256)]),
    ((2, 1), 256, 512, [(2, 256, 128), (3, 0, 128)]),
]
NEAR_Y = [(0, 0, 256), (1, 0, 256), (4, 0, 256)]
NEAR_X = [(2, 256, 256), (3, 256, 256), (5, 0, 256)]
PACK_2 = [NEAR_Y + [(2, 0, 128)], NEAR_Y + [(3, 128, 128)], NEAR_X + [(0, 256, 128)], NEAR_X + [(1, 384, 128)]]
PACK_3 = [[(0, 0, 384)], [(1, 384, 384)], [(2, 0, 384)], [(3, 384, 384)]]


def tables_of(positions):
    inverse_freq = ROPE_BASE ** (-(jnp.arange(HD // 2, dtype=jnp.float32) * 2.0 / HD))
    inverse_freq = jnp.concatenate([inverse_freq, inverse_freq])
    phases = positions.astype(jnp.float32)[:, None] * inverse_freq[None, :]
    signs = jnp.where(jnp.arange(HD) < HD // 2, -1.0, 1.0).astype(jnp.float32)
    return jnp.cos(phases), jnp.sin(phases) * signs[None, :]


def shift_z(array, dz):
    pairs = [(i, ((i // 2 + dz) % 4) * 2 + i % 2) for i in range(8)]
    return lax.ppermute(array, "ctx", pairs)


def per_device(context, question, w_query, w_key, w_value, lengths, owner):
    ctx = lax.axis_index("ctx")
    z, core = ctx // 2, ctx % 2
    heads = lax.axis_index("heads")
    y, x = heads // 4, heads % 4
    weights = (w_query, w_key.T, w_value.T)
    ids = jnp.arange(8, dtype=jnp.int32)
    own_offset = jnp.sum(jnp.where(ids < ctx, lengths, 0))
    own_length = jnp.sum(jnp.where(ids == ctx, lengths, 0))
    filled = jnp.sum(lengths)
    anchor_length = jnp.where(ctx > 0, lengths[0], 0)

    def length_of(dz):
        return jnp.sum(jnp.where(ids == ((z + dz) % 4) * 2 + core, lengths, 0))

    info = jnp.stack(
        [y, x, z, core, ctx, own_length, anchor_length, length_of(3), length_of(1), length_of(2)]
    ).astype(jnp.int32)

    far_y = shift_heads(lax.slice_in_dim(context, 0, 256, axis=0), 2, 0)
    far_x = shift_heads(lax.slice_in_dim(context, 256, 512, axis=0), 0, 2)
    up = shift_heads(context, 1, 0)
    right = shift_heads(context, 0, 1)
    left = shift_heads(context, 0, -1)
    far_y, far_x, again, asked = lax.optimization_barrier((far_y, far_x, context, question))
    down = shift_heads(again, -1, 0)

    share = lax.all_to_all(asked[0].reshape(8, 32, 512), "ctx", 0, 0)
    share = lax.dynamic_index_in_dim(share, owner[0], 0, False)
    tables = tables_of(
        jnp.concatenate(
            [own_offset + jnp.arange(ROWS, dtype=jnp.int32), filled + 32 * ctx + jnp.arange(ASKED, dtype=jnp.int32)]
        )
    )
    up, share = lax.optimization_barrier((up, share))

    to_right, to_left, to_up, to_down = pack(PACK_2, [up, down, right, left, far_y, far_x])
    a_right, a_left = shift_heads(to_right, 0, 1), shift_heads(to_left, 0, -1)
    b_up, b_down = shift_heads(to_up, 1, 0), shift_heads(to_down, -1, 0)
    up, to_right = lax.optimization_barrier((up, to_right))
    accs = project(info, [context, up, down, right, left, far_y, far_x], PLAN_1, weights, None, True, True)
    share, accs = lax.optimization_barrier((share, accs))
    pieces = lax.all_to_all(jnp.broadcast_to(share[None], (16, 32, 512)), "heads", 0, 0)

    a_right, a_left, b_up, b_down, accs = lax.optimization_barrier((a_right, a_left, b_up, b_down, accs))
    to_right, to_left, to_up, to_down = pack(PACK_3, [a_right, a_left, b_up, b_down])
    last = [
        shift_heads(to_right, 0, 1),
        shift_heads(to_left, 0, -1),
        shift_heads(to_up, 1, 0),
        shift_heads(to_down, -1, 0),
    ]
    accs = project(info, [a_right, a_left, b_up, b_down], PLAN_2, weights, accs, True, True)
    q_share = question_project(pieces, weights, tables)

    (halves,) = project(info, last, PLAN_3, weights, accs, False, True, True, asked=q_share)
    (queries,) = project(info, last, PLAN_3, weights, accs, True, False, True, tables)
    partner = swap_heads(halves, 0, 1)
    q_asked = q_share[:, :512]
    q_other = swap_ctx(q_asked, 0, 1)
    partner, queries, q_other = lax.optimization_barrier((partner, queries, q_other))
    kv = key_value(info, halves, partner, *tables)

    below, above, across = shift_z(kv, 1), shift_z(kv, -1), shift_z(kv, 2)
    weighted, stats = own_attention(info, queries, kv)
    below, above, across, weighted = lax.optimization_barrier((below, above, across, weighted))
    nearer = jnp.where(z == 0, kv[:ROWS], jnp.where(z == 1, below[:ROWS], jnp.where(z == 2, across[:ROWS], above[:ROWS])))
    from_zero = lax.ppermute(nearer, "ctx", [(0, 1), (2, 3), (4, 5), (6, 7)])
    part, part_other = question_attention(info, q_asked, q_other, [kv, below, above, across])
    from_zero, part = lax.optimization_barrier((from_zero, part))
    context_attn = anchor_attention(info, queries, nearer, from_zero, weighted, stats)
    question_attn = merge(part, swap_ctx(part_other, 0, 1))
    return (context_attn, question_attn)


def solution(mesh):
    in_specs = (
        P("ctx", "heads"),
        P("ctx", None, "heads"),
        P(None, "heads"),
        P(None, "heads"),
        P(None, "heads"),
        P(),
        P(),
    )
    out_specs = (P("ctx", "heads"), P("ctx", "heads"))
    return jax.shard_map(
        per_device, mesh=mesh, in_specs=in_specs, out_specs=out_specs, check_vma=False
    )
```

```python
import functools

import jax
import jax.numpy as jnp
from jax import lax
from jax.experimental import pallas as pl
from jax.experimental.pallas import tpu as pltpu
from jax.sharding import PartitionSpec as P

HD = 128
ROPE_BASE = 500000.0
BF = jnp.bfloat16
F32 = jnp.float32
VMEM_LIMIT = 8 * 1024 * 1024
HOLD_LIMIT = 37 * 1024 * 1024
NEG = -1e30
SCALE2 = HD ** (-0.5) * 1.4426950408889634
ROWS = 512
ASKED = 32
ALL = ROWS + ASKED

HBM = pl.BlockSpec(memory_space=pltpu.HBM)
VM = pl.BlockSpec(memory_space=pltpu.VMEM)
SM = pl.BlockSpec(memory_space=pltpu.SMEM)


def shift_heads(array, dy, dx):
    pairs = [(i, ((i // 4 + dy) % 4) * 4 + (i % 4 + dx) % 4) for i in range(16)]
    return lax.ppermute(array, "heads", pairs)


def swap_heads(array, my, mx):
    pairs = [(i, ((i // 4) ^ my) * 4 + ((i % 4) ^ mx)) for i in range(16)]
    return lax.ppermute(array, "heads", pairs)


def swap_ctx(array, mz, mc):
    pairs = [(i, ((i // 2) ^ mz) * 2 + ((i % 2) ^ mc)) for i in range(8)]
    return lax.ppermute(array, "ctx", pairs)


def pack_kernel(plan, n_in, *refs):
    ins, outs = refs[:n_in], refs[n_in:]
    for out, pieces in zip(outs, plan):
        row = 0
        for operand, start, count in pieces:
            out[row : row + count, :] = ins[operand][start : start + count, :]
            row += count


def pack(plan, ins):
    return pl.pallas_call(
        functools.partial(pack_kernel, plan, len(ins)),
        out_shape=[jax.ShapeDtypeStruct((sum(p[2] for p in pieces), 512), BF) for pieces in plan],
        in_specs=[VM] * len(ins),
        out_specs=[VM] * len(plan),
        compiler_params=pltpu.CompilerParams(vmem_limit_bytes=VMEM_LIMIT),
        cost_estimate=pl.CostEstimate(flops=0, bytes_accessed=1 << 20, transcendentals=0),
    )(*ins)


def hold_kernel(wq, wk, wv, q_out, kv_out, sem):
    copies = []
    for part in range(8):
        rows = pl.ds(part * 1024, 1024)
        copies.append(pltpu.make_async_copy(wq.at[rows, :], q_out.at[rows, :], sem.at[part]))
    for part in range(4):
        cols = pl.ds(part * 2048, 2048)
        copies.append(pltpu.make_async_copy(wk.at[:, cols], kv_out.at[pl.ds(0, 64), cols], sem.at[8 + part]))
        copies.append(pltpu.make_async_copy(wv.at[:, cols], kv_out.at[pl.ds(64, 64), cols], sem.at[12 + part]))
    for copy in copies:
        copy.start()
    for copy in copies:
        copy.wait()


def hold(wq, wk, wv):
    return pl.pallas_call(
        hold_kernel,
        out_shape=[jax.ShapeDtypeStruct((8192, 512), BF), jax.ShapeDtypeStruct((128, 8192), BF)],
        in_specs=[HBM] * 3,
        out_specs=[VM, VM],
        scratch_shapes=[pltpu.SemaphoreType.DMA((16,))],
        compiler_params=pltpu.CompilerParams(vmem_limit_bytes=HOLD_LIMIT),
        cost_estimate=pl.CostEstimate(flops=0, bytes_accessed=20 << 20, transcendentals=0),
    )(wq, wk, wv)


def turn(part, cos, sin):
    return (part * cos + pltpu.roll(part, HD // 2, 1) * sin).astype(BF)


def project_kernel(plan, n_x, with_q, with_kv, has_acc, finish, *refs):
    refs = list(refs)
    take = lambda count: [refs.pop(0) for _ in range(count)]
    (info,) = take(1)
    xs = take(n_x)
    wq = take(1)[0] if with_q else None
    wkv = take(1)[0] if with_kv else None
    acc_q = take(1)[0] if has_acc and with_q else None
    acc_kv = take(1)[0] if has_acc and with_kv else None
    cos, sin = take(2) if finish and with_q else (None, None)
    asked = take(1)[0] if finish and with_kv else None
    q_out = take(1)[0] if with_q else None
    kv_out = take(1)[0] if with_kv else None
    q_sum = take(1)[0] if finish and with_q else q_out
    kv_sum = take(1)[0] if finish and with_kv else kv_out
    y, x = info[0], info[1]
    if has_acc:
        if with_q:
            q_sum[...] = acc_q[...]
        if with_kv:
            kv_sum[...] = acc_kv[...]
    for slot, ((dy, dx), low, high, uses) in enumerate(plan):
        base = pl.multiple_of((((y + dy + 4) % 4) * 4 + (x + dx + 4) % 4) * 512, 512)
        parts = [xs[operand][pl.ds(start, count), :] for operand, start, count in uses]
        piece = parts[0] if len(parts) == 1 else jnp.concatenate(parts, axis=0)
        fresh = slot == 0 and not has_acc
        if with_kv:
            both = wkv[:, pl.ds(base, 512)]
            term = lax.dot_general(piece, both, (((1,), (1,)), ((), ())), preferred_element_type=F32)
            kv_sum[low:high, :] = term if fresh else kv_sum[low:high, :] + term
        if with_q:
            term = jnp.dot(piece, wq[pl.ds(base, 512), :], preferred_element_type=F32)
            q_sum[low:high, :] = term if fresh else q_sum[low:high, :] + term
    if finish and with_kv:
        kv_out[:ROWS, :] = kv_sum[...].astype(BF)
        kv_out[ROWS:, :] = asked[:, 512:640]
    if finish and with_q:
        for head in range(4):
            cols = slice(head * HD, (head + 1) * HD)
            q_out[:, cols] = turn(q_sum[:, cols], cos[:ROWS, :], sin[:ROWS, :])


def project(info, xs, plan, weights, accs, with_q, with_kv, finish=False, tables=None, asked=None):
    wq, wkv = weights
    operands, specs = [info] + list(xs), [SM] + [VM] * len(xs)
    if with_q:
        operands.append(wq)
        specs.append(VM)
    if with_kv:
        operands.append(wkv)
        specs.append(VM)
    has_acc = accs is not None
    if has_acc:
        if with_q:
            operands.append(accs[0])
            specs.append(VM)
        if with_kv:
            operands.append(accs[1])
            specs.append(VM)
    if finish and with_q:
        operands += list(tables)
        specs += [VM, VM]
    if finish and with_kv:
        operands.append(asked)
        specs.append(VM)
    outs, scratch = [], []
    if with_q:
        outs.append(jax.ShapeDtypeStruct((ROWS, 512), BF if finish else F32))
        if finish:
            scratch.append(pltpu.VMEM((ROWS, 512), F32))
    if with_kv:
        outs.append(jax.ShapeDtypeStruct((ALL, 128), BF) if finish else jax.ShapeDtypeStruct((ROWS, 128), F32))
        if finish:
            scratch.append(pltpu.VMEM((ROWS, 128), F32))
    columns = (512 if with_q else 0) + (128 if with_kv else 0)
    used = sum(high - low for _, low, high, _ in plan)
    return pl.pallas_call(
        functools.partial(project_kernel, plan, len(xs), with_q, with_kv, has_acc, finish),
        out_shape=outs,
        in_specs=specs,
        out_specs=[VM] * len(outs),
        scratch_shapes=scratch,
        compiler_params=pltpu.CompilerParams(vmem_limit_bytes=VMEM_LIMIT),
        cost_estimate=pl.CostEstimate(
            flops=2 * used * 512 * columns, bytes_accessed=len(plan) * 512 * columns * 2, transcendentals=0
        ),
    )(*operands)


def question_project_kernel(pieces, wq, wkv, cos, sin, out):
    q_sum, kv_sum = None, None
    for place in range(16):
        base = place * 512
        piece = pieces[place]
        both = wkv[:, pl.ds(base, 512)]
        kv_term = lax.dot_general(piece, both, (((1,), (1,)), ((), ())), preferred_element_type=F32)
        q_term = jnp.dot(piece, wq[pl.ds(base, 512), :], preferred_element_type=F32)
        q_sum = q_term if q_sum is None else q_sum + q_term
        kv_sum = kv_term if kv_sum is None else kv_sum + kv_term
    for head in range(4):
        cols = slice(head * HD, (head + 1) * HD)
        out[:, cols] = turn(q_sum[:, cols], cos[ROWS : ROWS + 32, :], sin[ROWS : ROWS + 32, :])
    out[:, 512:640] = kv_sum.astype(BF)


def question_project(pieces, weights, tables):
    return pl.pallas_call(
        question_project_kernel,
        out_shape=jax.ShapeDtypeStruct((32, 640), BF),
        in_specs=[VM] * 5,
        out_specs=VM,
        compiler_params=pltpu.CompilerParams(vmem_limit_bytes=VMEM_LIMIT),
        cost_estimate=pl.CostEstimate(flops=2 * 256 * 8192 * 640, bytes_accessed=8192 * 640 * 2, transcendentals=0),
    )(pieces, *weights, *tables)


def key_value_kernel(info, own, partner, cos, sin, out):
    is_lower = info[1] % 2 == 0
    mine, other = own[...].astype(F32), partner[...].astype(F32)
    low = jnp.where(is_lower, mine, other)
    high = jnp.where(is_lower, other, mine)
    lane = lax.broadcasted_iota(jnp.int32, low.shape, 1)
    keys = jnp.where(lane < 64, low, pltpu.roll(high, 64, 1))
    values = jnp.where(lane < 64, pltpu.roll(low, 64, 1), high)
    out[:, :HD] = (keys * cos[...] + pltpu.roll(keys, 64, 1) * sin[...]).astype(BF)
    out[:, HD:] = values.astype(BF)


def key_value(info, own, partner, cos, sin):
    return pl.pallas_call(
        key_value_kernel,
        out_shape=jax.ShapeDtypeStruct((ALL, 2 * HD), BF),
        in_specs=[SM, VM, VM, VM, VM],
        out_specs=VM,
        compiler_params=pltpu.CompilerParams(vmem_limit_bytes=VMEM_LIMIT),
    )(info, own, partner, cos, sin)


def scores_of(queries, keys):
    return lax.dot_general(queries, keys, (((1,), (1,)), ((), ())), preferred_element_type=F32)


def weights_of(scores, top):
    return jnp.exp2(scores * SCALE2 - top * SCALE2)


def columns_to_stats(columns):
    rows = columns[0].shape[0]
    lane = lax.broadcasted_iota(jnp.int32, (rows, 128), 1)
    stats = jnp.zeros((rows, 128), F32)
    for index, column in enumerate(columns):
        stats = jnp.where(lane == index, column, stats)
    return stats


def own_kernel(info, q, kv, weighted, stats):
    length = info[5]
    for tile in range(2):
        rows = slice(tile * 256, tile * 256 + 256)
        width = 256 * (tile + 1)
        row = tile * 256 + lax.broadcasted_iota(jnp.int32, (256, width), 0)
        key = lax.broadcasted_iota(jnp.int32, (256, width), 1)
        bias = jnp.where((key <= row) & (key < length), 0.0, NEG)
        tops, totals = [], []
        for head in range(4):
            cols = slice(head * HD, (head + 1) * HD)
            s = scores_of(q[rows, cols], kv[:width, :HD]) + bias
            top = jnp.max(s, axis=1, keepdims=True)
            e = weights_of(s, top)
            totals.append(jnp.sum(e, axis=1, keepdims=True))
            tops.append(top)
            weighted[rows, cols] = jnp.dot(e.astype(BF), kv[:width, HD:], preferred_element_type=F32)
        stats[rows, :] = columns_to_stats(tops + totals)


def own_attention(info, q, kv):
    return pl.pallas_call(
        own_kernel,
        out_shape=[jax.ShapeDtypeStruct((512, 512), F32), jax.ShapeDtypeStruct((512, 128), F32)],
        in_specs=[SM, VM, VM],
        out_specs=[VM, VM],
        compiler_params=pltpu.CompilerParams(vmem_limit_bytes=VMEM_LIMIT),
        cost_estimate=pl.CostEstimate(flops=4 * 4 * 512 * 512 * 128, bytes_accessed=3 << 20, transcendentals=1 << 20),
    )(info, q, kv)


def anchor_kernel(info, q, kv_zero, kv_one, weighted, stats, out):
    length, anchor_length = info[5], info[6]
    first_core = info[3] == 0
    kv = jnp.where(first_core, kv_zero[...], kv_one[...])
    keys, values = kv[:, :HD], kv[:, HD:]
    key = lax.broadcasted_iota(jnp.int32, (1, 512), 1)
    bias = jnp.where(key < anchor_length, 0.0, NEG)
    for tile in range(2):
        rows = slice(tile * 256, tile * 256 + 256)
        block = stats[rows, :]
        row = tile * 256 + lax.broadcasted_iota(jnp.int32, (256, HD), 0)
        for head in range(4):
            cols = slice(head * HD, (head + 1) * HD)
            s = scores_of(q[rows, cols], keys) + bias
            own_top, own_sum = block[:, head : head + 1], block[:, head + 4 : head + 5]
            top = jnp.maximum(own_top, jnp.max(s, axis=1, keepdims=True))
            e = weights_of(s, top)
            factor = weights_of(own_top, top)
            total = own_sum * factor + jnp.sum(e, axis=1, keepdims=True)
            both = weighted[rows, cols] * factor + jnp.dot(e.astype(BF), values, preferred_element_type=F32)
            out[rows, cols] = jnp.where(row < length, both / total, 0.0).astype(BF)


def anchor_attention(info, q, kv_zero, kv_one, weighted, stats):
    return pl.pallas_call(
        anchor_kernel,
        out_shape=jax.ShapeDtypeStruct((512, 512), BF),
        in_specs=[SM, VM, VM, VM, VM, VM],
        out_specs=VM,
        compiler_params=pltpu.CompilerParams(vmem_limit_bytes=VMEM_LIMIT),
        cost_estimate=pl.CostEstimate(flops=4 * 4 * 512 * 512 * 128, bytes_accessed=3 << 20, transcendentals=1 << 20),
    )(info, q, kv_zero, kv_one, weighted, stats)


def question_kernel(info, q_own, q_other, kv_0, kv_1, kv_2, kv_3, out_own, out_other):
    kvs = (kv_0, kv_1, kv_2, kv_3)
    z, core, ctx = info[2], info[3], info[4]
    lengths = [info[5], info[7], info[8], info[9]]
    places = [z, (z + 3) % 4, (z + 1) % 4, (z + 2) % 4]
    stacked = [q_own[:, h * HD : (h + 1) * HD] for h in range(4)]
    stacked += [q_other[:, h * HD : (h + 1) * HD] for h in range(4)]
    q = jnp.concatenate(stacked, axis=0)
    scores = []
    key = lax.broadcasted_iota(jnp.int32, (1, 512), 1)
    for kv, length in zip(kvs, lengths):
        scores.append(scores_of(q, kv[:ROWS, :HD]) + jnp.where(key < length, 0.0, NEG))
    row = lax.broadcasted_iota(jnp.int32, (256, 128), 0)
    lane = lax.broadcasted_iota(jnp.int32, (256, 128), 1)
    row_id = row % 32 + 32 * jnp.where(row < 128, ctx, ctx + 1 - 2 * core)
    block = jnp.where(lane < 64, jnp.where(lane < 32, places[0], places[1]), jnp.where(lane < 96, places[2], places[3]))
    key_id = lane % 32 + 32 * (2 * block + core)
    asked_keys = jnp.concatenate([kv[ROWS:, :HD] for kv in kvs], axis=0)
    asked_values = jnp.concatenate([kv[ROWS:, HD:] for kv in kvs], axis=0)
    scores.append(jnp.where(key_id <= row_id, scores_of(q, asked_keys), NEG))
    top = jnp.max(scores[-1], axis=1, keepdims=True)
    for s in scores[:-1]:
        top = jnp.maximum(top, jnp.max(s, axis=1, keepdims=True))
    values = [kv[:ROWS, HD:] for kv in kvs] + [asked_values]
    total = jnp.zeros((256, 1), F32)
    both = jnp.zeros((256, HD), F32)
    for s, value in zip(scores, values):
        e = weights_of(s, top)
        total = total + jnp.sum(e, axis=1, keepdims=True)
        both = both + jnp.dot(e.astype(BF), value, preferred_element_type=F32)
    for out, start in ((out_own, 0), (out_other, 128)):
        tops, totals = [], []
        for head in range(4):
            rows = slice(start + head * 32, start + head * 32 + 32)
            out[:, head * HD : (head + 1) * HD] = both[rows]
            tops.append(top[rows])
            totals.append(total[rows])
        out[:, 512:640] = columns_to_stats(tops + totals)


def question_attention(info, q_own, q_other, kvs):
    part = jax.ShapeDtypeStruct((32, 640), F32)
    return pl.pallas_call(
        question_kernel,
        out_shape=[part, part],
        in_specs=[SM] + [VM] * 6,
        out_specs=[VM, VM],
        compiler_params=pltpu.CompilerParams(vmem_limit_bytes=VMEM_LIMIT),
        cost_estimate=pl.CostEstimate(flops=4 * 256 * 2176 * 128, bytes_accessed=2 << 20, transcendentals=1 << 19),
    )(info, q_own, q_other, *kvs)


def merge_kernel(a, b, out):
    stat_a, stat_b = a[:, 512:640], b[:, 512:640]
    for head in range(4):
        cols = slice(head * HD, (head + 1) * HD)
        top_a, top_b = stat_a[:, head : head + 1], stat_b[:, head : head + 1]
        top = jnp.maximum(top_a, top_b)
        factor_a, factor_b = weights_of(top_a, top), weights_of(top_b, top)
        total = stat_a[:, head + 4 : head + 5] * factor_a + stat_b[:, head + 4 : head + 5] * factor_b
        out[:, cols] = ((a[:, cols] * factor_a + b[:, cols] * factor_b) / total).astype(BF)


def merge(a, b):
    return pl.pallas_call(
        merge_kernel,
        out_shape=jax.ShapeDtypeStruct((32, 512), BF),
        in_specs=[VM, VM],
        out_specs=VM,
        compiler_params=pltpu.CompilerParams(vmem_limit_bytes=VMEM_LIMIT),
    )(a, b)


PLAN_1 = [
    ((0, 0), 0, 512, [(0, 0, 512)]),
    ((-1, 0), 0, 512, [(1, 0, 512)]),
    ((1, 0), 0, 512, [(2, 0, 512)]),
    ((0, -1), 0, 512, [(3, 0, 512)]),
    ((0, 1), 0, 512, [(4, 0, 512)]),
    ((2, 0), 0, 256, [(5, 0, 256)]),
    ((0, 2), 256, 512, [(6, 0, 256)]),
]
PLAN_2 = [
    ((-1, -1), 0, 512, [(0, 0, 256), (2, 0, 256)]),
    ((1, -1), 0, 512, [(0, 256, 256), (3, 0, 256)]),
    ((-1, 1), 0, 512, [(1, 0, 256), (2, 256, 256)]),
    ((1, 1), 0, 512, [(1, 256, 256), (3, 256, 256)]),
    ((2, -1), 0, 256, [(0, 512, 256)]),
    ((2, 1), 0, 256, [(1, 512, 256)]),
    ((-1, 2), 256, 512, [(2, 512, 256)]),
    ((1, 2), 256, 512, [(3, 512, 256)]),
    ((0, 2), 0, 256, [(0, 768, 128), (1, 768, 128)]),
    ((2, 0), 256, 512, [(2, 768, 128), (3, 768, 128)]),
]
PLAN_3 = [
    ((2, 2), 0, 512, [(1, 128, 256), (3, 128, 256)]),
    ((-1, 2), 0, 256, [(0, 0, 256)]),
    ((1, 2), 0, 256, [(0, 256, 128), (1, 0, 128)]),
    ((2, -1), 256, 512, [(2, 0, 256)]),
    ((2, 1), 256, 512, [(2, 256, 128), (3, 0, 128)]),
]
NEAR_Y = [(0, 0, 256), (1, 0, 256), (4, 0, 256)]
NEAR_X = [(2, 256, 256), (3, 256, 256), (5, 0, 256)]
PACK_2 = [NEAR_Y + [(2, 0, 128)], NEAR_Y + [(3, 128, 128)], NEAR_X + [(0, 256, 128)], NEAR_X + [(1, 384, 128)]]
PACK_3 = [[(0, 0, 384)], [(1, 384, 384)], [(2, 0, 384)], [(3, 384, 384)]]


def tables_of(positions):
    inverse_freq = ROPE_BASE ** (-(jnp.arange(HD // 2, dtype=jnp.float32) * 2.0 / HD))
    inverse_freq = jnp.concatenate([inverse_freq, inverse_freq])
    phases = positions.astype(jnp.float32)[:, None] * inverse_freq[None, :]
    signs = jnp.where(jnp.arange(HD) < HD // 2, -1.0, 1.0).astype(jnp.float32)
    return jnp.cos(phases), jnp.sin(phases) * signs[None, :]


def shift_z(array, dz):
    pairs = [(i, ((i // 2 + dz) % 4) * 2 + i % 2) for i in range(8)]
    return lax.ppermute(array, "ctx", pairs)


def per_device(context, question, w_query, w_key, w_value, lengths, owner):
    ctx = lax.axis_index("ctx")
    z, core = ctx // 2, ctx % 2
    heads = lax.axis_index("heads")
    y, x = heads // 4, heads % 4
    ids = jnp.arange(8, dtype=jnp.int32)
    own_offset = jnp.sum(jnp.where(ids < ctx, lengths, 0))
    own_length = jnp.sum(jnp.where(ids == ctx, lengths, 0))
    filled = jnp.sum(lengths)
    anchor_length = jnp.where(ctx > 0, lengths[0], 0)

    def length_of(dz):
        return jnp.sum(jnp.where(ids == ((z + dz) % 4) * 2 + core, lengths, 0))

    info = jnp.stack(
        [y, x, z, core, ctx, own_length, anchor_length, length_of(3), length_of(1), length_of(2)]
    ).astype(jnp.int32)

    up = shift_heads(context, 1, 0)
    down = shift_heads(context, -1, 0)
    right = shift_heads(context, 0, 1)
    left = shift_heads(context, 0, -1)
    far_y = shift_heads(lax.slice_in_dim(context, 0, 256, axis=0), 2, 0)
    up, again, asked = lax.optimization_barrier((up, context, question))
    far_x = shift_heads(lax.slice_in_dim(again, 256, 512, axis=0), 0, 2)

    weights = hold(w_query, w_key.T, w_value.T)
    share = lax.all_to_all(asked[0].reshape(8, 32, 512), "ctx", 0, 0)
    tables = tables_of(
        jnp.concatenate(
            [own_offset + jnp.arange(ROWS, dtype=jnp.int32), filled + 32 * ctx + jnp.arange(ASKED, dtype=jnp.int32)]
        )
    )
    up, share, weights = lax.optimization_barrier((up, share, weights))

    to_right, to_left, to_up, to_down = pack(PACK_2, [up, down, right, left, far_y, far_x])
    a_right, a_left = shift_heads(to_right, 0, 1), shift_heads(to_left, 0, -1)
    b_up, b_down = shift_heads(to_up, 1, 0), shift_heads(to_down, -1, 0)
    up, to_right = lax.optimization_barrier((up, to_right))
    accs = project(info, [context, up, down, right, left, far_y, far_x], PLAN_1, weights, None, True, True)
    share, accs = lax.optimization_barrier((share, accs))
    share = lax.dynamic_index_in_dim(share, owner[0], 0, False)
    pieces = lax.all_to_all(jnp.broadcast_to(share[None], (16, 32, 512)), "heads", 0, 0)

    a_right, a_left, b_up, b_down, accs = lax.optimization_barrier((a_right, a_left, b_up, b_down, accs))
    to_right, to_left, to_up, to_down = pack(PACK_3, [a_right, a_left, b_up, b_down])
    last = [
        shift_heads(to_right, 0, 1),
        shift_heads(to_left, 0, -1),
        shift_heads(to_up, 1, 0),
        shift_heads(to_down, -1, 0),
    ]
    accs = project(info, [a_right, a_left, b_up, b_down], PLAN_2, weights, accs, True, True)
    q_share = question_project(pieces, weights, tables)

    (halves,) = project(info, last, PLAN_3, weights, accs, False, True, True, asked=q_share)
    (queries,) = project(info, last, PLAN_3, weights, accs, True, False, True, tables)
    partner = swap_heads(halves, 0, 1)
    q_asked = q_share[:, :512]
    q_other = swap_ctx(q_asked, 0, 1)
    partner, queries, q_other = lax.optimization_barrier((partner, queries, q_other))
    kv = key_value(info, halves, partner, *tables)

    below, above, across = shift_z(kv, 1), shift_z(kv, -1), shift_z(kv, 2)
    weighted, stats = own_attention(info, queries, kv)
    below, above, across, weighted = lax.optimization_barrier((below, above, across, weighted))
    nearer = jnp.where(z == 0, kv[:ROWS], jnp.where(z == 1, below[:ROWS], jnp.where(z == 2, across[:ROWS], above[:ROWS])))
    from_zero = lax.ppermute(nearer, "ctx", [(0, 1), (2, 3), (4, 5), (6, 7)])
    part, part_other = question_attention(info, q_asked, q_other, [kv, below, above, across])
    from_zero, part = lax.optimization_barrier((from_zero, part))
    context_attn = anchor_attention(info, queries, nearer, from_zero, weighted, stats)
    question_attn = merge(part, swap_ctx(part_other, 0, 1))
    return (context_attn, question_attn)


def solution(mesh):
    in_specs = (
        P("ctx", "heads"),
        P("ctx", None, "heads"),
        P(None, "heads"),
        P(None, "heads"),
        P(None, "heads"),
        P(),
        P(),
    )
    out_specs = (P("ctx", "heads"), P("ctx", "heads"))
    return jax.shard_map(
        per_device, mesh=mesh, in_specs=in_specs, out_specs=out_specs, check_vma=False
    )
```

```python
import functools

import jax
import jax.numpy as jnp
from jax import lax
from jax.experimental import pallas as pl
from jax.experimental.pallas import tpu as pltpu
from jax.sharding import PartitionSpec as P

HD = 128
ROPE_BASE = 500000.0
BF = jnp.bfloat16
F32 = jnp.float32
VMEM_LIMIT = 8 * 1024 * 1024
HOLD_LIMIT = 37 * 1024 * 1024
NEG = -1e30
SCALE2 = HD ** (-0.5) * 1.4426950408889634
ROWS = 512
ASKED = 32
ALL = ROWS + ASKED

HBM = pl.BlockSpec(memory_space=pltpu.HBM)
VM = pl.BlockSpec(memory_space=pltpu.VMEM)
SM = pl.BlockSpec(memory_space=pltpu.SMEM)


def shift_heads(array, dy, dx):
    pairs = [(i, ((i // 4 + dy) % 4) * 4 + (i % 4 + dx) % 4) for i in range(16)]
    return lax.ppermute(array, "heads", pairs)


def swap_heads(array, my, mx):
    pairs = [(i, ((i // 4) ^ my) * 4 + ((i % 4) ^ mx)) for i in range(16)]
    return lax.ppermute(array, "heads", pairs)


def swap_ctx(array, mz, mc):
    pairs = [(i, ((i // 2) ^ mz) * 2 + ((i % 2) ^ mc)) for i in range(8)]
    return lax.ppermute(array, "ctx", pairs)


def pack_kernel(plan, n_in, *refs):
    ins, outs = refs[:n_in], refs[n_in:]
    for out, pieces in zip(outs, plan):
        row = 0
        for operand, start, count in pieces:
            out[row : row + count, :] = ins[operand][start : start + count, :]
            row += count


def pack(plan, ins):
    return pl.pallas_call(
        functools.partial(pack_kernel, plan, len(ins)),
        out_shape=[jax.ShapeDtypeStruct((sum(p[2] for p in pieces), 512), BF) for pieces in plan],
        in_specs=[VM] * len(ins),
        out_specs=[VM] * len(plan),
        compiler_params=pltpu.CompilerParams(vmem_limit_bytes=VMEM_LIMIT),
        cost_estimate=pl.CostEstimate(flops=0, bytes_accessed=1 << 20, transcendentals=0),
    )(*ins)


def hold_kernel(wq, wk, wv, q_out, kv_out, sem):
    copies = []
    for part in range(8):
        rows = pl.ds(part * 1024, 1024)
        copies.append(pltpu.make_async_copy(wq.at[rows, :], q_out.at[rows, :], sem.at[part]))
    for part in range(4):
        cols = pl.ds(part * 2048, 2048)
        copies.append(pltpu.make_async_copy(wk.at[:, cols], kv_out.at[pl.ds(0, 64), cols], sem.at[8 + part]))
        copies.append(pltpu.make_async_copy(wv.at[:, cols], kv_out.at[pl.ds(64, 64), cols], sem.at[12 + part]))
    for copy in copies:
        copy.start()
    for copy in copies:
        copy.wait()


def hold(wq, wk, wv):
    return pl.pallas_call(
        hold_kernel,
        out_shape=[jax.ShapeDtypeStruct((8192, 512), BF), jax.ShapeDtypeStruct((128, 8192), BF)],
        in_specs=[HBM] * 3,
        out_specs=[VM, VM],
        scratch_shapes=[pltpu.SemaphoreType.DMA((16,))],
        compiler_params=pltpu.CompilerParams(vmem_limit_bytes=HOLD_LIMIT),
        cost_estimate=pl.CostEstimate(flops=0, bytes_accessed=20 << 20, transcendentals=0),
    )(wq, wk, wv)


def turn(part, cos, sin):
    return (part * cos + pltpu.roll(part, HD // 2, 1) * sin).astype(BF)


def project_kernel(plan, n_x, with_q, with_kv, has_acc, finish, *refs):
    refs = list(refs)
    take = lambda count: [refs.pop(0) for _ in range(count)]
    (info,) = take(1)
    xs = take(n_x)
    wq = take(1)[0] if with_q else None
    wkv = take(1)[0] if with_kv else None
    acc_q = take(1)[0] if has_acc and with_q else None
    acc_kv = take(1)[0] if has_acc and with_kv else None
    cos, sin = take(2) if finish and with_q else (None, None)
    asked = take(1)[0] if finish and with_kv else None
    q_out = take(1)[0] if with_q else None
    kv_out = take(1)[0] if with_kv else None
    q_sum = take(1)[0] if finish and with_q else q_out
    kv_sum = take(1)[0] if finish and with_kv else kv_out
    y, x = info[0], info[1]
    if has_acc:
        if with_q:
            q_sum[...] = acc_q[...]
        if with_kv:
            kv_sum[...] = acc_kv[...]
    for slot, ((dy, dx), low, high, uses) in enumerate(plan):
        base = pl.multiple_of((((y + dy + 4) % 4) * 4 + (x + dx + 4) % 4) * 512, 512)
        parts = [xs[operand][pl.ds(start, count), :] for operand, start, count in uses]
        piece = parts[0] if len(parts) == 1 else jnp.concatenate(parts, axis=0)
        fresh = slot == 0 and not has_acc
        if with_kv:
            both = wkv[:, pl.ds(base, 512)]
            term = lax.dot_general(piece, both, (((1,), (1,)), ((), ())), preferred_element_type=F32)
            kv_sum[low:high, :] = term if fresh else kv_sum[low:high, :] + term
        if with_q:
            term = jnp.dot(piece, wq[pl.ds(base, 512), :], preferred_element_type=F32)
            q_sum[low:high, :] = term if fresh else q_sum[low:high, :] + term
    if finish and with_kv:
        kv_out[:ROWS, :] = kv_sum[...].astype(BF)
        kv_out[ROWS:, :] = asked[:, 512:640]
    if finish and with_q:
        for head in range(4):
            cols = slice(head * HD, (head + 1) * HD)
            q_out[:, cols] = turn(q_sum[:, cols], cos[:ROWS, :], sin[:ROWS, :])


def project(info, xs, plan, weights, accs, with_q, with_kv, finish=False, tables=None, asked=None):
    wq, wkv = weights
    operands, specs = [info] + list(xs), [SM] + [VM] * len(xs)
    if with_q:
        operands.append(wq)
        specs.append(VM)
    if with_kv:
        operands.append(wkv)
        specs.append(VM)
    has_acc = accs is not None
    if has_acc:
        if with_q:
            operands.append(accs[0])
            specs.append(VM)
        if with_kv:
            operands.append(accs[1])
            specs.append(VM)
    if finish and with_q:
        operands += list(tables)
        specs += [VM, VM]
    if finish and with_kv:
        operands.append(asked)
        specs.append(VM)
    outs, scratch = [], []
    if with_q:
        outs.append(jax.ShapeDtypeStruct((ROWS, 512), BF if finish else F32))
        if finish:
            scratch.append(pltpu.VMEM((ROWS, 512), F32))
    if with_kv:
        outs.append(jax.ShapeDtypeStruct((ALL, 128), BF) if finish else jax.ShapeDtypeStruct((ROWS, 128), F32))
        if finish:
            scratch.append(pltpu.VMEM((ROWS, 128), F32))
    columns = (512 if with_q else 0) + (128 if with_kv else 0)
    used = sum(high - low for _, low, high, _ in plan)
    return pl.pallas_call(
        functools.partial(project_kernel, plan, len(xs), with_q, with_kv, has_acc, finish),
        out_shape=outs,
        in_specs=specs,
        out_specs=[VM] * len(outs),
        scratch_shapes=scratch,
        compiler_params=pltpu.CompilerParams(vmem_limit_bytes=VMEM_LIMIT),
        cost_estimate=pl.CostEstimate(
            flops=2 * used * 512 * columns, bytes_accessed=len(plan) * 512 * columns * 2, transcendentals=0
        ),
    )(*operands)


def question_project_kernel(pieces, wq, wkv, cos, sin, out):
    q_sum, kv_sum = None, None
    for place in range(16):
        base = place * 512
        piece = pieces[place]
        both = wkv[:, pl.ds(base, 512)]
        kv_term = lax.dot_general(piece, both, (((1,), (1,)), ((), ())), preferred_element_type=F32)
        q_term = jnp.dot(piece, wq[pl.ds(base, 512), :], preferred_element_type=F32)
        q_sum = q_term if q_sum is None else q_sum + q_term
        kv_sum = kv_term if kv_sum is None else kv_sum + kv_term
    for head in range(4):
        cols = slice(head * HD, (head + 1) * HD)
        out[:, cols] = turn(q_sum[:, cols], cos[ROWS : ROWS + 32, :], sin[ROWS : ROWS + 32, :])
    out[:, 512:640] = kv_sum.astype(BF)


def question_project(pieces, weights, tables):
    return pl.pallas_call(
        question_project_kernel,
        out_shape=jax.ShapeDtypeStruct((32, 640), BF),
        in_specs=[VM] * 5,
        out_specs=VM,
        compiler_params=pltpu.CompilerParams(vmem_limit_bytes=VMEM_LIMIT),
        cost_estimate=pl.CostEstimate(flops=2 * 256 * 8192 * 640, bytes_accessed=8192 * 640 * 2, transcendentals=0),
    )(pieces, *weights, *tables)


def key_value_kernel(info, own, partner, cos, sin, out):
    is_lower = info[1] % 2 == 0
    mine, other = own[...].astype(F32), partner[...].astype(F32)
    low = jnp.where(is_lower, mine, other)
    high = jnp.where(is_lower, other, mine)
    lane = lax.broadcasted_iota(jnp.int32, low.shape, 1)
    keys = jnp.where(lane < 64, low, pltpu.roll(high, 64, 1))
    values = jnp.where(lane < 64, pltpu.roll(low, 64, 1), high)
    out[:, :HD] = (keys * cos[...] + pltpu.roll(keys, 64, 1) * sin[...]).astype(BF)
    out[:, HD:] = values.astype(BF)


def key_value(info, own, partner, cos, sin):
    return pl.pallas_call(
        key_value_kernel,
        out_shape=jax.ShapeDtypeStruct((ALL, 2 * HD), BF),
        in_specs=[SM, VM, VM, VM, VM],
        out_specs=VM,
        compiler_params=pltpu.CompilerParams(vmem_limit_bytes=VMEM_LIMIT),
    )(info, own, partner, cos, sin)


def scores_of(queries, keys):
    return lax.dot_general(queries, keys, (((1,), (1,)), ((), ())), preferred_element_type=F32)


def weights_of(scores, top):
    return jnp.exp2(scores * SCALE2 - top * SCALE2)


def columns_to_stats(columns):
    rows = columns[0].shape[0]
    lane = lax.broadcasted_iota(jnp.int32, (rows, 128), 1)
    stats = jnp.zeros((rows, 128), F32)
    for index, column in enumerate(columns):
        stats = jnp.where(lane == index, column, stats)
    return stats


def own_kernel(info, q, kv, weighted, stats):
    length = info[5]
    for tile in range(2):
        rows = slice(tile * 256, tile * 256 + 256)
        width = 256 * (tile + 1)
        row = tile * 256 + lax.broadcasted_iota(jnp.int32, (256, width), 0)
        key = lax.broadcasted_iota(jnp.int32, (256, width), 1)
        bias = jnp.where((key <= row) & (key < length), 0.0, NEG)
        tops, totals = [], []
        for head in range(4):
            cols = slice(head * HD, (head + 1) * HD)
            s = scores_of(q[rows, cols], kv[:width, :HD]) + bias
            top = jnp.max(s, axis=1, keepdims=True)
            e = weights_of(s, top)
            totals.append(jnp.sum(e, axis=1, keepdims=True))
            tops.append(top)
            weighted[rows, cols] = jnp.dot(e.astype(BF), kv[:width, HD:], preferred_element_type=F32)
        stats[rows, :] = columns_to_stats(tops + totals)


def own_attention(info, q, kv):
    return pl.pallas_call(
        own_kernel,
        out_shape=[jax.ShapeDtypeStruct((512, 512), F32), jax.ShapeDtypeStruct((512, 128), F32)],
        in_specs=[SM, VM, VM],
        out_specs=[VM, VM],
        compiler_params=pltpu.CompilerParams(vmem_limit_bytes=VMEM_LIMIT),
        cost_estimate=pl.CostEstimate(flops=4 * 4 * 512 * 512 * 128, bytes_accessed=3 << 20, transcendentals=1 << 20),
    )(info, q, kv)


def anchor_kernel(info, q, kv_zero, kv_one, weighted, stats, out):
    length, anchor_length = info[5], info[6]
    first_core = info[3] == 0
    kv = jnp.where(first_core, kv_zero[...], kv_one[...])
    keys, values = kv[:, :HD], kv[:, HD:]
    key = lax.broadcasted_iota(jnp.int32, (1, 512), 1)
    bias = jnp.where(key < anchor_length, 0.0, NEG)
    for tile in range(2):
        rows = slice(tile * 256, tile * 256 + 256)
        block = stats[rows, :]
        row = tile * 256 + lax.broadcasted_iota(jnp.int32, (256, HD), 0)
        for head in range(4):
            cols = slice(head * HD, (head + 1) * HD)
            s = scores_of(q[rows, cols], keys) + bias
            own_top, own_sum = block[:, head : head + 1], block[:, head + 4 : head + 5]
            top = jnp.maximum(own_top, jnp.max(s, axis=1, keepdims=True))
            e = weights_of(s, top)
            factor = weights_of(own_top, top)
            total = own_sum * factor + jnp.sum(e, axis=1, keepdims=True)
            both = weighted[rows, cols] * factor + jnp.dot(e.astype(BF), values, preferred_element_type=F32)
            out[rows, cols] = jnp.where(row < length, both / total, 0.0).astype(BF)


def anchor_attention(info, q, kv_zero, kv_one, weighted, stats):
    return pl.pallas_call(
        anchor_kernel,
        out_shape=jax.ShapeDtypeStruct((512, 512), BF),
        in_specs=[SM, VM, VM, VM, VM, VM],
        out_specs=VM,
        compiler_params=pltpu.CompilerParams(vmem_limit_bytes=VMEM_LIMIT),
        cost_estimate=pl.CostEstimate(flops=4 * 4 * 512 * 512 * 128, bytes_accessed=3 << 20, transcendentals=1 << 20),
    )(info, q, kv_zero, kv_one, weighted, stats)


def question_kernel(info, q_own, q_other, kv_0, kv_1, kv_2, kv_3, out_own, out_other):
    kvs = (kv_0, kv_1, kv_2, kv_3)
    z, core, ctx = info[2], info[3], info[4]
    lengths = [info[5], info[7], info[8], info[9]]
    places = [z, (z + 3) % 4, (z + 1) % 4, (z + 2) % 4]
    stacked = [q_own[:, h * HD : (h + 1) * HD] for h in range(4)]
    stacked += [q_other[:, h * HD : (h + 1) * HD] for h in range(4)]
    q = jnp.concatenate(stacked, axis=0)
    scores = []
    key = lax.broadcasted_iota(jnp.int32, (1, 512), 1)
    for kv, length in zip(kvs, lengths):
        scores.append(scores_of(q, kv[:ROWS, :HD]) + jnp.where(key < length, 0.0, NEG))
    row = lax.broadcasted_iota(jnp.int32, (256, 128), 0)
    lane = lax.broadcasted_iota(jnp.int32, (256, 128), 1)
    row_id = row % 32 + 32 * jnp.where(row < 128, ctx, ctx + 1 - 2 * core)
    block = jnp.where(lane < 64, jnp.where(lane < 32, places[0], places[1]), jnp.where(lane < 96, places[2], places[3]))
    key_id = lane % 32 + 32 * (2 * block + core)
    asked_keys = jnp.concatenate([kv[ROWS:, :HD] for kv in kvs], axis=0)
    asked_values = jnp.concatenate([kv[ROWS:, HD:] for kv in kvs], axis=0)
    scores.append(jnp.where(key_id <= row_id, scores_of(q, asked_keys), NEG))
    top = jnp.max(scores[-1], axis=1, keepdims=True)
    for s in scores[:-1]:
        top = jnp.maximum(top, jnp.max(s, axis=1, keepdims=True))
    values = [kv[:ROWS, HD:] for kv in kvs] + [asked_values]
    total = jnp.zeros((256, 1), F32)
    both = jnp.zeros((256, HD), F32)
    for s, value in zip(scores, values):
        e = weights_of(s, top)
        total = total + jnp.sum(e, axis=1, keepdims=True)
        both = both + jnp.dot(e.astype(BF), value, preferred_element_type=F32)
    for out, start in ((out_own, 0), (out_other, 128)):
        tops, totals = [], []
        for head in range(4):
            rows = slice(start + head * 32, start + head * 32 + 32)
            out[:, head * HD : (head + 1) * HD] = both[rows]
            tops.append(top[rows])
            totals.append(total[rows])
        out[:, 512:640] = columns_to_stats(tops + totals)


def question_attention(info, q_own, q_other, kvs):
    part = jax.ShapeDtypeStruct((32, 640), F32)
    return pl.pallas_call(
        question_kernel,
        out_shape=[part, part],
        in_specs=[SM] + [VM] * 6,
        out_specs=[VM, VM],
        compiler_params=pltpu.CompilerParams(vmem_limit_bytes=VMEM_LIMIT),
        cost_estimate=pl.CostEstimate(flops=4 * 256 * 2176 * 128, bytes_accessed=2 << 20, transcendentals=1 << 19),
    )(info, q_own, q_other, *kvs)


def merge_kernel(a, b, out):
    stat_a, stat_b = a[:, 512:640], b[:, 512:640]
    for head in range(4):
        cols = slice(head * HD, (head + 1) * HD)
        top_a, top_b = stat_a[:, head : head + 1], stat_b[:, head : head + 1]
        top = jnp.maximum(top_a, top_b)
        factor_a, factor_b = weights_of(top_a, top), weights_of(top_b, top)
        total = stat_a[:, head + 4 : head + 5] * factor_a + stat_b[:, head + 4 : head + 5] * factor_b
        out[:, cols] = ((a[:, cols] * factor_a + b[:, cols] * factor_b) / total).astype(BF)


def merge(a, b):
    return pl.pallas_call(
        merge_kernel,
        out_shape=jax.ShapeDtypeStruct((32, 512), BF),
        in_specs=[VM, VM],
        out_specs=VM,
        compiler_params=pltpu.CompilerParams(vmem_limit_bytes=VMEM_LIMIT),
    )(a, b)


PLAN_1 = [
    ((0, 0), 0, 512, [(0, 0, 512)]),
    ((-1, 0), 0, 512, [(1, 0, 512)]),
    ((1, 0), 0, 512, [(2, 0, 512)]),
    ((0, -1), 0, 512, [(3, 0, 512)]),
    ((0, 1), 0, 512, [(4, 0, 512)]),
    ((2, 0), 0, 256, [(5, 0, 256)]),
    ((0, 2), 256, 512, [(6, 0, 256)]),
]
PLAN_2 = [
    ((-1, -1), 0, 512, [(0, 0, 256), (2, 0, 256)]),
    ((1, -1), 0, 512, [(0, 256, 256), (3, 0, 256)]),
    ((-1, 1), 0, 512, [(1, 0, 256), (2, 256, 256)]),
    ((1, 1), 0, 512, [(1, 256, 256), (3, 256, 256)]),
    ((2, -1), 0, 256, [(0, 512, 256)]),
    ((2, 1), 0, 256, [(1, 512, 256)]),
    ((-1, 2), 256, 512, [(2, 512, 256)]),
    ((1, 2), 256, 512, [(3, 512, 256)]),
    ((0, 2), 0, 256, [(0, 768, 128), (1, 768, 128)]),
    ((2, 0), 256, 512, [(2, 768, 128), (3, 768, 128)]),
]
PLAN_3 = [
    ((2, 2), 0, 512, [(1, 128, 256), (3, 128, 256)]),
    ((-1, 2), 0, 256, [(0, 0, 256)]),
    ((1, 2), 0, 256, [(0, 256, 128), (1, 0, 128)]),
    ((2, -1), 256, 512, [(2, 0, 256)]),
    ((2, 1), 256, 512, [(2, 256, 128), (3, 0, 128)]),
]
NEAR_Y = [(0, 0, 256), (1, 0, 256), (4, 0, 256)]
NEAR_X = [(2, 256, 256), (3, 256, 256), (5, 0, 256)]
PACK_2 = [NEAR_Y + [(2, 0, 128)], NEAR_Y + [(3, 128, 128)], NEAR_X + [(0, 256, 128)], NEAR_X + [(1, 384, 128)]]
PACK_3 = [[(0, 0, 384)], [(1, 384, 384)], [(2, 0, 384)], [(3, 384, 384)]]


def tables_of(positions):
    inverse_freq = ROPE_BASE ** (-(jnp.arange(HD // 2, dtype=jnp.float32) * 2.0 / HD))
    inverse_freq = jnp.concatenate([inverse_freq, inverse_freq])
    phases = positions.astype(jnp.float32)[:, None] * inverse_freq[None, :]
    signs = jnp.where(jnp.arange(HD) < HD // 2, -1.0, 1.0).astype(jnp.float32)
    return jnp.cos(phases), jnp.sin(phases) * signs[None, :]


def shift_z(array, dz):
    pairs = [(i, ((i // 2 + dz) % 4) * 2 + i % 2) for i in range(8)]
    return lax.ppermute(array, "ctx", pairs)


def per_device(context, question, w_query, w_key, w_value, lengths, owner):
    ctx = lax.axis_index("ctx")
    z, core = ctx // 2, ctx % 2
    heads = lax.axis_index("heads")
    y, x = heads // 4, heads % 4
    ids = jnp.arange(8, dtype=jnp.int32)
    own_offset = jnp.sum(jnp.where(ids < ctx, lengths, 0))
    own_length = jnp.sum(jnp.where(ids == ctx, lengths, 0))
    filled = jnp.sum(lengths)
    anchor_length = jnp.where(ctx > 0, lengths[0], 0)

    def length_of(dz):
        return jnp.sum(jnp.where(ids == ((z + dz) % 4) * 2 + core, lengths, 0))

    places = jnp.arange(16, dtype=jnp.int32)
    info = jnp.zeros((16,), jnp.int32)
    for place, value in enumerate(
        [y, x, z, core, ctx, own_length, anchor_length, length_of(3), length_of(1), length_of(2)]
    ):
        info = jnp.where(places == place, value, info)

    up = shift_heads(context, 1, 0)
    down = shift_heads(context, -1, 0)
    right = shift_heads(context, 0, 1)
    left = shift_heads(context, 0, -1)
    low, high = pack([[(0, 0, 256)], [(0, 256, 256)]], [context])
    far_y = shift_heads(low, 2, 0)
    up, high = lax.optimization_barrier((up, high))
    far_x = shift_heads(high, 0, 2)

    share = lax.all_to_all(question[0].reshape(8, 32, 512), "ctx", 0, 0)
    up, share = lax.optimization_barrier((up, share))

    to_right, to_left, to_up, to_down = pack(PACK_2, [up, down, right, left, far_y, far_x])
    a_right, a_left = shift_heads(to_right, 0, 1), shift_heads(to_left, 0, -1)
    b_up, b_down = shift_heads(to_up, 1, 0), shift_heads(to_down, -1, 0)
    up, share, to_right = lax.optimization_barrier((up, share, to_right))
    share = lax.dynamic_index_in_dim(share, owner[0], 0, False)
    tables = tables_of(
        jnp.concatenate(
            [own_offset + jnp.arange(ROWS, dtype=jnp.int32), filled + 32 * ctx + jnp.arange(ASKED, dtype=jnp.int32)]
        )
    )
    pieces = lax.all_to_all(jnp.broadcast_to(share[None], (16, 32, 512)), "heads", 0, 0)
    pieces, w_query, w_key, w_value, info, tables = lax.optimization_barrier(
        (pieces, w_query, w_key, w_value, info, tables)
    )
    weights = hold(w_query, w_key.T, w_value.T)
    accs = project(info, [context, up, down, right, left, far_y, far_x], PLAN_1, weights, None, True, True)

    a_right, a_left, b_up, b_down, accs = lax.optimization_barrier((a_right, a_left, b_up, b_down, accs))
    to_right, to_left, to_up, to_down = pack(PACK_3, [a_right, a_left, b_up, b_down])
    last = [
        shift_heads(to_right, 0, 1),
        shift_heads(to_left, 0, -1),
        shift_heads(to_up, 1, 0),
        shift_heads(to_down, -1, 0),
    ]
    accs = project(info, [a_right, a_left, b_up, b_down], PLAN_2, weights, accs, True, True)
    q_share = question_project(pieces, weights, tables)

    (halves,) = project(info, last, PLAN_3, weights, accs, False, True, True, asked=q_share)
    (queries,) = project(info, last, PLAN_3, weights, accs, True, False, True, tables)
    partner = swap_heads(halves, 0, 1)
    q_asked = q_share[:, :512]
    q_other = swap_ctx(q_asked, 0, 1)
    partner, queries, q_other = lax.optimization_barrier((partner, queries, q_other))
    kv = key_value(info, halves, partner, *tables)

    below, above, across = shift_z(kv, 1), shift_z(kv, -1), shift_z(kv, 2)
    weighted, stats = own_attention(info, queries, kv)
    below, above, across, weighted = lax.optimization_barrier((below, above, across, weighted))
    nearer = jnp.where(z == 0, kv[:ROWS], jnp.where(z == 1, below[:ROWS], jnp.where(z == 2, across[:ROWS], above[:ROWS])))
    from_zero = lax.ppermute(nearer, "ctx", [(0, 1), (2, 3), (4, 5), (6, 7)])
    part, part_other = question_attention(info, q_asked, q_other, [kv, below, above, across])
    from_zero, part = lax.optimization_barrier((from_zero, part))
    context_attn = anchor_attention(info, queries, nearer, from_zero, weighted, stats)
    question_attn = merge(part, swap_ctx(part_other, 0, 1))
    return (context_attn, question_attn)


def solution(mesh):
    in_specs = (
        P("ctx", "heads"),
        P("ctx", None, "heads"),
        P(None, "heads"),
        P(None, "heads"),
        P(None, "heads"),
        P(),
        P(),
    )
    out_specs = (P("ctx", "heads"), P("ctx", "heads"))
    return jax.shard_map(
        per_device, mesh=mesh, in_specs=in_specs, out_specs=out_specs, check_vma=False
    )
```

```python
import functools

import jax
import jax.numpy as jnp
from jax import lax
from jax.experimental import pallas as pl
from jax.experimental.pallas import tpu as pltpu
from jax.sharding import PartitionSpec as P

HD = 128
ROPE_BASE = 500000.0
BF = jnp.bfloat16
F32 = jnp.float32
VMEM_LIMIT = 8 * 1024 * 1024
HOLD_LIMIT = 37 * 1024 * 1024
NEG = -1e30
SCALE2 = HD ** (-0.5) * 1.4426950408889634
ROWS = 512
ASKED = 32
ALL = ROWS + ASKED

HBM = pl.BlockSpec(memory_space=pltpu.HBM)
VM = pl.BlockSpec(memory_space=pltpu.VMEM)
SM = pl.BlockSpec(memory_space=pltpu.SMEM)


def shift_heads(array, dy, dx):
    pairs = [(i, ((i // 4 + dy) % 4) * 4 + (i % 4 + dx) % 4) for i in range(16)]
    return lax.ppermute(array, "heads", pairs)


def swap_heads(array, my, mx):
    pairs = [(i, ((i // 4) ^ my) * 4 + ((i % 4) ^ mx)) for i in range(16)]
    return lax.ppermute(array, "heads", pairs)


def swap_ctx(array, mz, mc):
    pairs = [(i, ((i // 2) ^ mz) * 2 + ((i % 2) ^ mc)) for i in range(8)]
    return lax.ppermute(array, "ctx", pairs)


def pack_kernel(plan, n_in, *refs):
    ins, outs = refs[:n_in], refs[n_in:]
    for out, pieces in zip(outs, plan):
        row = 0
        for operand, start, count in pieces:
            out[row : row + count, :] = ins[operand][start : start + count, :]
            row += count


def pack(plan, ins):
    return pl.pallas_call(
        functools.partial(pack_kernel, plan, len(ins)),
        out_shape=[jax.ShapeDtypeStruct((sum(p[2] for p in pieces), 512), BF) for pieces in plan],
        in_specs=[VM] * len(ins),
        out_specs=[VM] * len(plan),
        compiler_params=pltpu.CompilerParams(vmem_limit_bytes=VMEM_LIMIT),
        cost_estimate=pl.CostEstimate(flops=0, bytes_accessed=1 << 20, transcendentals=0),
    )(*ins)


def hold_kernel(wq, wk, wv, q_out, kv_out, sem):
    copies = []
    for part in range(8):
        rows = pl.ds(part * 1024, 1024)
        copies.append(pltpu.make_async_copy(wq.at[rows, :], q_out.at[rows, :], sem.at[part]))
    for part in range(4):
        cols = pl.ds(part * 2048, 2048)
        copies.append(pltpu.make_async_copy(wk.at[:, cols], kv_out.at[pl.ds(0, 64), cols], sem.at[8 + part]))
        copies.append(pltpu.make_async_copy(wv.at[:, cols], kv_out.at[pl.ds(64, 64), cols], sem.at[12 + part]))
    for copy in copies:
        copy.start()
    for copy in copies:
        copy.wait()


def hold(wq, wk, wv):
    return pl.pallas_call(
        hold_kernel,
        out_shape=[jax.ShapeDtypeStruct((8192, 512), BF), jax.ShapeDtypeStruct((128, 8192), BF)],
        in_specs=[HBM] * 3,
        out_specs=[VM, VM],
        scratch_shapes=[pltpu.SemaphoreType.DMA((16,))],
        compiler_params=pltpu.CompilerParams(vmem_limit_bytes=HOLD_LIMIT),
        cost_estimate=pl.CostEstimate(flops=0, bytes_accessed=20 << 20, transcendentals=0),
    )(wq, wk, wv)


def turn(part, cos, sin):
    return (part * cos + pltpu.roll(part, HD // 2, 1) * sin).astype(BF)


def project_kernel(plan, n_x, with_q, with_kv, has_acc, finish, *refs):
    refs = list(refs)
    take = lambda count: [refs.pop(0) for _ in range(count)]
    (info,) = take(1)
    xs = take(n_x)
    wq = take(1)[0] if with_q else None
    wkv = take(1)[0] if with_kv else None
    acc_q = take(1)[0] if has_acc and with_q else None
    acc_kv = take(1)[0] if has_acc and with_kv else None
    cos, sin = take(2) if finish and with_q else (None, None)
    asked = take(1)[0] if finish and with_kv else None
    q_out = take(1)[0] if with_q else None
    kv_out = take(1)[0] if with_kv else None
    q_sum = take(1)[0] if finish and with_q else q_out
    kv_sum = take(1)[0] if finish and with_kv else kv_out
    y, x = info[0], info[1]
    if has_acc:
        if with_q:
            q_sum[...] = acc_q[...]
        if with_kv:
            kv_sum[...] = acc_kv[...]
    for slot, ((dy, dx), low, high, uses) in enumerate(plan):
        base = pl.multiple_of((((y + dy + 4) % 4) * 4 + (x + dx + 4) % 4) * 512, 512)
        parts = [xs[operand][pl.ds(start, count), :] for operand, start, count in uses]
        piece = parts[0] if len(parts) == 1 else jnp.concatenate(parts, axis=0)
        fresh = slot == 0 and not has_acc
        if with_kv:
            both = wkv[:, pl.ds(base, 512)]
            term = lax.dot_general(piece, both, (((1,), (1,)), ((), ())), preferred_element_type=F32)
            kv_sum[low:high, :] = term if fresh else kv_sum[low:high, :] + term
        if with_q:
            term = jnp.dot(piece, wq[pl.ds(base, 512), :], preferred_element_type=F32)
            q_sum[low:high, :] = term if fresh else q_sum[low:high, :] + term
    if finish and with_kv:
        kv_out[:ROWS, :] = kv_sum[...].astype(BF)
        kv_out[ROWS:, :] = asked[:, 512:640]
    if finish and with_q:
        for head in range(4):
            cols = slice(head * HD, (head + 1) * HD)
            q_out[:, cols] = turn(q_sum[:, cols], cos[:ROWS, :], sin[:ROWS, :])


def project(info, xs, plan, weights, accs, with_q, with_kv, finish=False, tables=None, asked=None):
    wq, wkv = weights
    operands, specs = [info] + list(xs), [SM] + [VM] * len(xs)
    if with_q:
        operands.append(wq)
        specs.append(VM)
    if with_kv:
        operands.append(wkv)
        specs.append(VM)
    has_acc = accs is not None
    if has_acc:
        if with_q:
            operands.append(accs[0])
            specs.append(VM)
        if with_kv:
            operands.append(accs[1])
            specs.append(VM)
    if finish and with_q:
        operands += list(tables)
        specs += [VM, VM]
    if finish and with_kv:
        operands.append(asked)
        specs.append(VM)
    outs, scratch = [], []
    if with_q:
        outs.append(jax.ShapeDtypeStruct((ROWS, 512), BF if finish else F32))
        if finish:
            scratch.append(pltpu.VMEM((ROWS, 512), F32))
    if with_kv:
        outs.append(jax.ShapeDtypeStruct((ALL, 128), BF) if finish else jax.ShapeDtypeStruct((ROWS, 128), F32))
        if finish:
            scratch.append(pltpu.VMEM((ROWS, 128), F32))
    columns = (512 if with_q else 0) + (128 if with_kv else 0)
    used = sum(high - low for _, low, high, _ in plan)
    return pl.pallas_call(
        functools.partial(project_kernel, plan, len(xs), with_q, with_kv, has_acc, finish),
        out_shape=outs,
        in_specs=specs,
        out_specs=[VM] * len(outs),
        scratch_shapes=scratch,
        compiler_params=pltpu.CompilerParams(vmem_limit_bytes=VMEM_LIMIT),
        cost_estimate=pl.CostEstimate(
            flops=2 * used * 512 * columns, bytes_accessed=len(plan) * 512 * columns * 2, transcendentals=0
        ),
    )(*operands)


def question_project_kernel(pieces, wq, wkv, cos, sin, out):
    q_sum, kv_sum = None, None
    for place in range(16):
        base = place * 512
        piece = pieces[place]
        both = wkv[:, pl.ds(base, 512)]
        kv_term = lax.dot_general(piece, both, (((1,), (1,)), ((), ())), preferred_element_type=F32)
        q_term = jnp.dot(piece, wq[pl.ds(base, 512), :], preferred_element_type=F32)
        q_sum = q_term if q_sum is None else q_sum + q_term
        kv_sum = kv_term if kv_sum is None else kv_sum + kv_term
    for head in range(4):
        cols = slice(head * HD, (head + 1) * HD)
        out[:, cols] = turn(q_sum[:, cols], cos[ROWS : ROWS + 32, :], sin[ROWS : ROWS + 32, :])
    out[:, 512:640] = kv_sum.astype(BF)


def question_project(pieces, weights, tables):
    return pl.pallas_call(
        question_project_kernel,
        out_shape=jax.ShapeDtypeStruct((32, 640), BF),
        in_specs=[VM] * 5,
        out_specs=VM,
        compiler_params=pltpu.CompilerParams(vmem_limit_bytes=VMEM_LIMIT),
        cost_estimate=pl.CostEstimate(flops=2 * 256 * 8192 * 640, bytes_accessed=8192 * 640 * 2, transcendentals=0),
    )(pieces, *weights, *tables)


def key_value_kernel(info, own, partner, cos, sin, out):
    is_lower = info[1] % 2 == 0
    mine, other = own[...].astype(F32), partner[...].astype(F32)
    low = jnp.where(is_lower, mine, other)
    high = jnp.where(is_lower, other, mine)
    lane = lax.broadcasted_iota(jnp.int32, low.shape, 1)
    keys = jnp.where(lane < 64, low, pltpu.roll(high, 64, 1))
    values = jnp.where(lane < 64, pltpu.roll(low, 64, 1), high)
    out[:, :HD] = (keys * cos[...] + pltpu.roll(keys, 64, 1) * sin[...]).astype(BF)
    out[:, HD:] = values.astype(BF)


def key_value(info, own, partner, cos, sin):
    return pl.pallas_call(
        key_value_kernel,
        out_shape=jax.ShapeDtypeStruct((ALL, 2 * HD), BF),
        in_specs=[SM, VM, VM, VM, VM],
        out_specs=VM,
        compiler_params=pltpu.CompilerParams(vmem_limit_bytes=VMEM_LIMIT),
    )(info, own, partner, cos, sin)


def scores_of(queries, keys):
    return lax.dot_general(queries, keys, (((1,), (1,)), ((), ())), preferred_element_type=F32)


def weights_of(scores, top):
    return jnp.exp2(scores * SCALE2 - top * SCALE2)


def columns_to_stats(columns):
    rows = columns[0].shape[0]
    lane = lax.broadcasted_iota(jnp.int32, (rows, 128), 1)
    stats = jnp.zeros((rows, 128), F32)
    for index, column in enumerate(columns):
        stats = jnp.where(lane == index, column, stats)
    return stats


def own_kernel(info, q, kv, weighted, stats):
    length = info[5]
    for tile in range(2):
        rows = slice(tile * 256, tile * 256 + 256)
        width = 256 * (tile + 1)
        row = tile * 256 + lax.broadcasted_iota(jnp.int32, (256, width), 0)
        key = lax.broadcasted_iota(jnp.int32, (256, width), 1)
        bias = jnp.where((key <= row) & (key < length), 0.0, NEG)
        tops, totals = [], []
        for head in range(4):
            cols = slice(head * HD, (head + 1) * HD)
            s = scores_of(q[rows, cols], kv[:width, :HD]) + bias
            top = jnp.max(s, axis=1, keepdims=True)
            e = weights_of(s, top)
            totals.append(jnp.sum(e, axis=1, keepdims=True))
            tops.append(top)
            weighted[rows, cols] = jnp.dot(e.astype(BF), kv[:width, HD:], preferred_element_type=F32)
        stats[rows, :] = columns_to_stats(tops + totals)


def own_attention(info, q, kv):
    return pl.pallas_call(
        own_kernel,
        out_shape=[jax.ShapeDtypeStruct((512, 512), F32), jax.ShapeDtypeStruct((512, 128), F32)],
        in_specs=[SM, VM, VM],
        out_specs=[VM, VM],
        compiler_params=pltpu.CompilerParams(vmem_limit_bytes=VMEM_LIMIT),
        cost_estimate=pl.CostEstimate(flops=4 * 4 * 512 * 512 * 128, bytes_accessed=3 << 20, transcendentals=1 << 20),
    )(info, q, kv)


def anchor_kernel(info, q, kv_zero, kv_one, weighted, stats, out):
    length, anchor_length = info[5], info[6]
    first_core = info[3] == 0
    kv = jnp.where(first_core, kv_zero[...], kv_one[...])
    keys, values = kv[:, :HD], kv[:, HD:]
    key = lax.broadcasted_iota(jnp.int32, (1, 512), 1)
    bias = jnp.where(key < anchor_length, 0.0, NEG)
    for tile in range(2):
        rows = slice(tile * 256, tile * 256 + 256)
        block = stats[rows, :]
        row = tile * 256 + lax.broadcasted_iota(jnp.int32, (256, HD), 0)
        for head in range(4):
            cols = slice(head * HD, (head + 1) * HD)
            s = scores_of(q[rows, cols], keys) + bias
            own_top, own_sum = block[:, head : head + 1], block[:, head + 4 : head + 5]
            top = jnp.maximum(own_top, jnp.max(s, axis=1, keepdims=True))
            e = weights_of(s, top)
            factor = weights_of(own_top, top)
            total = own_sum * factor + jnp.sum(e, axis=1, keepdims=True)
            both = weighted[rows, cols] * factor + jnp.dot(e.astype(BF), values, preferred_element_type=F32)
            out[rows, cols] = jnp.where(row < length, both / total, 0.0).astype(BF)


def anchor_attention(info, q, kv_zero, kv_one, weighted, stats):
    return pl.pallas_call(
        anchor_kernel,
        out_shape=jax.ShapeDtypeStruct((512, 512), BF),
        in_specs=[SM, VM, VM, VM, VM, VM],
        out_specs=VM,
        compiler_params=pltpu.CompilerParams(vmem_limit_bytes=VMEM_LIMIT),
        cost_estimate=pl.CostEstimate(flops=4 * 4 * 512 * 512 * 128, bytes_accessed=3 << 20, transcendentals=1 << 20),
    )(info, q, kv_zero, kv_one, weighted, stats)


def question_kernel(info, q_own, q_other, kv_0, kv_1, kv_2, kv_3, out_own, out_other):
    kvs = (kv_0, kv_1, kv_2, kv_3)
    z, core, ctx = info[2], info[3], info[4]
    lengths = [info[5], info[7], info[8], info[9]]
    places = [z, (z + 3) % 4, (z + 1) % 4, (z + 2) % 4]
    stacked = [q_own[:, h * HD : (h + 1) * HD] for h in range(4)]
    stacked += [q_other[:, h * HD : (h + 1) * HD] for h in range(4)]
    q = jnp.concatenate(stacked, axis=0)
    scores = []
    key = lax.broadcasted_iota(jnp.int32, (1, 512), 1)
    for kv, length in zip(kvs, lengths):
        scores.append(scores_of(q, kv[:ROWS, :HD]) + jnp.where(key < length, 0.0, NEG))
    row = lax.broadcasted_iota(jnp.int32, (256, 128), 0)
    lane = lax.broadcasted_iota(jnp.int32, (256, 128), 1)
    row_id = row % 32 + 32 * jnp.where(row < 128, ctx, ctx + 1 - 2 * core)
    block = jnp.where(lane < 64, jnp.where(lane < 32, places[0], places[1]), jnp.where(lane < 96, places[2], places[3]))
    key_id = lane % 32 + 32 * (2 * block + core)
    asked_keys = jnp.concatenate([kv[ROWS:, :HD] for kv in kvs], axis=0)
    asked_values = jnp.concatenate([kv[ROWS:, HD:] for kv in kvs], axis=0)
    scores.append(jnp.where(key_id <= row_id, scores_of(q, asked_keys), NEG))
    top = jnp.max(scores[-1], axis=1, keepdims=True)
    for s in scores[:-1]:
        top = jnp.maximum(top, jnp.max(s, axis=1, keepdims=True))
    values = [kv[:ROWS, HD:] for kv in kvs] + [asked_values]
    total = jnp.zeros((256, 1), F32)
    both = jnp.zeros((256, HD), F32)
    for s, value in zip(scores, values):
        e = weights_of(s, top)
        total = total + jnp.sum(e, axis=1, keepdims=True)
        both = both + jnp.dot(e.astype(BF), value, preferred_element_type=F32)
    for out, start in ((out_own, 0), (out_other, 128)):
        tops, totals = [], []
        for head in range(4):
            rows = slice(start + head * 32, start + head * 32 + 32)
            out[:, head * HD : (head + 1) * HD] = both[rows]
            tops.append(top[rows])
            totals.append(total[rows])
        out[:, 512:640] = columns_to_stats(tops + totals)


def question_attention(info, q_own, q_other, kvs):
    part = jax.ShapeDtypeStruct((32, 640), F32)
    return pl.pallas_call(
        question_kernel,
        out_shape=[part, part],
        in_specs=[SM] + [VM] * 6,
        out_specs=[VM, VM],
        compiler_params=pltpu.CompilerParams(vmem_limit_bytes=VMEM_LIMIT),
        cost_estimate=pl.CostEstimate(flops=4 * 256 * 2176 * 128, bytes_accessed=2 << 20, transcendentals=1 << 19),
    )(info, q_own, q_other, *kvs)


def merge_kernel(a, b, out):
    stat_a, stat_b = a[:, 512:640], b[:, 512:640]
    for head in range(4):
        cols = slice(head * HD, (head + 1) * HD)
        top_a, top_b = stat_a[:, head : head + 1], stat_b[:, head : head + 1]
        top = jnp.maximum(top_a, top_b)
        factor_a, factor_b = weights_of(top_a, top), weights_of(top_b, top)
        total = stat_a[:, head + 4 : head + 5] * factor_a + stat_b[:, head + 4 : head + 5] * factor_b
        out[:, cols] = ((a[:, cols] * factor_a + b[:, cols] * factor_b) / total).astype(BF)


def merge(a, b):
    return pl.pallas_call(
        merge_kernel,
        out_shape=jax.ShapeDtypeStruct((32, 512), BF),
        in_specs=[VM, VM],
        out_specs=VM,
        compiler_params=pltpu.CompilerParams(vmem_limit_bytes=VMEM_LIMIT),
    )(a, b)


PLAN_1 = [
    ((0, 0), 0, 512, [(0, 0, 512)]),
    ((-1, 0), 0, 512, [(1, 0, 512)]),
    ((1, 0), 0, 512, [(2, 0, 512)]),
    ((0, -1), 0, 512, [(3, 0, 512)]),
    ((0, 1), 0, 512, [(4, 0, 512)]),
    ((2, 0), 0, 256, [(5, 0, 256)]),
    ((0, 2), 256, 512, [(6, 0, 256)]),
]
PLAN_2 = [
    ((-1, -1), 0, 512, [(0, 0, 256), (2, 0, 256)]),
    ((1, -1), 0, 512, [(0, 256, 256), (3, 0, 256)]),
    ((-1, 1), 0, 512, [(1, 0, 256), (2, 256, 256)]),
    ((1, 1), 0, 512, [(1, 256, 256), (3, 256, 256)]),
    ((2, -1), 0, 256, [(0, 512, 256)]),
    ((2, 1), 0, 256, [(1, 512, 256)]),
    ((-1, 2), 256, 512, [(2, 512, 256)]),
    ((1, 2), 256, 512, [(3, 512, 256)]),
    ((0, 2), 0, 256, [(0, 768, 128), (1, 768, 128)]),
    ((2, 0), 256, 512, [(2, 768, 128), (3, 768, 128)]),
]
PLAN_3 = [
    ((2, 2), 0, 512, [(1, 128, 256), (3, 128, 256)]),
    ((-1, 2), 0, 256, [(0, 0, 256)]),
    ((1, 2), 0, 256, [(0, 256, 128), (1, 0, 128)]),
    ((2, -1), 256, 512, [(2, 0, 256)]),
    ((2, 1), 256, 512, [(2, 256, 128), (3, 0, 128)]),
]
NEAR_Y = [(0, 0, 256), (1, 0, 256), (4, 0, 256)]
NEAR_X = [(2, 256, 256), (3, 256, 256), (5, 0, 256)]
PACK_2 = [NEAR_Y + [(2, 0, 128)], NEAR_Y + [(3, 128, 128)], NEAR_X + [(0, 256, 128)], NEAR_X + [(1, 384, 128)]]
PACK_3 = [[(0, 0, 384)], [(1, 384, 384)], [(2, 0, 384)], [(3, 384, 384)]]


def tables_of(positions):
    inverse_freq = ROPE_BASE ** (-(jnp.arange(HD // 2, dtype=jnp.float32) * 2.0 / HD))
    inverse_freq = jnp.concatenate([inverse_freq, inverse_freq])
    phases = positions.astype(jnp.float32)[:, None] * inverse_freq[None, :]
    signs = jnp.where(jnp.arange(HD) < HD // 2, -1.0, 1.0).astype(jnp.float32)
    return jnp.cos(phases), jnp.sin(phases) * signs[None, :]


def shift_z(array, dz):
    pairs = [(i, ((i // 2 + dz) % 4) * 2 + i % 2) for i in range(8)]
    return lax.ppermute(array, "ctx", pairs)


def per_device(context, question, w_query, w_key, w_value, lengths, owner):
    ctx = lax.axis_index("ctx")
    z, core = lax.shift_right_logical(ctx, 1), ctx & 1
    heads = lax.axis_index("heads")
    y, x = lax.shift_right_logical(heads, 2), heads & 3
    ids = jnp.arange(8, dtype=jnp.int32)
    own_offset = jnp.sum(jnp.where(ids < ctx, lengths, 0))
    own_length = jnp.sum(jnp.where(ids == ctx, lengths, 0))
    filled = jnp.sum(lengths)
    anchor_length = jnp.where(ctx > 0, lengths[0], 0)

    def length_of(dz):
        return jnp.sum(jnp.where(ids == ((z + dz) & 3) * 2 + core, lengths, 0))

    places = jnp.arange(16, dtype=jnp.int32)
    info = jnp.zeros((16,), jnp.int32)
    for place, value in enumerate(
        [y, x, z, core, ctx, own_length, anchor_length, length_of(3), length_of(1), length_of(2)]
    ):
        info = jnp.where(places == place, value, info)

    up = shift_heads(context, 1, 0)
    down = shift_heads(context, -1, 0)
    right = shift_heads(context, 0, 1)
    left = shift_heads(context, 0, -1)
    low, high = pack([[(0, 0, 256)], [(0, 256, 256)]], [context])
    far_y = shift_heads(low, 2, 0)
    up, high = lax.optimization_barrier((up, high))
    far_x = shift_heads(high, 0, 2)

    share = lax.all_to_all(question[0].reshape(8, 32, 512), "ctx", 0, 0)
    share = lax.dynamic_index_in_dim(share, owner[0], 0, False)
    share = jnp.broadcast_to(share[None], (16, 32, 512))
    up, share, info = lax.optimization_barrier((up, share, info))
    pieces = lax.all_to_all(share, "heads", 0, 0)
    up, pieces = lax.optimization_barrier((up, pieces))

    to_right, to_left, to_up, to_down = pack(PACK_2, [up, down, right, left, far_y, far_x])
    a_right, a_left = shift_heads(to_right, 0, 1), shift_heads(to_left, 0, -1)
    b_up, b_down = shift_heads(to_up, 1, 0), shift_heads(to_down, -1, 0)
    up, to_right = lax.optimization_barrier((up, to_right))
    tables = tables_of(
        jnp.concatenate(
            [own_offset + jnp.arange(ROWS, dtype=jnp.int32), filled + 32 * ctx + jnp.arange(ASKED, dtype=jnp.int32)]
        )
    )
    pieces, w_query, w_key, w_value, tables = lax.optimization_barrier(
        (pieces, w_query, w_key, w_value, tables)
    )
    weights = hold(w_query, w_key.T, w_value.T)
    accs = project(info, [context, up, down, right, left, far_y, far_x], PLAN_1, weights, None, True, True)
    q_share = question_project(pieces, weights, tables)

    a_right, a_left, b_up, b_down, accs, q_share = lax.optimization_barrier(
        (a_right, a_left, b_up, b_down, accs, q_share)
    )
    to_right, to_left, to_up, to_down = pack(PACK_3, [a_right, a_left, b_up, b_down])
    last = [
        shift_heads(to_right, 0, 1),
        shift_heads(to_left, 0, -1),
        shift_heads(to_up, 1, 0),
        shift_heads(to_down, -1, 0),
    ]
    accs = project(info, [a_right, a_left, b_up, b_down], PLAN_2, weights, accs, True, True)

    (halves,) = project(info, last, PLAN_3, weights, accs, False, True, True, asked=q_share)
    (queries,) = project(info, last, PLAN_3, weights, accs, True, False, True, tables)
    partner = swap_heads(halves, 0, 1)
    q_asked = q_share[:, :512]
    q_other = swap_ctx(q_asked, 0, 1)
    partner, queries, q_other = lax.optimization_barrier((partner, queries, q_other))
    kv = key_value(info, halves, partner, *tables)

    below, above, across = shift_z(kv, 1), shift_z(kv, -1), shift_z(kv, 2)
    weighted, stats = own_attention(info, queries, kv)
    below, above, across, weighted = lax.optimization_barrier((below, above, across, weighted))
    nearer = jnp.where(z == 0, kv[:ROWS], jnp.where(z == 1, below[:ROWS], jnp.where(z == 2, across[:ROWS], above[:ROWS])))
    from_zero = lax.ppermute(nearer, "ctx", [(0, 1), (2, 3), (4, 5), (6, 7)])
    part, part_other = question_attention(info, q_asked, q_other, [kv, below, above, across])
    from_zero, part = lax.optimization_barrier((from_zero, part))
    context_attn = anchor_attention(info, queries, nearer, from_zero, weighted, stats)
    question_attn = merge(part, swap_ctx(part_other, 0, 1))
    return (context_attn, question_attn)


def solution(mesh):
    in_specs = (
        P("ctx", "heads"),
        P("ctx", None, "heads"),
        P(None, "heads"),
        P(None, "heads"),
        P(None, "heads"),
        P(),
        P(),
    )
    out_specs = (P("ctx", "heads"), P("ctx", "heads"))
    return jax.shard_map(
        per_device, mesh=mesh, in_specs=in_specs, out_specs=out_specs, check_vma=False
    )
```

```python
import functools

import jax
import jax.numpy as jnp
from jax import lax
from jax.experimental import pallas as pl
from jax.experimental.pallas import tpu as pltpu
from jax.sharding import PartitionSpec as P

HD = 128
ROPE_BASE = 500000.0
BF = jnp.bfloat16
F32 = jnp.float32
VMEM_LIMIT = 8 * 1024 * 1024
HOLD_LIMIT = 37 * 1024 * 1024
NEG = -1e30
SCALE2 = HD ** (-0.5) * 1.4426950408889634
ROWS = 512
ASKED = 32
ALL = ROWS + ASKED

HBM = pl.BlockSpec(memory_space=pltpu.HBM)
VM = pl.BlockSpec(memory_space=pltpu.VMEM)
SM = pl.BlockSpec(memory_space=pltpu.SMEM)


def shift_heads(array, dy, dx):
    pairs = [(i, ((i // 4 + dy) % 4) * 4 + (i % 4 + dx) % 4) for i in range(16)]
    return lax.ppermute(array, "heads", pairs)


def swap_heads(array, my, mx):
    pairs = [(i, ((i // 4) ^ my) * 4 + ((i % 4) ^ mx)) for i in range(16)]
    return lax.ppermute(array, "heads", pairs)


def swap_ctx(array, mz, mc):
    pairs = [(i, ((i // 2) ^ mz) * 2 + ((i % 2) ^ mc)) for i in range(8)]
    return lax.ppermute(array, "ctx", pairs)


def places():
    heads, ctx = lax.axis_index("heads"), lax.axis_index("ctx")
    return lax.shift_right_logical(heads, 2), heads & 3, lax.shift_right_logical(ctx, 1), ctx & 1


def pack_kernel(plan, n_in, *refs):
    ins, outs = refs[:n_in], refs[n_in:]
    for out, pieces in zip(outs, plan):
        row = 0
        for operand, start, count in pieces:
            out[row : row + count, :] = ins[operand][start : start + count, :]
            row += count


def pack(plan, ins):
    return pl.pallas_call(
        functools.partial(pack_kernel, plan, len(ins)),
        out_shape=[jax.ShapeDtypeStruct((sum(p[2] for p in pieces), 512), BF) for pieces in plan],
        in_specs=[VM] * len(ins),
        out_specs=[VM] * len(plan),
        compiler_params=pltpu.CompilerParams(vmem_limit_bytes=VMEM_LIMIT),
        cost_estimate=pl.CostEstimate(flops=0, bytes_accessed=1 << 20, transcendentals=0),
    )(*ins)


def hold_kernel(wq, wk, wv, q_out, kv_out, sem):
    copies = []
    for part in range(8):
        rows = pl.ds(part * 1024, 1024)
        copies.append(pltpu.make_async_copy(wq.at[rows, :], q_out.at[rows, :], sem.at[part]))
    for part in range(4):
        cols = pl.ds(part * 2048, 2048)
        copies.append(pltpu.make_async_copy(wk.at[:, cols], kv_out.at[pl.ds(0, 64), cols], sem.at[8 + part]))
        copies.append(pltpu.make_async_copy(wv.at[:, cols], kv_out.at[pl.ds(64, 64), cols], sem.at[12 + part]))
    for copy in copies:
        copy.start()
    for copy in copies:
        copy.wait()


def hold(wq, wk, wv):
    return pl.pallas_call(
        hold_kernel,
        out_shape=[jax.ShapeDtypeStruct((8192, 512), BF), jax.ShapeDtypeStruct((128, 8192), BF)],
        in_specs=[HBM] * 3,
        out_specs=[VM, VM],
        scratch_shapes=[pltpu.SemaphoreType.DMA((16,))],
        compiler_params=pltpu.CompilerParams(vmem_limit_bytes=HOLD_LIMIT),
        cost_estimate=pl.CostEstimate(flops=0, bytes_accessed=20 << 20, transcendentals=0),
    )(wq, wk, wv)


def turn(part, cos, sin):
    return (part * cos + pltpu.roll(part, HD // 2, 1) * sin).astype(BF)


def project_kernel(plan, n_x, with_q, with_kv, has_acc, finish, *refs):
    refs = list(refs)
    take = lambda count: [refs.pop(0) for _ in range(count)]
    xs = take(n_x)
    wq = take(1)[0] if with_q else None
    wkv = take(1)[0] if with_kv else None
    acc_q = take(1)[0] if has_acc and with_q else None
    acc_kv = take(1)[0] if has_acc and with_kv else None
    cos, sin = take(2) if finish and with_q else (None, None)
    asked = take(1)[0] if finish and with_kv else None
    q_out = take(1)[0] if with_q else None
    kv_out = take(1)[0] if with_kv else None
    q_sum = take(1)[0] if finish and with_q else q_out
    kv_sum = take(1)[0] if finish and with_kv else kv_out
    y, x, _, _ = places()
    if has_acc:
        if with_q:
            q_sum[...] = acc_q[...]
        if with_kv:
            kv_sum[...] = acc_kv[...]
    for slot, ((dy, dx), low, high, uses) in enumerate(plan):
        base = pl.multiple_of((((y + dy) & 3) * 4 + ((x + dx) & 3)) * 512, 512)
        parts = [xs[operand][pl.ds(start, count), :] for operand, start, count in uses]
        piece = parts[0] if len(parts) == 1 else jnp.concatenate(parts, axis=0)
        fresh = slot == 0 and not has_acc
        if with_kv:
            both = wkv[:, pl.ds(base, 512)]
            term = lax.dot_general(piece, both, (((1,), (1,)), ((), ())), preferred_element_type=F32)
            kv_sum[low:high, :] = term if fresh else kv_sum[low:high, :] + term
        if with_q:
            term = jnp.dot(piece, wq[pl.ds(base, 512), :], preferred_element_type=F32)
            q_sum[low:high, :] = term if fresh else q_sum[low:high, :] + term
    if finish and with_kv:
        kv_out[:ROWS, :] = kv_sum[...].astype(BF)
        kv_out[ROWS:, :] = asked[:, 512:640]
    if finish and with_q:
        for head in range(4):
            cols = slice(head * HD, (head + 1) * HD)
            q_out[:, cols] = turn(q_sum[:, cols], cos[:ROWS, :], sin[:ROWS, :])


def project(xs, plan, weights, accs, with_q, with_kv, finish=False, tables=None, asked=None):
    wq, wkv = weights
    operands, specs = list(xs), [VM] * len(xs)
    if with_q:
        operands.append(wq)
        specs.append(VM)
    if with_kv:
        operands.append(wkv)
        specs.append(VM)
    has_acc = accs is not None
    if has_acc:
        if with_q:
            operands.append(accs[0])
            specs.append(VM)
        if with_kv:
            operands.append(accs[1])
            specs.append(VM)
    if finish and with_q:
        operands += list(tables)
        specs += [VM, VM]
    if finish and with_kv:
        operands.append(asked)
        specs.append(VM)
    outs, scratch = [], []
    if with_q:
        outs.append(jax.ShapeDtypeStruct((ROWS, 512), BF if finish else F32))
        if finish:
            scratch.append(pltpu.VMEM((ROWS, 512), F32))
    if with_kv:
        outs.append(jax.ShapeDtypeStruct((ALL, 128), BF) if finish else jax.ShapeDtypeStruct((ROWS, 128), F32))
        if finish:
            scratch.append(pltpu.VMEM((ROWS, 128), F32))
    columns = (512 if with_q else 0) + (128 if with_kv else 0)
    used = sum(high - low for _, low, high, _ in plan)
    return pl.pallas_call(
        functools.partial(project_kernel, plan, len(xs), with_q, with_kv, has_acc, finish),
        out_shape=outs,
        in_specs=specs,
        out_specs=[VM] * len(outs),
        scratch_shapes=scratch,
        compiler_params=pltpu.CompilerParams(vmem_limit_bytes=VMEM_LIMIT),
        cost_estimate=pl.CostEstimate(
            flops=2 * used * 512 * columns, bytes_accessed=len(plan) * 512 * columns * 2, transcendentals=0
        ),
    )(*operands)


def question_project_kernel(pieces, wq, wkv, cos, sin, out):
    q_sum, kv_sum = None, None
    for place in range(16):
        base = place * 512
        piece = pieces[place]
        both = wkv[:, pl.ds(base, 512)]
        kv_term = lax.dot_general(piece, both, (((1,), (1,)), ((), ())), preferred_element_type=F32)
        q_term = jnp.dot(piece, wq[pl.ds(base, 512), :], preferred_element_type=F32)
        q_sum = q_term if q_sum is None else q_sum + q_term
        kv_sum = kv_term if kv_sum is None else kv_sum + kv_term
    for head in range(4):
        cols = slice(head * HD, (head + 1) * HD)
        out[:, cols] = turn(q_sum[:, cols], cos[ROWS : ROWS + 32, :], sin[ROWS : ROWS + 32, :])
    out[:, 512:640] = kv_sum.astype(BF)


def question_project(pieces, weights, tables):
    return pl.pallas_call(
        question_project_kernel,
        out_shape=jax.ShapeDtypeStruct((32, 640), BF),
        in_specs=[VM] * 5,
        out_specs=VM,
        compiler_params=pltpu.CompilerParams(vmem_limit_bytes=VMEM_LIMIT),
        cost_estimate=pl.CostEstimate(flops=2 * 256 * 8192 * 640, bytes_accessed=8192 * 640 * 2, transcendentals=0),
    )(pieces, *weights, *tables)


def key_value_kernel(own, partner, cos, sin, out):
    is_lower = (places()[1] & 1) == 0
    mine, other = own[...].astype(F32), partner[...].astype(F32)
    low = jnp.where(is_lower, mine, other)
    high = jnp.where(is_lower, other, mine)
    lane = lax.broadcasted_iota(jnp.int32, low.shape, 1)
    keys = jnp.where(lane < 64, low, pltpu.roll(high, 64, 1))
    values = jnp.where(lane < 64, pltpu.roll(low, 64, 1), high)
    out[:, :HD] = (keys * cos[...] + pltpu.roll(keys, 64, 1) * sin[...]).astype(BF)
    out[:, HD:] = values.astype(BF)


def key_value(own, partner, cos, sin):
    return pl.pallas_call(
        key_value_kernel,
        out_shape=jax.ShapeDtypeStruct((ALL, 2 * HD), BF),
        in_specs=[VM, VM, VM, VM],
        out_specs=VM,
        compiler_params=pltpu.CompilerParams(vmem_limit_bytes=VMEM_LIMIT),
    )(own, partner, cos, sin)


def scores_of(queries, keys):
    return lax.dot_general(queries, keys, (((1,), (1,)), ((), ())), preferred_element_type=F32)


def weights_of(scores, top):
    return jnp.exp2(scores * SCALE2 - top * SCALE2)


def columns_to_stats(columns):
    rows = columns[0].shape[0]
    lane = lax.broadcasted_iota(jnp.int32, (rows, 128), 1)
    stats = jnp.zeros((rows, 128), F32)
    for index, column in enumerate(columns):
        stats = jnp.where(lane == index, column, stats)
    return stats


def own_kernel(lengths, q, kv, weighted, stats):
    _, _, z, core = places()
    length = lengths[2 * z + core]
    for tile in range(2):
        rows = slice(tile * 256, tile * 256 + 256)
        width = 256 * (tile + 1)
        row = tile * 256 + lax.broadcasted_iota(jnp.int32, (256, width), 0)
        key = lax.broadcasted_iota(jnp.int32, (256, width), 1)
        bias = jnp.where((key <= row) & (key < length), 0.0, NEG)
        tops, totals = [], []
        for head in range(4):
            cols = slice(head * HD, (head + 1) * HD)
            s = scores_of(q[rows, cols], kv[:width, :HD]) + bias
            top = jnp.max(s, axis=1, keepdims=True)
            e = weights_of(s, top)
            totals.append(jnp.sum(e, axis=1, keepdims=True))
            tops.append(top)
            weighted[rows, cols] = jnp.dot(e.astype(BF), kv[:width, HD:], preferred_element_type=F32)
        stats[rows, :] = columns_to_stats(tops + totals)


def own_attention(lengths, q, kv):
    return pl.pallas_call(
        own_kernel,
        out_shape=[jax.ShapeDtypeStruct((512, 512), F32), jax.ShapeDtypeStruct((512, 128), F32)],
        in_specs=[SM, VM, VM],
        out_specs=[VM, VM],
        compiler_params=pltpu.CompilerParams(vmem_limit_bytes=VMEM_LIMIT),
        cost_estimate=pl.CostEstimate(flops=4 * 4 * 512 * 512 * 128, bytes_accessed=3 << 20, transcendentals=1 << 20),
    )(lengths, q, kv)


def anchor_kernel(lengths, q, kv_zero, kv_one, weighted, stats, out):
    _, _, z, core = places()
    length = lengths[2 * z + core]
    anchor_length = jnp.where(2 * z + core > 0, lengths[0], 0)
    first_core = core == 0
    kv = jnp.where(first_core, kv_zero[...], kv_one[...])
    keys, values = kv[:, :HD], kv[:, HD:]
    key = lax.broadcasted_iota(jnp.int32, (1, 512), 1)
    bias = jnp.where(key < anchor_length, 0.0, NEG)
    for tile in range(2):
        rows = slice(tile * 256, tile * 256 + 256)
        block = stats[rows, :]
        row = tile * 256 + lax.broadcasted_iota(jnp.int32, (256, HD), 0)
        for head in range(4):
            cols = slice(head * HD, (head + 1) * HD)
            s = scores_of(q[rows, cols], keys) + bias
            own_top, own_sum = block[:, head : head + 1], block[:, head + 4 : head + 5]
            top = jnp.maximum(own_top, jnp.max(s, axis=1, keepdims=True))
            e = weights_of(s, top)
            factor = weights_of(own_top, top)
            total = own_sum * factor + jnp.sum(e, axis=1, keepdims=True)
            both = weighted[rows, cols] * factor + jnp.dot(e.astype(BF), values, preferred_element_type=F32)
            out[rows, cols] = jnp.where(row < length, both / total, 0.0).astype(BF)


def anchor_attention(lengths, q, kv_zero, kv_one, weighted, stats):
    return pl.pallas_call(
        anchor_kernel,
        out_shape=jax.ShapeDtypeStruct((512, 512), BF),
        in_specs=[SM, VM, VM, VM, VM, VM],
        out_specs=VM,
        compiler_params=pltpu.CompilerParams(vmem_limit_bytes=VMEM_LIMIT),
        cost_estimate=pl.CostEstimate(flops=4 * 4 * 512 * 512 * 128, bytes_accessed=3 << 20, transcendentals=1 << 20),
    )(lengths, q, kv_zero, kv_one, weighted, stats)


def question_kernel(lengths_ref, q_own, q_other, kv_0, kv_1, kv_2, kv_3, out_own, out_other):
    kvs = (kv_0, kv_1, kv_2, kv_3)
    _, _, z, core = places()
    ctx = 2 * z + core
    blocks = [z, (z + 3) & 3, (z + 1) & 3, (z + 2) & 3]
    lengths = [lengths_ref[2 * block + core] for block in blocks]
    stacked = [q_own[:, h * HD : (h + 1) * HD] for h in range(4)]
    stacked += [q_other[:, h * HD : (h + 1) * HD] for h in range(4)]
    q = jnp.concatenate(stacked, axis=0)
    scores = []
    key = lax.broadcasted_iota(jnp.int32, (1, 512), 1)
    for kv, length in zip(kvs, lengths):
        scores.append(scores_of(q, kv[:ROWS, :HD]) + jnp.where(key < length, 0.0, NEG))
    row = lax.broadcasted_iota(jnp.int32, (256, 128), 0)
    lane = lax.broadcasted_iota(jnp.int32, (256, 128), 1)
    row_id = row % 32 + 32 * jnp.where(row < 128, ctx, ctx + 1 - 2 * core)
    block = jnp.where(lane < 64, jnp.where(lane < 32, blocks[0], blocks[1]), jnp.where(lane < 96, blocks[2], blocks[3]))
    key_id = lane % 32 + 32 * (2 * block + core)
    asked_keys = jnp.concatenate([kv[ROWS:, :HD] for kv in kvs], axis=0)
    asked_values = jnp.concatenate([kv[ROWS:, HD:] for kv in kvs], axis=0)
    scores.append(jnp.where(key_id <= row_id, scores_of(q, asked_keys), NEG))
    top = jnp.max(scores[-1], axis=1, keepdims=True)
    for s in scores[:-1]:
        top = jnp.maximum(top, jnp.max(s, axis=1, keepdims=True))
    values = [kv[:ROWS, HD:] for kv in kvs] + [asked_values]
    total = jnp.zeros((256, 1), F32)
    both = jnp.zeros((256, HD), F32)
    for s, value in zip(scores, values):
        e = weights_of(s, top)
        total = total + jnp.sum(e, axis=1, keepdims=True)
        both = both + jnp.dot(e.astype(BF), value, preferred_element_type=F32)
    for out, start in ((out_own, 0), (out_other, 128)):
        tops, totals = [], []
        for head in range(4):
            rows = slice(start + head * 32, start + head * 32 + 32)
            out[:, head * HD : (head + 1) * HD] = both[rows]
            tops.append(top[rows])
            totals.append(total[rows])
        out[:, 512:640] = columns_to_stats(tops + totals)


def question_attention(lengths, q_own, q_other, kvs):
    part = jax.ShapeDtypeStruct((32, 640), F32)
    return pl.pallas_call(
        question_kernel,
        out_shape=[part, part],
        in_specs=[SM] + [VM] * 6,
        out_specs=[VM, VM],
        compiler_params=pltpu.CompilerParams(vmem_limit_bytes=VMEM_LIMIT),
        cost_estimate=pl.CostEstimate(flops=4 * 256 * 2176 * 128, bytes_accessed=2 << 20, transcendentals=1 << 19),
    )(lengths, q_own, q_other, *kvs)


def merge_kernel(a, b, out):
    stat_a, stat_b = a[:, 512:640], b[:, 512:640]
    for head in range(4):
        cols = slice(head * HD, (head + 1) * HD)
        top_a, top_b = stat_a[:, head : head + 1], stat_b[:, head : head + 1]
        top = jnp.maximum(top_a, top_b)
        factor_a, factor_b = weights_of(top_a, top), weights_of(top_b, top)
        total = stat_a[:, head + 4 : head + 5] * factor_a + stat_b[:, head + 4 : head + 5] * factor_b
        out[:, cols] = ((a[:, cols] * factor_a + b[:, cols] * factor_b) / total).astype(BF)


def merge(a, b):
    return pl.pallas_call(
        merge_kernel,
        out_shape=jax.ShapeDtypeStruct((32, 512), BF),
        in_specs=[VM, VM],
        out_specs=VM,
        compiler_params=pltpu.CompilerParams(vmem_limit_bytes=VMEM_LIMIT),
    )(a, b)


PLAN_1 = [
    ((0, 0), 0, 512, [(0, 0, 512)]),
    ((-1, 0), 0, 512, [(1, 0, 512)]),
    ((1, 0), 0, 512, [(2, 0, 512)]),
    ((0, -1), 0, 512, [(3, 0, 512)]),
    ((0, 1), 0, 512, [(4, 0, 512)]),
    ((2, 0), 0, 256, [(5, 0, 256)]),
    ((0, 2), 256, 512, [(6, 0, 256)]),
]
PLAN_2 = [
    ((-1, -1), 0, 512, [(0, 0, 256), (2, 0, 256)]),
    ((1, -1), 0, 512, [(0, 256, 256), (3, 0, 256)]),
    ((-1, 1), 0, 512, [(1, 0, 256), (2, 256, 256)]),
    ((1, 1), 0, 512, [(1, 256, 256), (3, 256, 256)]),
    ((2, -1), 0, 256, [(0, 512, 256)]),
    ((2, 1), 0, 256, [(1, 512, 256)]),
    ((-1, 2), 256, 512, [(2, 512, 256)]),
    ((1, 2), 256, 512, [(3, 512, 256)]),
    ((0, 2), 0, 256, [(0, 768, 128), (1, 768, 128)]),
    ((2, 0), 256, 512, [(2, 768, 128), (3, 768, 128)]),
]
PLAN_3 = [
    ((2, 2), 0, 512, [(1, 128, 256), (3, 128, 256)]),
    ((-1, 2), 0, 256, [(0, 0, 256)]),
    ((1, 2), 0, 256, [(0, 256, 128), (1, 0, 128)]),
    ((2, -1), 256, 512, [(2, 0, 256)]),
    ((2, 1), 256, 512, [(2, 256, 128), (3, 0, 128)]),
]
NEAR_Y = [(0, 0, 256), (1, 0, 256), (4, 0, 256)]
NEAR_X = [(2, 256, 256), (3, 256, 256), (4, 0, 256)]
PACK_2 = [NEAR_Y + [(2, 0, 128)], NEAR_Y + [(3, 128, 128)], NEAR_X + [(0, 256, 128)], NEAR_X + [(1, 384, 128)]]
PACK_3 = [[(0, 0, 384)], [(1, 384, 384)]]


def tables_of(positions):
    inverse_freq = ROPE_BASE ** (-(jnp.arange(HD // 2, dtype=jnp.float32) * 2.0 / HD))
    inverse_freq = jnp.concatenate([inverse_freq, inverse_freq])
    phases = positions.astype(jnp.float32)[:, None] * inverse_freq[None, :]
    signs = jnp.where(jnp.arange(HD) < HD // 2, -1.0, 1.0).astype(jnp.float32)
    return jnp.cos(phases), jnp.sin(phases) * signs[None, :]


def shift_z(array, dz):
    pairs = [(i, ((i // 2 + dz) % 4) * 2 + i % 2) for i in range(8)]
    return lax.ppermute(array, "ctx", pairs)


def per_device(context, question, w_query, w_key, w_value, lengths, owner):
    ctx = lax.axis_index("ctx")
    z, core = lax.shift_right_logical(ctx, 1), ctx & 1
    ids = jnp.arange(8, dtype=jnp.int32)
    own_offset = jnp.sum(jnp.where(ids < ctx, lengths, 0))
    filled = jnp.sum(lengths)

    up = shift_heads(context, 1, 0)
    down = shift_heads(context, -1, 0)
    right = shift_heads(context, 0, 1)
    left = shift_heads(context, 0, -1)
    low, high = pack([[(0, 0, 256)], [(0, 256, 256)]], [context])
    far_y = shift_heads(low, 2, 0)
    low, asked = lax.optimization_barrier((low, question))
    up, high = lax.optimization_barrier((up, high))
    far_x = shift_heads(high, 0, 2)

    share = lax.all_to_all(asked[0].reshape(8, 32, 512), "ctx", 0, 0)
    share = lax.dynamic_index_in_dim(share, owner[0], 0, False)
    share = jnp.broadcast_to(share[None], (16, 32, 512))
    far_y, share = lax.optimization_barrier((far_y, share))
    pieces = lax.all_to_all(share, "heads", 0, 0)
    up, pieces = lax.optimization_barrier((up, pieces))

    to_right, to_left = pack(PACK_2[:2], [up, down, right, left, far_y])
    to_up, to_down = pack(PACK_2[2:], [up, down, right, left, far_x])
    a_right, a_left = shift_heads(to_right, 0, 1), shift_heads(to_left, 0, -1)
    b_up, b_down = shift_heads(to_up, 1, 0), shift_heads(to_down, -1, 0)
    up, to_right = lax.optimization_barrier((up, to_right))
    tables = tables_of(
        jnp.concatenate(
            [own_offset + jnp.arange(ROWS, dtype=jnp.int32), filled + 32 * ctx + jnp.arange(ASKED, dtype=jnp.int32)]
        )
    )
    pieces, w_query, w_key, w_value, tables = lax.optimization_barrier(
        (pieces, w_query, w_key, w_value, tables)
    )
    weights = hold(w_query, w_key.T, w_value.T)
    accs = project([context, up, down, right, left, far_y, far_x], PLAN_1, weights, None, True, True)
    q_share = question_project(pieces, weights, tables)

    a_right, a_left, accs, q_share = lax.optimization_barrier((a_right, a_left, accs, q_share))
    to_right, to_left = pack(PACK_3, [a_right, a_left])
    to_up, to_down = pack(PACK_3, [b_up, b_down])
    last = [
        shift_heads(to_right, 0, 1),
        shift_heads(to_left, 0, -1),
        shift_heads(to_up, 1, 0),
        shift_heads(to_down, -1, 0),
    ]
    accs = project([a_right, a_left, b_up, b_down], PLAN_2, weights, accs, True, True)

    (halves,) = project(last, PLAN_3, weights, accs, False, True, True, asked=q_share)
    (queries,) = project(last, PLAN_3, weights, accs, True, False, True, tables)
    partner = swap_heads(halves, 0, 1)
    q_asked = q_share[:, :512]
    q_other = swap_ctx(q_asked, 0, 1)
    partner, queries, q_other = lax.optimization_barrier((partner, queries, q_other))
    kv = key_value(halves, partner, *tables)

    below, above, across = shift_z(kv, 1), shift_z(kv, -1), shift_z(kv, 2)
    weighted, stats = own_attention(lengths, queries, kv)
    below, above, across, weighted = lax.optimization_barrier((below, above, across, weighted))
    nearer = jnp.where(z == 0, kv[:ROWS], jnp.where(z == 1, below[:ROWS], jnp.where(z == 2, across[:ROWS], above[:ROWS])))
    from_zero = lax.ppermute(nearer, "ctx", [(0, 1), (2, 3), (4, 5), (6, 7)])
    part, part_other = question_attention(lengths, q_asked, q_other, [kv, below, above, across])
    from_zero, part = lax.optimization_barrier((from_zero, part))
    context_attn = anchor_attention(lengths, queries, nearer, from_zero, weighted, stats)
    question_attn = merge(part, swap_ctx(part_other, 0, 1))
    return (context_attn, question_attn)


def solution(mesh):
    in_specs = (
        P("ctx", "heads"),
        P("ctx", None, "heads"),
        P(None, "heads"),
        P(None, "heads"),
        P(None, "heads"),
        P(),
        P(),
    )
    out_specs = (P("ctx", "heads"), P("ctx", "heads"))
    return jax.shard_map(
        per_device, mesh=mesh, in_specs=in_specs, out_specs=out_specs, check_vma=False
    )
```

```python
import functools

import jax
import jax.numpy as jnp
from jax import lax
from jax.experimental import pallas as pl
from jax.experimental.pallas import tpu as pltpu
from jax.sharding import PartitionSpec as P

HD = 128
ROPE_BASE = 500000.0
BF = jnp.bfloat16
F32 = jnp.float32
VMEM_LIMIT = 8 * 1024 * 1024
HOLD_LIMIT = 37 * 1024 * 1024
NEG = -1e30
SCALE2 = HD ** (-0.5) * 1.4426950408889634
ROWS = 512
ASKED = 32
FAR = -1
ALL = ROWS + ASKED

HBM = pl.BlockSpec(memory_space=pltpu.HBM)
VM = pl.BlockSpec(memory_space=pltpu.VMEM)
SM = pl.BlockSpec(memory_space=pltpu.SMEM)


def shift_heads(array, dy, dx):
    pairs = [(i, ((i // 4 + dy) % 4) * 4 + (i % 4 + dx) % 4) for i in range(16)]
    return lax.ppermute(array, "heads", pairs)


def swap_heads(array, my, mx):
    pairs = [(i, ((i // 4) ^ my) * 4 + ((i % 4) ^ mx)) for i in range(16)]
    return lax.ppermute(array, "heads", pairs)


def swap_ctx(array, mz, mc):
    pairs = [(i, ((i // 2) ^ mz) * 2 + ((i % 2) ^ mc)) for i in range(8)]
    return lax.ppermute(array, "ctx", pairs)


def places():
    heads, ctx = lax.axis_index("heads"), lax.axis_index("ctx")
    return lax.shift_right_logical(heads, 2), heads & 3, lax.shift_right_logical(ctx, 1), ctx & 1


def from_far(start):
    return pl.multiple_of(256 - (places()[1] & 2) * 128, 256) if start == FAR else start


def pack_kernel(plan, n_in, *refs):
    ins, outs = refs[:n_in], refs[n_in:]
    for out, pieces in zip(outs, plan):
        row = 0
        for operand, start, count in pieces:
            out[row : row + count, :] = ins[operand][pl.ds(from_far(start), count), :]
            row += count


def pack(plan, ins):
    return pl.pallas_call(
        functools.partial(pack_kernel, plan, len(ins)),
        out_shape=[jax.ShapeDtypeStruct((sum(p[2] for p in pieces), 512), BF) for pieces in plan],
        in_specs=[VM] * len(ins),
        out_specs=[VM] * len(plan),
        compiler_params=pltpu.CompilerParams(vmem_limit_bytes=VMEM_LIMIT),
        cost_estimate=pl.CostEstimate(flops=0, bytes_accessed=1 << 20, transcendentals=0),
    )(*ins)


def hold_kernel(wq, wk, wv, q_out, kv_out, sem):
    copies = []
    for part in range(8):
        rows = pl.ds(part * 1024, 1024)
        copies.append(pltpu.make_async_copy(wq.at[rows, :], q_out.at[rows, :], sem.at[part]))
    for part in range(4):
        cols = pl.ds(part * 2048, 2048)
        copies.append(pltpu.make_async_copy(wk.at[:, cols], kv_out.at[pl.ds(0, 64), cols], sem.at[8 + part]))
        copies.append(pltpu.make_async_copy(wv.at[:, cols], kv_out.at[pl.ds(64, 64), cols], sem.at[12 + part]))
    for copy in copies:
        copy.start()
    for copy in copies:
        copy.wait()


def hold(wq, wk, wv):
    return pl.pallas_call(
        hold_kernel,
        out_shape=[jax.ShapeDtypeStruct((8192, 512), BF), jax.ShapeDtypeStruct((128, 8192), BF)],
        in_specs=[HBM] * 3,
        out_specs=[VM, VM],
        scratch_shapes=[pltpu.SemaphoreType.DMA((16,))],
        compiler_params=pltpu.CompilerParams(vmem_limit_bytes=HOLD_LIMIT),
        cost_estimate=pl.CostEstimate(flops=0, bytes_accessed=20 << 20, transcendentals=0),
    )(wq, wk, wv)


def turn(part, cos, sin):
    return (part * cos + pltpu.roll(part, HD // 2, 1) * sin).astype(BF)


def project_kernel(plan, n_x, with_q, with_kv, has_acc, finish, *refs):
    refs = list(refs)
    take = lambda count: [refs.pop(0) for _ in range(count)]
    xs = take(n_x)
    wq = take(1)[0] if with_q else None
    wkv = take(1)[0] if with_kv else None
    acc_q = take(1)[0] if has_acc and with_q else None
    acc_kv = take(1)[0] if has_acc and with_kv else None
    cos, sin = take(2) if finish and with_q else (None, None)
    asked = take(1)[0] if finish and with_kv else None
    q_out = take(1)[0] if with_q else None
    kv_out = take(1)[0] if with_kv else None
    q_sum = take(1)[0] if finish and with_q else q_out
    kv_sum = take(1)[0] if finish and with_kv else kv_out
    y, x, _, _ = places()
    if has_acc:
        if with_q:
            q_sum[...] = acc_q[...]
        if with_kv:
            kv_sum[...] = acc_kv[...]
    for slot, ((dy, dx), low, high, uses) in enumerate(plan):
        base = pl.multiple_of((((y + dy) & 3) * 4 + ((x + dx) & 3)) * 512, 512)
        parts = [xs[operand][pl.ds(from_far(start), count), :] for operand, start, count in uses]
        piece = parts[0] if len(parts) == 1 else jnp.concatenate(parts, axis=0)
        fresh = slot == 0 and not has_acc
        if with_kv:
            both = wkv[:, pl.ds(base, 512)]
            term = lax.dot_general(piece, both, (((1,), (1,)), ((), ())), preferred_element_type=F32)
            kv_sum[low:high, :] = term if fresh else kv_sum[low:high, :] + term
        if with_q:
            term = jnp.dot(piece, wq[pl.ds(base, 512), :], preferred_element_type=F32)
            q_sum[low:high, :] = term if fresh else q_sum[low:high, :] + term
    if finish and with_kv:
        kv_out[:ROWS, :] = kv_sum[...].astype(BF)
        kv_out[ROWS:, :] = asked[:, 512:640]
    if finish and with_q:
        for head in range(4):
            cols = slice(head * HD, (head + 1) * HD)
            q_out[:, cols] = turn(q_sum[:, cols], cos[:ROWS, :], sin[:ROWS, :])


def project(xs, plan, weights, accs, with_q, with_kv, finish=False, tables=None, asked=None):
    wq, wkv = weights
    operands, specs = list(xs), [VM] * len(xs)
    if with_q:
        operands.append(wq)
        specs.append(VM)
    if with_kv:
        operands.append(wkv)
        specs.append(VM)
    has_acc = accs is not None
    if has_acc:
        if with_q:
            operands.append(accs[0])
            specs.append(VM)
        if with_kv:
            operands.append(accs[1])
            specs.append(VM)
    if finish and with_q:
        operands += list(tables)
        specs += [VM, VM]
    if finish and with_kv:
        operands.append(asked)
        specs.append(VM)
    outs, scratch = [], []
    if with_q:
        outs.append(jax.ShapeDtypeStruct((ROWS, 512), BF if finish else F32))
        if finish:
            scratch.append(pltpu.VMEM((ROWS, 512), F32))
    if with_kv:
        outs.append(jax.ShapeDtypeStruct((ALL, 128), BF) if finish else jax.ShapeDtypeStruct((ROWS, 128), F32))
        if finish:
            scratch.append(pltpu.VMEM((ROWS, 128), F32))
    columns = (512 if with_q else 0) + (128 if with_kv else 0)
    used = sum(high - low for _, low, high, _ in plan)
    return pl.pallas_call(
        functools.partial(project_kernel, plan, len(xs), with_q, with_kv, has_acc, finish),
        out_shape=outs,
        in_specs=specs,
        out_specs=[VM] * len(outs),
        scratch_shapes=scratch,
        compiler_params=pltpu.CompilerParams(vmem_limit_bytes=VMEM_LIMIT),
        cost_estimate=pl.CostEstimate(
            flops=2 * used * 512 * columns, bytes_accessed=len(plan) * 512 * columns * 2, transcendentals=0
        ),
    )(*operands)


def question_project_kernel(pieces, wq, wkv, cos, sin, out):
    q_sum, kv_sum = None, None
    for place in range(16):
        base = place * 512
        piece = pieces[place]
        both = wkv[:, pl.ds(base, 512)]
        kv_term = lax.dot_general(piece, both, (((1,), (1,)), ((), ())), preferred_element_type=F32)
        q_term = jnp.dot(piece, wq[pl.ds(base, 512), :], preferred_element_type=F32)
        q_sum = q_term if q_sum is None else q_sum + q_term
        kv_sum = kv_term if kv_sum is None else kv_sum + kv_term
    for head in range(4):
        cols = slice(head * HD, (head + 1) * HD)
        out[:, cols] = turn(q_sum[:, cols], cos[ROWS : ROWS + 32, :], sin[ROWS : ROWS + 32, :])
    out[:, 512:640] = kv_sum.astype(BF)


def question_project(pieces, weights, tables):
    return pl.pallas_call(
        question_project_kernel,
        out_shape=jax.ShapeDtypeStruct((32, 640), BF),
        in_specs=[VM] * 5,
        out_specs=VM,
        compiler_params=pltpu.CompilerParams(vmem_limit_bytes=VMEM_LIMIT),
        cost_estimate=pl.CostEstimate(flops=2 * 256 * 8192 * 640, bytes_accessed=8192 * 640 * 2, transcendentals=0),
    )(pieces, *weights, *tables)


def key_value_kernel(own, partner, cos, sin, out):
    is_lower = (places()[1] & 1) == 0
    mine, other = own[...].astype(F32), partner[...].astype(F32)
    low = jnp.where(is_lower, mine, other)
    high = jnp.where(is_lower, other, mine)
    lane = lax.broadcasted_iota(jnp.int32, low.shape, 1)
    keys = jnp.where(lane < 64, low, pltpu.roll(high, 64, 1))
    values = jnp.where(lane < 64, pltpu.roll(low, 64, 1), high)
    out[:, :HD] = (keys * cos[...] + pltpu.roll(keys, 64, 1) * sin[...]).astype(BF)
    out[:, HD:] = values.astype(BF)


def key_value(own, partner, cos, sin):
    return pl.pallas_call(
        key_value_kernel,
        out_shape=jax.ShapeDtypeStruct((ALL, 2 * HD), BF),
        in_specs=[VM, VM, VM, VM],
        out_specs=VM,
        compiler_params=pltpu.CompilerParams(vmem_limit_bytes=VMEM_LIMIT),
    )(own, partner, cos, sin)


def scores_of(queries, keys):
    return lax.dot_general(queries, keys, (((1,), (1,)), ((), ())), preferred_element_type=F32)


def weights_of(scores, top):
    return jnp.exp2(scores * SCALE2 - top * SCALE2)


def columns_to_stats(columns):
    rows = columns[0].shape[0]
    lane = lax.broadcasted_iota(jnp.int32, (rows, 128), 1)
    stats = jnp.zeros((rows, 128), F32)
    for index, column in enumerate(columns):
        stats = jnp.where(lane == index, column, stats)
    return stats


def own_kernel(lengths, q, kv, weighted, stats):
    _, _, z, core = places()
    length = lengths[2 * z + core]
    for tile in range(2):
        rows = slice(tile * 256, tile * 256 + 256)
        width = 256 * (tile + 1)
        row = tile * 256 + lax.broadcasted_iota(jnp.int32, (256, width), 0)
        key = lax.broadcasted_iota(jnp.int32, (256, width), 1)
        bias = jnp.where((key <= row) & (key < length), 0.0, NEG)
        tops, totals = [], []
        for head in range(4):
            cols = slice(head * HD, (head + 1) * HD)
            s = scores_of(q[rows, cols], kv[:width, :HD]) + bias
            top = jnp.max(s, axis=1, keepdims=True)
            e = weights_of(s, top)
            totals.append(jnp.sum(e, axis=1, keepdims=True))
            tops.append(top)
            weighted[rows, cols] = jnp.dot(e.astype(BF), kv[:width, HD:], preferred_element_type=F32)
        stats[rows, :] = columns_to_stats(tops + totals)


def own_attention(lengths, q, kv):
    return pl.pallas_call(
        own_kernel,
        out_shape=[jax.ShapeDtypeStruct((512, 512), F32), jax.ShapeDtypeStruct((512, 128), F32)],
        in_specs=[SM, VM, VM],
        out_specs=[VM, VM],
        compiler_params=pltpu.CompilerParams(vmem_limit_bytes=VMEM_LIMIT),
        cost_estimate=pl.CostEstimate(flops=4 * 4 * 512 * 512 * 128, bytes_accessed=3 << 20, transcendentals=1 << 20),
    )(lengths, q, kv)


def anchor_kernel(lengths, q, kv_zero, kv_one, weighted, stats, out):
    _, _, z, core = places()
    length = lengths[2 * z + core]
    anchor_length = jnp.where(2 * z + core > 0, lengths[0], 0)
    first_core = core == 0
    kv = jnp.where(first_core, kv_zero[...], kv_one[...])
    keys, values = kv[:, :HD], kv[:, HD:]
    key = lax.broadcasted_iota(jnp.int32, (1, 512), 1)
    bias = jnp.where(key < anchor_length, 0.0, NEG)
    for tile in range(2):
        rows = slice(tile * 256, tile * 256 + 256)
        block = stats[rows, :]
        row = tile * 256 + lax.broadcasted_iota(jnp.int32, (256, HD), 0)
        for head in range(4):
            cols = slice(head * HD, (head + 1) * HD)
            s = scores_of(q[rows, cols], keys) + bias
            own_top, own_sum = block[:, head : head + 1], block[:, head + 4 : head + 5]
            top = jnp.maximum(own_top, jnp.max(s, axis=1, keepdims=True))
            e = weights_of(s, top)
            factor = weights_of(own_top, top)
            total = own_sum * factor + jnp.sum(e, axis=1, keepdims=True)
            both = weighted[rows, cols] * factor + jnp.dot(e.astype(BF), values, preferred_element_type=F32)
            out[rows, cols] = jnp.where(row < length, both / total, 0.0).astype(BF)


def anchor_attention(lengths, q, kv_zero, kv_one, weighted, stats):
    return pl.pallas_call(
        anchor_kernel,
        out_shape=jax.ShapeDtypeStruct((512, 512), BF),
        in_specs=[SM, VM, VM, VM, VM, VM],
        out_specs=VM,
        compiler_params=pltpu.CompilerParams(vmem_limit_bytes=VMEM_LIMIT),
        cost_estimate=pl.CostEstimate(flops=4 * 4 * 512 * 512 * 128, bytes_accessed=3 << 20, transcendentals=1 << 20),
    )(lengths, q, kv_zero, kv_one, weighted, stats)


def question_kernel(lengths_ref, q_own, q_other, kv_0, kv_1, kv_2, kv_3, out_own, out_other):
    kvs = (kv_0, kv_1, kv_2, kv_3)
    _, _, z, core = places()
    ctx = 2 * z + core
    blocks = [z, (z + 3) & 3, (z + 1) & 3, (z + 2) & 3]
    lengths = [lengths_ref[2 * block + core] for block in blocks]
    stacked = [q_own[:, h * HD : (h + 1) * HD] for h in range(4)]
    stacked += [q_other[:, h * HD : (h + 1) * HD] for h in range(4)]
    q = jnp.concatenate(stacked, axis=0)
    scores = []
    key = lax.broadcasted_iota(jnp.int32, (1, 512), 1)
    for kv, length in zip(kvs, lengths):
        scores.append(scores_of(q, kv[:ROWS, :HD]) + jnp.where(key < length, 0.0, NEG))
    row = lax.broadcasted_iota(jnp.int32, (256, 128), 0)
    lane = lax.broadcasted_iota(jnp.int32, (256, 128), 1)
    row_id = row % 32 + 32 * jnp.where(row < 128, ctx, ctx + 1 - 2 * core)
    block = jnp.where(lane < 64, jnp.where(lane < 32, blocks[0], blocks[1]), jnp.where(lane < 96, blocks[2], blocks[3]))
    key_id = lane % 32 + 32 * (2 * block + core)
    asked_keys = jnp.concatenate([kv[ROWS:, :HD] for kv in kvs], axis=0)
    asked_values = jnp.concatenate([kv[ROWS:, HD:] for kv in kvs], axis=0)
    scores.append(jnp.where(key_id <= row_id, scores_of(q, asked_keys), NEG))
    top = jnp.max(scores[-1], axis=1, keepdims=True)
    for s in scores[:-1]:
        top = jnp.maximum(top, jnp.max(s, axis=1, keepdims=True))
    values = [kv[:ROWS, HD:] for kv in kvs] + [asked_values]
    total = jnp.zeros((256, 1), F32)
    both = jnp.zeros((256, HD), F32)
    for s, value in zip(scores, values):
        e = weights_of(s, top)
        total = total + jnp.sum(e, axis=1, keepdims=True)
        both = both + jnp.dot(e.astype(BF), value, preferred_element_type=F32)
    for out, start in ((out_own, 0), (out_other, 128)):
        tops, totals = [], []
        for head in range(4):
            rows = slice(start + head * 32, start + head * 32 + 32)
            out[:, head * HD : (head + 1) * HD] = both[rows]
            tops.append(top[rows])
            totals.append(total[rows])
        out[:, 512:640] = columns_to_stats(tops + totals)


def question_attention(lengths, q_own, q_other, kvs):
    part = jax.ShapeDtypeStruct((32, 640), F32)
    return pl.pallas_call(
        question_kernel,
        out_shape=[part, part],
        in_specs=[SM] + [VM] * 6,
        out_specs=[VM, VM],
        compiler_params=pltpu.CompilerParams(vmem_limit_bytes=VMEM_LIMIT),
        cost_estimate=pl.CostEstimate(flops=4 * 256 * 2176 * 128, bytes_accessed=2 << 20, transcendentals=1 << 19),
    )(lengths, q_own, q_other, *kvs)


def merge_kernel(a, b, out):
    stat_a, stat_b = a[:, 512:640], b[:, 512:640]
    for head in range(4):
        cols = slice(head * HD, (head + 1) * HD)
        top_a, top_b = stat_a[:, head : head + 1], stat_b[:, head : head + 1]
        top = jnp.maximum(top_a, top_b)
        factor_a, factor_b = weights_of(top_a, top), weights_of(top_b, top)
        total = stat_a[:, head + 4 : head + 5] * factor_a + stat_b[:, head + 4 : head + 5] * factor_b
        out[:, cols] = ((a[:, cols] * factor_a + b[:, cols] * factor_b) / total).astype(BF)


def merge(a, b):
    return pl.pallas_call(
        merge_kernel,
        out_shape=jax.ShapeDtypeStruct((32, 512), BF),
        in_specs=[VM, VM],
        out_specs=VM,
        compiler_params=pltpu.CompilerParams(vmem_limit_bytes=VMEM_LIMIT),
    )(a, b)


PLAN_1 = [
    ((0, 0), 0, 512, [(0, 0, 512)]),
    ((-1, 0), 0, 512, [(1, 0, 512)]),
    ((1, 0), 0, 512, [(2, 0, 512)]),
    ((0, -1), 0, 512, [(3, 0, 512)]),
    ((0, 1), 0, 512, [(4, 0, 512)]),
    ((2, 0), 0, 256, [(5, 0, 256)]),
    ((0, 2), 256, 512, [(6, FAR, 256)]),
]
PLAN_2 = [
    ((-1, -1), 0, 512, [(0, 0, 256), (2, 0, 256)]),
    ((1, -1), 0, 512, [(0, 256, 256), (3, 0, 256)]),
    ((-1, 1), 0, 512, [(1, 0, 256), (2, 256, 256)]),
    ((1, 1), 0, 512, [(1, 256, 256), (3, 256, 256)]),
    ((2, -1), 0, 256, [(0, 512, 256)]),
    ((2, 1), 0, 256, [(1, 512, 256)]),
    ((-1, 2), 256, 512, [(2, 512, 256)]),
    ((1, 2), 256, 512, [(3, 512, 256)]),
    ((0, 2), 0, 256, [(0, 768, 128), (1, 768, 128)]),
    ((2, 0), 256, 512, [(2, 768, 128), (3, 768, 128)]),
]
PLAN_3 = [
    ((2, 2), 0, 512, [(1, 128, 256), (3, 128, 256)]),
    ((-1, 2), 0, 256, [(0, 0, 256)]),
    ((1, 2), 0, 256, [(0, 256, 128), (1, 0, 128)]),
    ((2, -1), 256, 512, [(2, 0, 256)]),
    ((2, 1), 256, 512, [(2, 256, 128), (3, 0, 128)]),
]
NEAR_Y = [(0, 0, 256), (1, 0, 256), (4, 0, 256)]
NEAR_X = [(2, 256, 256), (3, 256, 256), (4, FAR, 256)]
PACK_2 = [NEAR_Y + [(2, 0, 128)], NEAR_Y + [(3, 128, 128)], NEAR_X + [(0, 256, 128)], NEAR_X + [(1, 384, 128)]]
PACK_3 = [[(0, 0, 384)], [(1, 384, 384)]]


def tables_of(positions):
    inverse_freq = ROPE_BASE ** (-(jnp.arange(HD // 2, dtype=jnp.float32) * 2.0 / HD))
    inverse_freq = jnp.concatenate([inverse_freq, inverse_freq])
    phases = positions.astype(jnp.float32)[:, None] * inverse_freq[None, :]
    signs = jnp.where(jnp.arange(HD) < HD // 2, -1.0, 1.0).astype(jnp.float32)
    return jnp.cos(phases), jnp.sin(phases) * signs[None, :]


def shift_z(array, dz):
    pairs = [(i, ((i // 2 + dz) % 4) * 2 + i % 2) for i in range(8)]
    return lax.ppermute(array, "ctx", pairs)


def per_device(context, question, w_query, w_key, w_value, lengths, owner):
    ctx = lax.axis_index("ctx")
    z, core = lax.shift_right_logical(ctx, 1), ctx & 1
    ids = jnp.arange(8, dtype=jnp.int32)
    own_offset = jnp.sum(jnp.where(ids < ctx, lengths, 0))
    filled = jnp.sum(lengths)

    up = shift_heads(context, 1, 0)
    down = shift_heads(context, -1, 0)
    right = shift_heads(context, 0, 1)
    left = shift_heads(context, 0, -1)
    low, high = pack([[(0, 0, 256)], [(0, 256, 256), (0, 256, 256)]], [context])
    far_y = shift_heads(low, 2, 0)
    pairs = [[4 * row + column, 4 * row + column + 2] for row in range(4) for column in range(2)]
    far_x = lax.all_to_all(high.reshape(2, 256, 512), "heads", 0, 0, axis_index_groups=pairs).reshape(512, 512)

    share = lax.all_to_all(question[0].reshape(8, 32, 512), "ctx", 0, 0)
    share = lax.dynamic_index_in_dim(share, owner[0], 0, False)
    share = jnp.broadcast_to(share[None], (16, 32, 512))
    pieces = lax.all_to_all(share, "heads", 0, 0)
    up, pieces = lax.optimization_barrier((up, pieces))

    to_right, to_left = pack(PACK_2[:2], [up, down, right, left, far_y])
    to_up, to_down = pack(PACK_2[2:], [up, down, right, left, far_x])
    a_right, a_left = shift_heads(to_right, 0, 1), shift_heads(to_left, 0, -1)
    b_up, b_down = shift_heads(to_up, 1, 0), shift_heads(to_down, -1, 0)
    up, to_right = lax.optimization_barrier((up, to_right))
    tables = tables_of(
        jnp.concatenate(
            [own_offset + jnp.arange(ROWS, dtype=jnp.int32), filled + 32 * ctx + jnp.arange(ASKED, dtype=jnp.int32)]
        )
    )
    pieces, w_query, w_key, w_value, tables = lax.optimization_barrier(
        (pieces, w_query, w_key, w_value, tables)
    )
    weights = hold(w_query, w_key.T, w_value.T)
    accs = project([context, up, down, right, left, far_y, far_x], PLAN_1, weights, None, True, True)
    q_share = question_project(pieces, weights, tables)

    a_right, a_left, accs, q_share = lax.optimization_barrier((a_right, a_left, accs, q_share))
    to_right, to_left = pack(PACK_3, [a_right, a_left])
    to_up, to_down = pack(PACK_3, [b_up, b_down])
    last = [
        shift_heads(to_right, 0, 1),
        shift_heads(to_left, 0, -1),
        shift_heads(to_up, 1, 0),
        shift_heads(to_down, -1, 0),
    ]
    accs = project([a_right, a_left, b_up, b_down], PLAN_2, weights, accs, True, True)

    (halves,) = project(last, PLAN_3, weights, accs, False, True, True, asked=q_share)
    (queries,) = project(last, PLAN_3, weights, accs, True, False, True, tables)
    partner = swap_heads(halves, 0, 1)
    q_asked = q_share[:, :512]
    q_other = swap_ctx(q_asked, 0, 1)
    partner, queries, q_other = lax.optimization_barrier((partner, queries, q_other))
    kv = key_value(halves, partner, *tables)

    below, above, across = shift_z(kv, 1), shift_z(kv, -1), shift_z(kv, 2)
    weighted, stats = own_attention(lengths, queries, kv)
    below, above, across, weighted = lax.optimization_barrier((below, above, across, weighted))
    nearer = jnp.where(z == 0, kv[:ROWS], jnp.where(z == 1, below[:ROWS], jnp.where(z == 2, across[:ROWS], above[:ROWS])))
    from_zero = lax.ppermute(nearer, "ctx", [(0, 1), (2, 3), (4, 5), (6, 7)])
    part, part_other = question_attention(lengths, q_asked, q_other, [kv, below, above, across])
    from_zero, part = lax.optimization_barrier((from_zero, part))
    context_attn = anchor_attention(lengths, queries, nearer, from_zero, weighted, stats)
    question_attn = merge(part, swap_ctx(part_other, 0, 1))
    return (context_attn, question_attn)


def solution(mesh):
    in_specs = (
        P("ctx", "heads"),
        P("ctx", None, "heads"),
        P(None, "heads"),
        P(None, "heads"),
        P(None, "heads"),
        P(),
        P(),
    )
    out_specs = (P("ctx", "heads"), P("ctx", "heads"))
    return jax.shard_map(
        per_device, mesh=mesh, in_specs=in_specs, out_specs=out_specs, check_vma=False
    )
```

```python
import functools

import jax
import jax.numpy as jnp
from jax import lax
from jax.experimental import pallas as pl
from jax.experimental.pallas import tpu as pltpu
from jax.sharding import PartitionSpec as P

HD = 128
ROPE_BASE = 500000.0
BF = jnp.bfloat16
F32 = jnp.float32
VMEM_LIMIT = 8 * 1024 * 1024
HOLD_LIMIT = 37 * 1024 * 1024
NEG = -1e30
SCALE2 = HD ** (-0.5) * 1.4426950408889634
ROWS = 512
ASKED = 32
ALL = ROWS + ASKED

HBM = pl.BlockSpec(memory_space=pltpu.HBM)
VM = pl.BlockSpec(memory_space=pltpu.VMEM)
SM = pl.BlockSpec(memory_space=pltpu.SMEM)


def shift_heads(array, dy, dx):
    pairs = [(i, ((i // 4 + dy) % 4) * 4 + (i % 4 + dx) % 4) for i in range(16)]
    return lax.ppermute(array, "heads", pairs)


def swap_heads(array, my, mx):
    pairs = [(i, ((i // 4) ^ my) * 4 + ((i % 4) ^ mx)) for i in range(16)]
    return lax.ppermute(array, "heads", pairs)


def swap_ctx(array, mz, mc):
    pairs = [(i, ((i // 2) ^ mz) * 2 + ((i % 2) ^ mc)) for i in range(8)]
    return lax.ppermute(array, "ctx", pairs)


def places():
    heads, ctx = lax.axis_index("heads"), lax.axis_index("ctx")
    return lax.shift_right_logical(heads, 2), heads & 3, lax.shift_right_logical(ctx, 1), ctx & 1


def pack_kernel(plan, n_in, *refs):
    ins, outs = refs[:n_in], refs[n_in:]
    for out, pieces in zip(outs, plan):
        row = 0
        for operand, start, count in pieces:
            out[row : row + count, :] = ins[operand][start : start + count, :]
            row += count


def pack(plan, ins):
    return pl.pallas_call(
        functools.partial(pack_kernel, plan, len(ins)),
        out_shape=[jax.ShapeDtypeStruct((sum(p[2] for p in pieces), 512), BF) for pieces in plan],
        in_specs=[VM] * len(ins),
        out_specs=[VM] * len(plan),
        compiler_params=pltpu.CompilerParams(vmem_limit_bytes=VMEM_LIMIT),
        cost_estimate=pl.CostEstimate(flops=0, bytes_accessed=1 << 20, transcendentals=0),
    )(*ins)


def hold_kernel(wq, wk, wv, q_out, kv_out, sem):
    copies = []
    for part in range(8):
        rows = pl.ds(part * 1024, 1024)
        copies.append(pltpu.make_async_copy(wq.at[rows, :], q_out.at[rows, :], sem.at[part]))
    for part in range(4):
        cols = pl.ds(part * 2048, 2048)
        copies.append(pltpu.make_async_copy(wk.at[:, cols], kv_out.at[pl.ds(0, 64), cols], sem.at[8 + part]))
        copies.append(pltpu.make_async_copy(wv.at[:, cols], kv_out.at[pl.ds(64, 64), cols], sem.at[12 + part]))
    for copy in copies:
        copy.start()
    for copy in copies:
        copy.wait()


def hold(wq, wk, wv):
    return pl.pallas_call(
        hold_kernel,
        out_shape=[jax.ShapeDtypeStruct((8192, 512), BF), jax.ShapeDtypeStruct((128, 8192), BF)],
        in_specs=[HBM] * 3,
        out_specs=[VM, VM],
        scratch_shapes=[pltpu.SemaphoreType.DMA((16,))],
        compiler_params=pltpu.CompilerParams(vmem_limit_bytes=HOLD_LIMIT),
        cost_estimate=pl.CostEstimate(flops=0, bytes_accessed=20 << 20, transcendentals=0),
    )(wq, wk, wv)


def turn(part, cos, sin):
    return (part * cos + pltpu.roll(part, HD // 2, 1) * sin).astype(BF)


def project_kernel(plan, n_x, with_q, with_kv, has_acc, finish, *refs):
    refs = list(refs)
    take = lambda count: [refs.pop(0) for _ in range(count)]
    xs = take(n_x)
    wq = take(1)[0] if with_q else None
    wkv = take(1)[0] if with_kv else None
    acc_q = take(1)[0] if has_acc and with_q else None
    acc_kv = take(1)[0] if has_acc and with_kv else None
    cos, sin = take(2) if finish and with_q else (None, None)
    asked = take(1)[0] if finish and with_kv else None
    q_out = take(1)[0] if with_q else None
    kv_out = take(1)[0] if with_kv else None
    q_sum = take(1)[0] if finish and with_q else q_out
    kv_sum = take(1)[0] if finish and with_kv else kv_out
    y, x, _, _ = places()
    if has_acc:
        if with_q:
            q_sum[...] = acc_q[...]
        if with_kv:
            kv_sum[...] = acc_kv[...]
    for slot, ((dy, dx), low, high, uses) in enumerate(plan):
        base = pl.multiple_of((((y + dy) & 3) * 4 + ((x + dx) & 3)) * 512, 512)
        parts = [xs[operand][pl.ds(start, count), :] for operand, start, count in uses]
        piece = parts[0] if len(parts) == 1 else jnp.concatenate(parts, axis=0)
        fresh = slot == 0 and not has_acc
        if with_kv:
            both = wkv[:, pl.ds(base, 512)]
            term = lax.dot_general(piece, both, (((1,), (1,)), ((), ())), preferred_element_type=F32)
            kv_sum[low:high, :] = term if fresh else kv_sum[low:high, :] + term
        if with_q:
            term = jnp.dot(piece, wq[pl.ds(base, 512), :], preferred_element_type=F32)
            q_sum[low:high, :] = term if fresh else q_sum[low:high, :] + term
    if finish and with_kv:
        kv_out[:ROWS, :] = kv_sum[...].astype(BF)
        kv_out[ROWS:, :] = asked[:, 512:640]
    if finish and with_q:
        for head in range(4):
            cols = slice(head * HD, (head + 1) * HD)
            q_out[:, cols] = turn(q_sum[:, cols], cos[:ROWS, :], sin[:ROWS, :])


def project(xs, plan, weights, accs, with_q, with_kv, finish=False, tables=None, asked=None):
    wq, wkv = weights
    operands, specs = list(xs), [VM] * len(xs)
    if with_q:
        operands.append(wq)
        specs.append(VM)
    if with_kv:
        operands.append(wkv)
        specs.append(VM)
    has_acc = accs is not None
    if has_acc:
        if with_q:
            operands.append(accs[0])
            specs.append(VM)
        if with_kv:
            operands.append(accs[1])
            specs.append(VM)
    if finish and with_q:
        operands += list(tables)
        specs += [VM, VM]
    if finish and with_kv:
        operands.append(asked)
        specs.append(VM)
    outs, scratch = [], []
    if with_q:
        outs.append(jax.ShapeDtypeStruct((ROWS, 512), BF if finish else F32))
        if finish:
            scratch.append(pltpu.VMEM((ROWS, 512), F32))
    if with_kv:
        outs.append(jax.ShapeDtypeStruct((ALL, 128), BF) if finish else jax.ShapeDtypeStruct((ROWS, 128), F32))
        if finish:
            scratch.append(pltpu.VMEM((ROWS, 128), F32))
    columns = (512 if with_q else 0) + (128 if with_kv else 0)
    used = sum(high - low for _, low, high, _ in plan)
    return pl.pallas_call(
        functools.partial(project_kernel, plan, len(xs), with_q, with_kv, has_acc, finish),
        out_shape=outs,
        in_specs=specs,
        out_specs=[VM] * len(outs),
        scratch_shapes=scratch,
        compiler_params=pltpu.CompilerParams(vmem_limit_bytes=VMEM_LIMIT),
        cost_estimate=pl.CostEstimate(
            flops=2 * used * 512 * columns, bytes_accessed=len(plan) * 512 * columns * 2, transcendentals=0
        ),
    )(*operands)


def question_project_kernel(pieces, wq, wkv, cos, sin, out):
    q_sum, kv_sum = None, None
    for place in range(16):
        base = place * 512
        piece = pieces[place]
        both = wkv[:, pl.ds(base, 512)]
        kv_term = lax.dot_general(piece, both, (((1,), (1,)), ((), ())), preferred_element_type=F32)
        q_term = jnp.dot(piece, wq[pl.ds(base, 512), :], preferred_element_type=F32)
        q_sum = q_term if q_sum is None else q_sum + q_term
        kv_sum = kv_term if kv_sum is None else kv_sum + kv_term
    for head in range(4):
        cols = slice(head * HD, (head + 1) * HD)
        out[:, cols] = turn(q_sum[:, cols], cos[ROWS : ROWS + 32, :], sin[ROWS : ROWS + 32, :])
    out[:, 512:640] = kv_sum.astype(BF)


def question_project(pieces, weights, tables):
    return pl.pallas_call(
        question_project_kernel,
        out_shape=jax.ShapeDtypeStruct((32, 640), BF),
        in_specs=[VM] * 5,
        out_specs=VM,
        compiler_params=pltpu.CompilerParams(vmem_limit_bytes=VMEM_LIMIT),
        cost_estimate=pl.CostEstimate(flops=2 * 256 * 8192 * 640, bytes_accessed=8192 * 640 * 2, transcendentals=0),
    )(pieces, *weights, *tables)


def key_value_kernel(own, partner, cos, sin, out):
    is_lower = (places()[1] & 1) == 0
    mine, other = own[...].astype(F32), partner[...].astype(F32)
    low = jnp.where(is_lower, mine, other)
    high = jnp.where(is_lower, other, mine)
    lane = lax.broadcasted_iota(jnp.int32, low.shape, 1)
    keys = jnp.where(lane < 64, low, pltpu.roll(high, 64, 1))
    values = jnp.where(lane < 64, pltpu.roll(low, 64, 1), high)
    out[:, :HD] = (keys * cos[...] + pltpu.roll(keys, 64, 1) * sin[...]).astype(BF)
    out[:, HD:] = values.astype(BF)


def key_value(own, partner, cos, sin):
    return pl.pallas_call(
        key_value_kernel,
        out_shape=jax.ShapeDtypeStruct((ALL, 2 * HD), BF),
        in_specs=[VM, VM, VM, VM],
        out_specs=VM,
        compiler_params=pltpu.CompilerParams(vmem_limit_bytes=VMEM_LIMIT),
    )(own, partner, cos, sin)


def scores_of(queries, keys):
    return lax.dot_general(queries, keys, (((1,), (1,)), ((), ())), preferred_element_type=F32)


def weights_of(scores, top):
    return jnp.exp2(scores * SCALE2 - top * SCALE2)


def columns_to_stats(columns):
    rows = columns[0].shape[0]
    lane = lax.broadcasted_iota(jnp.int32, (rows, 128), 1)
    stats = jnp.zeros((rows, 128), F32)
    for index, column in enumerate(columns):
        stats = jnp.where(lane == index, column, stats)
    return stats


def own_kernel(lengths, q, kv, weighted, stats):
    _, _, z, core = places()
    length = lengths[2 * z + core]
    for tile in range(2):
        rows = slice(tile * 256, tile * 256 + 256)
        width = 256 * (tile + 1)
        row = tile * 256 + lax.broadcasted_iota(jnp.int32, (256, width), 0)
        key = lax.broadcasted_iota(jnp.int32, (256, width), 1)
        bias = jnp.where((key <= row) & (key < length), 0.0, NEG)
        tops, totals = [], []
        for head in range(4):
            cols = slice(head * HD, (head + 1) * HD)
            s = scores_of(q[rows, cols], kv[:width, :HD]) + bias
            top = jnp.max(s, axis=1, keepdims=True)
            e = weights_of(s, top)
            totals.append(jnp.sum(e, axis=1, keepdims=True))
            tops.append(top)
            weighted[rows, cols] = jnp.dot(e.astype(BF), kv[:width, HD:], preferred_element_type=F32)
        stats[rows, :] = columns_to_stats(tops + totals)


def own_attention(lengths, q, kv):
    return pl.pallas_call(
        own_kernel,
        out_shape=[jax.ShapeDtypeStruct((512, 512), F32), jax.ShapeDtypeStruct((512, 128), F32)],
        in_specs=[SM, VM, VM],
        out_specs=[VM, VM],
        compiler_params=pltpu.CompilerParams(vmem_limit_bytes=VMEM_LIMIT),
        cost_estimate=pl.CostEstimate(flops=4 * 4 * 512 * 512 * 128, bytes_accessed=3 << 20, transcendentals=1 << 20),
    )(lengths, q, kv)


def anchor_kernel(lengths, q, kv_zero, kv_one, weighted, stats, out):
    _, _, z, core = places()
    length = lengths[2 * z + core]
    anchor_length = jnp.where(2 * z + core > 0, lengths[0], 0)
    first_core = core == 0
    kv = jnp.where(first_core, kv_zero[...], kv_one[...])
    keys, values = kv[:, :HD], kv[:, HD:]
    key = lax.broadcasted_iota(jnp.int32, (1, 512), 1)
    bias = jnp.where(key < anchor_length, 0.0, NEG)
    for tile in range(2):
        rows = slice(tile * 256, tile * 256 + 256)
        block = stats[rows, :]
        row = tile * 256 + lax.broadcasted_iota(jnp.int32, (256, HD), 0)
        for head in range(4):
            cols = slice(head * HD, (head + 1) * HD)
            s = scores_of(q[rows, cols], keys) + bias
            own_top, own_sum = block[:, head : head + 1], block[:, head + 4 : head + 5]
            top = jnp.maximum(own_top, jnp.max(s, axis=1, keepdims=True))
            e = weights_of(s, top)
            factor = weights_of(own_top, top)
            total = own_sum * factor + jnp.sum(e, axis=1, keepdims=True)
            both = weighted[rows, cols] * factor + jnp.dot(e.astype(BF), values, preferred_element_type=F32)
            out[rows, cols] = jnp.where(row < length, both / total, 0.0).astype(BF)


def anchor_attention(lengths, q, kv_zero, kv_one, weighted, stats):
    return pl.pallas_call(
        anchor_kernel,
        out_shape=jax.ShapeDtypeStruct((512, 512), BF),
        in_specs=[SM, VM, VM, VM, VM, VM],
        out_specs=VM,
        compiler_params=pltpu.CompilerParams(vmem_limit_bytes=VMEM_LIMIT),
        cost_estimate=pl.CostEstimate(flops=4 * 4 * 512 * 512 * 128, bytes_accessed=3 << 20, transcendentals=1 << 20),
    )(lengths, q, kv_zero, kv_one, weighted, stats)


def question_kernel(lengths_ref, q_own, q_other, kv_0, kv_1, kv_2, kv_3, out_own, out_other):
    kvs = (kv_0, kv_1, kv_2, kv_3)
    _, _, z, core = places()
    ctx = 2 * z + core
    blocks = [z, (z + 3) & 3, (z + 1) & 3, (z + 2) & 3]
    lengths = [lengths_ref[2 * block + core] for block in blocks]
    stacked = [q_own[:, h * HD : (h + 1) * HD] for h in range(4)]
    stacked += [q_other[:, h * HD : (h + 1) * HD] for h in range(4)]
    q = jnp.concatenate(stacked, axis=0)
    scores = []
    key = lax.broadcasted_iota(jnp.int32, (1, 512), 1)
    for kv, length in zip(kvs, lengths):
        scores.append(scores_of(q, kv[:ROWS, :HD]) + jnp.where(key < length, 0.0, NEG))
    row = lax.broadcasted_iota(jnp.int32, (256, 128), 0)
    lane = lax.broadcasted_iota(jnp.int32, (256, 128), 1)
    row_id = row % 32 + 32 * jnp.where(row < 128, ctx, ctx + 1 - 2 * core)
    block = jnp.where(lane < 64, jnp.where(lane < 32, blocks[0], blocks[1]), jnp.where(lane < 96, blocks[2], blocks[3]))
    key_id = lane % 32 + 32 * (2 * block + core)
    asked_keys = jnp.concatenate([kv[ROWS:, :HD] for kv in kvs], axis=0)
    asked_values = jnp.concatenate([kv[ROWS:, HD:] for kv in kvs], axis=0)
    scores.append(jnp.where(key_id <= row_id, scores_of(q, asked_keys), NEG))
    top = jnp.max(scores[-1], axis=1, keepdims=True)
    for s in scores[:-1]:
        top = jnp.maximum(top, jnp.max(s, axis=1, keepdims=True))
    values = [kv[:ROWS, HD:] for kv in kvs] + [asked_values]
    total = jnp.zeros((256, 1), F32)
    both = jnp.zeros((256, HD), F32)
    for s, value in zip(scores, values):
        e = weights_of(s, top)
        total = total + jnp.sum(e, axis=1, keepdims=True)
        both = both + jnp.dot(e.astype(BF), value, preferred_element_type=F32)
    for out, start in ((out_own, 0), (out_other, 128)):
        tops, totals = [], []
        for head in range(4):
            rows = slice(start + head * 32, start + head * 32 + 32)
            out[:, head * HD : (head + 1) * HD] = both[rows]
            tops.append(top[rows])
            totals.append(total[rows])
        out[:, 512:640] = columns_to_stats(tops + totals)


def question_attention(lengths, q_own, q_other, kvs):
    part = jax.ShapeDtypeStruct((32, 640), F32)
    return pl.pallas_call(
        question_kernel,
        out_shape=[part, part],
        in_specs=[SM] + [VM] * 6,
        out_specs=[VM, VM],
        compiler_params=pltpu.CompilerParams(vmem_limit_bytes=VMEM_LIMIT),
        cost_estimate=pl.CostEstimate(flops=4 * 256 * 2176 * 128, bytes_accessed=2 << 20, transcendentals=1 << 19),
    )(lengths, q_own, q_other, *kvs)


def merge_kernel(a, b, out):
    stat_a, stat_b = a[:, 512:640], b[:, 512:640]
    for head in range(4):
        cols = slice(head * HD, (head + 1) * HD)
        top_a, top_b = stat_a[:, head : head + 1], stat_b[:, head : head + 1]
        top = jnp.maximum(top_a, top_b)
        factor_a, factor_b = weights_of(top_a, top), weights_of(top_b, top)
        total = stat_a[:, head + 4 : head + 5] * factor_a + stat_b[:, head + 4 : head + 5] * factor_b
        out[:, cols] = ((a[:, cols] * factor_a + b[:, cols] * factor_b) / total).astype(BF)


def merge(a, b):
    return pl.pallas_call(
        merge_kernel,
        out_shape=jax.ShapeDtypeStruct((32, 512), BF),
        in_specs=[VM, VM],
        out_specs=VM,
        compiler_params=pltpu.CompilerParams(vmem_limit_bytes=VMEM_LIMIT),
    )(a, b)


PLAN_1 = [
    ((0, 0), 0, 512, [(0, 0, 512)]),
    ((-1, 0), 0, 512, [(1, 0, 512)]),
    ((1, 0), 0, 512, [(2, 0, 512)]),
    ((0, -1), 0, 512, [(3, 0, 512)]),
    ((0, 1), 0, 512, [(4, 0, 512)]),
    ((2, 0), 0, 256, [(5, 0, 256)]),
    ((0, 2), 256, 512, [(6, 0, 256)]),
]
PLAN_2 = [
    ((-1, -1), 0, 512, [(0, 0, 256), (2, 0, 256)]),
    ((1, -1), 0, 512, [(0, 256, 256), (3, 0, 256)]),
    ((-1, 1), 0, 512, [(1, 0, 256), (2, 256, 256)]),
    ((1, 1), 0, 512, [(1, 256, 256), (3, 256, 256)]),
    ((2, -1), 0, 256, [(0, 512, 256)]),
    ((2, 1), 0, 256, [(1, 512, 256)]),
    ((-1, 2), 256, 512, [(2, 512, 256)]),
    ((1, 2), 256, 512, [(3, 512, 256)]),
    ((0, 2), 0, 256, [(0, 768, 128), (1, 768, 128)]),
    ((2, 0), 256, 512, [(2, 768, 128), (3, 768, 128)]),
]
PLAN_3 = [
    ((2, 2), 0, 512, [(1, 128, 256), (3, 128, 256)]),
    ((-1, 2), 0, 256, [(0, 0, 256)]),
    ((1, 2), 0, 256, [(0, 256, 128), (1, 0, 128)]),
    ((2, -1), 256, 512, [(2, 0, 256)]),
    ((2, 1), 256, 512, [(2, 256, 128), (3, 0, 128)]),
]
NEAR_Y = [(0, 0, 256), (1, 0, 256), (4, 0, 256)]
NEAR_X = [(2, 256, 256), (3, 256, 256), (4, 0, 256)]
PACK_2 = [NEAR_Y + [(2, 0, 128)], NEAR_Y + [(3, 128, 128)], NEAR_X + [(0, 256, 128)], NEAR_X + [(1, 384, 128)]]
PACK_3 = [[(0, 0, 384)], [(1, 384, 384)]]


def tables_of(positions):
    inverse_freq = ROPE_BASE ** (-(jnp.arange(HD // 2, dtype=jnp.float32) * 2.0 / HD))
    inverse_freq = jnp.concatenate([inverse_freq, inverse_freq])
    phases = positions.astype(jnp.float32)[:, None] * inverse_freq[None, :]
    signs = jnp.where(jnp.arange(HD) < HD // 2, -1.0, 1.0).astype(jnp.float32)
    return jnp.cos(phases), jnp.sin(phases) * signs[None, :]


def shift_z(array, dz):
    pairs = [(i, ((i // 2 + dz) % 4) * 2 + i % 2) for i in range(8)]
    return lax.ppermute(array, "ctx", pairs)


def per_device(context, question, w_query, w_key, w_value, lengths, owner):
    ctx = lax.axis_index("ctx")
    z, core = lax.shift_right_logical(ctx, 1), ctx & 1
    ids = jnp.arange(8, dtype=jnp.int32)
    own_offset = jnp.sum(jnp.where(ids < ctx, lengths, 0))
    filled = jnp.sum(lengths)

    up = shift_heads(context, 1, 0)
    down = shift_heads(context, -1, 0)
    right = shift_heads(context, 0, 1)
    left = shift_heads(context, 0, -1)
    low, high = pack([[(0, 0, 256)], [(0, 256, 256)]], [context])
    far_y = shift_heads(low, 2, 0)
    low, asked = lax.optimization_barrier((low, question))
    up, high = lax.optimization_barrier((up, high))
    far_x = shift_heads(high, 0, 2)

    share = lax.all_to_all(asked[0].reshape(8, 32, 512), "ctx", 0, 0)
    share = lax.dynamic_index_in_dim(share, owner[0], 0, False)
    share = jnp.broadcast_to(share[None], (16, 32, 512))
    pieces = lax.all_to_all(share, "heads", 0, 0)
    up, pieces = lax.optimization_barrier((up, pieces))

    to_right, to_left = pack(PACK_2[:2], [up, down, right, left, far_y])
    to_up, to_down = pack(PACK_2[2:], [up, down, right, left, far_x])
    a_right, a_left = shift_heads(to_right, 0, 1), shift_heads(to_left, 0, -1)
    b_up, b_down = shift_heads(to_up, 1, 0), shift_heads(to_down, -1, 0)
    up, to_right = lax.optimization_barrier((up, to_right))
    tables = tables_of(
        jnp.concatenate(
            [own_offset + jnp.arange(ROWS, dtype=jnp.int32), filled + 32 * ctx + jnp.arange(ASKED, dtype=jnp.int32)]
        )
    )
    pieces, w_query, w_key, w_value, tables = lax.optimization_barrier(
        (pieces, w_query, w_key, w_value, tables)
    )
    weights = hold(w_query, w_key.T, w_value.T)
    accs = project([context, up, down, right, left, far_y, far_x], PLAN_1, weights, None, True, True)
    q_share = question_project(pieces, weights, tables)

    a_right, a_left, accs, q_share = lax.optimization_barrier((a_right, a_left, accs, q_share))
    to_right, to_left = pack(PACK_3, [a_right, a_left])
    to_up, to_down = pack(PACK_3, [b_up, b_down])
    last = [
        shift_heads(to_right, 0, 1),
        shift_heads(to_left, 0, -1),
        shift_heads(to_up, 1, 0),
        shift_heads(to_down, -1, 0),
    ]
    accs = project([a_right, a_left, b_up, b_down], PLAN_2, weights, accs, True, True)

    (halves,) = project(last, PLAN_3, weights, accs, False, True, True, asked=q_share)
    (queries,) = project(last, PLAN_3, weights, accs, True, False, True, tables)
    partner = swap_heads(halves, 0, 1)
    q_asked = q_share[:, :512]
    q_other = swap_ctx(q_asked, 0, 1)
    partner, queries, q_other = lax.optimization_barrier((partner, queries, q_other))
    kv = key_value(halves, partner, *tables)

    below, above, across = shift_z(kv, 1), shift_z(kv, -1), shift_z(kv, 2)
    weighted, stats = own_attention(lengths, queries, kv)
    below, above, across, weighted = lax.optimization_barrier((below, above, across, weighted))
    nearer = jnp.where(z == 0, kv[:ROWS], jnp.where(z == 1, below[:ROWS], jnp.where(z == 2, across[:ROWS], above[:ROWS])))
    from_zero = lax.ppermute(nearer, "ctx", [(0, 1), (2, 3), (4, 5), (6, 7)])
    part, part_other = question_attention(lengths, q_asked, q_other, [kv, below, above, across])
    from_zero, part = lax.optimization_barrier((from_zero, part))
    context_attn = anchor_attention(lengths, queries, nearer, from_zero, weighted, stats)
    question_attn = merge(part, swap_ctx(part_other, 0, 1))
    return (context_attn, question_attn)


def solution(mesh):
    in_specs = (
        P("ctx", "heads"),
        P("ctx", None, "heads"),
        P(None, "heads"),
        P(None, "heads"),
        P(None, "heads"),
        P(),
        P(),
    )
    out_specs = (P("ctx", "heads"), P("ctx", "heads"))
    return jax.shard_map(
        per_device, mesh=mesh, in_specs=in_specs, out_specs=out_specs, check_vma=False
    )
```

```python
import functools

import jax
import jax.numpy as jnp
from jax import lax
from jax.experimental import pallas as pl
from jax.experimental.pallas import tpu as pltpu
from jax.sharding import PartitionSpec as P

HD = 128
ROPE_BASE = 500000.0
BF = jnp.bfloat16
F32 = jnp.float32
VMEM_LIMIT = 8 * 1024 * 1024
HOLD_LIMIT = 37 * 1024 * 1024
NEG = -1e30
SCALE2 = HD ** (-0.5) * 1.4426950408889634
ROWS = 512
ASKED = 32
ALL = ROWS + ASKED

HBM = pl.BlockSpec(memory_space=pltpu.HBM)
VM = pl.BlockSpec(memory_space=pltpu.VMEM)
SM = pl.BlockSpec(memory_space=pltpu.SMEM)


def shift_heads(array, dy, dx):
    pairs = [(i, ((i // 4 + dy) % 4) * 4 + (i % 4 + dx) % 4) for i in range(16)]
    return lax.ppermute(array, "heads", pairs)


def swap_heads(array, my, mx):
    pairs = [(i, ((i // 4) ^ my) * 4 + ((i % 4) ^ mx)) for i in range(16)]
    return lax.ppermute(array, "heads", pairs)


def swap_ctx(array, mz, mc):
    pairs = [(i, ((i // 2) ^ mz) * 2 + ((i % 2) ^ mc)) for i in range(8)]
    return lax.ppermute(array, "ctx", pairs)


def places():
    heads, ctx = lax.axis_index("heads"), lax.axis_index("ctx")
    return lax.shift_right_logical(heads, 2), heads & 3, lax.shift_right_logical(ctx, 1), ctx & 1


def pack_kernel(plan, n_in, *refs):
    ins, outs = refs[:n_in], refs[n_in:]
    for out, pieces in zip(outs, plan):
        row = 0
        for operand, start, count in pieces:
            out[row : row + count, :] = ins[operand][start : start + count, :]
            row += count


def pack(plan, ins):
    return pl.pallas_call(
        functools.partial(pack_kernel, plan, len(ins)),
        out_shape=[jax.ShapeDtypeStruct((sum(p[2] for p in pieces), 512), BF) for pieces in plan],
        in_specs=[VM] * len(ins),
        out_specs=[VM] * len(plan),
        compiler_params=pltpu.CompilerParams(vmem_limit_bytes=VMEM_LIMIT),
        cost_estimate=pl.CostEstimate(flops=0, bytes_accessed=1 << 20, transcendentals=0),
    )(*ins)


def hold_kernel(wq, wk, wv, q_out, kv_out, sem):
    copies = []
    for part in range(8):
        rows = pl.ds(part * 1024, 1024)
        copies.append(pltpu.make_async_copy(wq.at[rows, :], q_out.at[rows, :], sem.at[part]))
    for part in range(4):
        cols = pl.ds(part * 2048, 2048)
        copies.append(pltpu.make_async_copy(wk.at[:, cols], kv_out.at[pl.ds(0, 64), cols], sem.at[8 + part]))
        copies.append(pltpu.make_async_copy(wv.at[:, cols], kv_out.at[pl.ds(64, 64), cols], sem.at[12 + part]))
    for copy in copies:
        copy.start()
    for copy in copies:
        copy.wait()


def hold(wq, wk, wv):
    return pl.pallas_call(
        hold_kernel,
        out_shape=[jax.ShapeDtypeStruct((8192, 512), BF), jax.ShapeDtypeStruct((128, 8192), BF)],
        in_specs=[HBM] * 3,
        out_specs=[VM, VM],
        scratch_shapes=[pltpu.SemaphoreType.DMA((16,))],
        compiler_params=pltpu.CompilerParams(vmem_limit_bytes=HOLD_LIMIT),
        cost_estimate=pl.CostEstimate(flops=0, bytes_accessed=20 << 20, transcendentals=0),
    )(wq, wk, wv)


def turn(part, cos, sin):
    return (part * cos + pltpu.roll(part, HD // 2, 1) * sin).astype(BF)


def project_kernel(plan, n_x, with_q, with_kv, has_acc, finish, *refs):
    refs = list(refs)
    take = lambda count: [refs.pop(0) for _ in range(count)]
    xs = take(n_x)
    wq = take(1)[0] if with_q else None
    wkv = take(1)[0] if with_kv else None
    acc_q = take(1)[0] if has_acc and with_q else None
    acc_kv = take(1)[0] if has_acc and with_kv else None
    cos, sin = take(2) if finish and with_q else (None, None)
    asked = take(1)[0] if finish and with_kv else None
    q_out = take(1)[0] if with_q else None
    kv_out = take(1)[0] if with_kv else None
    q_sum = take(1)[0] if finish and with_q else q_out
    kv_sum = take(1)[0] if finish and with_kv else kv_out
    y, x, _, _ = places()
    if has_acc:
        if with_q:
            q_sum[...] = acc_q[...]
        if with_kv:
            kv_sum[...] = acc_kv[...]
    for slot, ((dy, dx), low, high, uses) in enumerate(plan):
        base = pl.multiple_of((((y + dy) & 3) * 4 + ((x + dx) & 3)) * 512, 512)
        parts = [xs[operand][pl.ds(start, count), :] for operand, start, count in uses]
        piece = parts[0] if len(parts) == 1 else jnp.concatenate(parts, axis=0)
        fresh = slot == 0 and not has_acc
        if with_kv:
            both = wkv[:, pl.ds(base, 512)]
            term = lax.dot_general(piece, both, (((1,), (1,)), ((), ())), preferred_element_type=F32)
            kv_sum[low:high, :] = term if fresh else kv_sum[low:high, :] + term
        if with_q:
            term = jnp.dot(piece, wq[pl.ds(base, 512), :], preferred_element_type=F32)
            q_sum[low:high, :] = term if fresh else q_sum[low:high, :] + term
    if finish and with_kv:
        kv_out[:ROWS, :] = kv_sum[...].astype(BF)
        kv_out[ROWS:, :] = asked[:, 512:640]
    if finish and with_q:
        for head in range(4):
            cols = slice(head * HD, (head + 1) * HD)
            q_out[:, cols] = turn(q_sum[:, cols], cos[:ROWS, :], sin[:ROWS, :])


def project(xs, plan, weights, accs, with_q, with_kv, finish=False, tables=None, asked=None):
    wq, wkv = weights
    operands, specs = list(xs), [VM] * len(xs)
    if with_q:
        operands.append(wq)
        specs.append(VM)
    if with_kv:
        operands.append(wkv)
        specs.append(VM)
    has_acc = accs is not None
    if has_acc:
        if with_q:
            operands.append(accs[0])
            specs.append(VM)
        if with_kv:
            operands.append(accs[1])
            specs.append(VM)
    if finish and with_q:
        operands += list(tables)
        specs += [VM, VM]
    if finish and with_kv:
        operands.append(asked)
        specs.append(VM)
    outs, scratch = [], []
    if with_q:
        outs.append(jax.ShapeDtypeStruct((ROWS, 512), BF if finish else F32))
        if finish:
            scratch.append(pltpu.VMEM((ROWS, 512), F32))
    if with_kv:
        outs.append(jax.ShapeDtypeStruct((ALL, 128), BF) if finish else jax.ShapeDtypeStruct((ROWS, 128), F32))
        if finish:
            scratch.append(pltpu.VMEM((ROWS, 128), F32))
    columns = (512 if with_q else 0) + (128 if with_kv else 0)
    used = sum(high - low for _, low, high, _ in plan)
    return pl.pallas_call(
        functools.partial(project_kernel, plan, len(xs), with_q, with_kv, has_acc, finish),
        out_shape=outs,
        in_specs=specs,
        out_specs=[VM] * len(outs),
        scratch_shapes=scratch,
        compiler_params=pltpu.CompilerParams(vmem_limit_bytes=VMEM_LIMIT),
        cost_estimate=pl.CostEstimate(
            flops=2 * used * 512 * columns, bytes_accessed=len(plan) * 512 * columns * 2, transcendentals=0
        ),
    )(*operands)


def question_project_kernel(pieces, wq, wkv, cos, sin, out):
    q_sum, kv_sum = None, None
    for place in range(16):
        base = place * 512
        piece = pieces[place]
        both = wkv[:, pl.ds(base, 512)]
        kv_term = lax.dot_general(piece, both, (((1,), (1,)), ((), ())), preferred_element_type=F32)
        q_term = jnp.dot(piece, wq[pl.ds(base, 512), :], preferred_element_type=F32)
        q_sum = q_term if q_sum is None else q_sum + q_term
        kv_sum = kv_term if kv_sum is None else kv_sum + kv_term
    for head in range(4):
        cols = slice(head * HD, (head + 1) * HD)
        out[:, cols] = turn(q_sum[:, cols], cos[ROWS : ROWS + 32, :], sin[ROWS : ROWS + 32, :])
    out[:, 512:640] = kv_sum.astype(BF)


def question_project(pieces, weights, tables):
    return pl.pallas_call(
        question_project_kernel,
        out_shape=jax.ShapeDtypeStruct((32, 640), BF),
        in_specs=[VM] * 5,
        out_specs=VM,
        compiler_params=pltpu.CompilerParams(vmem_limit_bytes=VMEM_LIMIT),
        cost_estimate=pl.CostEstimate(flops=2 * 256 * 8192 * 640, bytes_accessed=8192 * 640 * 2, transcendentals=0),
    )(pieces, *weights, *tables)


def key_value_kernel(own, partner, cos, sin, out):
    is_lower = (places()[1] & 1) == 0
    mine, other = own[...].astype(F32), partner[...].astype(F32)
    low = jnp.where(is_lower, mine, other)
    high = jnp.where(is_lower, other, mine)
    lane = lax.broadcasted_iota(jnp.int32, low.shape, 1)
    keys = jnp.where(lane < 64, low, pltpu.roll(high, 64, 1))
    values = jnp.where(lane < 64, pltpu.roll(low, 64, 1), high)
    out[:, :HD] = (keys * cos[...] + pltpu.roll(keys, 64, 1) * sin[...]).astype(BF)
    out[:, HD:] = values.astype(BF)


def key_value(own, partner, cos, sin):
    return pl.pallas_call(
        key_value_kernel,
        out_shape=jax.ShapeDtypeStruct((ALL, 2 * HD), BF),
        in_specs=[VM, VM, VM, VM],
        out_specs=VM,
        compiler_params=pltpu.CompilerParams(vmem_limit_bytes=VMEM_LIMIT),
    )(own, partner, cos, sin)


def scores_of(queries, keys):
    return lax.dot_general(queries, keys, (((1,), (1,)), ((), ())), preferred_element_type=F32)


def weights_of(scores, top):
    return jnp.exp2(scores * SCALE2 - top * SCALE2)


def columns_to_stats(columns):
    rows = columns[0].shape[0]
    lane = lax.broadcasted_iota(jnp.int32, (rows, 128), 1)
    stats = jnp.zeros((rows, 128), F32)
    for index, column in enumerate(columns):
        stats = jnp.where(lane == index, column, stats)
    return stats


def own_kernel(lengths, q, kv, weighted, stats):
    _, _, z, core = places()
    length = lengths[2 * z + core]
    for tile in range(2):
        rows = slice(tile * 256, tile * 256 + 256)
        width = 256 * (tile + 1)
        row = tile * 256 + lax.broadcasted_iota(jnp.int32, (256, width), 0)
        key = lax.broadcasted_iota(jnp.int32, (256, width), 1)
        bias = jnp.where((key <= row) & (key < length), 0.0, NEG)
        tops, totals = [], []
        for head in range(4):
            cols = slice(head * HD, (head + 1) * HD)
            s = scores_of(q[rows, cols], kv[:width, :HD]) + bias
            top = jnp.max(s, axis=1, keepdims=True)
            e = weights_of(s, top)
            totals.append(jnp.sum(e, axis=1, keepdims=True))
            tops.append(top)
            weighted[rows, cols] = jnp.dot(e.astype(BF), kv[:width, HD:], preferred_element_type=F32)
        stats[rows, :] = columns_to_stats(tops + totals)


def own_attention(lengths, q, kv):
    return pl.pallas_call(
        own_kernel,
        out_shape=[jax.ShapeDtypeStruct((512, 512), F32), jax.ShapeDtypeStruct((512, 128), F32)],
        in_specs=[SM, VM, VM],
        out_specs=[VM, VM],
        compiler_params=pltpu.CompilerParams(vmem_limit_bytes=VMEM_LIMIT),
        cost_estimate=pl.CostEstimate(flops=4 * 4 * 512 * 512 * 128, bytes_accessed=3 << 20, transcendentals=1 << 20),
    )(lengths, q, kv)


def anchor_kernel(lengths, q, kv_zero, kv_one, weighted, stats, out):
    _, _, z, core = places()
    length = lengths[2 * z + core]
    anchor_length = jnp.where(2 * z + core > 0, lengths[0], 0)
    first_core = core == 0
    kv = jnp.where(first_core, kv_zero[...], kv_one[...])
    keys, values = kv[:, :HD], kv[:, HD:]
    key = lax.broadcasted_iota(jnp.int32, (1, 512), 1)
    bias = jnp.where(key < anchor_length, 0.0, NEG)
    for tile in range(2):
        rows = slice(tile * 256, tile * 256 + 256)
        block = stats[rows, :]
        row = tile * 256 + lax.broadcasted_iota(jnp.int32, (256, HD), 0)
        for head in range(4):
            cols = slice(head * HD, (head + 1) * HD)
            s = scores_of(q[rows, cols], keys) + bias
            own_top, own_sum = block[:, head : head + 1], block[:, head + 4 : head + 5]
            top = jnp.maximum(own_top, jnp.max(s, axis=1, keepdims=True))
            e = weights_of(s, top)
            factor = weights_of(own_top, top)
            total = own_sum * factor + jnp.sum(e, axis=1, keepdims=True)
            both = weighted[rows, cols] * factor + jnp.dot(e.astype(BF), values, preferred_element_type=F32)
            out[rows, cols] = jnp.where(row < length, both / total, 0.0).astype(BF)


def anchor_attention(lengths, q, kv_zero, kv_one, weighted, stats):
    return pl.pallas_call(
        anchor_kernel,
        out_shape=jax.ShapeDtypeStruct((512, 512), BF),
        in_specs=[SM, VM, VM, VM, VM, VM],
        out_specs=VM,
        compiler_params=pltpu.CompilerParams(vmem_limit_bytes=VMEM_LIMIT),
        cost_estimate=pl.CostEstimate(flops=4 * 4 * 512 * 512 * 128, bytes_accessed=3 << 20, transcendentals=1 << 20),
    )(lengths, q, kv_zero, kv_one, weighted, stats)


def question_kernel(lengths_ref, q_own, q_other, kv_0, kv_1, kv_2, kv_3, out_own, out_other):
    kvs = (kv_0, kv_1, kv_2, kv_3)
    _, _, z, core = places()
    ctx = 2 * z + core
    blocks = [z, (z + 3) & 3, (z + 1) & 3, (z + 2) & 3]
    lengths = [lengths_ref[2 * block + core] for block in blocks]
    stacked = [q_own[:, h * HD : (h + 1) * HD] for h in range(4)]
    stacked += [q_other[:, h * HD : (h + 1) * HD] for h in range(4)]
    q = jnp.concatenate(stacked, axis=0)
    scores = []
    key = lax.broadcasted_iota(jnp.int32, (1, 512), 1)
    for kv, length in zip(kvs, lengths):
        scores.append(scores_of(q, kv[:ROWS, :HD]) + jnp.where(key < length, 0.0, NEG))
    row = lax.broadcasted_iota(jnp.int32, (256, 128), 0)
    lane = lax.broadcasted_iota(jnp.int32, (256, 128), 1)
    row_id = row % 32 + 32 * jnp.where(row < 128, ctx, ctx + 1 - 2 * core)
    block = jnp.where(lane < 64, jnp.where(lane < 32, blocks[0], blocks[1]), jnp.where(lane < 96, blocks[2], blocks[3]))
    key_id = lane % 32 + 32 * (2 * block + core)
    asked_keys = jnp.concatenate([kv[ROWS:, :HD] for kv in kvs], axis=0)
    asked_values = jnp.concatenate([kv[ROWS:, HD:] for kv in kvs], axis=0)
    scores.append(jnp.where(key_id <= row_id, scores_of(q, asked_keys), NEG))
    top = jnp.max(scores[-1], axis=1, keepdims=True)
    for s in scores[:-1]:
        top = jnp.maximum(top, jnp.max(s, axis=1, keepdims=True))
    values = [kv[:ROWS, HD:] for kv in kvs] + [asked_values]
    total = jnp.zeros((256, 1), F32)
    both = jnp.zeros((256, HD), F32)
    for s, value in zip(scores, values):
        e = weights_of(s, top)
        total = total + jnp.sum(e, axis=1, keepdims=True)
        both = both + jnp.dot(e.astype(BF), value, preferred_element_type=F32)
    for out, start in ((out_own, 0), (out_other, 128)):
        tops, totals = [], []
        for head in range(4):
            rows = slice(start + head * 32, start + head * 32 + 32)
            out[:, head * HD : (head + 1) * HD] = both[rows]
            tops.append(top[rows])
            totals.append(total[rows])
        out[:, 512:640] = columns_to_stats(tops + totals)


def question_attention(lengths, q_own, q_other, kvs):
    part = jax.ShapeDtypeStruct((32, 640), F32)
    return pl.pallas_call(
        question_kernel,
        out_shape=[part, part],
        in_specs=[SM] + [VM] * 6,
        out_specs=[VM, VM],
        compiler_params=pltpu.CompilerParams(vmem_limit_bytes=VMEM_LIMIT),
        cost_estimate=pl.CostEstimate(flops=4 * 256 * 2176 * 128, bytes_accessed=2 << 20, transcendentals=1 << 19),
    )(lengths, q_own, q_other, *kvs)


def merge_kernel(a, b, out):
    stat_a, stat_b = a[:, 512:640], b[:, 512:640]
    for head in range(4):
        cols = slice(head * HD, (head + 1) * HD)
        top_a, top_b = stat_a[:, head : head + 1], stat_b[:, head : head + 1]
        top = jnp.maximum(top_a, top_b)
        factor_a, factor_b = weights_of(top_a, top), weights_of(top_b, top)
        total = stat_a[:, head + 4 : head + 5] * factor_a + stat_b[:, head + 4 : head + 5] * factor_b
        out[:, cols] = ((a[:, cols] * factor_a + b[:, cols] * factor_b) / total).astype(BF)


def merge(a, b):
    return pl.pallas_call(
        merge_kernel,
        out_shape=jax.ShapeDtypeStruct((32, 512), BF),
        in_specs=[VM, VM],
        out_specs=VM,
        compiler_params=pltpu.CompilerParams(vmem_limit_bytes=VMEM_LIMIT),
    )(a, b)


PLAN_1 = [
    ((0, 0), 0, 512, [(0, 0, 512)]),
    ((-1, 0), 0, 512, [(1, 0, 512)]),
    ((1, 0), 0, 512, [(2, 0, 512)]),
    ((0, -1), 0, 512, [(3, 0, 512)]),
    ((0, 1), 0, 512, [(4, 0, 512)]),
    ((2, 0), 0, 256, [(5, 0, 256)]),
    ((0, 2), 256, 512, [(6, 0, 256)]),
]
PLAN_2 = [
    ((-1, -1), 0, 512, [(0, 0, 256), (2, 0, 256)]),
    ((1, -1), 0, 512, [(0, 256, 256), (3, 0, 256)]),
    ((-1, 1), 0, 512, [(1, 0, 256), (2, 256, 256)]),
    ((1, 1), 0, 512, [(1, 256, 256), (3, 256, 256)]),
    ((2, -1), 0, 256, [(0, 512, 256)]),
    ((2, 1), 0, 256, [(1, 512, 256)]),
    ((-1, 2), 256, 512, [(2, 512, 256)]),
    ((1, 2), 256, 512, [(3, 512, 256)]),
    ((0, 2), 0, 256, [(0, 768, 128), (1, 768, 128)]),
    ((2, 0), 256, 512, [(2, 768, 128), (3, 768, 128)]),
]
PLAN_3 = [
    ((2, 2), 0, 512, [(1, 128, 256), (3, 128, 256)]),
    ((-1, 2), 0, 256, [(0, 0, 256)]),
    ((1, 2), 0, 256, [(0, 256, 128), (1, 0, 128)]),
    ((2, -1), 256, 512, [(2, 0, 256)]),
    ((2, 1), 256, 512, [(2, 256, 128), (3, 0, 128)]),
]
NEAR_Y = [(0, 0, 256), (1, 0, 256), (4, 0, 256)]
NEAR_X = [(2, 256, 256), (3, 256, 256), (4, 0, 256)]
PACK_2 = [NEAR_Y + [(2, 0, 128)], NEAR_Y + [(3, 128, 128)], NEAR_X + [(0, 256, 128)], NEAR_X + [(1, 384, 128)]]
PACK_3 = [[(0, 0, 384)], [(1, 384, 384)]]


def tables_of(positions):
    inverse_freq = ROPE_BASE ** (-(jnp.arange(HD // 2, dtype=jnp.float32) * 2.0 / HD))
    inverse_freq = jnp.concatenate([inverse_freq, inverse_freq])
    phases = positions.astype(jnp.float32)[:, None] * inverse_freq[None, :]
    signs = jnp.where(jnp.arange(HD) < HD // 2, -1.0, 1.0).astype(jnp.float32)
    return jnp.cos(phases), jnp.sin(phases) * signs[None, :]


def shift_z(array, dz):
    pairs = [(i, ((i // 2 + dz) % 4) * 2 + i % 2) for i in range(8)]
    return lax.ppermute(array, "ctx", pairs)


def per_device(context, question, w_query, w_key, w_value, lengths, owner):
    ctx = lax.axis_index("ctx")
    z, core = lax.shift_right_logical(ctx, 1), ctx & 1
    ids = jnp.arange(8, dtype=jnp.int32)
    own_offset = jnp.sum(jnp.where(ids < ctx, lengths, 0))
    filled = jnp.sum(lengths)

    up = shift_heads(context, 1, 0)
    down = shift_heads(context, -1, 0)
    right = shift_heads(context, 0, 1)
    left = shift_heads(context, 0, -1)
    low, high = pack([[(0, 0, 256)], [(0, 256, 256)]], [context])
    far_y = shift_heads(low, 2, 0)
    low, asked = lax.optimization_barrier((low, question))
    up, high = lax.optimization_barrier((up, high))
    far_x = shift_heads(high, 0, 2)

    share = lax.all_to_all(asked[0].reshape(8, 32, 512), "ctx", 0, 0)
    share = lax.dynamic_index_in_dim(share, owner[0], 0, False)
    share = jnp.broadcast_to(share[None], (16, 32, 512))
    far_x, down, right, left, share = lax.optimization_barrier((far_x, down, right, left, share))
    pieces = lax.all_to_all(share, "heads", 0, 0)
    up, pieces = lax.optimization_barrier((up, pieces))

    to_right, to_left = pack(PACK_2[:2], [up, down, right, left, far_y])
    to_up, to_down = pack(PACK_2[2:], [up, down, right, left, far_x])
    a_right, a_left = shift_heads(to_right, 0, 1), shift_heads(to_left, 0, -1)
    b_up, b_down = shift_heads(to_up, 1, 0), shift_heads(to_down, -1, 0)
    up, to_right = lax.optimization_barrier((up, to_right))
    tables = tables_of(
        jnp.concatenate(
            [own_offset + jnp.arange(ROWS, dtype=jnp.int32), filled + 32 * ctx + jnp.arange(ASKED, dtype=jnp.int32)]
        )
    )
    pieces, w_query, w_key, w_value, tables = lax.optimization_barrier(
        (pieces, w_query, w_key, w_value, tables)
    )
    weights = hold(w_query, w_key.T, w_value.T)
    accs = project([context, up, down, right, left, far_y, far_x], PLAN_1, weights, None, True, True)
    q_share = question_project(pieces, weights, tables)

    a_right, a_left, accs, q_share = lax.optimization_barrier((a_right, a_left, accs, q_share))
    to_right, to_left = pack(PACK_3, [a_right, a_left])
    to_up, to_down = pack(PACK_3, [b_up, b_down])
    last = [
        shift_heads(to_right, 0, 1),
        shift_heads(to_left, 0, -1),
        shift_heads(to_up, 1, 0),
        shift_heads(to_down, -1, 0),
    ]
    accs = project([a_right, a_left, b_up, b_down], PLAN_2, weights, accs, True, True)

    (halves,) = project(last, PLAN_3, weights, accs, False, True, True, asked=q_share)
    (queries,) = project(last, PLAN_3, weights, accs, True, False, True, tables)
    partner = swap_heads(halves, 0, 1)
    q_asked = q_share[:, :512]
    q_other = swap_ctx(q_asked, 0, 1)
    partner, queries, q_other = lax.optimization_barrier((partner, queries, q_other))
    kv = key_value(halves, partner, *tables)

    below, above, across = shift_z(kv, 1), shift_z(kv, -1), shift_z(kv, 2)
    weighted, stats = own_attention(lengths, queries, kv)
    below, above, across, weighted = lax.optimization_barrier((below, above, across, weighted))
    nearer = jnp.where(z == 0, kv[:ROWS], jnp.where(z == 1, below[:ROWS], jnp.where(z == 2, across[:ROWS], above[:ROWS])))
    from_zero = lax.ppermute(nearer, "ctx", [(0, 1), (2, 3), (4, 5), (6, 7)])
    part, part_other = question_attention(lengths, q_asked, q_other, [kv, below, above, across])
    from_zero, part = lax.optimization_barrier((from_zero, part))
    context_attn = anchor_attention(lengths, queries, nearer, from_zero, weighted, stats)
    question_attn = merge(part, swap_ctx(part_other, 0, 1))
    return (context_attn, question_attn)


def solution(mesh):
    in_specs = (
        P("ctx", "heads"),
        P("ctx", None, "heads"),
        P(None, "heads"),
        P(None, "heads"),
        P(None, "heads"),
        P(),
        P(),
    )
    out_specs = (P("ctx", "heads"), P("ctx", "heads"))
    return jax.shard_map(
        per_device, mesh=mesh, in_specs=in_specs, out_specs=out_specs, check_vma=False
    )
```

```python
import functools

import jax
import jax.numpy as jnp
from jax import lax
from jax.experimental import pallas as pl
from jax.experimental.pallas import tpu as pltpu
from jax.sharding import PartitionSpec as P

HD = 128
ROPE_BASE = 500000.0
BF = jnp.bfloat16
F32 = jnp.float32
VMEM_LIMIT = 8 * 1024 * 1024
HOLD_LIMIT = 37 * 1024 * 1024
NEG = -1e30
SCALE2 = HD ** (-0.5) * 1.4426950408889634
ROWS = 512
ASKED = 32
ALL = ROWS + ASKED

HBM = pl.BlockSpec(memory_space=pltpu.HBM)
VM = pl.BlockSpec(memory_space=pltpu.VMEM)
SM = pl.BlockSpec(memory_space=pltpu.SMEM)


def shift_heads(array, dy, dx):
    pairs = [(i, ((i // 4 + dy) % 4) * 4 + (i % 4 + dx) % 4) for i in range(16)]
    return lax.ppermute(array, "heads", pairs)


def swap_heads(array, my, mx):
    pairs = [(i, ((i // 4) ^ my) * 4 + ((i % 4) ^ mx)) for i in range(16)]
    return lax.ppermute(array, "heads", pairs)


def swap_ctx(array, mz, mc):
    pairs = [(i, ((i // 2) ^ mz) * 2 + ((i % 2) ^ mc)) for i in range(8)]
    return lax.ppermute(array, "ctx", pairs)


def places():
    heads, ctx = lax.axis_index("heads"), lax.axis_index("ctx")
    return lax.shift_right_logical(heads, 2), heads & 3, lax.shift_right_logical(ctx, 1), ctx & 1


def pack_kernel(plan, n_in, *refs):
    ins, outs = refs[:n_in], refs[n_in:]
    for out, pieces in zip(outs, plan):
        row = 0
        for operand, start, count in pieces:
            out[row : row + count, :] = ins[operand][start : start + count, :]
            row += count


def pack(plan, ins):
    return pl.pallas_call(
        functools.partial(pack_kernel, plan, len(ins)),
        out_shape=[jax.ShapeDtypeStruct((sum(p[2] for p in pieces), 512), BF) for pieces in plan],
        in_specs=[VM] * len(ins),
        out_specs=[VM] * len(plan),
        compiler_params=pltpu.CompilerParams(vmem_limit_bytes=VMEM_LIMIT),
        cost_estimate=pl.CostEstimate(flops=0, bytes_accessed=1 << 20, transcendentals=0),
    )(*ins)


def hold_kernel(wq, wk, wv, q_out, kv_out, sem):
    copies = []
    for part in range(8):
        rows = pl.ds(part * 1024, 1024)
        copies.append(pltpu.make_async_copy(wq.at[rows, :], q_out.at[rows, :], sem.at[part]))
    for part in range(4):
        cols = pl.ds(part * 2048, 2048)
        copies.append(pltpu.make_async_copy(wk.at[:, cols], kv_out.at[pl.ds(0, 64), cols], sem.at[8 + part]))
        copies.append(pltpu.make_async_copy(wv.at[:, cols], kv_out.at[pl.ds(64, 64), cols], sem.at[12 + part]))
    for copy in copies:
        copy.start()
    for copy in copies:
        copy.wait()


def hold(wq, wk, wv):
    return pl.pallas_call(
        hold_kernel,
        out_shape=[jax.ShapeDtypeStruct((8192, 512), BF), jax.ShapeDtypeStruct((128, 8192), BF)],
        in_specs=[HBM] * 3,
        out_specs=[VM, VM],
        scratch_shapes=[pltpu.SemaphoreType.DMA((16,))],
        compiler_params=pltpu.CompilerParams(vmem_limit_bytes=HOLD_LIMIT),
        cost_estimate=pl.CostEstimate(flops=0, bytes_accessed=20 << 20, transcendentals=0),
    )(wq, wk, wv)


def turn(part, cos, sin):
    return (part * cos + pltpu.roll(part, HD // 2, 1) * sin).astype(BF)


def project_kernel(plan, n_x, with_q, with_kv, has_acc, finish, *refs):
    refs = list(refs)
    take = lambda count: [refs.pop(0) for _ in range(count)]
    xs = take(n_x)
    wq = take(1)[0] if with_q else None
    wkv = take(1)[0] if with_kv else None
    acc_q = take(1)[0] if has_acc and with_q else None
    acc_kv = take(1)[0] if has_acc and with_kv else None
    cos, sin = take(2) if finish and with_q else (None, None)
    asked = take(1)[0] if finish and with_kv else None
    q_out = take(1)[0] if with_q else None
    kv_out = take(1)[0] if with_kv else None
    q_sum = take(1)[0] if finish and with_q else q_out
    kv_sum = take(1)[0] if finish and with_kv else kv_out
    y, x, _, _ = places()
    if has_acc:
        if with_q:
            q_sum[...] = acc_q[...]
        if with_kv:
            kv_sum[...] = acc_kv[...]
    for slot, ((dy, dx), low, high, uses) in enumerate(plan):
        base = pl.multiple_of((((y + dy) & 3) * 4 + ((x + dx) & 3)) * 512, 512)
        parts = [xs[operand][pl.ds(start, count), :] for operand, start, count in uses]
        piece = parts[0] if len(parts) == 1 else jnp.concatenate(parts, axis=0)
        fresh = slot == 0 and not has_acc
        if with_kv:
            both = wkv[:, pl.ds(base, 512)]
            term = lax.dot_general(piece, both, (((1,), (1,)), ((), ())), preferred_element_type=F32)
            kv_sum[low:high, :] = term if fresh else kv_sum[low:high, :] + term
        if with_q:
            term = jnp.dot(piece, wq[pl.ds(base, 512), :], preferred_element_type=F32)
            q_sum[low:high, :] = term if fresh else q_sum[low:high, :] + term
    if finish and with_kv:
        kv_out[:ROWS, :] = kv_sum[...].astype(BF)
        kv_out[ROWS:, :] = asked[:, 512:640]
    if finish and with_q:
        for head in range(4):
            cols = slice(head * HD, (head + 1) * HD)
            q_out[:, cols] = turn(q_sum[:, cols], cos[:ROWS, :], sin[:ROWS, :])


def project(xs, plan, weights, accs, with_q, with_kv, finish=False, tables=None, asked=None):
    wq, wkv = weights
    operands, specs = list(xs), [VM] * len(xs)
    if with_q:
        operands.append(wq)
        specs.append(VM)
    if with_kv:
        operands.append(wkv)
        specs.append(VM)
    has_acc = accs is not None
    if has_acc:
        if with_q:
            operands.append(accs[0])
            specs.append(VM)
        if with_kv:
            operands.append(accs[1])
            specs.append(VM)
    if finish and with_q:
        operands += list(tables)
        specs += [VM, VM]
    if finish and with_kv:
        operands.append(asked)
        specs.append(VM)
    outs, scratch = [], []
    if with_q:
        outs.append(jax.ShapeDtypeStruct((ROWS, 512), BF if finish else F32))
        if finish:
            scratch.append(pltpu.VMEM((ROWS, 512), F32))
    if with_kv:
        outs.append(jax.ShapeDtypeStruct((ALL, 128), BF) if finish else jax.ShapeDtypeStruct((ROWS, 128), F32))
        if finish:
            scratch.append(pltpu.VMEM((ROWS, 128), F32))
    columns = (512 if with_q else 0) + (128 if with_kv else 0)
    used = sum(high - low for _, low, high, _ in plan)
    return pl.pallas_call(
        functools.partial(project_kernel, plan, len(xs), with_q, with_kv, has_acc, finish),
        out_shape=outs,
        in_specs=specs,
        out_specs=[VM] * len(outs),
        scratch_shapes=scratch,
        compiler_params=pltpu.CompilerParams(vmem_limit_bytes=VMEM_LIMIT),
        cost_estimate=pl.CostEstimate(
            flops=2 * used * 512 * columns, bytes_accessed=len(plan) * 512 * columns * 2, transcendentals=0
        ),
    )(*operands)


def question_project_kernel(pieces, wq, wkv, cos, sin, out):
    q_sum, kv_sum = None, None
    for place in range(16):
        base = place * 512
        piece = pieces[place]
        both = wkv[:, pl.ds(base, 512)]
        kv_term = lax.dot_general(piece, both, (((1,), (1,)), ((), ())), preferred_element_type=F32)
        q_term = jnp.dot(piece, wq[pl.ds(base, 512), :], preferred_element_type=F32)
        q_sum = q_term if q_sum is None else q_sum + q_term
        kv_sum = kv_term if kv_sum is None else kv_sum + kv_term
    for head in range(4):
        cols = slice(head * HD, (head + 1) * HD)
        out[:, cols] = turn(q_sum[:, cols], cos[ROWS : ROWS + 32, :], sin[ROWS : ROWS + 32, :])
    out[:, 512:640] = kv_sum.astype(BF)


def question_project(pieces, weights, tables):
    return pl.pallas_call(
        question_project_kernel,
        out_shape=jax.ShapeDtypeStruct((32, 640), BF),
        in_specs=[VM] * 5,
        out_specs=VM,
        compiler_params=pltpu.CompilerParams(vmem_limit_bytes=VMEM_LIMIT),
        cost_estimate=pl.CostEstimate(flops=2 * 256 * 8192 * 640, bytes_accessed=8192 * 640 * 2, transcendentals=0),
    )(pieces, *weights, *tables)


def key_value_kernel(own, partner, cos, sin, out):
    is_lower = (places()[1] & 1) == 0
    mine, other = own[...].astype(F32), partner[...].astype(F32)
    low = jnp.where(is_lower, mine, other)
    high = jnp.where(is_lower, other, mine)
    lane = lax.broadcasted_iota(jnp.int32, low.shape, 1)
    keys = jnp.where(lane < 64, low, pltpu.roll(high, 64, 1))
    values = jnp.where(lane < 64, pltpu.roll(low, 64, 1), high)
    out[:, :HD] = (keys * cos[...] + pltpu.roll(keys, 64, 1) * sin[...]).astype(BF)
    out[:, HD:] = values.astype(BF)


def key_value(own, partner, cos, sin):
    return pl.pallas_call(
        key_value_kernel,
        out_shape=jax.ShapeDtypeStruct((ALL, 2 * HD), BF),
        in_specs=[VM, VM, VM, VM],
        out_specs=VM,
        compiler_params=pltpu.CompilerParams(vmem_limit_bytes=VMEM_LIMIT),
    )(own, partner, cos, sin)


def scores_of(queries, keys):
    return lax.dot_general(queries, keys, (((1,), (1,)), ((), ())), preferred_element_type=F32)


def weights_of(scores, top):
    return jnp.exp2(scores * SCALE2 - top * SCALE2)


def columns_to_stats(columns):
    rows = columns[0].shape[0]
    lane = lax.broadcasted_iota(jnp.int32, (rows, 128), 1)
    stats = jnp.zeros((rows, 128), F32)
    for index, column in enumerate(columns):
        stats = jnp.where(lane == index, column, stats)
    return stats


def own_kernel(lengths, q, kv, weighted, stats):
    _, _, z, core = places()
    length = lengths[2 * z + core]
    for tile in range(2):
        rows = slice(tile * 256, tile * 256 + 256)
        width = 256 * (tile + 1)
        row = tile * 256 + lax.broadcasted_iota(jnp.int32, (256, width), 0)
        key = lax.broadcasted_iota(jnp.int32, (256, width), 1)
        bias = jnp.where((key <= row) & (key < length), 0.0, NEG)
        tops, totals = [], []
        for head in range(4):
            cols = slice(head * HD, (head + 1) * HD)
            s = scores_of(q[rows, cols], kv[:width, :HD]) + bias
            top = jnp.max(s, axis=1, keepdims=True)
            e = weights_of(s, top)
            totals.append(jnp.sum(e, axis=1, keepdims=True))
            tops.append(top)
            weighted[rows, cols] = jnp.dot(e.astype(BF), kv[:width, HD:], preferred_element_type=F32)
        stats[rows, :] = columns_to_stats(tops + totals)


def own_attention(lengths, q, kv):
    return pl.pallas_call(
        own_kernel,
        out_shape=[jax.ShapeDtypeStruct((512, 512), F32), jax.ShapeDtypeStruct((512, 128), F32)],
        in_specs=[SM, VM, VM],
        out_specs=[VM, VM],
        compiler_params=pltpu.CompilerParams(vmem_limit_bytes=VMEM_LIMIT),
        cost_estimate=pl.CostEstimate(flops=4 * 4 * 512 * 512 * 128, bytes_accessed=3 << 20, transcendentals=1 << 20),
    )(lengths, q, kv)


def anchor_kernel(lengths, q, kv_zero, kv_one, weighted, stats, out):
    _, _, z, core = places()
    length = lengths[2 * z + core]
    anchor_length = jnp.where(2 * z + core > 0, lengths[0], 0)
    first_core = core == 0
    kv = jnp.where(first_core, kv_zero[...], kv_one[...])
    keys, values = kv[:, :HD], kv[:, HD:]
    key = lax.broadcasted_iota(jnp.int32, (1, 512), 1)
    bias = jnp.where(key < anchor_length, 0.0, NEG)
    for tile in range(2):
        rows = slice(tile * 256, tile * 256 + 256)
        block = stats[rows, :]
        row = tile * 256 + lax.broadcasted_iota(jnp.int32, (256, HD), 0)
        for head in range(4):
            cols = slice(head * HD, (head + 1) * HD)
            s = scores_of(q[rows, cols], keys) + bias
            own_top, own_sum = block[:, head : head + 1], block[:, head + 4 : head + 5]
            top = jnp.maximum(own_top, jnp.max(s, axis=1, keepdims=True))
            e = weights_of(s, top)
            factor = weights_of(own_top, top)
            total = own_sum * factor + jnp.sum(e, axis=1, keepdims=True)
            both = weighted[rows, cols] * factor + jnp.dot(e.astype(BF), values, preferred_element_type=F32)
            out[rows, cols] = jnp.where(row < length, both / total, 0.0).astype(BF)


def anchor_attention(lengths, q, kv_zero, kv_one, weighted, stats):
    return pl.pallas_call(
        anchor_kernel,
        out_shape=jax.ShapeDtypeStruct((512, 512), BF),
        in_specs=[SM, VM, VM, VM, VM, VM],
        out_specs=VM,
        compiler_params=pltpu.CompilerParams(vmem_limit_bytes=VMEM_LIMIT),
        cost_estimate=pl.CostEstimate(flops=4 * 4 * 512 * 512 * 128, bytes_accessed=3 << 20, transcendentals=1 << 20),
    )(lengths, q, kv_zero, kv_one, weighted, stats)


def question_kernel(lengths_ref, q_own, q_other, kv_0, kv_1, kv_2, kv_3, out_own, out_other):
    kvs = (kv_0, kv_1, kv_2, kv_3)
    _, _, z, core = places()
    ctx = 2 * z + core
    blocks = [z, (z + 3) & 3, (z + 1) & 3, (z + 2) & 3]
    lengths = [lengths_ref[2 * block + core] for block in blocks]
    stacked = [q_own[:, h * HD : (h + 1) * HD] for h in range(4)]
    stacked += [q_other[:, h * HD : (h + 1) * HD] for h in range(4)]
    q = jnp.concatenate(stacked, axis=0)
    scores = []
    key = lax.broadcasted_iota(jnp.int32, (1, 512), 1)
    for kv, length in zip(kvs, lengths):
        scores.append(scores_of(q, kv[:ROWS, :HD]) + jnp.where(key < length, 0.0, NEG))
    row = lax.broadcasted_iota(jnp.int32, (256, 128), 0)
    lane = lax.broadcasted_iota(jnp.int32, (256, 128), 1)
    row_id = row % 32 + 32 * jnp.where(row < 128, ctx, ctx + 1 - 2 * core)
    block = jnp.where(lane < 64, jnp.where(lane < 32, blocks[0], blocks[1]), jnp.where(lane < 96, blocks[2], blocks[3]))
    key_id = lane % 32 + 32 * (2 * block + core)
    asked_keys = jnp.concatenate([kv[ROWS:, :HD] for kv in kvs], axis=0)
    asked_values = jnp.concatenate([kv[ROWS:, HD:] for kv in kvs], axis=0)
    scores.append(jnp.where(key_id <= row_id, scores_of(q, asked_keys), NEG))
    top = jnp.max(scores[-1], axis=1, keepdims=True)
    for s in scores[:-1]:
        top = jnp.maximum(top, jnp.max(s, axis=1, keepdims=True))
    values = [kv[:ROWS, HD:] for kv in kvs] + [asked_values]
    total = jnp.zeros((256, 1), F32)
    both = jnp.zeros((256, HD), F32)
    for s, value in zip(scores, values):
        e = weights_of(s, top)
        total = total + jnp.sum(e, axis=1, keepdims=True)
        both = both + jnp.dot(e.astype(BF), value, preferred_element_type=F32)
    for out, start in ((out_own, 0), (out_other, 128)):
        tops, totals = [], []
        for head in range(4):
            rows = slice(start + head * 32, start + head * 32 + 32)
            out[:, head * HD : (head + 1) * HD] = both[rows]
            tops.append(top[rows])
            totals.append(total[rows])
        out[:, 512:640] = columns_to_stats(tops + totals)


def question_attention(lengths, q_own, q_other, kvs):
    part = jax.ShapeDtypeStruct((32, 640), F32)
    return pl.pallas_call(
        question_kernel,
        out_shape=[part, part],
        in_specs=[SM] + [VM] * 6,
        out_specs=[VM, VM],
        compiler_params=pltpu.CompilerParams(vmem_limit_bytes=VMEM_LIMIT),
        cost_estimate=pl.CostEstimate(flops=4 * 256 * 2176 * 128, bytes_accessed=2 << 20, transcendentals=1 << 19),
    )(lengths, q_own, q_other, *kvs)


def merge_kernel(a, b, out):
    stat_a, stat_b = a[:, 512:640], b[:, 512:640]
    for head in range(4):
        cols = slice(head * HD, (head + 1) * HD)
        top_a, top_b = stat_a[:, head : head + 1], stat_b[:, head : head + 1]
        top = jnp.maximum(top_a, top_b)
        factor_a, factor_b = weights_of(top_a, top), weights_of(top_b, top)
        total = stat_a[:, head + 4 : head + 5] * factor_a + stat_b[:, head + 4 : head + 5] * factor_b
        out[:, cols] = ((a[:, cols] * factor_a + b[:, cols] * factor_b) / total).astype(BF)


def merge(a, b):
    return pl.pallas_call(
        merge_kernel,
        out_shape=jax.ShapeDtypeStruct((32, 512), BF),
        in_specs=[VM, VM],
        out_specs=VM,
        compiler_params=pltpu.CompilerParams(vmem_limit_bytes=VMEM_LIMIT),
    )(a, b)


PLAN_1 = [
    ((0, 0), 0, 512, [(0, 0, 512)]),
    ((-1, 0), 0, 512, [(1, 0, 512)]),
    ((1, 0), 0, 512, [(2, 0, 512)]),
    ((0, -1), 0, 512, [(3, 0, 512)]),
    ((0, 1), 0, 512, [(4, 0, 512)]),
    ((2, 0), 0, 256, [(5, 0, 256)]),
    ((0, 2), 256, 512, [(6, 0, 256)]),
]
PLAN_2 = [
    ((-1, -1), 0, 512, [(0, 0, 256), (2, 0, 256)]),
    ((1, -1), 0, 512, [(0, 256, 256), (3, 0, 256)]),
    ((-1, 1), 0, 512, [(1, 0, 256), (2, 256, 256)]),
    ((1, 1), 0, 512, [(1, 256, 256), (3, 256, 256)]),
    ((2, -1), 0, 256, [(0, 512, 256)]),
    ((2, 1), 0, 256, [(1, 512, 256)]),
    ((-1, 2), 256, 512, [(2, 512, 256)]),
    ((1, 2), 256, 512, [(3, 512, 256)]),
    ((0, 2), 0, 256, [(0, 768, 128), (1, 768, 128)]),
    ((2, 0), 256, 512, [(2, 768, 128), (3, 768, 128)]),
]
PLAN_3 = [
    ((2, 2), 0, 512, [(1, 128, 256), (3, 128, 256)]),
    ((-1, 2), 0, 256, [(0, 0, 256)]),
    ((1, 2), 0, 256, [(0, 256, 128), (1, 0, 128)]),
    ((2, -1), 256, 512, [(2, 0, 256)]),
    ((2, 1), 256, 512, [(2, 256, 128), (3, 0, 128)]),
]
NEAR_Y = [(0, 0, 256), (1, 0, 256), (4, 0, 256)]
NEAR_X = [(2, 256, 256), (3, 256, 256), (4, 0, 256)]
PACK_2 = [NEAR_Y + [(2, 0, 128)], NEAR_Y + [(3, 128, 128)], NEAR_X + [(0, 256, 128)], NEAR_X + [(1, 384, 128)]]
PACK_3 = [[(0, 0, 384)], [(1, 384, 384)]]


def tables_of(positions):
    inverse_freq = ROPE_BASE ** (-(jnp.arange(HD // 2, dtype=jnp.float32) * 2.0 / HD))
    inverse_freq = jnp.concatenate([inverse_freq, inverse_freq])
    phases = positions.astype(jnp.float32)[:, None] * inverse_freq[None, :]
    signs = jnp.where(jnp.arange(HD) < HD // 2, -1.0, 1.0).astype(jnp.float32)
    return jnp.cos(phases), jnp.sin(phases) * signs[None, :]


def shift_z(array, dz):
    pairs = [(i, ((i // 2 + dz) % 4) * 2 + i % 2) for i in range(8)]
    return lax.ppermute(array, "ctx", pairs)


def per_device(context, question, w_query, w_key, w_value, lengths, owner):
    ctx = lax.axis_index("ctx")
    z, core = lax.shift_right_logical(ctx, 1), ctx & 1
    ids = jnp.arange(8, dtype=jnp.int32)
    own_offset = jnp.sum(jnp.where(ids < ctx, lengths, 0))
    filled = jnp.sum(lengths)

    up = shift_heads(context, 1, 0)
    down = shift_heads(context, -1, 0)
    right = shift_heads(context, 0, 1)
    left = shift_heads(context, 0, -1)
    low, high = pack([[(0, 0, 256)], [(0, 256, 256)]], [context])
    far_y = shift_heads(low, 2, 0)
    low, asked = lax.optimization_barrier((low, question))
    up, high = lax.optimization_barrier((up, high))
    far_x = shift_heads(high, 0, 2)

    share = lax.all_to_all(asked[0].reshape(8, 32, 512), "ctx", 0, 0)
    share = lax.dynamic_index_in_dim(share, owner[0], 0, False)
    share = jnp.broadcast_to(share[None], (16, 32, 512))
    far_x, far_y, down, right, left, share = lax.optimization_barrier((far_x, far_y, down, right, left, share))
    pieces = lax.all_to_all(share, "heads", 0, 0)
    up, pieces = lax.optimization_barrier((up, pieces))

    to_right, to_left = pack(PACK_2[:2], [up, down, right, left, far_y])
    to_up, to_down = pack(PACK_2[2:], [up, down, right, left, far_x])
    a_right, a_left = shift_heads(to_right, 0, 1), shift_heads(to_left, 0, -1)
    b_up, b_down = shift_heads(to_up, 1, 0), shift_heads(to_down, -1, 0)
    up, to_right = lax.optimization_barrier((up, to_right))
    tables = tables_of(
        jnp.concatenate(
            [own_offset + jnp.arange(ROWS, dtype=jnp.int32), filled + 32 * ctx + jnp.arange(ASKED, dtype=jnp.int32)]
        )
    )
    pieces, w_query, w_key, w_value, tables = lax.optimization_barrier(
        (pieces, w_query, w_key, w_value, tables)
    )
    weights = hold(w_query, w_key.T, w_value.T)
    accs = project([context, up, down, right, left, far_y, far_x], PLAN_1, weights, None, True, True)
    q_share = question_project(pieces, weights, tables)

    a_right, a_left, accs, q_share = lax.optimization_barrier((a_right, a_left, accs, q_share))
    to_right, to_left = pack(PACK_3, [a_right, a_left])
    to_up, to_down = pack(PACK_3, [b_up, b_down])
    last = [
        shift_heads(to_right, 0, 1),
        shift_heads(to_left, 0, -1),
        shift_heads(to_up, 1, 0),
        shift_heads(to_down, -1, 0),
    ]
    accs = project([a_right, a_left, b_up, b_down], PLAN_2, weights, accs, True, True)

    (halves,) = project(last, PLAN_3, weights, accs, False, True, True, asked=q_share)
    (queries,) = project(last, PLAN_3, weights, accs, True, False, True, tables)
    partner = swap_heads(halves, 0, 1)
    q_asked = q_share[:, :512]
    q_other = swap_ctx(q_asked, 0, 1)
    partner, queries, q_other = lax.optimization_barrier((partner, queries, q_other))
    kv = key_value(halves, partner, *tables)

    below, above, across = shift_z(kv, 1), shift_z(kv, -1), shift_z(kv, 2)
    weighted, stats = own_attention(lengths, queries, kv)
    below, above, across, weighted = lax.optimization_barrier((below, above, across, weighted))
    nearer = jnp.where(z == 0, kv[:ROWS], jnp.where(z == 1, below[:ROWS], jnp.where(z == 2, across[:ROWS], above[:ROWS])))
    from_zero = lax.ppermute(nearer, "ctx", [(0, 1), (2, 3), (4, 5), (6, 7)])
    part, part_other = question_attention(lengths, q_asked, q_other, [kv, below, above, across])
    from_zero, part = lax.optimization_barrier((from_zero, part))
    context_attn = anchor_attention(lengths, queries, nearer, from_zero, weighted, stats)
    question_attn = merge(part, swap_ctx(part_other, 0, 1))
    return (context_attn, question_attn)


def solution(mesh):
    in_specs = (
        P("ctx", "heads"),
        P("ctx", None, "heads"),
        P(None, "heads"),
        P(None, "heads"),
        P(None, "heads"),
        P(),
        P(),
    )
    out_specs = (P("ctx", "heads"), P("ctx", "heads"))
    return jax.shard_map(
        per_device, mesh=mesh, in_specs=in_specs, out_specs=out_specs, check_vma=False
    )
```

```python
import functools

import jax
import jax.numpy as jnp
from jax import lax
from jax.experimental import pallas as pl
from jax.experimental.pallas import tpu as pltpu
from jax.sharding import PartitionSpec as P

HD = 128
ROPE_BASE = 500000.0
BF = jnp.bfloat16
F32 = jnp.float32
VMEM_LIMIT = 8 * 1024 * 1024
HOLD_LIMIT = 37 * 1024 * 1024
NEG = -1e30
SCALE2 = HD ** (-0.5) * 1.4426950408889634
ROWS = 512
ASKED = 32
ALL = ROWS + ASKED

HBM = pl.BlockSpec(memory_space=pltpu.HBM)
VM = pl.BlockSpec(memory_space=pltpu.VMEM)
SM = pl.BlockSpec(memory_space=pltpu.SMEM)


def shift_heads(array, dy, dx):
    pairs = [(i, ((i // 4 + dy) % 4) * 4 + (i % 4 + dx) % 4) for i in range(16)]
    return lax.ppermute(array, "heads", pairs)


def swap_heads(array, my, mx):
    pairs = [(i, ((i // 4) ^ my) * 4 + ((i % 4) ^ mx)) for i in range(16)]
    return lax.ppermute(array, "heads", pairs)


def swap_ctx(array, mz, mc):
    pairs = [(i, ((i // 2) ^ mz) * 2 + ((i % 2) ^ mc)) for i in range(8)]
    return lax.ppermute(array, "ctx", pairs)


def places():
    heads, ctx = lax.axis_index("heads"), lax.axis_index("ctx")
    return lax.shift_right_logical(heads, 2), heads & 3, lax.shift_right_logical(ctx, 1), ctx & 1


def pack_kernel(plan, n_in, *refs):
    ins, outs = refs[:n_in], refs[n_in:]
    for out, pieces in zip(outs, plan):
        row = 0
        for operand, start, count in pieces:
            out[row : row + count, :] = ins[operand][start : start + count, :]
            row += count


def pack(plan, ins):
    return pl.pallas_call(
        functools.partial(pack_kernel, plan, len(ins)),
        out_shape=[jax.ShapeDtypeStruct((sum(p[2] for p in pieces), 512), BF) for pieces in plan],
        in_specs=[VM] * len(ins),
        out_specs=[VM] * len(plan),
        compiler_params=pltpu.CompilerParams(vmem_limit_bytes=VMEM_LIMIT),
        cost_estimate=pl.CostEstimate(flops=0, bytes_accessed=1 << 20, transcendentals=0),
    )(*ins)


def hold_kernel(wq, wk, wv, q_out, kv_out, sem):
    copies = []
    for part in range(8):
        rows = pl.ds(part * 1024, 1024)
        copies.append(pltpu.make_async_copy(wq.at[rows, :], q_out.at[rows, :], sem.at[part]))
    for part in range(4):
        cols = pl.ds(part * 2048, 2048)
        copies.append(pltpu.make_async_copy(wk.at[:, cols], kv_out.at[pl.ds(0, 64), cols], sem.at[8 + part]))
        copies.append(pltpu.make_async_copy(wv.at[:, cols], kv_out.at[pl.ds(64, 64), cols], sem.at[12 + part]))
    for copy in copies:
        copy.start()
    for copy in copies:
        copy.wait()


def hold(wq, wk, wv):
    return pl.pallas_call(
        hold_kernel,
        out_shape=[jax.ShapeDtypeStruct((8192, 512), BF), jax.ShapeDtypeStruct((128, 8192), BF)],
        in_specs=[HBM] * 3,
        out_specs=[VM, VM],
        scratch_shapes=[pltpu.SemaphoreType.DMA((16,))],
        compiler_params=pltpu.CompilerParams(vmem_limit_bytes=HOLD_LIMIT),
        cost_estimate=pl.CostEstimate(flops=0, bytes_accessed=20 << 20, transcendentals=0),
    )(wq, wk, wv)


def turn(part, cos, sin):
    return (part * cos + pltpu.roll(part, HD // 2, 1) * sin).astype(BF)


def project_kernel(plan, n_x, with_q, with_kv, has_acc, finish, *refs):
    refs = list(refs)
    take = lambda count: [refs.pop(0) for _ in range(count)]
    xs = take(n_x)
    wq = take(1)[0] if with_q else None
    wkv = take(1)[0] if with_kv else None
    acc_q = take(1)[0] if has_acc and with_q else None
    acc_kv = take(1)[0] if has_acc and with_kv else None
    cos, sin = take(2) if finish and with_q else (None, None)
    asked = take(1)[0] if finish and with_kv else None
    q_out = take(1)[0] if with_q else None
    kv_out = take(1)[0] if with_kv else None
    q_sum = take(1)[0] if finish and with_q else q_out
    kv_sum = take(1)[0] if finish and with_kv else kv_out
    y, x, _, _ = places()
    if has_acc:
        if with_q:
            q_sum[...] = acc_q[...]
        if with_kv:
            kv_sum[...] = acc_kv[...]
    for slot, ((dy, dx), low, high, uses) in enumerate(plan):
        base = pl.multiple_of((((y + dy) & 3) * 4 + ((x + dx) & 3)) * 512, 512)
        parts = [xs[operand][pl.ds(start, count), :] for operand, start, count in uses]
        piece = parts[0] if len(parts) == 1 else jnp.concatenate(parts, axis=0)
        fresh = slot == 0 and not has_acc
        if with_kv:
            both = wkv[:, pl.ds(base, 512)]
            term = lax.dot_general(piece, both, (((1,), (1,)), ((), ())), preferred_element_type=F32)
            kv_sum[low:high, :] = term if fresh else kv_sum[low:high, :] + term
        if with_q:
            term = jnp.dot(piece, wq[pl.ds(base, 512), :], preferred_element_type=F32)
            q_sum[low:high, :] = term if fresh else q_sum[low:high, :] + term
    if finish and with_kv:
        kv_out[:ROWS, :] = kv_sum[...].astype(BF)
        kv_out[ROWS:, :] = asked[:, 512:640]
    if finish and with_q:
        for head in range(4):
            cols = slice(head * HD, (head + 1) * HD)
            q_out[:, cols] = turn(q_sum[:, cols], cos[:ROWS, :], sin[:ROWS, :])


def project(xs, plan, weights, accs, with_q, with_kv, finish=False, tables=None, asked=None):
    wq, wkv = weights
    operands, specs = list(xs), [VM] * len(xs)
    if with_q:
        operands.append(wq)
        specs.append(VM)
    if with_kv:
        operands.append(wkv)
        specs.append(VM)
    has_acc = accs is not None
    if has_acc:
        if with_q:
            operands.append(accs[0])
            specs.append(VM)
        if with_kv:
            operands.append(accs[1])
            specs.append(VM)
    if finish and with_q:
        operands += list(tables)
        specs += [VM, VM]
    if finish and with_kv:
        operands.append(asked)
        specs.append(VM)
    outs, scratch = [], []
    if with_q:
        outs.append(jax.ShapeDtypeStruct((ROWS, 512), BF if finish else F32))
        if finish:
            scratch.append(pltpu.VMEM((ROWS, 512), F32))
    if with_kv:
        outs.append(jax.ShapeDtypeStruct((ALL, 128), BF) if finish else jax.ShapeDtypeStruct((ROWS, 128), F32))
        if finish:
            scratch.append(pltpu.VMEM((ROWS, 128), F32))
    columns = (512 if with_q else 0) + (128 if with_kv else 0)
    used = sum(high - low for _, low, high, _ in plan)
    return pl.pallas_call(
        functools.partial(project_kernel, plan, len(xs), with_q, with_kv, has_acc, finish),
        out_shape=outs,
        in_specs=specs,
        out_specs=[VM] * len(outs),
        scratch_shapes=scratch,
        compiler_params=pltpu.CompilerParams(vmem_limit_bytes=VMEM_LIMIT),
        cost_estimate=pl.CostEstimate(
            flops=2 * used * 512 * columns, bytes_accessed=len(plan) * 512 * columns * 2, transcendentals=0
        ),
    )(*operands)


def question_project_kernel(pieces, wq, wkv, cos, sin, out):
    q_sum, kv_sum = None, None
    for place in range(16):
        base = place * 512
        piece = pieces[place]
        both = wkv[:, pl.ds(base, 512)]
        kv_term = lax.dot_general(piece, both, (((1,), (1,)), ((), ())), preferred_element_type=F32)
        q_term = jnp.dot(piece, wq[pl.ds(base, 512), :], preferred_element_type=F32)
        q_sum = q_term if q_sum is None else q_sum + q_term
        kv_sum = kv_term if kv_sum is None else kv_sum + kv_term
    for head in range(4):
        cols = slice(head * HD, (head + 1) * HD)
        out[:, cols] = turn(q_sum[:, cols], cos[ROWS : ROWS + 32, :], sin[ROWS : ROWS + 32, :])
    out[:, 512:640] = kv_sum.astype(BF)


def question_project(pieces, weights, tables):
    return pl.pallas_call(
        question_project_kernel,
        out_shape=jax.ShapeDtypeStruct((32, 640), BF),
        in_specs=[VM] * 5,
        out_specs=VM,
        compiler_params=pltpu.CompilerParams(vmem_limit_bytes=VMEM_LIMIT),
        cost_estimate=pl.CostEstimate(flops=2 * 256 * 8192 * 640, bytes_accessed=8192 * 640 * 2, transcendentals=0),
    )(pieces, *weights, *tables)


def key_value_kernel(own, partner, cos, sin, out):
    is_lower = (places()[1] & 1) == 0
    mine, other = own[...].astype(F32), partner[...].astype(F32)
    low = jnp.where(is_lower, mine, other)
    high = jnp.where(is_lower, other, mine)
    lane = lax.broadcasted_iota(jnp.int32, low.shape, 1)
    keys = jnp.where(lane < 64, low, pltpu.roll(high, 64, 1))
    values = jnp.where(lane < 64, pltpu.roll(low, 64, 1), high)
    out[:, :HD] = (keys * cos[...] + pltpu.roll(keys, 64, 1) * sin[...]).astype(BF)
    out[:, HD:] = values.astype(BF)


def key_value(own, partner, cos, sin):
    return pl.pallas_call(
        key_value_kernel,
        out_shape=jax.ShapeDtypeStruct((ALL, 2 * HD), BF),
        in_specs=[VM, VM, VM, VM],
        out_specs=VM,
        compiler_params=pltpu.CompilerParams(vmem_limit_bytes=VMEM_LIMIT),
    )(own, partner, cos, sin)


def scores_of(queries, keys):
    return lax.dot_general(queries, keys, (((1,), (1,)), ((), ())), preferred_element_type=F32)


def weights_of(scores, top):
    return jnp.exp2(scores * SCALE2 - top * SCALE2)


def columns_to_stats(columns):
    rows = columns[0].shape[0]
    lane = lax.broadcasted_iota(jnp.int32, (rows, 128), 1)
    stats = jnp.zeros((rows, 128), F32)
    for index, column in enumerate(columns):
        stats = jnp.where(lane == index, column, stats)
    return stats


def own_kernel(lengths, q, kv, weighted, stats):
    _, _, z, core = places()
    length = lengths[2 * z + core]
    for tile in range(2):
        rows = slice(tile * 256, tile * 256 + 256)
        width = 256 * (tile + 1)
        row = tile * 256 + lax.broadcasted_iota(jnp.int32, (256, width), 0)
        key = lax.broadcasted_iota(jnp.int32, (256, width), 1)
        bias = jnp.where((key <= row) & (key < length), 0.0, NEG)
        tops, totals = [], []
        for head in range(4):
            cols = slice(head * HD, (head + 1) * HD)
            s = scores_of(q[rows, cols], kv[:width, :HD]) + bias
            top = jnp.max(s, axis=1, keepdims=True)
            e = weights_of(s, top)
            totals.append(jnp.sum(e, axis=1, keepdims=True))
            tops.append(top)
            weighted[rows, cols] = jnp.dot(e.astype(BF), kv[:width, HD:], preferred_element_type=F32)
        stats[rows, :] = columns_to_stats(tops + totals)


def own_attention(lengths, q, kv):
    return pl.pallas_call(
        own_kernel,
        out_shape=[jax.ShapeDtypeStruct((512, 512), F32), jax.ShapeDtypeStruct((512, 128), F32)],
        in_specs=[SM, VM, VM],
        out_specs=[VM, VM],
        compiler_params=pltpu.CompilerParams(vmem_limit_bytes=VMEM_LIMIT),
        cost_estimate=pl.CostEstimate(flops=4 * 4 * 512 * 512 * 128, bytes_accessed=3 << 20, transcendentals=1 << 20),
    )(lengths, q, kv)


def anchor_kernel(lengths, q, kv_zero, kv_one, weighted, stats, out):
    _, _, z, core = places()
    length = lengths[2 * z + core]
    anchor_length = jnp.where(2 * z + core > 0, lengths[0], 0)
    first_core = core == 0
    kv = jnp.where(first_core, kv_zero[...], kv_one[...])
    keys, values = kv[:, :HD], kv[:, HD:]
    key = lax.broadcasted_iota(jnp.int32, (1, 512), 1)
    bias = jnp.where(key < anchor_length, 0.0, NEG)
    for tile in range(2):
        rows = slice(tile * 256, tile * 256 + 256)
        block = stats[rows, :]
        row = tile * 256 + lax.broadcasted_iota(jnp.int32, (256, HD), 0)
        for head in range(4):
            cols = slice(head * HD, (head + 1) * HD)
            s = scores_of(q[rows, cols], keys) + bias
            own_top, own_sum = block[:, head : head + 1], block[:, head + 4 : head + 5]
            top = jnp.maximum(own_top, jnp.max(s, axis=1, keepdims=True))
            e = weights_of(s, top)
            factor = weights_of(own_top, top)
            total = own_sum * factor + jnp.sum(e, axis=1, keepdims=True)
            both = weighted[rows, cols] * factor + jnp.dot(e.astype(BF), values, preferred_element_type=F32)
            out[rows, cols] = jnp.where(row < length, both / total, 0.0).astype(BF)


def anchor_attention(lengths, q, kv_zero, kv_one, weighted, stats):
    return pl.pallas_call(
        anchor_kernel,
        out_shape=jax.ShapeDtypeStruct((512, 512), BF),
        in_specs=[SM, VM, VM, VM, VM, VM],
        out_specs=VM,
        compiler_params=pltpu.CompilerParams(vmem_limit_bytes=VMEM_LIMIT),
        cost_estimate=pl.CostEstimate(flops=4 * 4 * 512 * 512 * 128, bytes_accessed=3 << 20, transcendentals=1 << 20),
    )(lengths, q, kv_zero, kv_one, weighted, stats)


def question_kernel(lengths_ref, q_own, q_other, kv_0, kv_1, kv_2, kv_3, out_own, out_other):
    kvs = (kv_0, kv_1, kv_2, kv_3)
    _, _, z, core = places()
    ctx = 2 * z + core
    blocks = [z, (z + 3) & 3, (z + 1) & 3, (z + 2) & 3]
    lengths = [lengths_ref[2 * block + core] for block in blocks]
    stacked = [q_own[:, h * HD : (h + 1) * HD] for h in range(4)]
    stacked += [q_other[:, h * HD : (h + 1) * HD] for h in range(4)]
    q = jnp.concatenate(stacked, axis=0)
    scores = []
    key = lax.broadcasted_iota(jnp.int32, (1, 512), 1)
    for kv, length in zip(kvs, lengths):
        scores.append(scores_of(q, kv[:ROWS, :HD]) + jnp.where(key < length, 0.0, NEG))
    row = lax.broadcasted_iota(jnp.int32, (256, 128), 0)
    lane = lax.broadcasted_iota(jnp.int32, (256, 128), 1)
    row_id = row % 32 + 32 * jnp.where(row < 128, ctx, ctx + 1 - 2 * core)
    block = jnp.where(lane < 64, jnp.where(lane < 32, blocks[0], blocks[1]), jnp.where(lane < 96, blocks[2], blocks[3]))
    key_id = lane % 32 + 32 * (2 * block + core)
    asked_keys = jnp.concatenate([kv[ROWS:, :HD] for kv in kvs], axis=0)
    asked_values = jnp.concatenate([kv[ROWS:, HD:] for kv in kvs], axis=0)
    scores.append(jnp.where(key_id <= row_id, scores_of(q, asked_keys), NEG))
    top = jnp.max(scores[-1], axis=1, keepdims=True)
    for s in scores[:-1]:
        top = jnp.maximum(top, jnp.max(s, axis=1, keepdims=True))
    values = [kv[:ROWS, HD:] for kv in kvs] + [asked_values]
    total = jnp.zeros((256, 1), F32)
    both = jnp.zeros((256, HD), F32)
    for s, value in zip(scores, values):
        e = weights_of(s, top)
        total = total + jnp.sum(e, axis=1, keepdims=True)
        both = both + jnp.dot(e.astype(BF), value, preferred_element_type=F32)
    for out, start in ((out_own, 0), (out_other, 128)):
        tops, totals = [], []
        for head in range(4):
            rows = slice(start + head * 32, start + head * 32 + 32)
            out[:, head * HD : (head + 1) * HD] = both[rows]
            tops.append(top[rows])
            totals.append(total[rows])
        out[:, 512:640] = columns_to_stats(tops + totals)


def question_attention(lengths, q_own, q_other, kvs):
    part = jax.ShapeDtypeStruct((32, 640), F32)
    return pl.pallas_call(
        question_kernel,
        out_shape=[part, part],
        in_specs=[SM] + [VM] * 6,
        out_specs=[VM, VM],
        compiler_params=pltpu.CompilerParams(vmem_limit_bytes=VMEM_LIMIT),
        cost_estimate=pl.CostEstimate(flops=4 * 256 * 2176 * 128, bytes_accessed=2 << 20, transcendentals=1 << 19),
    )(lengths, q_own, q_other, *kvs)


def merge_kernel(a, b, out):
    stat_a, stat_b = a[:, 512:640], b[:, 512:640]
    for head in range(4):
        cols = slice(head * HD, (head + 1) * HD)
        top_a, top_b = stat_a[:, head : head + 1], stat_b[:, head : head + 1]
        top = jnp.maximum(top_a, top_b)
        factor_a, factor_b = weights_of(top_a, top), weights_of(top_b, top)
        total = stat_a[:, head + 4 : head + 5] * factor_a + stat_b[:, head + 4 : head + 5] * factor_b
        out[:, cols] = ((a[:, cols] * factor_a + b[:, cols] * factor_b) / total).astype(BF)


def merge(a, b):
    return pl.pallas_call(
        merge_kernel,
        out_shape=jax.ShapeDtypeStruct((32, 512), BF),
        in_specs=[VM, VM],
        out_specs=VM,
        compiler_params=pltpu.CompilerParams(vmem_limit_bytes=VMEM_LIMIT),
    )(a, b)


PLAN_1 = [
    ((0, 0), 0, 512, [(0, 0, 512)]),
    ((-1, 0), 0, 512, [(1, 0, 512)]),
    ((1, 0), 0, 512, [(2, 0, 512)]),
    ((0, -1), 0, 512, [(3, 0, 512)]),
    ((0, 1), 0, 512, [(4, 0, 512)]),
    ((2, 0), 0, 256, [(5, 0, 256)]),
    ((0, 2), 256, 512, [(6, 0, 256)]),
]
PLAN_2 = [
    ((-1, -1), 0, 512, [(0, 0, 256), (2, 0, 256)]),
    ((1, -1), 0, 512, [(0, 256, 256), (3, 0, 256)]),
    ((-1, 1), 0, 512, [(1, 0, 256), (2, 256, 256)]),
    ((1, 1), 0, 512, [(1, 256, 256), (3, 256, 256)]),
    ((2, -1), 0, 256, [(0, 512, 256)]),
    ((2, 1), 0, 256, [(1, 512, 256)]),
    ((-1, 2), 256, 512, [(2, 512, 256)]),
    ((1, 2), 256, 512, [(3, 512, 256)]),
    ((0, 2), 0, 256, [(0, 768, 128), (1, 768, 128)]),
    ((2, 0), 256, 512, [(2, 768, 128), (3, 768, 128)]),
]
PLAN_3 = [
    ((2, 2), 0, 512, [(1, 128, 256), (3, 128, 256)]),
    ((-1, 2), 0, 256, [(0, 0, 256)]),
    ((1, 2), 0, 256, [(0, 256, 128), (1, 0, 128)]),
    ((2, -1), 256, 512, [(2, 0, 256)]),
    ((2, 1), 256, 512, [(2, 256, 128), (3, 0, 128)]),
]
NEAR_Y = [(0, 0, 256), (1, 0, 256), (4, 0, 256)]
NEAR_X = [(2, 256, 256), (3, 256, 256), (4, 0, 256)]
PACK_2 = [NEAR_Y + [(2, 0, 128)], NEAR_Y + [(3, 128, 128)], NEAR_X + [(0, 256, 128)], NEAR_X + [(1, 384, 128)]]
PACK_3 = [[(0, 0, 384)], [(1, 384, 384)]]


def tables_of(positions):
    inverse_freq = ROPE_BASE ** (-(jnp.arange(HD // 2, dtype=jnp.float32) * 2.0 / HD))
    inverse_freq = jnp.concatenate([inverse_freq, inverse_freq])
    phases = positions.astype(jnp.float32)[:, None] * inverse_freq[None, :]
    signs = jnp.where(jnp.arange(HD) < HD // 2, -1.0, 1.0).astype(jnp.float32)
    return jnp.cos(phases), jnp.sin(phases) * signs[None, :]


def shift_z(array, dz):
    pairs = [(i, ((i // 2 + dz) % 4) * 2 + i % 2) for i in range(8)]
    return lax.ppermute(array, "ctx", pairs)


def per_device(context, question, w_query, w_key, w_value, lengths, owner):
    ctx = lax.axis_index("ctx")
    z, core = lax.shift_right_logical(ctx, 1), ctx & 1
    ids = jnp.arange(8, dtype=jnp.int32)
    own_offset = jnp.sum(jnp.where(ids < ctx, lengths, 0))
    filled = jnp.sum(lengths)

    up = shift_heads(context, 1, 0)
    down = shift_heads(context, -1, 0)
    right = shift_heads(context, 0, 1)
    left = shift_heads(context, 0, -1)
    low, high = pack([[(0, 0, 256)], [(0, 256, 256)]], [context])
    far_y = shift_heads(low, 2, 0)
    low, asked = lax.optimization_barrier((low, question))
    up, high = lax.optimization_barrier((up, high))
    far_x = shift_heads(high, 0, 2)

    share = lax.all_to_all(asked[0].reshape(8, 32, 512), "ctx", 0, 0)
    share = lax.dynamic_index_in_dim(share, owner[0], 0, False)
    share = jnp.broadcast_to(share[None], (16, 32, 512))
    far_x, far_y, up, down, right, left, share = lax.optimization_barrier(
        (far_x, far_y, up, down, right, left, share)
    )
    pieces = lax.all_to_all(share, "heads", 0, 0)

    to_right, to_left = pack(PACK_2[:2], [up, down, right, left, far_y])
    to_up, to_down = pack(PACK_2[2:], [up, down, right, left, far_x])
    a_right, a_left = shift_heads(to_right, 0, 1), shift_heads(to_left, 0, -1)
    b_up, b_down = shift_heads(to_up, 1, 0), shift_heads(to_down, -1, 0)
    up, to_right = lax.optimization_barrier((up, to_right))
    tables = tables_of(
        jnp.concatenate(
            [own_offset + jnp.arange(ROWS, dtype=jnp.int32), filled + 32 * ctx + jnp.arange(ASKED, dtype=jnp.int32)]
        )
    )
    pieces, w_query, w_key, w_value, tables = lax.optimization_barrier(
        (pieces, w_query, w_key, w_value, tables)
    )
    weights = hold(w_query, w_key.T, w_value.T)
    accs = project([context, up, down, right, left, far_y, far_x], PLAN_1, weights, None, True, True)
    q_share = question_project(pieces, weights, tables)

    a_right, a_left, accs, q_share = lax.optimization_barrier((a_right, a_left, accs, q_share))
    to_right, to_left = pack(PACK_3, [a_right, a_left])
    to_up, to_down = pack(PACK_3, [b_up, b_down])
    last = [
        shift_heads(to_right, 0, 1),
        shift_heads(to_left, 0, -1),
        shift_heads(to_up, 1, 0),
        shift_heads(to_down, -1, 0),
    ]
    accs = project([a_right, a_left, b_up, b_down], PLAN_2, weights, accs, True, True)

    (halves,) = project(last, PLAN_3, weights, accs, False, True, True, asked=q_share)
    (queries,) = project(last, PLAN_3, weights, accs, True, False, True, tables)
    partner = swap_heads(halves, 0, 1)
    q_asked = q_share[:, :512]
    q_other = swap_ctx(q_asked, 0, 1)
    partner, queries, q_other = lax.optimization_barrier((partner, queries, q_other))
    kv = key_value(halves, partner, *tables)

    below, above, across = shift_z(kv, 1), shift_z(kv, -1), shift_z(kv, 2)
    weighted, stats = own_attention(lengths, queries, kv)
    below, above, across, weighted = lax.optimization_barrier((below, above, across, weighted))
    nearer = jnp.where(z == 0, kv[:ROWS], jnp.where(z == 1, below[:ROWS], jnp.where(z == 2, across[:ROWS], above[:ROWS])))
    from_zero = lax.ppermute(nearer, "ctx", [(0, 1), (2, 3), (4, 5), (6, 7)])
    part, part_other = question_attention(lengths, q_asked, q_other, [kv, below, above, across])
    from_zero, part = lax.optimization_barrier((from_zero, part))
    context_attn = anchor_attention(lengths, queries, nearer, from_zero, weighted, stats)
    question_attn = merge(part, swap_ctx(part_other, 0, 1))
    return (context_attn, question_attn)


def solution(mesh):
    in_specs = (
        P("ctx", "heads"),
        P("ctx", None, "heads"),
        P(None, "heads"),
        P(None, "heads"),
        P(None, "heads"),
        P(),
        P(),
    )
    out_specs = (P("ctx", "heads"), P("ctx", "heads"))
    return jax.shard_map(
        per_device, mesh=mesh, in_specs=in_specs, out_specs=out_specs, check_vma=False
    )
```

```python
import functools

import jax
import jax.numpy as jnp
from jax import lax
from jax.experimental import pallas as pl
from jax.experimental.pallas import tpu as pltpu
from jax.sharding import PartitionSpec as P

HD = 128
ROPE_BASE = 500000.0
BF = jnp.bfloat16
F32 = jnp.float32
VMEM_LIMIT = 8 * 1024 * 1024
HOLD_LIMIT = 37 * 1024 * 1024
NEG = -1e30
SCALE2 = HD ** (-0.5) * 1.4426950408889634
ROWS = 512
ASKED = 32
ALL = ROWS + ASKED

HBM = pl.BlockSpec(memory_space=pltpu.HBM)
VM = pl.BlockSpec(memory_space=pltpu.VMEM)
SM = pl.BlockSpec(memory_space=pltpu.SMEM)


def shift_heads(array, dy, dx):
    pairs = [(i, ((i // 4 + dy) % 4) * 4 + (i % 4 + dx) % 4) for i in range(16)]
    return lax.ppermute(array, "heads", pairs)


def swap_heads(array, my, mx):
    pairs = [(i, ((i // 4) ^ my) * 4 + ((i % 4) ^ mx)) for i in range(16)]
    return lax.ppermute(array, "heads", pairs)


def swap_ctx(array, mz, mc):
    pairs = [(i, ((i // 2) ^ mz) * 2 + ((i % 2) ^ mc)) for i in range(8)]
    return lax.ppermute(array, "ctx", pairs)


def places():
    heads, ctx = lax.axis_index("heads"), lax.axis_index("ctx")
    return lax.shift_right_logical(heads, 2), heads & 3, lax.shift_right_logical(ctx, 1), ctx & 1


def pack_kernel(plan, n_in, *refs):
    ins, outs = refs[:n_in], refs[n_in:]
    for out, pieces in zip(outs, plan):
        row = 0
        for operand, start, count in pieces:
            out[row : row + count, :] = ins[operand][start : start + count, :]
            row += count


def pack(plan, ins):
    return pl.pallas_call(
        functools.partial(pack_kernel, plan, len(ins)),
        out_shape=[jax.ShapeDtypeStruct((sum(p[2] for p in pieces), 512), BF) for pieces in plan],
        in_specs=[VM] * len(ins),
        out_specs=[VM] * len(plan),
        compiler_params=pltpu.CompilerParams(vmem_limit_bytes=VMEM_LIMIT),
        cost_estimate=pl.CostEstimate(flops=0, bytes_accessed=1 << 20, transcendentals=0),
    )(*ins)


def hold_kernel(wq, wk, wv, q_out, kv_out, sem):
    copies = []
    for part in range(8):
        rows = pl.ds(part * 1024, 1024)
        copies.append(pltpu.make_async_copy(wq.at[rows, :], q_out.at[rows, :], sem.at[part]))
    for part in range(4):
        cols = pl.ds(part * 2048, 2048)
        copies.append(pltpu.make_async_copy(wk.at[:, cols], kv_out.at[pl.ds(0, 64), cols], sem.at[8 + part]))
        copies.append(pltpu.make_async_copy(wv.at[:, cols], kv_out.at[pl.ds(64, 64), cols], sem.at[12 + part]))
    for copy in copies:
        copy.start()
    for copy in copies:
        copy.wait()


def hold(wq, wk, wv):
    return pl.pallas_call(
        hold_kernel,
        out_shape=[jax.ShapeDtypeStruct((8192, 512), BF), jax.ShapeDtypeStruct((128, 8192), BF)],
        in_specs=[HBM] * 3,
        out_specs=[VM, VM],
        scratch_shapes=[pltpu.SemaphoreType.DMA((16,))],
        compiler_params=pltpu.CompilerParams(vmem_limit_bytes=HOLD_LIMIT),
        cost_estimate=pl.CostEstimate(flops=0, bytes_accessed=20 << 20, transcendentals=0),
    )(wq, wk, wv)


def turn(part, cos, sin):
    return (part * cos + pltpu.roll(part, HD // 2, 1) * sin).astype(BF)


def project_kernel(plan, n_x, with_q, with_kv, has_acc, finish, *refs):
    refs = list(refs)
    take = lambda count: [refs.pop(0) for _ in range(count)]
    xs = take(n_x)
    wq = take(1)[0] if with_q else None
    wkv = take(1)[0] if with_kv else None
    acc_q = take(1)[0] if has_acc and with_q else None
    acc_kv = take(1)[0] if has_acc and with_kv else None
    cos, sin = take(2) if finish and with_q else (None, None)
    asked = take(1)[0] if finish and with_kv else None
    q_out = take(1)[0] if with_q else None
    kv_out = take(1)[0] if with_kv else None
    q_sum = take(1)[0] if finish and with_q else q_out
    kv_sum = take(1)[0] if finish and with_kv else kv_out
    y, x, _, _ = places()
    if has_acc:
        if with_q:
            q_sum[...] = acc_q[...]
        if with_kv:
            kv_sum[...] = acc_kv[...]
    for slot, ((dy, dx), low, high, uses) in enumerate(plan):
        base = pl.multiple_of((((y + dy) & 3) * 4 + ((x + dx) & 3)) * 512, 512)
        parts = [xs[operand][pl.ds(start, count), :] for operand, start, count in uses]
        piece = parts[0] if len(parts) == 1 else jnp.concatenate(parts, axis=0)
        fresh = slot == 0 and not has_acc
        if with_kv:
            both = wkv[:, pl.ds(base, 512)]
            term = lax.dot_general(piece, both, (((1,), (1,)), ((), ())), preferred_element_type=F32)
            kv_sum[low:high, :] = term if fresh else kv_sum[low:high, :] + term
        if with_q:
            term = jnp.dot(piece, wq[pl.ds(base, 512), :], preferred_element_type=F32)
            q_sum[low:high, :] = term if fresh else q_sum[low:high, :] + term
    if finish and with_kv:
        kv_out[:ROWS, :] = kv_sum[...].astype(BF)
        kv_out[ROWS:, :] = asked[:, 512:640]
    if finish and with_q:
        for head in range(4):
            cols = slice(head * HD, (head + 1) * HD)
            q_out[:, cols] = turn(q_sum[:, cols], cos[:ROWS, :], sin[:ROWS, :])


def project(xs, plan, weights, accs, with_q, with_kv, finish=False, tables=None, asked=None):
    wq, wkv = weights
    operands, specs = list(xs), [VM] * len(xs)
    if with_q:
        operands.append(wq)
        specs.append(VM)
    if with_kv:
        operands.append(wkv)
        specs.append(VM)
    has_acc = accs is not None
    if has_acc:
        if with_q:
            operands.append(accs[0])
            specs.append(VM)
        if with_kv:
            operands.append(accs[1])
            specs.append(VM)
    if finish and with_q:
        operands += list(tables)
        specs += [VM, VM]
    if finish and with_kv:
        operands.append(asked)
        specs.append(VM)
    outs, scratch = [], []
    if with_q:
        outs.append(jax.ShapeDtypeStruct((ROWS, 512), BF if finish else F32))
        if finish:
            scratch.append(pltpu.VMEM((ROWS, 512), F32))
    if with_kv:
        outs.append(jax.ShapeDtypeStruct((ALL, 128), BF) if finish else jax.ShapeDtypeStruct((ROWS, 128), F32))
        if finish:
            scratch.append(pltpu.VMEM((ROWS, 128), F32))
    columns = (512 if with_q else 0) + (128 if with_kv else 0)
    used = sum(high - low for _, low, high, _ in plan)
    return pl.pallas_call(
        functools.partial(project_kernel, plan, len(xs), with_q, with_kv, has_acc, finish),
        out_shape=outs,
        in_specs=specs,
        out_specs=[VM] * len(outs),
        scratch_shapes=scratch,
        compiler_params=pltpu.CompilerParams(vmem_limit_bytes=VMEM_LIMIT),
        cost_estimate=pl.CostEstimate(
            flops=2 * used * 512 * columns, bytes_accessed=len(plan) * 512 * columns * 2, transcendentals=0
        ),
    )(*operands)


def question_project_kernel(pieces, wq, wkv, cos, sin, out):
    q_sum, kv_sum = None, None
    for place in range(16):
        base = place * 512
        piece = pieces[place]
        both = wkv[:, pl.ds(base, 512)]
        kv_term = lax.dot_general(piece, both, (((1,), (1,)), ((), ())), preferred_element_type=F32)
        q_term = jnp.dot(piece, wq[pl.ds(base, 512), :], preferred_element_type=F32)
        q_sum = q_term if q_sum is None else q_sum + q_term
        kv_sum = kv_term if kv_sum is None else kv_sum + kv_term
    for head in range(4):
        cols = slice(head * HD, (head + 1) * HD)
        out[:, cols] = turn(q_sum[:, cols], cos[ROWS : ROWS + 32, :], sin[ROWS : ROWS + 32, :])
    out[:, 512:640] = kv_sum.astype(BF)


def question_project(pieces, weights, tables):
    return pl.pallas_call(
        question_project_kernel,
        out_shape=jax.ShapeDtypeStruct((32, 640), BF),
        in_specs=[VM] * 5,
        out_specs=VM,
        compiler_params=pltpu.CompilerParams(vmem_limit_bytes=VMEM_LIMIT),
        cost_estimate=pl.CostEstimate(flops=2 * 256 * 8192 * 640, bytes_accessed=8192 * 640 * 2, transcendentals=0),
    )(pieces, *weights, *tables)


def key_value_kernel(own, partner, cos, sin, out):
    is_lower = (places()[1] & 1) == 0
    mine, other = own[...].astype(F32), partner[...].astype(F32)
    low = jnp.where(is_lower, mine, other)
    high = jnp.where(is_lower, other, mine)
    lane = lax.broadcasted_iota(jnp.int32, low.shape, 1)
    keys = jnp.where(lane < 64, low, pltpu.roll(high, 64, 1))
    values = jnp.where(lane < 64, pltpu.roll(low, 64, 1), high)
    out[:, :HD] = (keys * cos[...] + pltpu.roll(keys, 64, 1) * sin[...]).astype(BF)
    out[:, HD:] = values.astype(BF)


def key_value(own, partner, cos, sin):
    return pl.pallas_call(
        key_value_kernel,
        out_shape=jax.ShapeDtypeStruct((ALL, 2 * HD), BF),
        in_specs=[VM, VM, VM, VM],
        out_specs=VM,
        compiler_params=pltpu.CompilerParams(vmem_limit_bytes=VMEM_LIMIT),
    )(own, partner, cos, sin)


def scores_of(queries, keys):
    return lax.dot_general(queries, keys, (((1,), (1,)), ((), ())), preferred_element_type=F32)


def weights_of(scores, top):
    return jnp.exp2(scores * SCALE2 - top * SCALE2)


def columns_to_stats(columns):
    rows = columns[0].shape[0]
    lane = lax.broadcasted_iota(jnp.int32, (rows, 128), 1)
    stats = jnp.zeros((rows, 128), F32)
    for index, column in enumerate(columns):
        stats = jnp.where(lane == index, column, stats)
    return stats


def own_kernel(lengths, q, kv, weighted, stats):
    _, _, z, core = places()
    length = lengths[2 * z + core]
    for tile in range(2):
        rows = slice(tile * 256, tile * 256 + 256)
        width = 256 * (tile + 1)
        row = tile * 256 + lax.broadcasted_iota(jnp.int32, (256, width), 0)
        key = lax.broadcasted_iota(jnp.int32, (256, width), 1)
        bias = jnp.where((key <= row) & (key < length), 0.0, NEG)
        tops, totals = [], []
        for head in range(4):
            cols = slice(head * HD, (head + 1) * HD)
            s = scores_of(q[rows, cols], kv[:width, :HD]) + bias
            top = jnp.max(s, axis=1, keepdims=True)
            e = weights_of(s, top)
            totals.append(jnp.sum(e, axis=1, keepdims=True))
            tops.append(top)
            weighted[rows, cols] = jnp.dot(e.astype(BF), kv[:width, HD:], preferred_element_type=F32)
        stats[rows, :] = columns_to_stats(tops + totals)


def own_attention(lengths, q, kv):
    return pl.pallas_call(
        own_kernel,
        out_shape=[jax.ShapeDtypeStruct((512, 512), F32), jax.ShapeDtypeStruct((512, 128), F32)],
        in_specs=[SM, VM, VM],
        out_specs=[VM, VM],
        compiler_params=pltpu.CompilerParams(vmem_limit_bytes=VMEM_LIMIT),
        cost_estimate=pl.CostEstimate(flops=4 * 4 * 512 * 512 * 128, bytes_accessed=3 << 20, transcendentals=1 << 20),
    )(lengths, q, kv)


def anchor_kernel(lengths, q, kv_zero, kv_one, weighted, stats, out):
    _, _, z, core = places()
    length = lengths[2 * z + core]
    anchor_length = jnp.where(2 * z + core > 0, lengths[0], 0)
    first_core = core == 0
    kv = jnp.where(first_core, kv_zero[...], kv_one[...])
    keys, values = kv[:, :HD], kv[:, HD:]
    key = lax.broadcasted_iota(jnp.int32, (1, 512), 1)
    bias = jnp.where(key < anchor_length, 0.0, NEG)
    for tile in range(2):
        rows = slice(tile * 256, tile * 256 + 256)
        block = stats[rows, :]
        row = tile * 256 + lax.broadcasted_iota(jnp.int32, (256, HD), 0)
        for head in range(4):
            cols = slice(head * HD, (head + 1) * HD)
            s = scores_of(q[rows, cols], keys) + bias
            own_top, own_sum = block[:, head : head + 1], block[:, head + 4 : head + 5]
            top = jnp.maximum(own_top, jnp.max(s, axis=1, keepdims=True))
            e = weights_of(s, top)
            factor = weights_of(own_top, top)
            total = own_sum * factor + jnp.sum(e, axis=1, keepdims=True)
            both = weighted[rows, cols] * factor + jnp.dot(e.astype(BF), values, preferred_element_type=F32)
            out[rows, cols] = jnp.where(row < length, both / total, 0.0).astype(BF)


def anchor_attention(lengths, q, kv_zero, kv_one, weighted, stats):
    return pl.pallas_call(
        anchor_kernel,
        out_shape=jax.ShapeDtypeStruct((512, 512), BF),
        in_specs=[SM, VM, VM, VM, VM, VM],
        out_specs=VM,
        compiler_params=pltpu.CompilerParams(vmem_limit_bytes=VMEM_LIMIT),
        cost_estimate=pl.CostEstimate(flops=4 * 4 * 512 * 512 * 128, bytes_accessed=3 << 20, transcendentals=1 << 20),
    )(lengths, q, kv_zero, kv_one, weighted, stats)


def question_kernel(lengths_ref, q_own, q_other, kv_0, kv_1, kv_2, kv_3, out_own, out_other):
    kvs = (kv_0, kv_1, kv_2, kv_3)
    _, _, z, core = places()
    ctx = 2 * z + core
    blocks = [z, (z + 3) & 3, (z + 1) & 3, (z + 2) & 3]
    lengths = [lengths_ref[2 * block + core] for block in blocks]
    stacked = [q_own[:, h * HD : (h + 1) * HD] for h in range(4)]
    stacked += [q_other[:, h * HD : (h + 1) * HD] for h in range(4)]
    q = jnp.concatenate(stacked, axis=0)
    scores = []
    key = lax.broadcasted_iota(jnp.int32, (1, 512), 1)
    for kv, length in zip(kvs, lengths):
        scores.append(scores_of(q, kv[:ROWS, :HD]) + jnp.where(key < length, 0.0, NEG))
    row = lax.broadcasted_iota(jnp.int32, (256, 128), 0)
    lane = lax.broadcasted_iota(jnp.int32, (256, 128), 1)
    row_id = row % 32 + 32 * jnp.where(row < 128, ctx, ctx + 1 - 2 * core)
    block = jnp.where(lane < 64, jnp.where(lane < 32, blocks[0], blocks[1]), jnp.where(lane < 96, blocks[2], blocks[3]))
    key_id = lane % 32 + 32 * (2 * block + core)
    asked_keys = jnp.concatenate([kv[ROWS:, :HD] for kv in kvs], axis=0)
    asked_values = jnp.concatenate([kv[ROWS:, HD:] for kv in kvs], axis=0)
    scores.append(jnp.where(key_id <= row_id, scores_of(q, asked_keys), NEG))
    top = jnp.max(scores[-1], axis=1, keepdims=True)
    for s in scores[:-1]:
        top = jnp.maximum(top, jnp.max(s, axis=1, keepdims=True))
    values = [kv[:ROWS, HD:] for kv in kvs] + [asked_values]
    total = jnp.zeros((256, 1), F32)
    both = jnp.zeros((256, HD), F32)
    for s, value in zip(scores, values):
        e = weights_of(s, top)
        total = total + jnp.sum(e, axis=1, keepdims=True)
        both = both + jnp.dot(e.astype(BF), value, preferred_element_type=F32)
    for out, start in ((out_own, 0), (out_other, 128)):
        tops, totals = [], []
        for head in range(4):
            rows = slice(start + head * 32, start + head * 32 + 32)
            out[:, head * HD : (head + 1) * HD] = both[rows]
            tops.append(top[rows])
            totals.append(total[rows])
        out[:, 512:640] = columns_to_stats(tops + totals)


def question_attention(lengths, q_own, q_other, kvs):
    part = jax.ShapeDtypeStruct((32, 640), F32)
    return pl.pallas_call(
        question_kernel,
        out_shape=[part, part],
        in_specs=[SM] + [VM] * 6,
        out_specs=[VM, VM],
        compiler_params=pltpu.CompilerParams(vmem_limit_bytes=VMEM_LIMIT),
        cost_estimate=pl.CostEstimate(flops=4 * 256 * 2176 * 128, bytes_accessed=2 << 20, transcendentals=1 << 19),
    )(lengths, q_own, q_other, *kvs)


def merge_kernel(a, b, out):
    stat_a, stat_b = a[:, 512:640], b[:, 512:640]
    for head in range(4):
        cols = slice(head * HD, (head + 1) * HD)
        top_a, top_b = stat_a[:, head : head + 1], stat_b[:, head : head + 1]
        top = jnp.maximum(top_a, top_b)
        factor_a, factor_b = weights_of(top_a, top), weights_of(top_b, top)
        total = stat_a[:, head + 4 : head + 5] * factor_a + stat_b[:, head + 4 : head + 5] * factor_b
        out[:, cols] = ((a[:, cols] * factor_a + b[:, cols] * factor_b) / total).astype(BF)


def merge(a, b):
    return pl.pallas_call(
        merge_kernel,
        out_shape=jax.ShapeDtypeStruct((32, 512), BF),
        in_specs=[VM, VM],
        out_specs=VM,
        compiler_params=pltpu.CompilerParams(vmem_limit_bytes=VMEM_LIMIT),
    )(a, b)


PLAN_1 = [
    ((0, 0), 0, 512, [(0, 0, 512)]),
    ((-1, 0), 0, 512, [(1, 0, 512)]),
    ((1, 0), 0, 512, [(2, 0, 512)]),
    ((0, -1), 0, 512, [(3, 0, 512)]),
    ((0, 1), 0, 512, [(4, 0, 512)]),
    ((2, 0), 0, 288, [(5, 0, 288)]),
    ((0, 2), 288, 512, [(6, 0, 224)]),
]
PLAN_2 = [
    ((-1, -1), 0, 512, [(0, 0, 288), (2, 0, 224)]),
    ((1, -1), 0, 512, [(0, 288, 288), (3, 0, 224)]),
    ((-1, 1), 0, 512, [(1, 0, 288), (2, 224, 224)]),
    ((1, 1), 0, 512, [(1, 288, 288), (3, 224, 224)]),
    ((2, -1), 0, 288, [(0, 576, 288)]),
    ((2, 1), 0, 288, [(1, 576, 288)]),
    ((-1, 2), 288, 512, [(2, 448, 224)]),
    ((1, 2), 288, 512, [(3, 448, 224)]),
    ((0, 2), 0, 288, [(0, 864, 144), (1, 864, 144)]),
    ((2, 0), 288, 512, [(2, 672, 112), (3, 672, 112)]),
]
PLAN_3 = [
    ((2, 2), 0, 512, [(1, 144, 288), (3, 112, 224)]),
    ((-1, 2), 0, 288, [(0, 0, 288)]),
    ((1, 2), 0, 288, [(0, 288, 144), (1, 0, 144)]),
    ((2, -1), 288, 512, [(2, 0, 224)]),
    ((2, 1), 288, 512, [(2, 224, 112), (3, 0, 112)]),
]
NEAR_Y = [(0, 0, 288), (1, 0, 288), (4, 0, 288)]
NEAR_X = [(2, 288, 224), (3, 288, 224), (4, 0, 224)]
PACK_2 = [NEAR_Y + [(2, 0, 144)], NEAR_Y + [(3, 144, 144)], NEAR_X + [(0, 288, 112)], NEAR_X + [(1, 400, 112)]]
PACK_3_X = [[(0, 0, 432)], [(1, 432, 432)]]
PACK_3_Y = [[(0, 0, 336)], [(1, 336, 336)]]


def tables_of(positions):
    inverse_freq = ROPE_BASE ** (-(jnp.arange(HD // 2, dtype=jnp.float32) * 2.0 / HD))
    inverse_freq = jnp.concatenate([inverse_freq, inverse_freq])
    phases = positions.astype(jnp.float32)[:, None] * inverse_freq[None, :]
    signs = jnp.where(jnp.arange(HD) < HD // 2, -1.0, 1.0).astype(jnp.float32)
    return jnp.cos(phases), jnp.sin(phases) * signs[None, :]


def shift_z(array, dz):
    pairs = [(i, ((i // 2 + dz) % 4) * 2 + i % 2) for i in range(8)]
    return lax.ppermute(array, "ctx", pairs)


def per_device(context, question, w_query, w_key, w_value, lengths, owner):
    ctx = lax.axis_index("ctx")
    z, core = lax.shift_right_logical(ctx, 1), ctx & 1
    ids = jnp.arange(8, dtype=jnp.int32)
    own_offset = jnp.sum(jnp.where(ids < ctx, lengths, 0))
    filled = jnp.sum(lengths)

    up = shift_heads(context, 1, 0)
    down = shift_heads(context, -1, 0)
    right = shift_heads(context, 0, 1)
    left = shift_heads(context, 0, -1)
    low, high = pack([[(0, 0, 288)], [(0, 288, 224)]], [context])
    far_y = shift_heads(low, 2, 0)
    up, high = lax.optimization_barrier((up, high))
    far_x = shift_heads(high, 0, 2)

    share = lax.all_to_all(question[0].reshape(8, 32, 512), "ctx", 0, 0)
    share = lax.dynamic_index_in_dim(share, owner[0], 0, False)
    share = jnp.broadcast_to(share[None], (16, 32, 512))
    pieces = lax.all_to_all(share, "heads", 0, 0)
    up, pieces = lax.optimization_barrier((up, pieces))

    to_right, to_left = pack(PACK_2[:2], [up, down, right, left, far_y])
    to_up, to_down = pack(PACK_2[2:], [up, down, right, left, far_x])
    a_right, a_left = shift_heads(to_right, 0, 1), shift_heads(to_left, 0, -1)
    b_up, b_down = shift_heads(to_up, 1, 0), shift_heads(to_down, -1, 0)
    up, to_right = lax.optimization_barrier((up, to_right))
    tables = tables_of(
        jnp.concatenate(
            [own_offset + jnp.arange(ROWS, dtype=jnp.int32), filled + 32 * ctx + jnp.arange(ASKED, dtype=jnp.int32)]
        )
    )
    pieces, w_query, w_key, w_value, tables = lax.optimization_barrier(
        (pieces, w_query, w_key, w_value, tables)
    )
    weights = hold(w_query, w_key.T, w_value.T)
    accs = project([context, up, down, right, left, far_y, far_x], PLAN_1, weights, None, True, True)
    q_share = question_project(pieces, weights, tables)

    a_right, a_left, accs, q_share = lax.optimization_barrier((a_right, a_left, accs, q_share))
    to_right, to_left = pack(PACK_3_X, [a_right, a_left])
    to_up, to_down = pack(PACK_3_Y, [b_up, b_down])
    last = [
        shift_heads(to_right, 0, 1),
        shift_heads(to_left, 0, -1),
        shift_heads(to_up, 1, 0),
        shift_heads(to_down, -1, 0),
    ]
    accs = project([a_right, a_left, b_up, b_down], PLAN_2, weights, accs, True, True)

    (halves,) = project(last, PLAN_3, weights, accs, False, True, True, asked=q_share)
    (queries,) = project(last, PLAN_3, weights, accs, True, False, True, tables)
    partner = swap_heads(halves, 0, 1)
    q_asked = q_share[:, :512]
    q_other = swap_ctx(q_asked, 0, 1)
    partner, queries, q_other = lax.optimization_barrier((partner, queries, q_other))
    kv = key_value(halves, partner, *tables)

    below, above, across = shift_z(kv, 1), shift_z(kv, -1), shift_z(kv, 2)
    weighted, stats = own_attention(lengths, queries, kv)
    below, above, across, weighted = lax.optimization_barrier((below, above, across, weighted))
    nearer = jnp.where(z == 0, kv[:ROWS], jnp.where(z == 1, below[:ROWS], jnp.where(z == 2, across[:ROWS], above[:ROWS])))
    from_zero = lax.ppermute(nearer, "ctx", [(0, 1), (2, 3), (4, 5), (6, 7)])
    part, part_other = question_attention(lengths, q_asked, q_other, [kv, below, above, across])
    from_zero, part = lax.optimization_barrier((from_zero, part))
    context_attn = anchor_attention(lengths, queries, nearer, from_zero, weighted, stats)
    question_attn = merge(part, swap_ctx(part_other, 0, 1))
    return (context_attn, question_attn)


def solution(mesh):
    in_specs = (
        P("ctx", "heads"),
        P("ctx", None, "heads"),
        P(None, "heads"),
        P(None, "heads"),
        P(None, "heads"),
        P(),
        P(),
    )
    out_specs = (P("ctx", "heads"), P("ctx", "heads"))
    return jax.shard_map(
        per_device, mesh=mesh, in_specs=in_specs, out_specs=out_specs, check_vma=False
    )
```

```python
import functools

import jax
import jax.numpy as jnp
from jax import lax
from jax.experimental import pallas as pl
from jax.experimental.pallas import tpu as pltpu
from jax.sharding import PartitionSpec as P

HD = 128
ROPE_BASE = 500000.0
BF = jnp.bfloat16
F32 = jnp.float32
VMEM_LIMIT = 8 * 1024 * 1024
HOLD_LIMIT = 37 * 1024 * 1024
NEG = -1e30
SCALE2 = HD ** (-0.5) * 1.4426950408889634
ROWS = 512
ASKED = 32
ALL = ROWS + ASKED

HBM = pl.BlockSpec(memory_space=pltpu.HBM)
VM = pl.BlockSpec(memory_space=pltpu.VMEM)
SM = pl.BlockSpec(memory_space=pltpu.SMEM)


def shift_heads(array, dy, dx):
    pairs = [(i, ((i // 4 + dy) % 4) * 4 + (i % 4 + dx) % 4) for i in range(16)]
    return lax.ppermute(array, "heads", pairs)


def swap_heads(array, my, mx):
    pairs = [(i, ((i // 4) ^ my) * 4 + ((i % 4) ^ mx)) for i in range(16)]
    return lax.ppermute(array, "heads", pairs)


def swap_ctx(array, mz, mc):
    pairs = [(i, ((i // 2) ^ mz) * 2 + ((i % 2) ^ mc)) for i in range(8)]
    return lax.ppermute(array, "ctx", pairs)


def places():
    heads, ctx = lax.axis_index("heads"), lax.axis_index("ctx")
    return lax.shift_right_logical(heads, 2), heads & 3, lax.shift_right_logical(ctx, 1), ctx & 1


def pack_kernel(plan, n_in, *refs):
    ins, outs = refs[:n_in], refs[n_in:]
    for out, pieces in zip(outs, plan):
        row = 0
        for operand, start, count in pieces:
            out[row : row + count, :] = ins[operand][start : start + count, :]
            row += count


def pack(plan, ins):
    return pl.pallas_call(
        functools.partial(pack_kernel, plan, len(ins)),
        out_shape=[jax.ShapeDtypeStruct((sum(p[2] for p in pieces), 512), BF) for pieces in plan],
        in_specs=[VM] * len(ins),
        out_specs=[VM] * len(plan),
        compiler_params=pltpu.CompilerParams(vmem_limit_bytes=VMEM_LIMIT),
        cost_estimate=pl.CostEstimate(flops=0, bytes_accessed=1 << 20, transcendentals=0),
    )(*ins)


def hold_kernel(wq, wk, wv, q_out, kv_out, sem):
    copies = []
    for part in range(8):
        rows = pl.ds(part * 1024, 1024)
        copies.append(pltpu.make_async_copy(wq.at[rows, :], q_out.at[rows, :], sem.at[part]))
    for part in range(4):
        cols = pl.ds(part * 2048, 2048)
        copies.append(pltpu.make_async_copy(wk.at[:, cols], kv_out.at[pl.ds(0, 64), cols], sem.at[8 + part]))
        copies.append(pltpu.make_async_copy(wv.at[:, cols], kv_out.at[pl.ds(64, 64), cols], sem.at[12 + part]))
    for copy in copies:
        copy.start()
    for copy in copies:
        copy.wait()


def hold(wq, wk, wv):
    return pl.pallas_call(
        hold_kernel,
        out_shape=[jax.ShapeDtypeStruct((8192, 512), BF), jax.ShapeDtypeStruct((128, 8192), BF)],
        in_specs=[HBM] * 3,
        out_specs=[VM, VM],
        scratch_shapes=[pltpu.SemaphoreType.DMA((16,))],
        compiler_params=pltpu.CompilerParams(vmem_limit_bytes=HOLD_LIMIT),
        cost_estimate=pl.CostEstimate(flops=0, bytes_accessed=20 << 20, transcendentals=0),
    )(wq, wk, wv)


def turn(part, cos, sin):
    return (part * cos + pltpu.roll(part, HD // 2, 1) * sin).astype(BF)


def project_kernel(plan, n_x, with_q, with_kv, has_acc, finish, *refs):
    refs = list(refs)
    take = lambda count: [refs.pop(0) for _ in range(count)]
    xs = take(n_x)
    wq = take(1)[0] if with_q else None
    wkv = take(1)[0] if with_kv else None
    acc_q = take(1)[0] if has_acc and with_q else None
    acc_kv = take(1)[0] if has_acc and with_kv else None
    cos, sin = take(2) if finish and with_q else (None, None)
    asked = take(1)[0] if finish and with_kv else None
    q_out = take(1)[0] if with_q else None
    kv_out = take(1)[0] if with_kv else None
    q_sum = take(1)[0] if finish and with_q else q_out
    kv_sum = take(1)[0] if finish and with_kv else kv_out
    y, x, _, _ = places()
    if has_acc:
        if with_q:
            q_sum[...] = acc_q[...]
        if with_kv:
            kv_sum[...] = acc_kv[...]
    for slot, ((dy, dx), low, high, uses) in enumerate(plan):
        base = pl.multiple_of((((y + dy) & 3) * 4 + ((x + dx) & 3)) * 512, 512)
        parts = [xs[operand][pl.ds(start, count), :] for operand, start, count in uses]
        piece = parts[0] if len(parts) == 1 else jnp.concatenate(parts, axis=0)
        fresh = slot == 0 and not has_acc
        if with_kv:
            both = wkv[:, pl.ds(base, 512)]
            term = lax.dot_general(piece, both, (((1,), (1,)), ((), ())), preferred_element_type=F32)
            kv_sum[low:high, :] = term if fresh else kv_sum[low:high, :] + term
        if with_q:
            term = jnp.dot(piece, wq[pl.ds(base, 512), :], preferred_element_type=F32)
            q_sum[low:high, :] = term if fresh else q_sum[low:high, :] + term
    if finish and with_kv:
        kv_out[:ROWS, :] = kv_sum[...].astype(BF)
        kv_out[ROWS:, :] = asked[:, 512:640]
    if finish and with_q:
        for head in range(4):
            cols = slice(head * HD, (head + 1) * HD)
            q_out[:, cols] = turn(q_sum[:, cols], cos[:ROWS, :], sin[:ROWS, :])


def project(xs, plan, weights, accs, with_q, with_kv, finish=False, tables=None, asked=None):
    wq, wkv = weights
    operands, specs = list(xs), [VM] * len(xs)
    if with_q:
        operands.append(wq)
        specs.append(VM)
    if with_kv:
        operands.append(wkv)
        specs.append(VM)
    has_acc = accs is not None
    if has_acc:
        if with_q:
            operands.append(accs[0])
            specs.append(VM)
        if with_kv:
            operands.append(accs[1])
            specs.append(VM)
    if finish and with_q:
        operands += list(tables)
        specs += [VM, VM]
    if finish and with_kv:
        operands.append(asked)
        specs.append(VM)
    outs, scratch = [], []
    if with_q:
        outs.append(jax.ShapeDtypeStruct((ROWS, 512), BF if finish else F32))
        if finish:
            scratch.append(pltpu.VMEM((ROWS, 512), F32))
    if with_kv:
        outs.append(jax.ShapeDtypeStruct((ALL, 128), BF) if finish else jax.ShapeDtypeStruct((ROWS, 128), F32))
        if finish:
            scratch.append(pltpu.VMEM((ROWS, 128), F32))
    columns = (512 if with_q else 0) + (128 if with_kv else 0)
    used = sum(high - low for _, low, high, _ in plan)
    return pl.pallas_call(
        functools.partial(project_kernel, plan, len(xs), with_q, with_kv, has_acc, finish),
        out_shape=outs,
        in_specs=specs,
        out_specs=[VM] * len(outs),
        scratch_shapes=scratch,
        compiler_params=pltpu.CompilerParams(vmem_limit_bytes=VMEM_LIMIT),
        cost_estimate=pl.CostEstimate(
            flops=2 * used * 512 * columns, bytes_accessed=len(plan) * 512 * columns * 2, transcendentals=0
        ),
    )(*operands)


def question_project_kernel(pieces, wq, wkv, cos, sin, out):
    q_sum, kv_sum = None, None
    for place in range(16):
        base = place * 512
        piece = pieces[place]
        both = wkv[:, pl.ds(base, 512)]
        kv_term = lax.dot_general(piece, both, (((1,), (1,)), ((), ())), preferred_element_type=F32)
        q_term = jnp.dot(piece, wq[pl.ds(base, 512), :], preferred_element_type=F32)
        q_sum = q_term if q_sum is None else q_sum + q_term
        kv_sum = kv_term if kv_sum is None else kv_sum + kv_term
    for head in range(4):
        cols = slice(head * HD, (head + 1) * HD)
        out[:, cols] = turn(q_sum[:, cols], cos[ROWS : ROWS + 32, :], sin[ROWS : ROWS + 32, :])
    out[:, 512:640] = kv_sum.astype(BF)


def question_project(pieces, weights, tables):
    return pl.pallas_call(
        question_project_kernel,
        out_shape=jax.ShapeDtypeStruct((32, 640), BF),
        in_specs=[VM] * 5,
        out_specs=VM,
        compiler_params=pltpu.CompilerParams(vmem_limit_bytes=VMEM_LIMIT),
        cost_estimate=pl.CostEstimate(flops=2 * 256 * 8192 * 640, bytes_accessed=8192 * 640 * 2, transcendentals=0),
    )(pieces, *weights, *tables)


def key_value_kernel(own, partner, cos, sin, out):
    is_lower = (places()[1] & 1) == 0
    mine, other = own[...].astype(F32), partner[...].astype(F32)
    low = jnp.where(is_lower, mine, other)
    high = jnp.where(is_lower, other, mine)
    lane = lax.broadcasted_iota(jnp.int32, low.shape, 1)
    keys = jnp.where(lane < 64, low, pltpu.roll(high, 64, 1))
    values = jnp.where(lane < 64, pltpu.roll(low, 64, 1), high)
    out[:, :HD] = (keys * cos[...] + pltpu.roll(keys, 64, 1) * sin[...]).astype(BF)
    out[:, HD:] = values.astype(BF)


def key_value(own, partner, cos, sin):
    return pl.pallas_call(
        key_value_kernel,
        out_shape=jax.ShapeDtypeStruct((ALL, 2 * HD), BF),
        in_specs=[VM, VM, VM, VM],
        out_specs=VM,
        compiler_params=pltpu.CompilerParams(vmem_limit_bytes=VMEM_LIMIT),
    )(own, partner, cos, sin)


def scores_of(queries, keys):
    return lax.dot_general(queries, keys, (((1,), (1,)), ((), ())), preferred_element_type=F32)


def weights_of(scores, top):
    return jnp.exp2(scores * SCALE2 - top * SCALE2)


def columns_to_stats(columns):
    rows = columns[0].shape[0]
    lane = lax.broadcasted_iota(jnp.int32, (rows, 128), 1)
    stats = jnp.zeros((rows, 128), F32)
    for index, column in enumerate(columns):
        stats = jnp.where(lane == index, column, stats)
    return stats


def own_kernel(lengths, q, kv, weighted, stats):
    _, _, z, core = places()
    length = lengths[2 * z + core]
    for tile in range(2):
        rows = slice(tile * 256, tile * 256 + 256)
        width = 256 * (tile + 1)
        row = tile * 256 + lax.broadcasted_iota(jnp.int32, (256, width), 0)
        key = lax.broadcasted_iota(jnp.int32, (256, width), 1)
        bias = jnp.where((key <= row) & (key < length), 0.0, NEG)
        tops, totals = [], []
        for head in range(4):
            cols = slice(head * HD, (head + 1) * HD)
            s = scores_of(q[rows, cols], kv[:width, :HD]) + bias
            top = jnp.max(s, axis=1, keepdims=True)
            e = weights_of(s, top)
            totals.append(jnp.sum(e, axis=1, keepdims=True))
            tops.append(top)
            weighted[rows, cols] = jnp.dot(e.astype(BF), kv[:width, HD:], preferred_element_type=F32)
        stats[rows, :] = columns_to_stats(tops + totals)


def own_attention(lengths, q, kv):
    return pl.pallas_call(
        own_kernel,
        out_shape=[jax.ShapeDtypeStruct((512, 512), F32), jax.ShapeDtypeStruct((512, 128), F32)],
        in_specs=[SM, VM, VM],
        out_specs=[VM, VM],
        compiler_params=pltpu.CompilerParams(vmem_limit_bytes=VMEM_LIMIT),
        cost_estimate=pl.CostEstimate(flops=4 * 4 * 512 * 512 * 128, bytes_accessed=3 << 20, transcendentals=1 << 20),
    )(lengths, q, kv)


def anchor_kernel(lengths, q, kv_zero, kv_one, weighted, stats, out):
    _, _, z, core = places()
    length = lengths[2 * z + core]
    anchor_length = jnp.where(2 * z + core > 0, lengths[0], 0)
    first_core = core == 0
    kv = jnp.where(first_core, kv_zero[...], kv_one[...])
    keys, values = kv[:, :HD], kv[:, HD:]
    key = lax.broadcasted_iota(jnp.int32, (1, 512), 1)
    bias = jnp.where(key < anchor_length, 0.0, NEG)
    for tile in range(2):
        rows = slice(tile * 256, tile * 256 + 256)
        block = stats[rows, :]
        row = tile * 256 + lax.broadcasted_iota(jnp.int32, (256, HD), 0)
        for head in range(4):
            cols = slice(head * HD, (head + 1) * HD)
            s = scores_of(q[rows, cols], keys) + bias
            own_top, own_sum = block[:, head : head + 1], block[:, head + 4 : head + 5]
            top = jnp.maximum(own_top, jnp.max(s, axis=1, keepdims=True))
            e = weights_of(s, top)
            factor = weights_of(own_top, top)
            total = own_sum * factor + jnp.sum(e, axis=1, keepdims=True)
            both = weighted[rows, cols] * factor + jnp.dot(e.astype(BF), values, preferred_element_type=F32)
            out[rows, cols] = jnp.where(row < length, both / total, 0.0).astype(BF)


def anchor_attention(lengths, q, kv_zero, kv_one, weighted, stats):
    return pl.pallas_call(
        anchor_kernel,
        out_shape=jax.ShapeDtypeStruct((512, 512), BF),
        in_specs=[SM, VM, VM, VM, VM, VM],
        out_specs=VM,
        compiler_params=pltpu.CompilerParams(vmem_limit_bytes=VMEM_LIMIT),
        cost_estimate=pl.CostEstimate(flops=4 * 4 * 512 * 512 * 128, bytes_accessed=3 << 20, transcendentals=1 << 20),
    )(lengths, q, kv_zero, kv_one, weighted, stats)


def question_kernel(lengths_ref, q_own, q_other, kv_0, kv_1, kv_2, kv_3, out_own, out_other):
    kvs = (kv_0, kv_1, kv_2, kv_3)
    _, _, z, core = places()
    ctx = 2 * z + core
    blocks = [z, (z + 3) & 3, (z + 1) & 3, (z + 2) & 3]
    lengths = [lengths_ref[2 * block + core] for block in blocks]
    stacked = [q_own[:, h * HD : (h + 1) * HD] for h in range(4)]
    stacked += [q_other[:, h * HD : (h + 1) * HD] for h in range(4)]
    q = jnp.concatenate(stacked, axis=0)
    scores = []
    key = lax.broadcasted_iota(jnp.int32, (1, 512), 1)
    for kv, length in zip(kvs, lengths):
        scores.append(scores_of(q, kv[:ROWS, :HD]) + jnp.where(key < length, 0.0, NEG))
    row = lax.broadcasted_iota(jnp.int32, (256, 128), 0)
    lane = lax.broadcasted_iota(jnp.int32, (256, 128), 1)
    row_id = row % 32 + 32 * jnp.where(row < 128, ctx, ctx + 1 - 2 * core)
    block = jnp.where(lane < 64, jnp.where(lane < 32, blocks[0], blocks[1]), jnp.where(lane < 96, blocks[2], blocks[3]))
    key_id = lane % 32 + 32 * (2 * block + core)
    asked_keys = jnp.concatenate([kv[ROWS:, :HD] for kv in kvs], axis=0)
    asked_values = jnp.concatenate([kv[ROWS:, HD:] for kv in kvs], axis=0)
    scores.append(jnp.where(key_id <= row_id, scores_of(q, asked_keys), NEG))
    top = jnp.max(scores[-1], axis=1, keepdims=True)
    for s in scores[:-1]:
        top = jnp.maximum(top, jnp.max(s, axis=1, keepdims=True))
    values = [kv[:ROWS, HD:] for kv in kvs] + [asked_values]
    total = jnp.zeros((256, 1), F32)
    both = jnp.zeros((256, HD), F32)
    for s, value in zip(scores, values):
        e = weights_of(s, top)
        total = total + jnp.sum(e, axis=1, keepdims=True)
        both = both + jnp.dot(e.astype(BF), value, preferred_element_type=F32)
    for out, start in ((out_own, 0), (out_other, 128)):
        tops, totals = [], []
        for head in range(4):
            rows = slice(start + head * 32, start + head * 32 + 32)
            out[:, head * HD : (head + 1) * HD] = both[rows]
            tops.append(top[rows])
            totals.append(total[rows])
        out[:, 512:640] = columns_to_stats(tops + totals)


def question_attention(lengths, q_own, q_other, kvs):
    part = jax.ShapeDtypeStruct((32, 640), F32)
    return pl.pallas_call(
        question_kernel,
        out_shape=[part, part],
        in_specs=[SM] + [VM] * 6,
        out_specs=[VM, VM],
        compiler_params=pltpu.CompilerParams(vmem_limit_bytes=VMEM_LIMIT),
        cost_estimate=pl.CostEstimate(flops=4 * 256 * 2176 * 128, bytes_accessed=2 << 20, transcendentals=1 << 19),
    )(lengths, q_own, q_other, *kvs)


def merge_kernel(a, b, out):
    stat_a, stat_b = a[:, 512:640], b[:, 512:640]
    for head in range(4):
        cols = slice(head * HD, (head + 1) * HD)
        top_a, top_b = stat_a[:, head : head + 1], stat_b[:, head : head + 1]
        top = jnp.maximum(top_a, top_b)
        factor_a, factor_b = weights_of(top_a, top), weights_of(top_b, top)
        total = stat_a[:, head + 4 : head + 5] * factor_a + stat_b[:, head + 4 : head + 5] * factor_b
        out[:, cols] = ((a[:, cols] * factor_a + b[:, cols] * factor_b) / total).astype(BF)


def merge(a, b):
    return pl.pallas_call(
        merge_kernel,
        out_shape=jax.ShapeDtypeStruct((32, 512), BF),
        in_specs=[VM, VM],
        out_specs=VM,
        compiler_params=pltpu.CompilerParams(vmem_limit_bytes=VMEM_LIMIT),
    )(a, b)


PLAN_1 = [
    ((0, 0), 0, 512, [(0, 0, 512)]),
    ((-1, 0), 0, 512, [(1, 0, 512)]),
    ((1, 0), 0, 512, [(2, 0, 512)]),
    ((0, -1), 0, 512, [(3, 0, 512)]),
    ((0, 1), 0, 512, [(4, 0, 512)]),
    ((2, 0), 0, 256, [(5, 0, 256)]),
    ((0, 2), 256, 512, [(6, 0, 256)]),
]
PLAN_2 = [
    ((-1, -1), 0, 512, [(0, 0, 256), (2, 0, 256)]),
    ((1, -1), 0, 512, [(0, 256, 256), (3, 0, 256)]),
    ((-1, 1), 0, 512, [(1, 0, 256), (2, 256, 256)]),
    ((1, 1), 0, 512, [(1, 256, 256), (3, 256, 256)]),
    ((2, -1), 0, 256, [(0, 512, 256)]),
    ((2, 1), 0, 256, [(1, 512, 256)]),
    ((-1, 2), 256, 512, [(2, 512, 256)]),
    ((1, 2), 256, 512, [(3, 512, 256)]),
    ((0, 2), 0, 256, [(0, 768, 128), (1, 768, 128)]),
    ((2, 0), 256, 512, [(2, 768, 128), (3, 768, 128)]),
]
PLAN_3 = [
    ((2, 2), 0, 512, [(1, 128, 256), (3, 128, 256)]),
    ((-1, 2), 0, 256, [(0, 0, 256)]),
    ((1, 2), 0, 256, [(0, 256, 128), (1, 0, 128)]),
    ((2, -1), 256, 512, [(2, 0, 256)]),
    ((2, 1), 256, 512, [(2, 256, 128), (3, 0, 128)]),
]
NEAR_Y = [(0, 0, 256), (1, 0, 256), (4, 0, 256)]
NEAR_X = [(2, 256, 256), (3, 256, 256), (4, 0, 256)]
PACK_2 = [NEAR_Y + [(2, 0, 128)], NEAR_Y + [(3, 128, 128)], NEAR_X + [(0, 256, 128)], NEAR_X + [(1, 384, 128)]]
PACK_3 = [[(0, 0, 384)], [(1, 384, 384)]]


def tables_of(positions):
    inverse_freq = ROPE_BASE ** (-(jnp.arange(HD // 2, dtype=jnp.float32) * 2.0 / HD))
    inverse_freq = jnp.concatenate([inverse_freq, inverse_freq])
    phases = positions.astype(jnp.float32)[:, None] * inverse_freq[None, :]
    signs = jnp.where(jnp.arange(HD) < HD // 2, -1.0, 1.0).astype(jnp.float32)
    return jnp.cos(phases), jnp.sin(phases) * signs[None, :]


def shift_z(array, dz):
    pairs = [(i, ((i // 2 + dz) % 4) * 2 + i % 2) for i in range(8)]
    return lax.ppermute(array, "ctx", pairs)


def per_device(context, question, w_query, w_key, w_value, lengths, owner):
    ctx = lax.axis_index("ctx")
    z, core = lax.shift_right_logical(ctx, 1), ctx & 1
    ids = jnp.arange(8, dtype=jnp.int32)
    own_offset = jnp.sum(jnp.where(ids < ctx, lengths, 0))
    filled = jnp.sum(lengths)

    up = shift_heads(context, 1, 0)
    down = shift_heads(context, -1, 0)
    right = shift_heads(context, 0, 1)
    left = shift_heads(context, 0, -1)
    low, high = pack([[(0, 0, 256)], [(0, 256, 256)]], [context])
    low, high, cut = lax.optimization_barrier((low, high, owner))
    far_y = shift_heads(low, 2, 0)
    up, high = lax.optimization_barrier((up, high))
    far_x = shift_heads(high, 0, 2)

    share = lax.all_to_all(question[0].reshape(8, 32, 512), "ctx", 0, 0)
    share = lax.dynamic_index_in_dim(share, cut[0], 0, False)
    share = jnp.broadcast_to(share[None], (16, 32, 512))
    pieces = lax.all_to_all(share, "heads", 0, 0)
    up, pieces = lax.optimization_barrier((up, pieces))

    to_right, to_left = pack(PACK_2[:2], [up, down, right, left, far_y])
    to_up, to_down = pack(PACK_2[2:], [up, down, right, left, far_x])
    a_right, a_left = shift_heads(to_right, 0, 1), shift_heads(to_left, 0, -1)
    b_up, b_down = shift_heads(to_up, 1, 0), shift_heads(to_down, -1, 0)
    up, to_right = lax.optimization_barrier((up, to_right))
    tables = tables_of(
        jnp.concatenate(
            [own_offset + jnp.arange(ROWS, dtype=jnp.int32), filled + 32 * ctx + jnp.arange(ASKED, dtype=jnp.int32)]
        )
    )
    pieces, w_query, w_key, w_value, tables = lax.optimization_barrier(
        (pieces, w_query, w_key, w_value, tables)
    )
    weights = hold(w_query, w_key.T, w_value.T)
    accs = project([context, up, down, right, left, far_y, far_x], PLAN_1, weights, None, True, True)
    q_share = question_project(pieces, weights, tables)

    a_right, a_left, accs, q_share = lax.optimization_barrier((a_right, a_left, accs, q_share))
    to_right, to_left = pack(PACK_3, [a_right, a_left])
    to_up, to_down = pack(PACK_3, [b_up, b_down])
    last = [
        shift_heads(to_right, 0, 1),
        shift_heads(to_left, 0, -1),
        shift_heads(to_up, 1, 0),
        shift_heads(to_down, -1, 0),
    ]
    accs = project([a_right, a_left, b_up, b_down], PLAN_2, weights, accs, True, True)

    (halves,) = project(last, PLAN_3, weights, accs, False, True, True, asked=q_share)
    (queries,) = project(last, PLAN_3, weights, accs, True, False, True, tables)
    partner = swap_heads(halves, 0, 1)
    q_asked = q_share[:, :512]
    q_other = swap_ctx(q_asked, 0, 1)
    partner, queries, q_other = lax.optimization_barrier((partner, queries, q_other))
    kv = key_value(halves, partner, *tables)

    below, above, across = shift_z(kv, 1), shift_z(kv, -1), shift_z(kv, 2)
    weighted, stats = own_attention(lengths, queries, kv)
    below, above, across, weighted = lax.optimization_barrier((below, above, across, weighted))
    nearer = jnp.where(z == 0, kv[:ROWS], jnp.where(z == 1, below[:ROWS], jnp.where(z == 2, across[:ROWS], above[:ROWS])))
    from_zero = lax.ppermute(nearer, "ctx", [(0, 1), (2, 3), (4, 5), (6, 7)])
    part, part_other = question_attention(lengths, q_asked, q_other, [kv, below, above, across])
    from_zero, part = lax.optimization_barrier((from_zero, part))
    context_attn = anchor_attention(lengths, queries, nearer, from_zero, weighted, stats)
    question_attn = merge(part, swap_ctx(part_other, 0, 1))
    return (context_attn, question_attn)


def solution(mesh):
    in_specs = (
        P("ctx", "heads"),
        P("ctx", None, "heads"),
        P(None, "heads"),
        P(None, "heads"),
        P(None, "heads"),
        P(),
        P(),
    )
    out_specs = (P("ctx", "heads"), P("ctx", "heads"))
    return jax.shard_map(
        per_device, mesh=mesh, in_specs=in_specs, out_specs=out_specs, check_vma=False
    )
```

```python
import functools

import jax
import jax.numpy as jnp
from jax import lax
from jax.experimental import pallas as pl
from jax.experimental.pallas import tpu as pltpu
from jax.sharding import PartitionSpec as P

HD = 128
ROPE_BASE = 500000.0
BF = jnp.bfloat16
F32 = jnp.float32
VMEM_LIMIT = 8 * 1024 * 1024
HOLD_LIMIT = 37 * 1024 * 1024
NEG = -1e30
SCALE2 = HD ** (-0.5) * 1.4426950408889634
ROWS = 512
ASKED = 32
ALL = ROWS + ASKED

HBM = pl.BlockSpec(memory_space=pltpu.HBM)
VM = pl.BlockSpec(memory_space=pltpu.VMEM)
SM = pl.BlockSpec(memory_space=pltpu.SMEM)


def shift_heads(array, dy, dx):
    pairs = [(i, ((i // 4 + dy) % 4) * 4 + (i % 4 + dx) % 4) for i in range(16)]
    return lax.ppermute(array, "heads", pairs)


def swap_heads(array, my, mx):
    pairs = [(i, ((i // 4) ^ my) * 4 + ((i % 4) ^ mx)) for i in range(16)]
    return lax.ppermute(array, "heads", pairs)


def swap_ctx(array, mz, mc):
    pairs = [(i, ((i // 2) ^ mz) * 2 + ((i % 2) ^ mc)) for i in range(8)]
    return lax.ppermute(array, "ctx", pairs)


def places():
    heads, ctx = lax.axis_index("heads"), lax.axis_index("ctx")
    return lax.shift_right_logical(heads, 2), heads & 3, lax.shift_right_logical(ctx, 1), ctx & 1


def pack_kernel(plan, n_in, *refs):
    ins, outs = refs[:n_in], refs[n_in:]
    for out, pieces in zip(outs, plan):
        row = 0
        for operand, start, count in pieces:
            out[row : row + count, :] = ins[operand][start : start + count, :]
            row += count


def pack(plan, ins):
    return pl.pallas_call(
        functools.partial(pack_kernel, plan, len(ins)),
        out_shape=[jax.ShapeDtypeStruct((sum(p[2] for p in pieces), 512), BF) for pieces in plan],
        in_specs=[VM] * len(ins),
        out_specs=[VM] * len(plan),
        compiler_params=pltpu.CompilerParams(vmem_limit_bytes=VMEM_LIMIT),
        cost_estimate=pl.CostEstimate(flops=0, bytes_accessed=1 << 20, transcendentals=0),
    )(*ins)


def hold_kernel(wq, wk, wv, q_out, kv_out, sem):
    copies = []
    for part in range(8):
        rows = pl.ds(part * 1024, 1024)
        copies.append(pltpu.make_async_copy(wq.at[rows, :], q_out.at[rows, :], sem.at[part]))
    for part in range(4):
        cols = pl.ds(part * 2048, 2048)
        copies.append(pltpu.make_async_copy(wk.at[:, cols], kv_out.at[pl.ds(0, 64), cols], sem.at[8 + part]))
        copies.append(pltpu.make_async_copy(wv.at[:, cols], kv_out.at[pl.ds(64, 64), cols], sem.at[12 + part]))
    for copy in copies:
        copy.start()
    for copy in copies:
        copy.wait()


def hold(wq, wk, wv):
    return pl.pallas_call(
        hold_kernel,
        out_shape=[jax.ShapeDtypeStruct((8192, 512), BF), jax.ShapeDtypeStruct((128, 8192), BF)],
        in_specs=[HBM] * 3,
        out_specs=[VM, VM],
        scratch_shapes=[pltpu.SemaphoreType.DMA((16,))],
        compiler_params=pltpu.CompilerParams(vmem_limit_bytes=HOLD_LIMIT),
        cost_estimate=pl.CostEstimate(flops=0, bytes_accessed=20 << 20, transcendentals=0),
    )(wq, wk, wv)


def turn(part, cos, sin):
    return (part * cos + pltpu.roll(part, HD // 2, 1) * sin).astype(BF)


def project_kernel(plan, n_x, with_q, with_kv, has_acc, finish, *refs):
    refs = list(refs)
    take = lambda count: [refs.pop(0) for _ in range(count)]
    xs = take(n_x)
    wq = take(1)[0] if with_q else None
    wkv = take(1)[0] if with_kv else None
    acc_q = take(1)[0] if has_acc and with_q else None
    acc_kv = take(1)[0] if has_acc and with_kv else None
    cos, sin = take(2) if finish and with_q else (None, None)
    asked = take(1)[0] if finish and with_kv else None
    q_out = take(1)[0] if with_q else None
    kv_out = take(1)[0] if with_kv else None
    q_sum = take(1)[0] if finish and with_q else q_out
    kv_sum = take(1)[0] if finish and with_kv else kv_out
    y, x, _, _ = places()
    if has_acc:
        if with_q:
            q_sum[...] = acc_q[...]
        if with_kv:
            kv_sum[...] = acc_kv[...]
    for slot, ((dy, dx), low, high, uses) in enumerate(plan):
        base = pl.multiple_of((((y + dy) & 3) * 4 + ((x + dx) & 3)) * 512, 512)
        parts = [xs[operand][pl.ds(start, count), :] for operand, start, count in uses]
        piece = parts[0] if len(parts) == 1 else jnp.concatenate(parts, axis=0)
        fresh = slot == 0 and not has_acc
        if with_kv:
            both = wkv[:, pl.ds(base, 512)]
            term = lax.dot_general(piece, both, (((1,), (1,)), ((), ())), preferred_element_type=F32)
            kv_sum[low:high, :] = term if fresh else kv_sum[low:high, :] + term
        if with_q:
            term = jnp.dot(piece, wq[pl.ds(base, 512), :], preferred_element_type=F32)
            q_sum[low:high, :] = term if fresh else q_sum[low:high, :] + term
    if finish and with_kv:
        kv_out[:ROWS, :] = kv_sum[...].astype(BF)
        kv_out[ROWS:, :] = asked[:, 512:640]
    if finish and with_q:
        for head in range(4):
            cols = slice(head * HD, (head + 1) * HD)
            q_out[:, cols] = turn(q_sum[:, cols], cos[:ROWS, :], sin[:ROWS, :])


def project(xs, plan, weights, accs, with_q, with_kv, finish=False, tables=None, asked=None):
    wq, wkv = weights
    operands, specs = list(xs), [VM] * len(xs)
    if with_q:
        operands.append(wq)
        specs.append(VM)
    if with_kv:
        operands.append(wkv)
        specs.append(VM)
    has_acc = accs is not None
    if has_acc:
        if with_q:
            operands.append(accs[0])
            specs.append(VM)
        if with_kv:
            operands.append(accs[1])
            specs.append(VM)
    if finish and with_q:
        operands += list(tables)
        specs += [VM, VM]
    if finish and with_kv:
        operands.append(asked)
        specs.append(VM)
    outs, scratch = [], []
    if with_q:
        outs.append(jax.ShapeDtypeStruct((ROWS, 512), BF if finish else F32))
        if finish:
            scratch.append(pltpu.VMEM((ROWS, 512), F32))
    if with_kv:
        outs.append(jax.ShapeDtypeStruct((ALL, 128), BF) if finish else jax.ShapeDtypeStruct((ROWS, 128), F32))
        if finish:
            scratch.append(pltpu.VMEM((ROWS, 128), F32))
    columns = (512 if with_q else 0) + (128 if with_kv else 0)
    used = sum(high - low for _, low, high, _ in plan)
    return pl.pallas_call(
        functools.partial(project_kernel, plan, len(xs), with_q, with_kv, has_acc, finish),
        out_shape=outs,
        in_specs=specs,
        out_specs=[VM] * len(outs),
        scratch_shapes=scratch,
        compiler_params=pltpu.CompilerParams(vmem_limit_bytes=VMEM_LIMIT),
        cost_estimate=pl.CostEstimate(
            flops=2 * used * 512 * columns, bytes_accessed=len(plan) * 512 * columns * 2, transcendentals=0
        ),
    )(*operands)


def question_project_kernel(pieces, wq, wkv, cos, sin, out):
    q_sum, kv_sum = None, None
    for place in range(16):
        base = place * 512
        piece = pieces[place]
        both = wkv[:, pl.ds(base, 512)]
        kv_term = lax.dot_general(piece, both, (((1,), (1,)), ((), ())), preferred_element_type=F32)
        q_term = jnp.dot(piece, wq[pl.ds(base, 512), :], preferred_element_type=F32)
        q_sum = q_term if q_sum is None else q_sum + q_term
        kv_sum = kv_term if kv_sum is None else kv_sum + kv_term
    for head in range(4):
        cols = slice(head * HD, (head + 1) * HD)
        out[:, cols] = turn(q_sum[:, cols], cos[ROWS : ROWS + 32, :], sin[ROWS : ROWS + 32, :])
    out[:, 512:640] = kv_sum.astype(BF)


def question_project(pieces, weights, tables):
    return pl.pallas_call(
        question_project_kernel,
        out_shape=jax.ShapeDtypeStruct((32, 640), BF),
        in_specs=[VM] * 5,
        out_specs=VM,
        compiler_params=pltpu.CompilerParams(vmem_limit_bytes=VMEM_LIMIT),
        cost_estimate=pl.CostEstimate(flops=2 * 256 * 8192 * 640, bytes_accessed=8192 * 640 * 2, transcendentals=0),
    )(pieces, *weights, *tables)


def key_value_kernel(own, partner, cos, sin, out):
    is_lower = (places()[1] & 1) == 0
    mine, other = own[...].astype(F32), partner[...].astype(F32)
    low = jnp.where(is_lower, mine, other)
    high = jnp.where(is_lower, other, mine)
    lane = lax.broadcasted_iota(jnp.int32, low.shape, 1)
    keys = jnp.where(lane < 64, low, pltpu.roll(high, 64, 1))
    values = jnp.where(lane < 64, pltpu.roll(low, 64, 1), high)
    out[:, :HD] = (keys * cos[...] + pltpu.roll(keys, 64, 1) * sin[...]).astype(BF)
    out[:, HD:] = values.astype(BF)


def key_value(own, partner, cos, sin):
    return pl.pallas_call(
        key_value_kernel,
        out_shape=jax.ShapeDtypeStruct((ALL, 2 * HD), BF),
        in_specs=[VM, VM, VM, VM],
        out_specs=VM,
        compiler_params=pltpu.CompilerParams(vmem_limit_bytes=VMEM_LIMIT),
    )(own, partner, cos, sin)


def scores_of(queries, keys):
    return lax.dot_general(queries, keys, (((1,), (1,)), ((), ())), preferred_element_type=F32)


def weights_of(scores, top):
    return jnp.exp2(scores * SCALE2 - top * SCALE2)


def columns_to_stats(columns):
    rows = columns[0].shape[0]
    lane = lax.broadcasted_iota(jnp.int32, (rows, 128), 1)
    stats = jnp.zeros((rows, 128), F32)
    for index, column in enumerate(columns):
        stats = jnp.where(lane == index, column, stats)
    return stats


def dot_keys(values, weights):
    return lax.dot_general(values, weights, (((0,), (0,)), ((), ())), preferred_element_type=F32)


def own_kernel(lengths, q, kv, weighted, stats):
    _, _, z, core = places()
    length = lengths[2 * z + core]
    for tile in range(2):
        rows = slice(tile * 256, tile * 256 + 256)
        width = 256 * (tile + 1)
        key = lax.broadcasted_iota(jnp.int32, (width, 256), 0)
        row = tile * 256 + lax.broadcasted_iota(jnp.int32, (width, 256), 1)
        bias = jnp.where((key <= row) & (key < length), 0.0, NEG)
        for head in range(4):
            cols = slice(head * HD, (head + 1) * HD)
            s = scores_of(kv[:width, :HD], q[rows, cols]) + bias
            top = jnp.max(s, axis=0, keepdims=True)
            e = weights_of(s, top)
            stats[head : head + 1, rows] = top
            stats[head + 8 : head + 9, rows] = jnp.sum(e, axis=0, keepdims=True)
            weighted[cols, rows] = dot_keys(kv[:width, HD:], e.astype(BF))


def own_attention(lengths, q, kv):
    return pl.pallas_call(
        own_kernel,
        out_shape=[jax.ShapeDtypeStruct((512, 512), F32), jax.ShapeDtypeStruct((16, 512), F32)],
        in_specs=[SM, VM, VM],
        out_specs=[VM, VM],
        compiler_params=pltpu.CompilerParams(vmem_limit_bytes=VMEM_LIMIT),
        cost_estimate=pl.CostEstimate(flops=4 * 4 * 512 * 512 * 128, bytes_accessed=3 << 20, transcendentals=1 << 20),
    )(lengths, q, kv)


def nearer_kernel(own, below, across, above, out):
    _, _, z, _ = places()
    for plane, source in enumerate((own, below, across, above)):

        @pl.when(z == plane)
        def _(source=source):
            out[...] = source[:ROWS, :]


def nearer_anchor(own, below, across, above):
    return pl.pallas_call(
        nearer_kernel,
        out_shape=jax.ShapeDtypeStruct((ROWS, 2 * HD), BF),
        in_specs=[VM] * 4,
        out_specs=VM,
        compiler_params=pltpu.CompilerParams(vmem_limit_bytes=VMEM_LIMIT),
        cost_estimate=pl.CostEstimate(flops=0, bytes_accessed=1 << 19, transcendentals=0),
    )(own, below, across, above)


def anchor_kernel(lengths, q, kv_zero, kv_one, weighted, stats, out, kv):
    _, _, z, core = places()
    length = lengths[2 * z + core]
    anchor_length = jnp.where(2 * z + core > 0, lengths[0], 0)

    @pl.when(core == 0)
    def _():
        kv[...] = kv_zero[...]

    @pl.when(core != 0)
    def _():
        kv[...] = kv_one[...]

    key = lax.broadcasted_iota(jnp.int32, (512, 1), 0)
    bias = jnp.where(key < anchor_length, 0.0, NEG)
    for tile in range(2):
        rows = slice(tile * 256, tile * 256 + 256)
        live = tile * 256 + lax.broadcasted_iota(jnp.int32, (1, 256), 1) < length
        for head in range(4):
            cols = slice(head * HD, (head + 1) * HD)
            s = scores_of(kv[:, :HD], q[rows, cols]) + bias
            own_top, own_sum = stats[head : head + 1, rows], stats[head + 8 : head + 9, rows]
            top = jnp.maximum(own_top, jnp.max(s, axis=0, keepdims=True))
            e = weights_of(s, top)
            factor = weights_of(own_top, top)
            total = own_sum * factor + jnp.sum(e, axis=0, keepdims=True)
            share = jnp.where(live, 1.0 / total, 0.0)
            both = weighted[cols, rows] * (factor * share) + dot_keys(kv[:, HD:], e.astype(BF)) * share
            out[rows, cols] = both.T.astype(BF)


def anchor_attention(lengths, q, kv_zero, kv_one, weighted, stats):
    return pl.pallas_call(
        anchor_kernel,
        out_shape=jax.ShapeDtypeStruct((512, 512), BF),
        in_specs=[SM, VM, VM, VM, VM, VM],
        out_specs=VM,
        scratch_shapes=[pltpu.VMEM((ROWS, 2 * HD), BF)],
        compiler_params=pltpu.CompilerParams(vmem_limit_bytes=VMEM_LIMIT),
        cost_estimate=pl.CostEstimate(flops=4 * 4 * 512 * 512 * 128, bytes_accessed=3 << 20, transcendentals=1 << 20),
    )(lengths, q, kv_zero, kv_one, weighted, stats)


def question_kernel(lengths_ref, q_own, q_other, kv_0, kv_1, kv_2, kv_3, out_own, out_other):
    kvs = (kv_0, kv_1, kv_2, kv_3)
    _, _, z, core = places()
    ctx = 2 * z + core
    blocks = [z, (z + 3) & 3, (z + 1) & 3, (z + 2) & 3]
    lengths = [lengths_ref[2 * block + core] for block in blocks]
    stacked = [q_own[:, h * HD : (h + 1) * HD] for h in range(4)]
    stacked += [q_other[:, h * HD : (h + 1) * HD] for h in range(4)]
    q = jnp.concatenate(stacked, axis=0)
    scores = []
    key = lax.broadcasted_iota(jnp.int32, (1, 512), 1)
    for kv, length in zip(kvs, lengths):
        scores.append(scores_of(q, kv[:ROWS, :HD]) + jnp.where(key < length, 0.0, NEG))
    row = lax.broadcasted_iota(jnp.int32, (256, 128), 0)
    lane = lax.broadcasted_iota(jnp.int32, (256, 128), 1)
    row_id = row % 32 + 32 * jnp.where(row < 128, ctx, ctx + 1 - 2 * core)
    block = jnp.where(lane < 64, jnp.where(lane < 32, blocks[0], blocks[1]), jnp.where(lane < 96, blocks[2], blocks[3]))
    key_id = lane % 32 + 32 * (2 * block + core)
    asked_keys = jnp.concatenate([kv[ROWS:, :HD] for kv in kvs], axis=0)
    asked_values = jnp.concatenate([kv[ROWS:, HD:] for kv in kvs], axis=0)
    scores.append(jnp.where(key_id <= row_id, scores_of(q, asked_keys), NEG))
    top = jnp.max(scores[-1], axis=1, keepdims=True)
    for s in scores[:-1]:
        top = jnp.maximum(top, jnp.max(s, axis=1, keepdims=True))
    values = [kv[:ROWS, HD:] for kv in kvs] + [asked_values]
    total = jnp.zeros((256, 1), F32)
    both = jnp.zeros((256, HD), F32)
    for s, value in zip(scores, values):
        e = weights_of(s, top)
        total = total + jnp.sum(e, axis=1, keepdims=True)
        both = both + jnp.dot(e.astype(BF), value, preferred_element_type=F32)
    for out, start in ((out_own, 0), (out_other, 128)):
        tops, totals = [], []
        for head in range(4):
            rows = slice(start + head * 32, start + head * 32 + 32)
            out[:, head * HD : (head + 1) * HD] = both[rows]
            tops.append(top[rows])
            totals.append(total[rows])
        out[:, 512:640] = columns_to_stats(tops + totals)


def question_attention(lengths, q_own, q_other, kvs):
    part = jax.ShapeDtypeStruct((32, 640), F32)
    return pl.pallas_call(
        question_kernel,
        out_shape=[part, part],
        in_specs=[SM] + [VM] * 6,
        out_specs=[VM, VM],
        compiler_params=pltpu.CompilerParams(vmem_limit_bytes=VMEM_LIMIT),
        cost_estimate=pl.CostEstimate(flops=4 * 256 * 2176 * 128, bytes_accessed=2 << 20, transcendentals=1 << 19),
    )(lengths, q_own, q_other, *kvs)


def merge_kernel(a, b, out):
    stat_a, stat_b = a[:, 512:640], b[:, 512:640]
    for head in range(4):
        cols = slice(head * HD, (head + 1) * HD)
        top_a, top_b = stat_a[:, head : head + 1], stat_b[:, head : head + 1]
        top = jnp.maximum(top_a, top_b)
        factor_a, factor_b = weights_of(top_a, top), weights_of(top_b, top)
        total = stat_a[:, head + 4 : head + 5] * factor_a + stat_b[:, head + 4 : head + 5] * factor_b
        out[:, cols] = ((a[:, cols] * factor_a + b[:, cols] * factor_b) / total).astype(BF)


def merge(a, b):
    return pl.pallas_call(
        merge_kernel,
        out_shape=jax.ShapeDtypeStruct((32, 512), BF),
        in_specs=[VM, VM],
        out_specs=VM,
        compiler_params=pltpu.CompilerParams(vmem_limit_bytes=VMEM_LIMIT),
    )(a, b)


PLAN_1 = [
    ((0, 0), 0, 512, [(0, 0, 512)]),
    ((-1, 0), 0, 512, [(1, 0, 512)]),
    ((1, 0), 0, 512, [(2, 0, 512)]),
    ((0, -1), 0, 512, [(3, 0, 512)]),
    ((0, 1), 0, 512, [(4, 0, 512)]),
    ((2, 0), 0, 256, [(5, 0, 256)]),
    ((0, 2), 256, 512, [(6, 0, 256)]),
]
PLAN_2 = [
    ((-1, -1), 0, 512, [(0, 0, 256), (2, 0, 256)]),
    ((1, -1), 0, 512, [(0, 256, 256), (3, 0, 256)]),
    ((-1, 1), 0, 512, [(1, 0, 256), (2, 256, 256)]),
    ((1, 1), 0, 512, [(1, 256, 256), (3, 256, 256)]),
    ((2, -1), 0, 256, [(0, 512, 256)]),
    ((2, 1), 0, 256, [(1, 512, 256)]),
    ((-1, 2), 256, 512, [(2, 512, 256)]),
    ((1, 2), 256, 512, [(3, 512, 256)]),
    ((0, 2), 0, 256, [(0, 768, 128), (1, 768, 128)]),
    ((2, 0), 256, 512, [(2, 768, 128), (3, 768, 128)]),
]
PLAN_3 = [
    ((2, 2), 0, 512, [(1, 128, 256), (3, 128, 256)]),
    ((-1, 2), 0, 256, [(0, 0, 256)]),
    ((1, 2), 0, 256, [(0, 256, 128), (1, 0, 128)]),
    ((2, -1), 256, 512, [(2, 0, 256)]),
    ((2, 1), 256, 512, [(2, 256, 128), (3, 0, 128)]),
]
NEAR_Y = [(0, 0, 256), (1, 0, 256), (4, 0, 256)]
NEAR_X = [(2, 256, 256), (3, 256, 256), (4, 0, 256)]
PACK_2 = [NEAR_Y + [(2, 0, 128)], NEAR_Y + [(3, 128, 128)], NEAR_X + [(0, 256, 128)], NEAR_X + [(1, 384, 128)]]
PACK_3 = [[(0, 0, 384)], [(1, 384, 384)]]


def tables_of(positions):
    inverse_freq = ROPE_BASE ** (-(jnp.arange(HD // 2, dtype=jnp.float32) * 2.0 / HD))
    inverse_freq = jnp.concatenate([inverse_freq, inverse_freq])
    phases = positions.astype(jnp.float32)[:, None] * inverse_freq[None, :]
    signs = jnp.where(jnp.arange(HD) < HD // 2, -1.0, 1.0).astype(jnp.float32)
    return jnp.cos(phases), jnp.sin(phases) * signs[None, :]


def shift_z(array, dz):
    pairs = [(i, ((i // 2 + dz) % 4) * 2 + i % 2) for i in range(8)]
    return lax.ppermute(array, "ctx", pairs)


def per_device(context, question, w_query, w_key, w_value, lengths, owner):
    ctx = lax.axis_index("ctx")
    ids = jnp.arange(8, dtype=jnp.int32)
    own_offset = jnp.sum(jnp.where(ids < ctx, lengths, 0))
    filled = jnp.sum(lengths)

    up = shift_heads(context, 1, 0)
    down = shift_heads(context, -1, 0)
    right = shift_heads(context, 0, 1)
    left = shift_heads(context, 0, -1)
    low, high = pack([[(0, 0, 256)], [(0, 256, 256)]], [context])
    low, high, cut = lax.optimization_barrier((low, high, owner))
    far_y = shift_heads(low, 2, 0)
    up, high = lax.optimization_barrier((up, high))
    far_x = shift_heads(high, 0, 2)

    share = lax.all_to_all(question[0].reshape(8, 32, 512), "ctx", 0, 0)
    share = lax.dynamic_index_in_dim(share, cut[0], 0, False)
    share = jnp.broadcast_to(share[None], (16, 32, 512))
    pieces = lax.all_to_all(share, "heads", 0, 0)
    up, pieces = lax.optimization_barrier((up, pieces))

    to_right, to_left = pack(PACK_2[:2], [up, down, right, left, far_y])
    to_up, to_down = pack(PACK_2[2:], [up, down, right, left, far_x])
    a_right, a_left = shift_heads(to_right, 0, 1), shift_heads(to_left, 0, -1)
    b_up, b_down = shift_heads(to_up, 1, 0), shift_heads(to_down, -1, 0)
    up, to_right = lax.optimization_barrier((up, to_right))
    tables = tables_of(
        jnp.concatenate(
            [own_offset + jnp.arange(ROWS, dtype=jnp.int32), filled + 32 * ctx + jnp.arange(ASKED, dtype=jnp.int32)]
        )
    )
    pieces, w_query, w_key, w_value, tables = lax.optimization_barrier(
        (pieces, w_query, w_key, w_value, tables)
    )
    weights = hold(w_query, w_key.T, w_value.T)
    accs = project([context, up, down, right, left, far_y, far_x], PLAN_1, weights, None, True, True)
    q_share = question_project(pieces, weights, tables)

    a_right, a_left, accs, q_share = lax.optimization_barrier((a_right, a_left, accs, q_share))
    to_right, to_left = pack(PACK_3, [a_right, a_left])
    to_up, to_down = pack(PACK_3, [b_up, b_down])
    last = [
        shift_heads(to_right, 0, 1),
        shift_heads(to_left, 0, -1),
        shift_heads(to_up, 1, 0),
        shift_heads(to_down, -1, 0),
    ]
    accs = project([a_right, a_left, b_up, b_down], PLAN_2, weights, accs, True, True)

    (halves,) = project(last, PLAN_3, weights, accs, False, True, True, asked=q_share)
    (queries,) = project(last, PLAN_3, weights, accs, True, False, True, tables)
    partner = swap_heads(halves, 0, 1)
    q_asked = q_share[:, :512]
    q_other = swap_ctx(q_asked, 0, 1)
    partner, queries, q_other = lax.optimization_barrier((partner, queries, q_other))
    kv = key_value(halves, partner, *tables)

    below, above, across = shift_z(kv, 1), shift_z(kv, -1), shift_z(kv, 2)
    weighted, stats = own_attention(lengths, queries, kv)
    below, above, across, weighted = lax.optimization_barrier((below, above, across, weighted))
    nearer = nearer_anchor(kv, below, across, above)
    from_zero = lax.ppermute(nearer, "ctx", [(0, 1), (2, 3), (4, 5), (6, 7)])
    part, part_other = question_attention(lengths, q_asked, q_other, [kv, below, above, across])
    from_zero, part = lax.optimization_barrier((from_zero, part))
    context_attn = anchor_attention(lengths, queries, nearer, from_zero, weighted, stats)
    question_attn = merge(part, swap_ctx(part_other, 0, 1))
    return (context_attn, question_attn)


def solution(mesh):
    in_specs = (
        P("ctx", "heads"),
        P("ctx", None, "heads"),
        P(None, "heads"),
        P(None, "heads"),
        P(None, "heads"),
        P(),
        P(),
    )
    out_specs = (P("ctx", "heads"), P("ctx", "heads"))
    return jax.shard_map(
        per_device, mesh=mesh, in_specs=in_specs, out_specs=out_specs, check_vma=False
    )
```

```python
import functools

import jax
import jax.numpy as jnp
from jax import lax
from jax.experimental import pallas as pl
from jax.experimental.pallas import tpu as pltpu
from jax.sharding import PartitionSpec as P

HD = 128
ROPE_BASE = 500000.0
BF = jnp.bfloat16
F32 = jnp.float32
VMEM_LIMIT = 8 * 1024 * 1024
HOLD_LIMIT = 37 * 1024 * 1024
NEG = -1e30
SCALE2 = HD ** (-0.5) * 1.4426950408889634
ROWS = 512
ASKED = 32
ALL = ROWS + ASKED

HBM = pl.BlockSpec(memory_space=pltpu.HBM)
VM = pl.BlockSpec(memory_space=pltpu.VMEM)
SM = pl.BlockSpec(memory_space=pltpu.SMEM)


def shift_heads(array, dy, dx):
    pairs = [(i, ((i // 4 + dy) % 4) * 4 + (i % 4 + dx) % 4) for i in range(16)]
    return lax.ppermute(array, "heads", pairs)


def swap_heads(array, my, mx):
    pairs = [(i, ((i // 4) ^ my) * 4 + ((i % 4) ^ mx)) for i in range(16)]
    return lax.ppermute(array, "heads", pairs)


def swap_ctx(array, mz, mc):
    pairs = [(i, ((i // 2) ^ mz) * 2 + ((i % 2) ^ mc)) for i in range(8)]
    return lax.ppermute(array, "ctx", pairs)


def places():
    heads, ctx = lax.axis_index("heads"), lax.axis_index("ctx")
    return lax.shift_right_logical(heads, 2), heads & 3, lax.shift_right_logical(ctx, 1), ctx & 1


def pack_kernel(plan, n_in, *refs):
    ins, outs = refs[:n_in], refs[n_in:]
    for out, pieces in zip(outs, plan):
        row = 0
        for operand, start, count in pieces:
            out[row : row + count, :] = ins[operand][start : start + count, :]
            row += count


def pack(plan, ins):
    return pl.pallas_call(
        functools.partial(pack_kernel, plan, len(ins)),
        out_shape=[jax.ShapeDtypeStruct((sum(p[2] for p in pieces), 512), BF) for pieces in plan],
        in_specs=[VM] * len(ins),
        out_specs=[VM] * len(plan),
        compiler_params=pltpu.CompilerParams(vmem_limit_bytes=VMEM_LIMIT),
        cost_estimate=pl.CostEstimate(flops=0, bytes_accessed=1 << 20, transcendentals=0),
    )(*ins)


def hold_kernel(wq, wk, wv, q_out, kv_out, sem):
    copies = []
    for part in range(8):
        rows = pl.ds(part * 1024, 1024)
        copies.append(pltpu.make_async_copy(wq.at[rows, :], q_out.at[rows, :], sem.at[part]))
    for part in range(4):
        cols = pl.ds(part * 2048, 2048)
        copies.append(pltpu.make_async_copy(wk.at[:, cols], kv_out.at[pl.ds(0, 64), cols], sem.at[8 + part]))
        copies.append(pltpu.make_async_copy(wv.at[:, cols], kv_out.at[pl.ds(64, 64), cols], sem.at[12 + part]))
    for copy in copies:
        copy.start()
    for copy in copies:
        copy.wait()


def hold(wq, wk, wv):
    return pl.pallas_call(
        hold_kernel,
        out_shape=[jax.ShapeDtypeStruct((8192, 512), BF), jax.ShapeDtypeStruct((128, 8192), BF)],
        in_specs=[HBM] * 3,
        out_specs=[VM, VM],
        scratch_shapes=[pltpu.SemaphoreType.DMA((16,))],
        compiler_params=pltpu.CompilerParams(vmem_limit_bytes=HOLD_LIMIT),
        cost_estimate=pl.CostEstimate(flops=0, bytes_accessed=20 << 20, transcendentals=0),
    )(wq, wk, wv)


def turn(part, cos, sin):
    return (part * cos + pltpu.roll(part, HD // 2, 1) * sin).astype(BF)


def project_kernel(plan, n_x, with_q, with_kv, has_acc, finish, *refs):
    refs = list(refs)
    take = lambda count: [refs.pop(0) for _ in range(count)]
    xs = take(n_x)
    wq = take(1)[0] if with_q else None
    wkv = take(1)[0] if with_kv else None
    acc_q = take(1)[0] if has_acc and with_q else None
    acc_kv = take(1)[0] if has_acc and with_kv else None
    cos, sin = take(2) if finish and with_q else (None, None)
    asked = take(1)[0] if finish and with_kv else None
    q_out = take(1)[0] if with_q else None
    kv_out = take(1)[0] if with_kv else None
    q_sum = take(1)[0] if finish and with_q else q_out
    kv_sum = take(1)[0] if finish and with_kv else kv_out
    y, x, _, _ = places()
    if has_acc:
        if with_q:
            q_sum[...] = acc_q[...]
        if with_kv:
            kv_sum[...] = acc_kv[...]
    for slot, ((dy, dx), low, high, uses) in enumerate(plan):
        base = pl.multiple_of((((y + dy) & 3) * 4 + ((x + dx) & 3)) * 512, 512)
        parts = [xs[operand][pl.ds(start, count), :] for operand, start, count in uses]
        piece = parts[0] if len(parts) == 1 else jnp.concatenate(parts, axis=0)
        fresh = slot == 0 and not has_acc
        if with_kv:
            both = wkv[:, pl.ds(base, 512)]
            term = lax.dot_general(piece, both, (((1,), (1,)), ((), ())), preferred_element_type=F32)
            kv_sum[low:high, :] = term if fresh else kv_sum[low:high, :] + term
        if with_q:
            term = jnp.dot(piece, wq[pl.ds(base, 512), :], preferred_element_type=F32)
            q_sum[low:high, :] = term if fresh else q_sum[low:high, :] + term
    if finish and with_kv:
        kv_out[:ROWS, :] = kv_sum[...].astype(BF)
        kv_out[ROWS:, :] = asked[:, 512:640]
    if finish and with_q:
        for head in range(4):
            cols = slice(head * HD, (head + 1) * HD)
            q_out[:, cols] = turn(q_sum[:, cols], cos[:ROWS, :], sin[:ROWS, :])


def project(xs, plan, weights, accs, with_q, with_kv, finish=False, tables=None, asked=None):
    wq, wkv = weights
    operands, specs = list(xs), [VM] * len(xs)
    if with_q:
        operands.append(wq)
        specs.append(VM)
    if with_kv:
        operands.append(wkv)
        specs.append(VM)
    has_acc = accs is not None
    if has_acc:
        if with_q:
            operands.append(accs[0])
            specs.append(VM)
        if with_kv:
            operands.append(accs[1])
            specs.append(VM)
    if finish and with_q:
        operands += list(tables)
        specs += [VM, VM]
    if finish and with_kv:
        operands.append(asked)
        specs.append(VM)
    outs, scratch = [], []
    if with_q:
        outs.append(jax.ShapeDtypeStruct((ROWS, 512), BF if finish else F32))
        if finish:
            scratch.append(pltpu.VMEM((ROWS, 512), F32))
    if with_kv:
        outs.append(jax.ShapeDtypeStruct((ALL, 128), BF) if finish else jax.ShapeDtypeStruct((ROWS, 128), F32))
        if finish:
            scratch.append(pltpu.VMEM((ROWS, 128), F32))
    columns = (512 if with_q else 0) + (128 if with_kv else 0)
    used = sum(high - low for _, low, high, _ in plan)
    return pl.pallas_call(
        functools.partial(project_kernel, plan, len(xs), with_q, with_kv, has_acc, finish),
        out_shape=outs,
        in_specs=specs,
        out_specs=[VM] * len(outs),
        scratch_shapes=scratch,
        compiler_params=pltpu.CompilerParams(vmem_limit_bytes=VMEM_LIMIT),
        cost_estimate=pl.CostEstimate(
            flops=2 * used * 512 * columns, bytes_accessed=len(plan) * 512 * columns * 2, transcendentals=0
        ),
    )(*operands)


def question_project_kernel(pieces, wq, wkv, cos, sin, out):
    q_sum, kv_sum = None, None
    for place in range(16):
        base = place * 512
        piece = pieces[place]
        both = wkv[:, pl.ds(base, 512)]
        kv_term = lax.dot_general(piece, both, (((1,), (1,)), ((), ())), preferred_element_type=F32)
        q_term = jnp.dot(piece, wq[pl.ds(base, 512), :], preferred_element_type=F32)
        q_sum = q_term if q_sum is None else q_sum + q_term
        kv_sum = kv_term if kv_sum is None else kv_sum + kv_term
    for head in range(4):
        cols = slice(head * HD, (head + 1) * HD)
        out[:, cols] = turn(q_sum[:, cols], cos[ROWS : ROWS + 32, :], sin[ROWS : ROWS + 32, :])
    out[:, 512:640] = kv_sum.astype(BF)


def question_project(pieces, weights, tables):
    return pl.pallas_call(
        question_project_kernel,
        out_shape=jax.ShapeDtypeStruct((32, 640), BF),
        in_specs=[VM] * 5,
        out_specs=VM,
        compiler_params=pltpu.CompilerParams(vmem_limit_bytes=VMEM_LIMIT),
        cost_estimate=pl.CostEstimate(flops=2 * 256 * 8192 * 640, bytes_accessed=8192 * 640 * 2, transcendentals=0),
    )(pieces, *weights, *tables)


def key_value_kernel(own, partner, cos, sin, out):
    is_lower = (places()[1] & 1) == 0
    mine, other = own[...].astype(F32), partner[...].astype(F32)
    low = jnp.where(is_lower, mine, other)
    high = jnp.where(is_lower, other, mine)
    lane = lax.broadcasted_iota(jnp.int32, low.shape, 1)
    keys = jnp.where(lane < 64, low, pltpu.roll(high, 64, 1))
    values = jnp.where(lane < 64, pltpu.roll(low, 64, 1), high)
    out[:, :HD] = (keys * cos[...] + pltpu.roll(keys, 64, 1) * sin[...]).astype(BF)
    out[:, HD:] = values.astype(BF)


def key_value(own, partner, cos, sin):
    return pl.pallas_call(
        key_value_kernel,
        out_shape=jax.ShapeDtypeStruct((ALL, 2 * HD), BF),
        in_specs=[VM, VM, VM, VM],
        out_specs=VM,
        compiler_params=pltpu.CompilerParams(vmem_limit_bytes=VMEM_LIMIT),
    )(own, partner, cos, sin)


def scores_of(queries, keys):
    return lax.dot_general(queries, keys, (((1,), (1,)), ((), ())), preferred_element_type=F32)


def weights_of(scores, top):
    return jnp.exp2(scores * SCALE2 - top * SCALE2)


def columns_to_stats(columns):
    rows = columns[0].shape[0]
    lane = lax.broadcasted_iota(jnp.int32, (rows, 128), 1)
    stats = jnp.zeros((rows, 128), F32)
    for index, column in enumerate(columns):
        stats = jnp.where(lane == index, column, stats)
    return stats


def dot_keys(weights, values):
    return lax.dot_general(weights, values, (((0,), (0,)), ((), ())), preferred_element_type=F32)


def own_kernel(lengths, q, kv, weighted, stats):
    _, _, z, core = places()
    length = lengths[2 * z + core]
    for tile in range(2):
        rows = slice(tile * 256, tile * 256 + 256)
        width = 256 * (tile + 1)
        key = lax.broadcasted_iota(jnp.int32, (width, 256), 0)
        row = tile * 256 + lax.broadcasted_iota(jnp.int32, (width, 256), 1)
        bias = jnp.where((key <= row) & (key < length), 0.0, NEG)
        for head in range(4):
            cols = slice(head * HD, (head + 1) * HD)
            s = scores_of(kv[:width, :HD], q[rows, cols]) + bias
            top = jnp.max(s, axis=0, keepdims=True)
            e = weights_of(s, top)
            stats[head : head + 1, rows] = top
            stats[head + 8 : head + 9, rows] = jnp.sum(e, axis=0, keepdims=True)
            weighted[rows, cols] = dot_keys(e.astype(BF), kv[:width, HD:])


def own_attention(lengths, q, kv):
    return pl.pallas_call(
        own_kernel,
        out_shape=[jax.ShapeDtypeStruct((512, 512), F32), jax.ShapeDtypeStruct((16, 512), F32)],
        in_specs=[SM, VM, VM],
        out_specs=[VM, VM],
        compiler_params=pltpu.CompilerParams(vmem_limit_bytes=VMEM_LIMIT),
        cost_estimate=pl.CostEstimate(flops=4 * 4 * 512 * 512 * 128, bytes_accessed=3 << 20, transcendentals=1 << 20),
    )(lengths, q, kv)


def nearer_kernel(own, below, across, above, out):
    _, _, z, _ = places()
    for plane, source in enumerate((own, below, across, above)):

        @pl.when(z == plane)
        def _(source=source):
            out[...] = source[:ROWS, :]


def nearer_anchor(own, below, across, above):
    return pl.pallas_call(
        nearer_kernel,
        out_shape=jax.ShapeDtypeStruct((ROWS, 2 * HD), BF),
        in_specs=[VM] * 4,
        out_specs=VM,
        compiler_params=pltpu.CompilerParams(vmem_limit_bytes=VMEM_LIMIT),
        cost_estimate=pl.CostEstimate(flops=0, bytes_accessed=1 << 19, transcendentals=0),
    )(own, below, across, above)


def anchor_kernel(lengths, q, kv_zero, kv_one, weighted, stats, out, kv):
    _, _, z, core = places()
    length = lengths[2 * z + core]
    anchor_length = jnp.where(2 * z + core > 0, lengths[0], 0)

    @pl.when(core == 0)
    def _():
        kv[...] = kv_zero[...]

    @pl.when(core != 0)
    def _():
        kv[...] = kv_one[...]

    key = lax.broadcasted_iota(jnp.int32, (512, 1), 0)
    bias = jnp.where(key < anchor_length, 0.0, NEG)
    for tile in range(2):
        rows = slice(tile * 256, tile * 256 + 256)
        live = tile * 256 + lax.broadcasted_iota(jnp.int32, (1, 256), 1) < length
        scaled, factors = [], []
        for head in range(4):
            cols = slice(head * HD, (head + 1) * HD)
            s = scores_of(kv[:, :HD], q[rows, cols]) + bias
            own_top, own_sum = stats[head : head + 1, rows], stats[head + 8 : head + 9, rows]
            top = jnp.maximum(own_top, jnp.max(s, axis=0, keepdims=True))
            e = weights_of(s, top)
            factor = weights_of(own_top, top)
            total = own_sum * factor + jnp.sum(e, axis=0, keepdims=True)
            share = jnp.where(live, 1.0 / total, 0.0)
            scaled.append(dot_keys((e * share).astype(BF), kv[:, HD:]))
            factors.append(factor * share)
        across = jnp.concatenate(factors + factors, axis=0).T
        for head in range(4):
            cols = slice(head * HD, (head + 1) * HD)
            out[rows, cols] = (weighted[rows, cols] * across[:, head : head + 1] + scaled[head]).astype(BF)


def anchor_attention(lengths, q, kv_zero, kv_one, weighted, stats):
    return pl.pallas_call(
        anchor_kernel,
        out_shape=jax.ShapeDtypeStruct((512, 512), BF),
        in_specs=[SM, VM, VM, VM, VM, VM],
        out_specs=VM,
        scratch_shapes=[pltpu.VMEM((ROWS, 2 * HD), BF)],
        compiler_params=pltpu.CompilerParams(vmem_limit_bytes=VMEM_LIMIT),
        cost_estimate=pl.CostEstimate(flops=4 * 4 * 512 * 512 * 128, bytes_accessed=3 << 20, transcendentals=1 << 20),
    )(lengths, q, kv_zero, kv_one, weighted, stats)


def question_kernel(lengths_ref, q_own, q_other, kv_0, kv_1, kv_2, kv_3, out_own, out_other):
    kvs = (kv_0, kv_1, kv_2, kv_3)
    _, _, z, core = places()
    ctx = 2 * z + core
    blocks = [z, (z + 3) & 3, (z + 1) & 3, (z + 2) & 3]
    lengths = [lengths_ref[2 * block + core] for block in blocks]
    stacked = [q_own[:, h * HD : (h + 1) * HD] for h in range(4)]
    stacked += [q_other[:, h * HD : (h + 1) * HD] for h in range(4)]
    q = jnp.concatenate(stacked, axis=0)
    scores = []
    key = lax.broadcasted_iota(jnp.int32, (1, 512), 1)
    for kv, length in zip(kvs, lengths):
        scores.append(scores_of(q, kv[:ROWS, :HD]) + jnp.where(key < length, 0.0, NEG))
    row = lax.broadcasted_iota(jnp.int32, (256, 128), 0)
    lane = lax.broadcasted_iota(jnp.int32, (256, 128), 1)
    row_id = row % 32 + 32 * jnp.where(row < 128, ctx, ctx + 1 - 2 * core)
    block = jnp.where(lane < 64, jnp.where(lane < 32, blocks[0], blocks[1]), jnp.where(lane < 96, blocks[2], blocks[3]))
    key_id = lane % 32 + 32 * (2 * block + core)
    asked_keys = jnp.concatenate([kv[ROWS:, :HD] for kv in kvs], axis=0)
    asked_values = jnp.concatenate([kv[ROWS:, HD:] for kv in kvs], axis=0)
    scores.append(jnp.where(key_id <= row_id, scores_of(q, asked_keys), NEG))
    top = jnp.max(scores[-1], axis=1, keepdims=True)
    for s in scores[:-1]:
        top = jnp.maximum(top, jnp.max(s, axis=1, keepdims=True))
    values = [kv[:ROWS, HD:] for kv in kvs] + [asked_values]
    total = jnp.zeros((256, 1), F32)
    both = jnp.zeros((256, HD), F32)
    for s, value in zip(scores, values):
        e = weights_of(s, top)
        total = total + jnp.sum(e, axis=1, keepdims=True)
        both = both + jnp.dot(e.astype(BF), value, preferred_element_type=F32)
    for out, start in ((out_own, 0), (out_other, 128)):
        tops, totals = [], []
        for head in range(4):
            rows = slice(start + head * 32, start + head * 32 + 32)
            out[:, head * HD : (head + 1) * HD] = both[rows]
            tops.append(top[rows])
            totals.append(total[rows])
        out[:, 512:640] = columns_to_stats(tops + totals)


def question_attention(lengths, q_own, q_other, kvs):
    part = jax.ShapeDtypeStruct((32, 640), F32)
    return pl.pallas_call(
        question_kernel,
        out_shape=[part, part],
        in_specs=[SM] + [VM] * 6,
        out_specs=[VM, VM],
        compiler_params=pltpu.CompilerParams(vmem_limit_bytes=VMEM_LIMIT),
        cost_estimate=pl.CostEstimate(flops=4 * 256 * 2176 * 128, bytes_accessed=2 << 20, transcendentals=1 << 19),
    )(lengths, q_own, q_other, *kvs)


def merge_kernel(a, b, out):
    stat_a, stat_b = a[:, 512:640], b[:, 512:640]
    for head in range(4):
        cols = slice(head * HD, (head + 1) * HD)
        top_a, top_b = stat_a[:, head : head + 1], stat_b[:, head : head + 1]
        top = jnp.maximum(top_a, top_b)
        factor_a, factor_b = weights_of(top_a, top), weights_of(top_b, top)
        total = stat_a[:, head + 4 : head + 5] * factor_a + stat_b[:, head + 4 : head + 5] * factor_b
        out[:, cols] = ((a[:, cols] * factor_a + b[:, cols] * factor_b) / total).astype(BF)


def merge(a, b):
    return pl.pallas_call(
        merge_kernel,
        out_shape=jax.ShapeDtypeStruct((32, 512), BF),
        in_specs=[VM, VM],
        out_specs=VM,
        compiler_params=pltpu.CompilerParams(vmem_limit_bytes=VMEM_LIMIT),
    )(a, b)


PLAN_1 = [
    ((0, 0), 0, 512, [(0, 0, 512)]),
    ((-1, 0), 0, 512, [(1, 0, 512)]),
    ((1, 0), 0, 512, [(2, 0, 512)]),
    ((0, -1), 0, 512, [(3, 0, 512)]),
    ((0, 1), 0, 512, [(4, 0, 512)]),
    ((2, 0), 0, 256, [(5, 0, 256)]),
    ((0, 2), 256, 512, [(6, 0, 256)]),
]
PLAN_2 = [
    ((-1, -1), 0, 512, [(0, 0, 256), (2, 0, 256)]),
    ((1, -1), 0, 512, [(0, 256, 256), (3, 0, 256)]),
    ((-1, 1), 0, 512, [(1, 0, 256), (2, 256, 256)]),
    ((1, 1), 0, 512, [(1, 256, 256), (3, 256, 256)]),
    ((2, -1), 0, 256, [(0, 512, 256)]),
    ((2, 1), 0, 256, [(1, 512, 256)]),
    ((-1, 2), 256, 512, [(2, 512, 256)]),
    ((1, 2), 256, 512, [(3, 512, 256)]),
    ((0, 2), 0, 256, [(0, 768, 128), (1, 768, 128)]),
    ((2, 0), 256, 512, [(2, 768, 128), (3, 768, 128)]),
]
PLAN_3 = [
    ((2, 2), 0, 512, [(1, 128, 256), (3, 128, 256)]),
    ((-1, 2), 0, 256, [(0, 0, 256)]),
    ((1, 2), 0, 256, [(0, 256, 128), (1, 0, 128)]),
    ((2, -1), 256, 512, [(2, 0, 256)]),
    ((2, 1), 256, 512, [(2, 256, 128), (3, 0, 128)]),
]
NEAR_Y = [(0, 0, 256), (1, 0, 256), (4, 0, 256)]
NEAR_X = [(2, 256, 256), (3, 256, 256), (4, 0, 256)]
PACK_2 = [NEAR_Y + [(2, 0, 128)], NEAR_Y + [(3, 128, 128)], NEAR_X + [(0, 256, 128)], NEAR_X + [(1, 384, 128)]]
PACK_3 = [[(0, 0, 384)], [(1, 384, 384)]]


def tables_of(positions):
    inverse_freq = ROPE_BASE ** (-(jnp.arange(HD // 2, dtype=jnp.float32) * 2.0 / HD))
    inverse_freq = jnp.concatenate([inverse_freq, inverse_freq])
    phases = positions.astype(jnp.float32)[:, None] * inverse_freq[None, :]
    signs = jnp.where(jnp.arange(HD) < HD // 2, -1.0, 1.0).astype(jnp.float32)
    return jnp.cos(phases), jnp.sin(phases) * signs[None, :]


def shift_z(array, dz):
    pairs = [(i, ((i // 2 + dz) % 4) * 2 + i % 2) for i in range(8)]
    return lax.ppermute(array, "ctx", pairs)


def per_device(context, question, w_query, w_key, w_value, lengths, owner):
    ctx = lax.axis_index("ctx")
    ids = jnp.arange(8, dtype=jnp.int32)
    own_offset = jnp.sum(jnp.where(ids < ctx, lengths, 0))
    filled = jnp.sum(lengths)

    up = shift_heads(context, 1, 0)
    down = shift_heads(context, -1, 0)
    right = shift_heads(context, 0, 1)
    left = shift_heads(context, 0, -1)
    low, high = pack([[(0, 0, 256)], [(0, 256, 256)]], [context])
    low, high, cut = lax.optimization_barrier((low, high, owner))
    far_y = shift_heads(low, 2, 0)
    up, high = lax.optimization_barrier((up, high))
    far_x = shift_heads(high, 0, 2)

    share = lax.all_to_all(question[0].reshape(8, 32, 512), "ctx", 0, 0)
    share = lax.dynamic_index_in_dim(share, cut[0], 0, False)
    share = jnp.broadcast_to(share[None], (16, 32, 512))
    pieces = lax.all_to_all(share, "heads", 0, 0)
    up, pieces = lax.optimization_barrier((up, pieces))

    to_right, to_left = pack(PACK_2[:2], [up, down, right, left, far_y])
    to_up, to_down = pack(PACK_2[2:], [up, down, right, left, far_x])
    a_right, a_left = shift_heads(to_right, 0, 1), shift_heads(to_left, 0, -1)
    b_up, b_down = shift_heads(to_up, 1, 0), shift_heads(to_down, -1, 0)
    up, to_right = lax.optimization_barrier((up, to_right))
    tables = tables_of(
        jnp.concatenate(
            [own_offset + jnp.arange(ROWS, dtype=jnp.int32), filled + 32 * ctx + jnp.arange(ASKED, dtype=jnp.int32)]
        )
    )
    pieces, w_query, w_key, w_value, tables = lax.optimization_barrier(
        (pieces, w_query, w_key, w_value, tables)
    )
    weights = hold(w_query, w_key.T, w_value.T)
    accs = project([context, up, down, right, left, far_y, far_x], PLAN_1, weights, None, True, True)
    q_share = question_project(pieces, weights, tables)

    a_right, a_left, accs, q_share = lax.optimization_barrier((a_right, a_left, accs, q_share))
    to_right, to_left = pack(PACK_3, [a_right, a_left])
    to_up, to_down = pack(PACK_3, [b_up, b_down])
    last = [
        shift_heads(to_right, 0, 1),
        shift_heads(to_left, 0, -1),
        shift_heads(to_up, 1, 0),
        shift_heads(to_down, -1, 0),
    ]
    accs = project([a_right, a_left, b_up, b_down], PLAN_2, weights, accs, True, True)

    (halves,) = project(last, PLAN_3, weights, accs, False, True, True, asked=q_share)
    (queries,) = project(last, PLAN_3, weights, accs, True, False, True, tables)
    partner = swap_heads(halves, 0, 1)
    q_asked = q_share[:, :512]
    q_other = swap_ctx(q_asked, 0, 1)
    partner, queries, q_other = lax.optimization_barrier((partner, queries, q_other))
    kv = key_value(halves, partner, *tables)

    below, above, across = shift_z(kv, 1), shift_z(kv, -1), shift_z(kv, 2)
    weighted, stats = own_attention(lengths, queries, kv)
    below, above, across, weighted = lax.optimization_barrier((below, above, across, weighted))
    nearer = nearer_anchor(kv, below, across, above)
    from_zero = lax.ppermute(nearer, "ctx", [(0, 1), (2, 3), (4, 5), (6, 7)])
    part, part_other = question_attention(lengths, q_asked, q_other, [kv, below, above, across])
    from_zero, part = lax.optimization_barrier((from_zero, part))
    context_attn = anchor_attention(lengths, queries, nearer, from_zero, weighted, stats)
    question_attn = merge(part, swap_ctx(part_other, 0, 1))
    return (context_attn, question_attn)


def solution(mesh):
    in_specs = (
        P("ctx", "heads"),
        P("ctx", None, "heads"),
        P(None, "heads"),
        P(None, "heads"),
        P(None, "heads"),
        P(),
        P(),
    )
    out_specs = (P("ctx", "heads"), P("ctx", "heads"))
    return jax.shard_map(
        per_device, mesh=mesh, in_specs=in_specs, out_specs=out_specs, check_vma=False
    )
```

```python
import functools

import jax
import jax.numpy as jnp
from jax import lax
from jax.experimental import pallas as pl
from jax.experimental.pallas import tpu as pltpu
from jax.sharding import PartitionSpec as P

HD = 128
ROPE_BASE = 500000.0
BF = jnp.bfloat16
F32 = jnp.float32
VMEM_LIMIT = 8 * 1024 * 1024
HOLD_LIMIT = 37 * 1024 * 1024
NEG = -3.4e38
SCALE2 = HD ** (-0.5) * 1.4426950408889634
ROWS = 512
ASKED = 32
ALL = ROWS + ASKED

HBM = pl.BlockSpec(memory_space=pltpu.HBM)
VM = pl.BlockSpec(memory_space=pltpu.VMEM)
SM = pl.BlockSpec(memory_space=pltpu.SMEM)


def shift_heads(array, dy, dx):
    pairs = [(i, ((i // 4 + dy) % 4) * 4 + (i % 4 + dx) % 4) for i in range(16)]
    return lax.ppermute(array, "heads", pairs)


def swap_heads(array, my, mx):
    pairs = [(i, ((i // 4) ^ my) * 4 + ((i % 4) ^ mx)) for i in range(16)]
    return lax.ppermute(array, "heads", pairs)


def swap_ctx(array, mz, mc):
    pairs = [(i, ((i // 2) ^ mz) * 2 + ((i % 2) ^ mc)) for i in range(8)]
    return lax.ppermute(array, "ctx", pairs)


def places():
    heads, ctx = lax.axis_index("heads"), lax.axis_index("ctx")
    return lax.shift_right_logical(heads, 2), heads & 3, lax.shift_right_logical(ctx, 1), ctx & 1


def pack_kernel(plan, n_in, *refs):
    ins, outs = refs[:n_in], refs[n_in:]
    for out, pieces in zip(outs, plan):
        row = 0
        for operand, start, count in pieces:
            out[row : row + count, :] = ins[operand][start : start + count, :]
            row += count


def pack(plan, ins):
    return pl.pallas_call(
        functools.partial(pack_kernel, plan, len(ins)),
        out_shape=[jax.ShapeDtypeStruct((sum(p[2] for p in pieces), 512), BF) for pieces in plan],
        in_specs=[VM] * len(ins),
        out_specs=[VM] * len(plan),
        compiler_params=pltpu.CompilerParams(vmem_limit_bytes=VMEM_LIMIT),
        cost_estimate=pl.CostEstimate(flops=0, bytes_accessed=1 << 20, transcendentals=0),
    )(*ins)


def hold_kernel(wq, wk, wv, q_out, kv_out, sem):
    copies = []
    for part in range(8):
        rows = pl.ds(part * 1024, 1024)
        copies.append(pltpu.make_async_copy(wq.at[rows, :], q_out.at[rows, :], sem.at[part]))
    for part in range(4):
        cols = pl.ds(part * 2048, 2048)
        copies.append(pltpu.make_async_copy(wk.at[:, cols], kv_out.at[pl.ds(0, 64), cols], sem.at[8 + part]))
        copies.append(pltpu.make_async_copy(wv.at[:, cols], kv_out.at[pl.ds(64, 64), cols], sem.at[12 + part]))
    for copy in copies:
        copy.start()
    for copy in copies:
        copy.wait()


def hold(wq, wk, wv):
    return pl.pallas_call(
        hold_kernel,
        out_shape=[jax.ShapeDtypeStruct((8192, 512), BF), jax.ShapeDtypeStruct((128, 8192), BF)],
        in_specs=[HBM] * 3,
        out_specs=[VM, VM],
        scratch_shapes=[pltpu.SemaphoreType.DMA((16,))],
        compiler_params=pltpu.CompilerParams(vmem_limit_bytes=HOLD_LIMIT),
        cost_estimate=pl.CostEstimate(flops=0, bytes_accessed=20 << 20, transcendentals=0),
    )(wq, wk, wv)


def turn(part, cos, sin):
    return (part * cos + pltpu.roll(part, HD // 2, 1) * sin).astype(BF)


def project_kernel(plan, n_x, with_q, with_kv, has_acc, finish, *refs):
    refs = list(refs)
    take = lambda count: [refs.pop(0) for _ in range(count)]
    xs = take(n_x)
    wq = take(1)[0] if with_q else None
    wkv = take(1)[0] if with_kv else None
    acc_q = take(1)[0] if has_acc and with_q else None
    acc_kv = take(1)[0] if has_acc and with_kv else None
    cos, sin = take(2) if finish and with_q else (None, None)
    asked = take(1)[0] if finish and with_kv else None
    q_out = take(1)[0] if with_q else None
    kv_out = take(1)[0] if with_kv else None
    q_sum = take(1)[0] if finish and with_q else q_out
    kv_sum = take(1)[0] if finish and with_kv else kv_out
    y, x, _, _ = places()
    if has_acc:
        if with_q:
            q_sum[...] = acc_q[...]
        if with_kv:
            kv_sum[...] = acc_kv[...]
    for slot, ((dy, dx), low, high, uses) in enumerate(plan):
        base = pl.multiple_of((((y + dy) & 3) * 4 + ((x + dx) & 3)) * 512, 512)
        parts = [xs[operand][pl.ds(start, count), :] for operand, start, count in uses]
        piece = parts[0] if len(parts) == 1 else jnp.concatenate(parts, axis=0)
        fresh = slot == 0 and not has_acc
        if with_kv:
            both = wkv[:, pl.ds(base, 512)]
            term = lax.dot_general(piece, both, (((1,), (1,)), ((), ())), preferred_element_type=F32)
            kv_sum[low:high, :] = term if fresh else kv_sum[low:high, :] + term
        if with_q:
            term = jnp.dot(piece, wq[pl.ds(base, 512), :], preferred_element_type=F32)
            q_sum[low:high, :] = term if fresh else q_sum[low:high, :] + term
    if finish and with_kv:
        kv_out[:ROWS, :] = kv_sum[...].astype(BF)
        kv_out[ROWS:, :] = asked[:, 512:640]
    if finish and with_q:
        for head in range(4):
            cols = slice(head * HD, (head + 1) * HD)
            q_out[:, cols] = turn(q_sum[:, cols], cos[:ROWS, :], sin[:ROWS, :])


def project(xs, plan, weights, accs, with_q, with_kv, finish=False, tables=None, asked=None):
    wq, wkv = weights
    operands, specs = list(xs), [VM] * len(xs)
    if with_q:
        operands.append(wq)
        specs.append(VM)
    if with_kv:
        operands.append(wkv)
        specs.append(VM)
    has_acc = accs is not None
    if has_acc:
        if with_q:
            operands.append(accs[0])
            specs.append(VM)
        if with_kv:
            operands.append(accs[1])
            specs.append(VM)
    if finish and with_q:
        operands += list(tables)
        specs += [VM, VM]
    if finish and with_kv:
        operands.append(asked)
        specs.append(VM)
    outs, scratch = [], []
    if with_q:
        outs.append(jax.ShapeDtypeStruct((ROWS, 512), BF if finish else F32))
        if finish:
            scratch.append(pltpu.VMEM((ROWS, 512), F32))
    if with_kv:
        outs.append(jax.ShapeDtypeStruct((ALL, 128), BF) if finish else jax.ShapeDtypeStruct((ROWS, 128), F32))
        if finish:
            scratch.append(pltpu.VMEM((ROWS, 128), F32))
    columns = (512 if with_q else 0) + (128 if with_kv else 0)
    used = sum(high - low for _, low, high, _ in plan)
    return pl.pallas_call(
        functools.partial(project_kernel, plan, len(xs), with_q, with_kv, has_acc, finish),
        out_shape=outs,
        in_specs=specs,
        out_specs=[VM] * len(outs),
        scratch_shapes=scratch,
        compiler_params=pltpu.CompilerParams(vmem_limit_bytes=VMEM_LIMIT),
        cost_estimate=pl.CostEstimate(
            flops=2 * used * 512 * columns, bytes_accessed=len(plan) * 512 * columns * 2, transcendentals=0
        ),
    )(*operands)


def question_project_kernel(pieces, wq, wkv, cos, sin, out):
    q_sum, kv_sum = None, None
    for place in range(16):
        base = place * 512
        piece = pieces[place]
        both = wkv[:, pl.ds(base, 512)]
        kv_term = lax.dot_general(piece, both, (((1,), (1,)), ((), ())), preferred_element_type=F32)
        q_term = jnp.dot(piece, wq[pl.ds(base, 512), :], preferred_element_type=F32)
        q_sum = q_term if q_sum is None else q_sum + q_term
        kv_sum = kv_term if kv_sum is None else kv_sum + kv_term
    for head in range(4):
        cols = slice(head * HD, (head + 1) * HD)
        out[:, cols] = turn(q_sum[:, cols], cos[ROWS : ROWS + 32, :], sin[ROWS : ROWS + 32, :])
    out[:, 512:640] = kv_sum.astype(BF)


def question_project(pieces, weights, tables):
    return pl.pallas_call(
        question_project_kernel,
        out_shape=jax.ShapeDtypeStruct((32, 640), BF),
        in_specs=[VM] * 5,
        out_specs=VM,
        compiler_params=pltpu.CompilerParams(vmem_limit_bytes=VMEM_LIMIT),
        cost_estimate=pl.CostEstimate(flops=2 * 256 * 8192 * 640, bytes_accessed=8192 * 640 * 2, transcendentals=0),
    )(pieces, *weights, *tables)


def key_value_kernel(own, partner, cos, sin, out):
    is_lower = (places()[1] & 1) == 0
    mine, other = own[...].astype(F32), partner[...].astype(F32)
    low = jnp.where(is_lower, mine, other)
    high = jnp.where(is_lower, other, mine)
    lane = lax.broadcasted_iota(jnp.int32, low.shape, 1)
    keys = jnp.where(lane < 64, low, pltpu.roll(high, 64, 1))
    values = jnp.where(lane < 64, pltpu.roll(low, 64, 1), high)
    out[:, :HD] = (keys * cos[...] + pltpu.roll(keys, 64, 1) * sin[...]).astype(BF)
    out[:, HD:] = values.astype(BF)


def key_value(own, partner, cos, sin):
    return pl.pallas_call(
        key_value_kernel,
        out_shape=jax.ShapeDtypeStruct((ALL, 2 * HD), BF),
        in_specs=[VM, VM, VM, VM],
        out_specs=VM,
        compiler_params=pltpu.CompilerParams(vmem_limit_bytes=VMEM_LIMIT),
    )(own, partner, cos, sin)


def scores_of(queries, keys):
    return lax.dot_general(queries, keys, (((1,), (1,)), ((), ())), preferred_element_type=F32)


def weights_of(scores, top):
    return jnp.exp2(scores * SCALE2 - top * SCALE2)


def columns_to_stats(columns):
    rows = columns[0].shape[0]
    lane = lax.broadcasted_iota(jnp.int32, (rows, 128), 1)
    stats = jnp.zeros((rows, 128), F32)
    for index, column in enumerate(columns):
        stats = jnp.where(lane == index, column, stats)
    return stats


def dot_keys(weights, values):
    return lax.dot_general(weights, values, (((0,), (0,)), ((), ())), preferred_element_type=F32)


def own_kernel(lengths, q, kv, weighted, stats):
    _, _, z, core = places()
    length = lengths[2 * z + core]
    for tile in range(2):
        rows = slice(tile * 256, tile * 256 + 256)
        width = 256 * (tile + 1)
        key = lax.broadcasted_iota(jnp.int32, (width, 256), 0)
        row = tile * 256 + lax.broadcasted_iota(jnp.int32, (width, 256), 1)
        cap = jnp.where((key <= row) & (key < length), -NEG, NEG)
        for head in range(4):
            cols = slice(head * HD, (head + 1) * HD)
            s = jnp.minimum(scores_of(kv[:width, :HD], q[rows, cols]), cap)
            top = jnp.max(s, axis=0, keepdims=True)
            e = weights_of(s, top)
            stats[head : head + 1, rows] = top
            stats[head + 8 : head + 9, rows] = jnp.sum(e, axis=0, keepdims=True)
            weighted[rows, cols] = dot_keys(e.astype(BF), kv[:width, HD:])


def own_attention(lengths, q, kv):
    return pl.pallas_call(
        own_kernel,
        out_shape=[jax.ShapeDtypeStruct((512, 512), F32), jax.ShapeDtypeStruct((16, 512), F32)],
        in_specs=[SM, VM, VM],
        out_specs=[VM, VM],
        compiler_params=pltpu.CompilerParams(vmem_limit_bytes=VMEM_LIMIT),
        cost_estimate=pl.CostEstimate(flops=4 * 4 * 512 * 512 * 128, bytes_accessed=3 << 20, transcendentals=1 << 20),
    )(lengths, q, kv)


def nearer_kernel(own, below, across, above, out):
    _, _, z, _ = places()
    for plane, source in enumerate((own, below, across, above)):

        @pl.when(z == plane)
        def _(source=source):
            out[...] = source[:ROWS, :]


def nearer_anchor(own, below, across, above):
    return pl.pallas_call(
        nearer_kernel,
        out_shape=jax.ShapeDtypeStruct((ROWS, 2 * HD), BF),
        in_specs=[VM] * 4,
        out_specs=VM,
        compiler_params=pltpu.CompilerParams(vmem_limit_bytes=VMEM_LIMIT),
        cost_estimate=pl.CostEstimate(flops=0, bytes_accessed=1 << 19, transcendentals=0),
    )(own, below, across, above)


def anchor_kernel(lengths, q, kv_zero, kv_one, weighted, stats, out, kv):
    _, _, z, core = places()
    length = lengths[2 * z + core]
    anchor_length = jnp.where(2 * z + core > 0, lengths[0], 0)

    @pl.when(core == 0)
    def _():
        kv[...] = kv_zero[...]

    @pl.when(core != 0)
    def _():
        kv[...] = kv_one[...]

    key = lax.broadcasted_iota(jnp.int32, (512, 1), 0)
    cap = jnp.where(key < anchor_length, -NEG, NEG)
    for tile in range(2):
        rows = slice(tile * 256, tile * 256 + 256)
        live = tile * 256 + lax.broadcasted_iota(jnp.int32, (1, 256), 1) < length
        scaled, factors = [], []
        for head in range(4):
            cols = slice(head * HD, (head + 1) * HD)
            s = jnp.minimum(scores_of(kv[:, :HD], q[rows, cols]), cap)
            own_top, own_sum = stats[head : head + 1, rows], stats[head + 8 : head + 9, rows]
            top = jnp.maximum(own_top, jnp.max(s, axis=0, keepdims=True))
            e = weights_of(s, top)
            factor = weights_of(own_top, top)
            total = own_sum * factor + jnp.sum(e, axis=0, keepdims=True)
            share = jnp.where(live, 1.0 / total, 0.0)
            scaled.append(dot_keys((e * share).astype(BF), kv[:, HD:]))
            factors.append(factor * share)
        across = jnp.concatenate(factors + factors, axis=0).T
        for head in range(4):
            cols = slice(head * HD, (head + 1) * HD)
            out[rows, cols] = (weighted[rows, cols] * across[:, head : head + 1] + scaled[head]).astype(BF)


def anchor_attention(lengths, q, kv_zero, kv_one, weighted, stats):
    return pl.pallas_call(
        anchor_kernel,
        out_shape=jax.ShapeDtypeStruct((512, 512), BF),
        in_specs=[SM, VM, VM, VM, VM, VM],
        out_specs=VM,
        scratch_shapes=[pltpu.VMEM((ROWS, 2 * HD), BF)],
        compiler_params=pltpu.CompilerParams(vmem_limit_bytes=VMEM_LIMIT),
        cost_estimate=pl.CostEstimate(flops=4 * 4 * 512 * 512 * 128, bytes_accessed=3 << 20, transcendentals=1 << 20),
    )(lengths, q, kv_zero, kv_one, weighted, stats)


def question_kernel(lengths_ref, q_own, q_other, kv_0, kv_1, kv_2, kv_3, out_own, out_other):
    kvs = (kv_0, kv_1, kv_2, kv_3)
    _, _, z, core = places()
    ctx = 2 * z + core
    blocks = [z, (z + 3) & 3, (z + 1) & 3, (z + 2) & 3]
    lengths = [lengths_ref[2 * block + core] for block in blocks]
    stacked = [q_own[:, h * HD : (h + 1) * HD] for h in range(4)]
    stacked += [q_other[:, h * HD : (h + 1) * HD] for h in range(4)]
    q = jnp.concatenate(stacked, axis=0)
    scores = []
    key = lax.broadcasted_iota(jnp.int32, (1, 512), 1)
    for kv, length in zip(kvs, lengths):
        scores.append(jnp.minimum(scores_of(q, kv[:ROWS, :HD]), jnp.where(key < length, -NEG, NEG)))
    row = lax.broadcasted_iota(jnp.int32, (256, 128), 0)
    lane = lax.broadcasted_iota(jnp.int32, (256, 128), 1)
    row_id = row % 32 + 32 * jnp.where(row < 128, ctx, ctx + 1 - 2 * core)
    block = jnp.where(lane < 64, jnp.where(lane < 32, blocks[0], blocks[1]), jnp.where(lane < 96, blocks[2], blocks[3]))
    key_id = lane % 32 + 32 * (2 * block + core)
    asked_keys = jnp.concatenate([kv[ROWS:, :HD] for kv in kvs], axis=0)
    asked_values = jnp.concatenate([kv[ROWS:, HD:] for kv in kvs], axis=0)
    scores.append(jnp.where(key_id <= row_id, scores_of(q, asked_keys), NEG))
    top = jnp.max(scores[-1], axis=1, keepdims=True)
    for s in scores[:-1]:
        top = jnp.maximum(top, jnp.max(s, axis=1, keepdims=True))
    values = [kv[:ROWS, HD:] for kv in kvs] + [asked_values]
    total = jnp.zeros((256, 1), F32)
    both = jnp.zeros((256, HD), F32)
    for s, value in zip(scores, values):
        e = weights_of(s, top)
        total = total + jnp.sum(e, axis=1, keepdims=True)
        both = both + jnp.dot(e.astype(BF), value, preferred_element_type=F32)
    for out, start in ((out_own, 0), (out_other, 128)):
        tops, totals = [], []
        for head in range(4):
            rows = slice(start + head * 32, start + head * 32 + 32)
            out[:, head * HD : (head + 1) * HD] = both[rows]
            tops.append(top[rows])
            totals.append(total[rows])
        out[:, 512:640] = columns_to_stats(tops + totals)


def question_attention(lengths, q_own, q_other, kvs):
    part = jax.ShapeDtypeStruct((32, 640), F32)
    return pl.pallas_call(
        question_kernel,
        out_shape=[part, part],
        in_specs=[SM] + [VM] * 6,
        out_specs=[VM, VM],
        compiler_params=pltpu.CompilerParams(vmem_limit_bytes=VMEM_LIMIT),
        cost_estimate=pl.CostEstimate(flops=4 * 256 * 2176 * 128, bytes_accessed=2 << 20, transcendentals=1 << 19),
    )(lengths, q_own, q_other, *kvs)


def merge_kernel(a, b, out):
    stat_a, stat_b = a[:, 512:640], b[:, 512:640]
    for head in range(4):
        cols = slice(head * HD, (head + 1) * HD)
        top_a, top_b = stat_a[:, head : head + 1], stat_b[:, head : head + 1]
        top = jnp.maximum(top_a, top_b)
        factor_a, factor_b = weights_of(top_a, top), weights_of(top_b, top)
        total = stat_a[:, head + 4 : head + 5] * factor_a + stat_b[:, head + 4 : head + 5] * factor_b
        out[:, cols] = ((a[:, cols] * factor_a + b[:, cols] * factor_b) / total).astype(BF)


def merge(a, b):
    return pl.pallas_call(
        merge_kernel,
        out_shape=jax.ShapeDtypeStruct((32, 512), BF),
        in_specs=[VM, VM],
        out_specs=VM,
        compiler_params=pltpu.CompilerParams(vmem_limit_bytes=VMEM_LIMIT),
    )(a, b)


PLAN_1 = [
    ((0, 0), 0, 512, [(0, 0, 512)]),
    ((-1, 0), 0, 512, [(1, 0, 512)]),
    ((1, 0), 0, 512, [(2, 0, 512)]),
    ((0, -1), 0, 512, [(3, 0, 512)]),
    ((0, 1), 0, 512, [(4, 0, 512)]),
    ((2, 0), 0, 256, [(5, 0, 256)]),
    ((0, 2), 256, 512, [(6, 0, 256)]),
]
PLAN_2 = [
    ((-1, -1), 0, 512, [(0, 0, 256), (2, 0, 256)]),
    ((1, -1), 0, 512, [(0, 256, 256), (3, 0, 256)]),
    ((-1, 1), 0, 512, [(1, 0, 256), (2, 256, 256)]),
    ((1, 1), 0, 512, [(1, 256, 256), (3, 256, 256)]),
    ((2, -1), 0, 256, [(0, 512, 256)]),
    ((2, 1), 0, 256, [(1, 512, 256)]),
    ((-1, 2), 256, 512, [(2, 512, 256)]),
    ((1, 2), 256, 512, [(3, 512, 256)]),
    ((0, 2), 0, 256, [(0, 768, 128), (1, 768, 128)]),
    ((2, 0), 256, 512, [(2, 768, 128), (3, 768, 128)]),
]
PLAN_3 = [
    ((2, 2), 0, 512, [(1, 128, 256), (3, 128, 256)]),
    ((-1, 2), 0, 256, [(0, 0, 256)]),
    ((1, 2), 0, 256, [(0, 256, 128), (1, 0, 128)]),
    ((2, -1), 256, 512, [(2, 0, 256)]),
    ((2, 1), 256, 512, [(2, 256, 128), (3, 0, 128)]),
]
NEAR_Y = [(0, 0, 256), (1, 0, 256), (4, 0, 256)]
NEAR_X = [(2, 256, 256), (3, 256, 256), (4, 0, 256)]
PACK_2 = [NEAR_Y + [(2, 0, 128)], NEAR_Y + [(3, 128, 128)], NEAR_X + [(0, 256, 128)], NEAR_X + [(1, 384, 128)]]
PACK_3 = [[(0, 0, 384)], [(1, 384, 384)]]


def tables_of(positions):
    inverse_freq = ROPE_BASE ** (-(jnp.arange(HD // 2, dtype=jnp.float32) * 2.0 / HD))
    inverse_freq = jnp.concatenate([inverse_freq, inverse_freq])
    phases = positions.astype(jnp.float32)[:, None] * inverse_freq[None, :]
    signs = jnp.where(jnp.arange(HD) < HD // 2, -1.0, 1.0).astype(jnp.float32)
    return jnp.cos(phases), jnp.sin(phases) * signs[None, :]


def shift_z(array, dz):
    pairs = [(i, ((i // 2 + dz) % 4) * 2 + i % 2) for i in range(8)]
    return lax.ppermute(array, "ctx", pairs)


def per_device(context, question, w_query, w_key, w_value, lengths, owner):
    ctx = lax.axis_index("ctx")
    ids = jnp.arange(8, dtype=jnp.int32)
    own_offset = jnp.sum(jnp.where(ids < ctx, lengths, 0))
    filled = jnp.sum(lengths)

    up = shift_heads(context, 1, 0)
    down = shift_heads(context, -1, 0)
    right = shift_heads(context, 0, 1)
    left = shift_heads(context, 0, -1)
    low, high = pack([[(0, 0, 256)], [(0, 256, 256)]], [context])
    low, high, cut = lax.optimization_barrier((low, high, owner))
    far_y = shift_heads(low, 2, 0)
    up, high = lax.optimization_barrier((up, high))
    far_x = shift_heads(high, 0, 2)

    share = lax.all_to_all(question[0].reshape(8, 32, 512), "ctx", 0, 0)
    share = lax.dynamic_index_in_dim(share, cut[0], 0, False)
    share = jnp.broadcast_to(share[None], (16, 32, 512))
    pieces = lax.all_to_all(share, "heads", 0, 0)
    up, pieces = lax.optimization_barrier((up, pieces))

    to_right, to_left = pack(PACK_2[:2], [up, down, right, left, far_y])
    to_up, to_down = pack(PACK_2[2:], [up, down, right, left, far_x])
    a_right, a_left = shift_heads(to_right, 0, 1), shift_heads(to_left, 0, -1)
    b_up, b_down = shift_heads(to_up, 1, 0), shift_heads(to_down, -1, 0)
    up, to_right = lax.optimization_barrier((up, to_right))
    tables = tables_of(
        jnp.concatenate(
            [own_offset + jnp.arange(ROWS, dtype=jnp.int32), filled + 32 * ctx + jnp.arange(ASKED, dtype=jnp.int32)]
        )
    )
    pieces, w_query, w_key, w_value, tables = lax.optimization_barrier(
        (pieces, w_query, w_key, w_value, tables)
    )
    weights = hold(w_query, w_key.T, w_value.T)
    accs = project([context, up, down, right, left, far_y, far_x], PLAN_1, weights, None, True, True)
    q_share = question_project(pieces, weights, tables)

    a_right, a_left, accs, q_share = lax.optimization_barrier((a_right, a_left, accs, q_share))
    to_right, to_left = pack(PACK_3, [a_right, a_left])
    to_up, to_down = pack(PACK_3, [b_up, b_down])
    last = [
        shift_heads(to_right, 0, 1),
        shift_heads(to_left, 0, -1),
        shift_heads(to_up, 1, 0),
        shift_heads(to_down, -1, 0),
    ]
    accs = project([a_right, a_left, b_up, b_down], PLAN_2, weights, accs, True, True)

    (halves,) = project(last, PLAN_3, weights, accs, False, True, True, asked=q_share)
    (queries,) = project(last, PLAN_3, weights, accs, True, False, True, tables)
    partner = swap_heads(halves, 0, 1)
    q_asked = q_share[:, :512]
    q_other = swap_ctx(q_asked, 0, 1)
    partner, queries, q_other = lax.optimization_barrier((partner, queries, q_other))
    kv = key_value(halves, partner, *tables)

    below, above, across = shift_z(kv, 1), shift_z(kv, -1), shift_z(kv, 2)
    weighted, stats = own_attention(lengths, queries, kv)
    below, above, across, weighted = lax.optimization_barrier((below, above, across, weighted))
    nearer = nearer_anchor(kv, below, across, above)
    from_zero = lax.ppermute(nearer, "ctx", [(0, 1), (2, 3), (4, 5), (6, 7)])
    part, part_other = question_attention(lengths, q_asked, q_other, [kv, below, above, across])
    from_zero, part = lax.optimization_barrier((from_zero, part))
    context_attn = anchor_attention(lengths, queries, nearer, from_zero, weighted, stats)
    question_attn = merge(part, swap_ctx(part_other, 0, 1))
    return (context_attn, question_attn)


def solution(mesh):
    in_specs = (
        P("ctx", "heads"),
        P("ctx", None, "heads"),
        P(None, "heads"),
        P(None, "heads"),
        P(None, "heads"),
        P(),
        P(),
    )
    out_specs = (P("ctx", "heads"), P("ctx", "heads"))
    return jax.shard_map(
        per_device, mesh=mesh, in_specs=in_specs, out_specs=out_specs, check_vma=False
    )
```

```python
import functools

import jax
import jax.numpy as jnp
from jax import lax
from jax.experimental import pallas as pl
from jax.experimental.pallas import tpu as pltpu
from jax.sharding import PartitionSpec as P

HD = 128
ROPE_BASE = 500000.0
BF = jnp.bfloat16
F32 = jnp.float32
VMEM_LIMIT = 8 * 1024 * 1024
HOLD_LIMIT = 37 * 1024 * 1024
NEG = -3.4e38
SCALE2 = HD ** (-0.5) * 1.4426950408889634
ROWS = 512
ASKED = 32
ALL = ROWS + ASKED

HBM = pl.BlockSpec(memory_space=pltpu.HBM)
VM = pl.BlockSpec(memory_space=pltpu.VMEM)
SM = pl.BlockSpec(memory_space=pltpu.SMEM)


def shift_heads(array, dy, dx):
    pairs = [(i, ((i // 4 + dy) % 4) * 4 + (i % 4 + dx) % 4) for i in range(16)]
    return lax.ppermute(array, "heads", pairs)


def swap_heads(array, my, mx):
    pairs = [(i, ((i // 4) ^ my) * 4 + ((i % 4) ^ mx)) for i in range(16)]
    return lax.ppermute(array, "heads", pairs)


def swap_ctx(array, mz, mc):
    pairs = [(i, ((i // 2) ^ mz) * 2 + ((i % 2) ^ mc)) for i in range(8)]
    return lax.ppermute(array, "ctx", pairs)


def places():
    heads, ctx = lax.axis_index("heads"), lax.axis_index("ctx")
    return lax.shift_right_logical(heads, 2), heads & 3, lax.shift_right_logical(ctx, 1), ctx & 1


def pack_kernel(plan, n_in, *refs):
    ins, outs = refs[:n_in], refs[n_in:]
    for out, pieces in zip(outs, plan):
        row = 0
        for operand, start, count in pieces:
            out[row : row + count, :] = ins[operand][start : start + count, :]
            row += count


def pack(plan, ins):
    return pl.pallas_call(
        functools.partial(pack_kernel, plan, len(ins)),
        out_shape=[jax.ShapeDtypeStruct((sum(p[2] for p in pieces), 512), BF) for pieces in plan],
        in_specs=[VM] * len(ins),
        out_specs=[VM] * len(plan),
        compiler_params=pltpu.CompilerParams(vmem_limit_bytes=VMEM_LIMIT),
        cost_estimate=pl.CostEstimate(flops=0, bytes_accessed=1 << 20, transcendentals=0),
    )(*ins)


def hold_kernel(wq, wk, wv, q_out, kv_out, sem):
    copies = []
    for part in range(8):
        rows = pl.ds(part * 1024, 1024)
        copies.append(pltpu.make_async_copy(wq.at[rows, :], q_out.at[rows, :], sem.at[part]))
    for part in range(4):
        cols = pl.ds(part * 2048, 2048)
        copies.append(pltpu.make_async_copy(wk.at[:, cols], kv_out.at[pl.ds(0, 64), cols], sem.at[8 + part]))
        copies.append(pltpu.make_async_copy(wv.at[:, cols], kv_out.at[pl.ds(64, 64), cols], sem.at[12 + part]))
    for copy in copies:
        copy.start()
    for copy in copies:
        copy.wait()


def hold(wq, wk, wv):
    return pl.pallas_call(
        hold_kernel,
        out_shape=[jax.ShapeDtypeStruct((8192, 512), BF), jax.ShapeDtypeStruct((128, 8192), BF)],
        in_specs=[HBM] * 3,
        out_specs=[VM, VM],
        scratch_shapes=[pltpu.SemaphoreType.DMA((16,))],
        compiler_params=pltpu.CompilerParams(vmem_limit_bytes=HOLD_LIMIT),
        cost_estimate=pl.CostEstimate(flops=0, bytes_accessed=20 << 20, transcendentals=0),
    )(wq, wk, wv)


def turn(part, cos, sin):
    return (part * cos + pltpu.roll(part, HD // 2, 1) * sin).astype(BF)


def project_kernel(plan, n_x, with_q, with_kv, has_acc, finish, *refs):
    refs = list(refs)
    take = lambda count: [refs.pop(0) for _ in range(count)]
    xs = take(n_x)
    wq = take(1)[0] if with_q else None
    wkv = take(1)[0] if with_kv else None
    acc_q = take(1)[0] if has_acc and with_q else None
    acc_kv = take(1)[0] if has_acc and with_kv else None
    cos, sin = take(2) if finish and with_q else (None, None)
    asked = take(1)[0] if finish and with_kv else None
    q_out = take(1)[0] if with_q else None
    kv_out = take(1)[0] if with_kv else None
    q_sum = take(1)[0] if finish and with_q else q_out
    kv_sum = take(1)[0] if finish and with_kv else kv_out
    y, x, _, _ = places()
    if has_acc:
        if with_q:
            q_sum[...] = acc_q[...]
        if with_kv:
            kv_sum[...] = acc_kv[...]
    for slot, ((dy, dx), low, high, uses) in enumerate(plan):
        base = pl.multiple_of((((y + dy) & 3) * 4 + ((x + dx) & 3)) * 512, 512)
        parts = [xs[operand][pl.ds(start, count), :] for operand, start, count in uses]
        piece = parts[0] if len(parts) == 1 else jnp.concatenate(parts, axis=0)
        fresh = slot == 0 and not has_acc
        if with_kv:
            both = wkv[:, pl.ds(base, 512)]
            term = lax.dot_general(piece, both, (((1,), (1,)), ((), ())), preferred_element_type=F32)
            kv_sum[low:high, :] = term if fresh else kv_sum[low:high, :] + term
        if with_q:
            term = jnp.dot(piece, wq[pl.ds(base, 512), :], preferred_element_type=F32)
            q_sum[low:high, :] = term if fresh else q_sum[low:high, :] + term
    if finish and with_kv:
        kv_out[:ROWS, :] = kv_sum[...].astype(BF)
        kv_out[ROWS:, :] = asked[:, 512:640]
    if finish and with_q:
        for head in range(4):
            cols = slice(head * HD, (head + 1) * HD)
            q_out[:, cols] = turn(q_sum[:, cols], cos[:ROWS, :], sin[:ROWS, :])


def project(xs, plan, weights, accs, with_q, with_kv, finish=False, tables=None, asked=None):
    wq, wkv = weights
    operands, specs = list(xs), [VM] * len(xs)
    if with_q:
        operands.append(wq)
        specs.append(VM)
    if with_kv:
        operands.append(wkv)
        specs.append(VM)
    has_acc = accs is not None
    if has_acc:
        if with_q:
            operands.append(accs[0])
            specs.append(VM)
        if with_kv:
            operands.append(accs[1])
            specs.append(VM)
    if finish and with_q:
        operands += list(tables)
        specs += [VM, VM]
    if finish and with_kv:
        operands.append(asked)
        specs.append(VM)
    outs, scratch = [], []
    if with_q:
        outs.append(jax.ShapeDtypeStruct((ROWS, 512), BF if finish else F32))
        if finish:
            scratch.append(pltpu.VMEM((ROWS, 512), F32))
    if with_kv:
        outs.append(jax.ShapeDtypeStruct((ALL, 128), BF) if finish else jax.ShapeDtypeStruct((ROWS, 128), F32))
        if finish:
            scratch.append(pltpu.VMEM((ROWS, 128), F32))
    columns = (512 if with_q else 0) + (128 if with_kv else 0)
    used = sum(high - low for _, low, high, _ in plan)
    return pl.pallas_call(
        functools.partial(project_kernel, plan, len(xs), with_q, with_kv, has_acc, finish),
        out_shape=outs,
        in_specs=specs,
        out_specs=[VM] * len(outs),
        scratch_shapes=scratch,
        compiler_params=pltpu.CompilerParams(vmem_limit_bytes=VMEM_LIMIT),
        cost_estimate=pl.CostEstimate(
            flops=2 * used * 512 * columns, bytes_accessed=len(plan) * 512 * columns * 2, transcendentals=0
        ),
    )(*operands)


def question_project_kernel(pieces, wq, wkv, cos, sin, out):
    q_sum, kv_sum = None, None
    for place in range(16):
        base = place * 512
        piece = pieces[place]
        both = wkv[:, pl.ds(base, 512)]
        kv_term = lax.dot_general(piece, both, (((1,), (1,)), ((), ())), preferred_element_type=F32)
        q_term = jnp.dot(piece, wq[pl.ds(base, 512), :], preferred_element_type=F32)
        q_sum = q_term if q_sum is None else q_sum + q_term
        kv_sum = kv_term if kv_sum is None else kv_sum + kv_term
    for head in range(4):
        cols = slice(head * HD, (head + 1) * HD)
        out[:, cols] = turn(q_sum[:, cols], cos[ROWS : ROWS + 32, :], sin[ROWS : ROWS + 32, :])
    out[:, 512:640] = kv_sum.astype(BF)


def question_project(pieces, weights, tables):
    return pl.pallas_call(
        question_project_kernel,
        out_shape=jax.ShapeDtypeStruct((32, 640), BF),
        in_specs=[VM] * 5,
        out_specs=VM,
        compiler_params=pltpu.CompilerParams(vmem_limit_bytes=VMEM_LIMIT),
        cost_estimate=pl.CostEstimate(flops=2 * 256 * 8192 * 640, bytes_accessed=8192 * 640 * 2, transcendentals=0),
    )(pieces, *weights, *tables)


def key_value_kernel(own, partner, cos, sin, out):
    is_lower = (places()[1] & 1) == 0
    mine, other = own[...].astype(F32), partner[...].astype(F32)
    low = jnp.where(is_lower, mine, other)
    high = jnp.where(is_lower, other, mine)
    lane = lax.broadcasted_iota(jnp.int32, low.shape, 1)
    keys = jnp.where(lane < 64, low, pltpu.roll(high, 64, 1))
    values = jnp.where(lane < 64, pltpu.roll(low, 64, 1), high)
    out[:, :HD] = (keys * cos[...] + pltpu.roll(keys, 64, 1) * sin[...]).astype(BF)
    out[:, HD:] = values.astype(BF)


def key_value(own, partner, cos, sin):
    return pl.pallas_call(
        key_value_kernel,
        out_shape=jax.ShapeDtypeStruct((ALL, 2 * HD), BF),
        in_specs=[VM, VM, VM, VM],
        out_specs=VM,
        compiler_params=pltpu.CompilerParams(vmem_limit_bytes=VMEM_LIMIT),
    )(own, partner, cos, sin)


def scores_of(queries, keys):
    return lax.dot_general(queries, keys, (((1,), (1,)), ((), ())), preferred_element_type=F32)


def weights_of(scores, top):
    return jnp.exp2(scores * SCALE2 - top * SCALE2)


def columns_to_stats(columns):
    rows = columns[0].shape[0]
    lane = lax.broadcasted_iota(jnp.int32, (rows, 128), 1)
    stats = jnp.zeros((rows, 128), F32)
    for index, column in enumerate(columns):
        stats = jnp.where(lane == index, column, stats)
    return stats


def dot_keys(weights, values):
    return lax.dot_general(weights, values, (((0,), (0,)), ((), ())), preferred_element_type=F32)


def own_kernel(lengths, q, kv, weighted, stats):
    _, _, z, core = places()
    length = lengths[2 * z + core]
    for tile in range(2):
        rows = slice(tile * 256, tile * 256 + 256)
        width = 256 * (tile + 1)
        key = lax.broadcasted_iota(jnp.int32, (width, 256), 0)
        row = tile * 256 + lax.broadcasted_iota(jnp.int32, (width, 256), 1)
        cap = jnp.where((key <= row) & (key < length), -NEG, NEG)
        for head in range(4):
            cols = slice(head * HD, (head + 1) * HD)
            s = jnp.minimum(scores_of(kv[:width, :HD], q[rows, cols]), cap)
            top = jnp.max(s, axis=0, keepdims=True)
            e = weights_of(s, top)
            stats[head : head + 1, rows] = top
            stats[head + 8 : head + 9, rows] = jnp.sum(e, axis=0, keepdims=True)
            weighted[rows, cols] = dot_keys(e.astype(BF), kv[:width, HD:])


def own_attention(lengths, q, kv):
    return pl.pallas_call(
        own_kernel,
        out_shape=[jax.ShapeDtypeStruct((512, 512), F32), jax.ShapeDtypeStruct((16, 512), F32)],
        in_specs=[SM, VM, VM],
        out_specs=[VM, VM],
        compiler_params=pltpu.CompilerParams(vmem_limit_bytes=VMEM_LIMIT),
        cost_estimate=pl.CostEstimate(flops=4 * 4 * 512 * 512 * 128, bytes_accessed=3 << 20, transcendentals=1 << 20),
    )(lengths, q, kv)


def nearer_kernel(own, below, across, above, out):
    _, _, z, _ = places()
    for plane, source in enumerate((own, below, across, above)):

        @pl.when(z == plane)
        def _(source=source):
            out[...] = source[:ROWS, :]


def nearer_anchor(own, below, across, above):
    return pl.pallas_call(
        nearer_kernel,
        out_shape=jax.ShapeDtypeStruct((ROWS, 2 * HD), BF),
        in_specs=[VM] * 4,
        out_specs=VM,
        compiler_params=pltpu.CompilerParams(vmem_limit_bytes=VMEM_LIMIT),
        cost_estimate=pl.CostEstimate(flops=0, bytes_accessed=1 << 19, transcendentals=0),
    )(own, below, across, above)


def anchor_kernel(lengths, q, kv_zero, kv_one, weighted, stats, out, kv):
    _, _, z, core = places()
    length = lengths[2 * z + core]
    anchor_length = jnp.where(2 * z + core > 0, lengths[0], 0)

    @pl.when(core == 0)
    def _():
        kv[...] = kv_zero[...]

    @pl.when(core != 0)
    def _():
        kv[...] = kv_one[...]

    key = lax.broadcasted_iota(jnp.int32, (512, 1), 0)
    cap = jnp.where(key < anchor_length, -NEG, NEG)
    for tile in range(2):
        rows = slice(tile * 256, tile * 256 + 256)
        live = tile * 256 + lax.broadcasted_iota(jnp.int32, (1, 256), 1) < length
        scaled, factors = [], []
        for head in range(4):
            cols = slice(head * HD, (head + 1) * HD)
            s = jnp.minimum(scores_of(kv[:, :HD], q[rows, cols]), cap)
            own_top, own_sum = stats[head : head + 1, rows], stats[head + 8 : head + 9, rows]
            top = jnp.maximum(own_top, jnp.max(s, axis=0, keepdims=True))
            e = weights_of(s, top)
            factor = weights_of(own_top, top)
            total = own_sum * factor + jnp.sum(e, axis=0, keepdims=True)
            share = jnp.where(live, 1.0 / total, 0.0)
            scaled.append(dot_keys((e * share).astype(BF), kv[:, HD:]))
            factors.append(factor * share)
        across = jnp.concatenate(factors + factors, axis=0).T
        for head in range(4):
            cols = slice(head * HD, (head + 1) * HD)
            out[rows, cols] = (weighted[rows, cols] * across[:, head : head + 1] + scaled[head]).astype(BF)


def anchor_attention(lengths, q, kv_zero, kv_one, weighted, stats):
    return pl.pallas_call(
        anchor_kernel,
        out_shape=jax.ShapeDtypeStruct((512, 512), BF),
        in_specs=[SM, VM, VM, VM, VM, VM],
        out_specs=VM,
        scratch_shapes=[pltpu.VMEM((ROWS, 2 * HD), BF)],
        compiler_params=pltpu.CompilerParams(vmem_limit_bytes=VMEM_LIMIT),
        cost_estimate=pl.CostEstimate(flops=4 * 4 * 512 * 512 * 128, bytes_accessed=3 << 20, transcendentals=1 << 20),
    )(lengths, q, kv_zero, kv_one, weighted, stats)


def question_kernel(lengths_ref, q_own, q_other, kv_0, kv_1, kv_2, kv_3, out_own, out_other):
    kvs = (kv_0, kv_1, kv_2, kv_3)
    _, _, z, core = places()
    ctx = 2 * z + core
    blocks = [z, (z + 3) & 3, (z + 1) & 3, (z + 2) & 3]
    lengths = [lengths_ref[2 * block + core] for block in blocks]
    stacked = [q_own[:, h * HD : (h + 1) * HD] for h in range(4)]
    stacked += [q_other[:, h * HD : (h + 1) * HD] for h in range(4)]
    q = jnp.concatenate(stacked, axis=0)
    scores = []
    key = lax.broadcasted_iota(jnp.int32, (1, 512), 1)
    for kv, length in zip(kvs, lengths):
        scores.append(jnp.minimum(scores_of(q, kv[:ROWS, :HD]), jnp.where(key < length, -NEG, NEG)))
    row = lax.broadcasted_iota(jnp.int32, (256, 128), 0)
    lane = lax.broadcasted_iota(jnp.int32, (256, 128), 1)
    row_id = row % 32 + 32 * jnp.where(row < 128, ctx, ctx + 1 - 2 * core)
    block = jnp.where(lane < 64, jnp.where(lane < 32, blocks[0], blocks[1]), jnp.where(lane < 96, blocks[2], blocks[3]))
    key_id = lane % 32 + 32 * (2 * block + core)
    asked_keys = jnp.concatenate([kv[ROWS:, :HD] for kv in kvs], axis=0)
    asked_values = jnp.concatenate([kv[ROWS:, HD:] for kv in kvs], axis=0)
    scores.append(jnp.where(key_id <= row_id, scores_of(q, asked_keys), NEG))
    top = jnp.max(scores[-1], axis=1, keepdims=True)
    for s in scores[:-1]:
        top = jnp.maximum(top, jnp.max(s, axis=1, keepdims=True))
    values = [kv[:ROWS, HD:] for kv in kvs] + [asked_values]
    total = jnp.zeros((256, 1), F32)
    both = jnp.zeros((256, HD), F32)
    for s, value in zip(scores, values):
        e = weights_of(s, top)
        total = total + jnp.sum(e, axis=1, keepdims=True)
        both = both + jnp.dot(e.astype(BF), value, preferred_element_type=F32)
    for out, start in ((out_own, 0), (out_other, 128)):
        tops, totals = [], []
        for head in range(4):
            rows = slice(start + head * 32, start + head * 32 + 32)
            out[:, head * HD : (head + 1) * HD] = both[rows]
            tops.append(top[rows])
            totals.append(total[rows])
        out[:, 512:640] = columns_to_stats(tops + totals)


def question_attention(lengths, q_own, q_other, kvs):
    part = jax.ShapeDtypeStruct((32, 640), F32)
    return pl.pallas_call(
        question_kernel,
        out_shape=[part, part],
        in_specs=[SM] + [VM] * 6,
        out_specs=[VM, VM],
        compiler_params=pltpu.CompilerParams(vmem_limit_bytes=VMEM_LIMIT),
        cost_estimate=pl.CostEstimate(flops=4 * 256 * 2176 * 128, bytes_accessed=2 << 20, transcendentals=1 << 19),
    )(lengths, q_own, q_other, *kvs)


def merge_kernel(a, b, out):
    stat_a, stat_b = a[:, 512:640], b[:, 512:640]
    for head in range(4):
        cols = slice(head * HD, (head + 1) * HD)
        top_a, top_b = stat_a[:, head : head + 1], stat_b[:, head : head + 1]
        top = jnp.maximum(top_a, top_b)
        factor_a, factor_b = weights_of(top_a, top), weights_of(top_b, top)
        total = stat_a[:, head + 4 : head + 5] * factor_a + stat_b[:, head + 4 : head + 5] * factor_b
        out[:, cols] = ((a[:, cols] * factor_a + b[:, cols] * factor_b) / total).astype(BF)


def merge(a, b):
    return pl.pallas_call(
        merge_kernel,
        out_shape=jax.ShapeDtypeStruct((32, 512), BF),
        in_specs=[VM, VM],
        out_specs=VM,
        compiler_params=pltpu.CompilerParams(vmem_limit_bytes=VMEM_LIMIT),
    )(a, b)


PLAN_1 = [
    ((0, 0), 0, 512, [(0, 0, 512)]),
    ((-1, 0), 0, 512, [(1, 0, 512)]),
    ((1, 0), 0, 512, [(2, 0, 512)]),
    ((0, -1), 0, 512, [(3, 0, 512)]),
    ((0, 1), 0, 512, [(4, 0, 512)]),
    ((2, 0), 0, 256, [(5, 0, 256)]),
    ((0, 2), 256, 512, [(6, 0, 256)]),
]
PLAN_2 = [
    ((-1, -1), 0, 512, [(0, 0, 256), (2, 0, 256)]),
    ((1, -1), 0, 512, [(0, 256, 256), (3, 0, 256)]),
    ((-1, 1), 0, 512, [(1, 0, 256), (2, 256, 256)]),
    ((1, 1), 0, 512, [(1, 256, 256), (3, 256, 256)]),
    ((2, -1), 0, 256, [(0, 512, 256)]),
    ((2, 1), 0, 256, [(1, 512, 256)]),
    ((-1, 2), 256, 512, [(2, 512, 256)]),
    ((1, 2), 256, 512, [(3, 512, 256)]),
    ((0, 2), 0, 256, [(0, 768, 128), (1, 768, 128)]),
    ((2, 0), 256, 512, [(2, 768, 128), (3, 768, 128)]),
]
PLAN_3 = [
    ((2, 2), 0, 512, [(1, 128, 256), (3, 128, 256)]),
    ((-1, 2), 0, 256, [(0, 0, 256)]),
    ((1, 2), 0, 256, [(0, 256, 128), (1, 0, 128)]),
    ((2, -1), 256, 512, [(2, 0, 256)]),
    ((2, 1), 256, 512, [(2, 256, 128), (3, 0, 128)]),
]
NEAR_Y = [(0, 0, 256), (1, 0, 256), (4, 0, 256)]
NEAR_X = [(2, 256, 256), (3, 256, 256), (4, 0, 256)]
PACK_2 = [NEAR_Y + [(2, 0, 128)], NEAR_Y + [(3, 128, 128)], NEAR_X + [(0, 256, 128)], NEAR_X + [(1, 384, 128)]]
PACK_3 = [[(0, 0, 384)], [(1, 384, 384)]]


def tables_of(positions):
    inverse_freq = ROPE_BASE ** (-(jnp.arange(HD // 2, dtype=jnp.float32) * 2.0 / HD))
    inverse_freq = jnp.concatenate([inverse_freq, inverse_freq])
    phases = positions.astype(jnp.float32)[:, None] * inverse_freq[None, :]
    signs = jnp.where(jnp.arange(HD) < HD // 2, -1.0, 1.0).astype(jnp.float32)
    return jnp.cos(phases), jnp.sin(phases) * signs[None, :]


def shift_z(array, dz):
    pairs = [(i, ((i // 2 + dz) % 4) * 2 + i % 2) for i in range(8)]
    return lax.ppermute(array, "ctx", pairs)


def per_device(context, question, w_query, w_key, w_value, lengths, owner):
    ctx = lax.axis_index("ctx")
    ids = jnp.arange(8, dtype=jnp.int32)
    own_offset = jnp.sum(jnp.where(ids < ctx, lengths, 0))
    filled = jnp.sum(lengths)

    up = shift_heads(context, 1, 0)
    down = shift_heads(context, -1, 0)
    right = shift_heads(context, 0, 1)
    left = shift_heads(context, 0, -1)
    low, high = pack([[(0, 0, 256)], [(0, 256, 256)]], [context])
    low, high, cut = lax.optimization_barrier((low, high, owner))
    far_y = shift_heads(low, 2, 0)
    left, high = lax.optimization_barrier((left, high))
    far_x = shift_heads(high, 0, 2)

    share = lax.all_to_all(question[0].reshape(8, 32, 512), "ctx", 0, 0)
    share = lax.dynamic_index_in_dim(share, cut[0], 0, False)
    share = jnp.broadcast_to(share[None], (16, 32, 512))
    pieces = lax.all_to_all(share, "heads", 0, 0)
    up, pieces = lax.optimization_barrier((up, pieces))

    to_right, to_left = pack(PACK_2[:2], [up, down, right, left, far_y])
    to_up, to_down = pack(PACK_2[2:], [up, down, right, left, far_x])
    a_right, a_left = shift_heads(to_right, 0, 1), shift_heads(to_left, 0, -1)
    b_up, b_down = shift_heads(to_up, 1, 0), shift_heads(to_down, -1, 0)
    up, to_right = lax.optimization_barrier((up, to_right))
    tables = tables_of(
        jnp.concatenate(
            [own_offset + jnp.arange(ROWS, dtype=jnp.int32), filled + 32 * ctx + jnp.arange(ASKED, dtype=jnp.int32)]
        )
    )
    pieces, w_query, w_key, w_value, tables = lax.optimization_barrier(
        (pieces, w_query, w_key, w_value, tables)
    )
    weights = hold(w_query, w_key.T, w_value.T)
    accs = project([context, up, down, right, left, far_y, far_x], PLAN_1, weights, None, True, True)
    q_share = question_project(pieces, weights, tables)

    a_right, a_left, accs, q_share = lax.optimization_barrier((a_right, a_left, accs, q_share))
    to_right, to_left = pack(PACK_3, [a_right, a_left])
    to_up, to_down = pack(PACK_3, [b_up, b_down])
    last = [
        shift_heads(to_right, 0, 1),
        shift_heads(to_left, 0, -1),
        shift_heads(to_up, 1, 0),
        shift_heads(to_down, -1, 0),
    ]
    accs = project([a_right, a_left, b_up, b_down], PLAN_2, weights, accs, True, True)

    (halves,) = project(last, PLAN_3, weights, accs, False, True, True, asked=q_share)
    (queries,) = project(last, PLAN_3, weights, accs, True, False, True, tables)
    partner = swap_heads(halves, 0, 1)
    q_asked = q_share[:, :512]
    q_other = swap_ctx(q_asked, 0, 1)
    partner, queries, q_other = lax.optimization_barrier((partner, queries, q_other))
    kv = key_value(halves, partner, *tables)

    below, above, across = shift_z(kv, 1), shift_z(kv, -1), shift_z(kv, 2)
    weighted, stats = own_attention(lengths, queries, kv)
    below, above, across, weighted = lax.optimization_barrier((below, above, across, weighted))
    nearer = nearer_anchor(kv, below, across, above)
    from_zero = lax.ppermute(nearer, "ctx", [(0, 1), (2, 3), (4, 5), (6, 7)])
    part, part_other = question_attention(lengths, q_asked, q_other, [kv, below, above, across])
    from_zero, part = lax.optimization_barrier((from_zero, part))
    context_attn = anchor_attention(lengths, queries, nearer, from_zero, weighted, stats)
    question_attn = merge(part, swap_ctx(part_other, 0, 1))
    return (context_attn, question_attn)


def solution(mesh):
    in_specs = (
        P("ctx", "heads"),
        P("ctx", None, "heads"),
        P(None, "heads"),
        P(None, "heads"),
        P(None, "heads"),
        P(),
        P(),
    )
    out_specs = (P("ctx", "heads"), P("ctx", "heads"))
    return jax.shard_map(
        per_device, mesh=mesh, in_specs=in_specs, out_specs=out_specs, check_vma=False
    )
```

```python
import functools

import jax
import jax.numpy as jnp
from jax import lax
from jax.experimental import pallas as pl
from jax.experimental.pallas import tpu as pltpu
from jax.sharding import PartitionSpec as P

HD = 128
ROPE_BASE = 500000.0
BF = jnp.bfloat16
F32 = jnp.float32
VMEM_LIMIT = 8 * 1024 * 1024
HOLD_LIMIT = 37 * 1024 * 1024
NEG = -3.4e38
SCALE2 = HD ** (-0.5) * 1.4426950408889634
ROWS = 512
ASKED = 32
ALL = ROWS + ASKED

HBM = pl.BlockSpec(memory_space=pltpu.HBM)
VM = pl.BlockSpec(memory_space=pltpu.VMEM)
SM = pl.BlockSpec(memory_space=pltpu.SMEM)


def shift_heads(array, dy, dx):
    pairs = [(i, ((i // 4 + dy) % 4) * 4 + (i % 4 + dx) % 4) for i in range(16)]
    return lax.ppermute(array, "heads", pairs)


def swap_heads(array, my, mx):
    pairs = [(i, ((i // 4) ^ my) * 4 + ((i % 4) ^ mx)) for i in range(16)]
    return lax.ppermute(array, "heads", pairs)


def swap_ctx(array, mz, mc):
    pairs = [(i, ((i // 2) ^ mz) * 2 + ((i % 2) ^ mc)) for i in range(8)]
    return lax.ppermute(array, "ctx", pairs)


def places():
    heads, ctx = lax.axis_index("heads"), lax.axis_index("ctx")
    return lax.shift_right_logical(heads, 2), heads & 3, lax.shift_right_logical(ctx, 1), ctx & 1


def pack_kernel(plan, n_in, *refs):
    ins, outs = refs[:n_in], refs[n_in:]
    for out, pieces in zip(outs, plan):
        row = 0
        for operand, start, count in pieces:
            out[row : row + count, :] = ins[operand][start : start + count, :]
            row += count


def pack(plan, ins):
    return pl.pallas_call(
        functools.partial(pack_kernel, plan, len(ins)),
        out_shape=[jax.ShapeDtypeStruct((sum(p[2] for p in pieces), 512), BF) for pieces in plan],
        in_specs=[VM] * len(ins),
        out_specs=[VM] * len(plan),
        compiler_params=pltpu.CompilerParams(vmem_limit_bytes=VMEM_LIMIT),
        cost_estimate=pl.CostEstimate(flops=0, bytes_accessed=1 << 20, transcendentals=0),
    )(*ins)


def hold_kernel(wq, wk, wv, q_out, kv_out, sem):
    copies = []
    for part in range(8):
        rows = pl.ds(part * 1024, 1024)
        copies.append(pltpu.make_async_copy(wq.at[rows, :], q_out.at[rows, :], sem.at[part]))
    for part in range(4):
        cols = pl.ds(part * 2048, 2048)
        copies.append(pltpu.make_async_copy(wk.at[:, cols], kv_out.at[pl.ds(0, 64), cols], sem.at[8 + part]))
        copies.append(pltpu.make_async_copy(wv.at[:, cols], kv_out.at[pl.ds(64, 64), cols], sem.at[12 + part]))
    for copy in copies:
        copy.start()
    for copy in copies:
        copy.wait()


def hold(wq, wk, wv):
    return pl.pallas_call(
        hold_kernel,
        out_shape=[jax.ShapeDtypeStruct((8192, 512), BF), jax.ShapeDtypeStruct((128, 8192), BF)],
        in_specs=[HBM] * 3,
        out_specs=[VM, VM],
        scratch_shapes=[pltpu.SemaphoreType.DMA((16,))],
        compiler_params=pltpu.CompilerParams(vmem_limit_bytes=HOLD_LIMIT),
        cost_estimate=pl.CostEstimate(flops=0, bytes_accessed=20 << 20, transcendentals=0),
    )(wq, wk, wv)


def turn(part, cos, sin):
    return (part * cos + pltpu.roll(part, HD // 2, 1) * sin).astype(BF)


def project_kernel(plan, n_x, with_q, with_kv, has_acc, finish, *refs):
    refs = list(refs)
    take = lambda count: [refs.pop(0) for _ in range(count)]
    xs = take(n_x)
    wq = take(1)[0] if with_q else None
    wkv = take(1)[0] if with_kv else None
    acc_q = take(1)[0] if has_acc and with_q else None
    acc_kv = take(1)[0] if has_acc and with_kv else None
    cos, sin = take(2) if finish and with_q else (None, None)
    asked = take(1)[0] if finish and with_kv else None
    q_out = take(1)[0] if with_q else None
    kv_out = take(1)[0] if with_kv else None
    q_sum = take(1)[0] if finish and with_q else q_out
    kv_sum = take(1)[0] if finish and with_kv else kv_out
    y, x, _, _ = places()
    if has_acc:
        if with_q:
            q_sum[...] = acc_q[...]
        if with_kv:
            kv_sum[...] = acc_kv[...]
    for slot, ((dy, dx), low, high, uses) in enumerate(plan):
        base = pl.multiple_of((((y + dy) & 3) * 4 + ((x + dx) & 3)) * 512, 512)
        parts = [xs[operand][pl.ds(start, count), :] for operand, start, count in uses]
        piece = parts[0] if len(parts) == 1 else jnp.concatenate(parts, axis=0)
        fresh = slot == 0 and not has_acc
        if with_kv:
            both = wkv[:, pl.ds(base, 512)]
            term = lax.dot_general(piece, both, (((1,), (1,)), ((), ())), preferred_element_type=F32)
            kv_sum[low:high, :] = term if fresh else kv_sum[low:high, :] + term
        if with_q:
            term = jnp.dot(piece, wq[pl.ds(base, 512), :], preferred_element_type=F32)
            q_sum[low:high, :] = term if fresh else q_sum[low:high, :] + term
    if finish and with_kv:
        kv_out[:ROWS, :] = kv_sum[...].astype(BF)
        kv_out[ROWS:, :] = asked[:, 512:640]
    if finish and with_q:
        for head in range(4):
            cols = slice(head * HD, (head + 1) * HD)
            q_out[:, cols] = turn(q_sum[:, cols], cos[:ROWS, :], sin[:ROWS, :])


def project(xs, plan, weights, accs, with_q, with_kv, finish=False, tables=None, asked=None):
    wq, wkv = weights
    operands, specs = list(xs), [VM] * len(xs)
    if with_q:
        operands.append(wq)
        specs.append(VM)
    if with_kv:
        operands.append(wkv)
        specs.append(VM)
    has_acc = accs is not None
    if has_acc:
        if with_q:
            operands.append(accs[0])
            specs.append(VM)
        if with_kv:
            operands.append(accs[1])
            specs.append(VM)
    if finish and with_q:
        operands += list(tables)
        specs += [VM, VM]
    if finish and with_kv:
        operands.append(asked)
        specs.append(VM)
    outs, scratch = [], []
    if with_q:
        outs.append(jax.ShapeDtypeStruct((ROWS, 512), BF if finish else F32))
        if finish:
            scratch.append(pltpu.VMEM((ROWS, 512), F32))
    if with_kv:
        outs.append(jax.ShapeDtypeStruct((ALL, 128), BF) if finish else jax.ShapeDtypeStruct((ROWS, 128), F32))
        if finish:
            scratch.append(pltpu.VMEM((ROWS, 128), F32))
    columns = (512 if with_q else 0) + (128 if with_kv else 0)
    used = sum(high - low for _, low, high, _ in plan)
    return pl.pallas_call(
        functools.partial(project_kernel, plan, len(xs), with_q, with_kv, has_acc, finish),
        out_shape=outs,
        in_specs=specs,
        out_specs=[VM] * len(outs),
        scratch_shapes=scratch,
        compiler_params=pltpu.CompilerParams(vmem_limit_bytes=VMEM_LIMIT),
        cost_estimate=pl.CostEstimate(
            flops=2 * used * 512 * columns, bytes_accessed=len(plan) * 512 * columns * 2, transcendentals=0
        ),
    )(*operands)


def question_project_kernel(pieces, wq, wkv, cos, sin, out):
    q_sum, kv_sum = None, None
    for place in range(16):
        base = place * 512
        piece = pieces[place]
        both = wkv[:, pl.ds(base, 512)]
        kv_term = lax.dot_general(piece, both, (((1,), (1,)), ((), ())), preferred_element_type=F32)
        q_term = jnp.dot(piece, wq[pl.ds(base, 512), :], preferred_element_type=F32)
        q_sum = q_term if q_sum is None else q_sum + q_term
        kv_sum = kv_term if kv_sum is None else kv_sum + kv_term
    for head in range(4):
        cols = slice(head * HD, (head + 1) * HD)
        out[:, cols] = turn(q_sum[:, cols], cos[ROWS : ROWS + 32, :], sin[ROWS : ROWS + 32, :])
    out[:, 512:640] = kv_sum.astype(BF)


def question_project(pieces, weights, tables):
    return pl.pallas_call(
        question_project_kernel,
        out_shape=jax.ShapeDtypeStruct((32, 640), BF),
        in_specs=[VM] * 5,
        out_specs=VM,
        compiler_params=pltpu.CompilerParams(vmem_limit_bytes=VMEM_LIMIT),
        cost_estimate=pl.CostEstimate(flops=2 * 256 * 8192 * 640, bytes_accessed=8192 * 640 * 2, transcendentals=0),
    )(pieces, *weights, *tables)


def key_value_kernel(own, partner, cos, sin, out):
    is_lower = (places()[1] & 1) == 0
    mine, other = own[...].astype(F32), partner[...].astype(F32)
    low = jnp.where(is_lower, mine, other)
    high = jnp.where(is_lower, other, mine)
    lane = lax.broadcasted_iota(jnp.int32, low.shape, 1)
    keys = jnp.where(lane < 64, low, pltpu.roll(high, 64, 1))
    values = jnp.where(lane < 64, pltpu.roll(low, 64, 1), high)
    out[:, :HD] = (keys * cos[...] + pltpu.roll(keys, 64, 1) * sin[...]).astype(BF)
    out[:, HD:] = values.astype(BF)


def key_value(own, partner, cos, sin):
    return pl.pallas_call(
        key_value_kernel,
        out_shape=jax.ShapeDtypeStruct((ALL, 2 * HD), BF),
        in_specs=[VM, VM, VM, VM],
        out_specs=VM,
        compiler_params=pltpu.CompilerParams(vmem_limit_bytes=VMEM_LIMIT),
    )(own, partner, cos, sin)


def scores_of(queries, keys):
    return lax.dot_general(queries, keys, (((1,), (1,)), ((), ())), preferred_element_type=F32)


def weights_of(scores, top):
    return jnp.exp2(scores * SCALE2 - top * SCALE2)


def columns_to_stats(columns):
    rows = columns[0].shape[0]
    lane = lax.broadcasted_iota(jnp.int32, (rows, 128), 1)
    stats = jnp.zeros((rows, 128), F32)
    for index, column in enumerate(columns):
        stats = jnp.where(lane == index, column, stats)
    return stats


def dot_keys(weights, values):
    return lax.dot_general(weights, values, (((0,), (0,)), ((), ())), preferred_element_type=F32)


def own_kernel(lengths, q, kv, weighted, stats):
    _, _, z, core = places()
    length = lengths[2 * z + core]
    for tile in range(2):
        rows = slice(tile * 256, tile * 256 + 256)
        width = 256 * (tile + 1)
        key = lax.broadcasted_iota(jnp.int32, (width, 256), 0)
        row = tile * 256 + lax.broadcasted_iota(jnp.int32, (width, 256), 1)
        cap = jnp.where((key <= row) & (key < length), -NEG, NEG)
        for head in range(4):
            cols = slice(head * HD, (head + 1) * HD)
            s = jnp.minimum(scores_of(kv[:width, :HD], q[rows, cols]), cap)
            top = jnp.max(s, axis=0, keepdims=True)
            e = weights_of(s, top)
            stats[head : head + 1, rows] = top
            stats[head + 8 : head + 9, rows] = jnp.sum(e, axis=0, keepdims=True)
            weighted[rows, cols] = dot_keys(e.astype(BF), kv[:width, HD:])


def own_attention(lengths, q, kv):
    return pl.pallas_call(
        own_kernel,
        out_shape=[jax.ShapeDtypeStruct((512, 512), F32), jax.ShapeDtypeStruct((16, 512), F32)],
        in_specs=[SM, VM, VM],
        out_specs=[VM, VM],
        compiler_params=pltpu.CompilerParams(vmem_limit_bytes=VMEM_LIMIT),
        cost_estimate=pl.CostEstimate(flops=4 * 4 * 512 * 512 * 128, bytes_accessed=3 << 20, transcendentals=1 << 20),
    )(lengths, q, kv)


def nearer_kernel(own, below, across, above, out):
    _, _, z, _ = places()
    for plane, source in enumerate((own, below, across, above)):

        @pl.when(z == plane)
        def _(source=source):
            out[...] = source[:ROWS, :]


def nearer_anchor(own, below, across, above):
    return pl.pallas_call(
        nearer_kernel,
        out_shape=jax.ShapeDtypeStruct((ROWS, 2 * HD), BF),
        in_specs=[VM] * 4,
        out_specs=VM,
        compiler_params=pltpu.CompilerParams(vmem_limit_bytes=VMEM_LIMIT),
        cost_estimate=pl.CostEstimate(flops=0, bytes_accessed=1 << 19, transcendentals=0),
    )(own, below, across, above)


def anchor_kernel(lengths, q, kv_zero, kv_one, weighted, stats, out, kv):
    _, _, z, core = places()
    length = lengths[2 * z + core]
    anchor_length = jnp.where(2 * z + core > 0, lengths[0], 0)

    @pl.when(core == 0)
    def _():
        kv[...] = kv_zero[...]

    @pl.when(core != 0)
    def _():
        kv[...] = kv_one[...]

    key = lax.broadcasted_iota(jnp.int32, (512, 1), 0)
    cap = jnp.where(key < anchor_length, -NEG, NEG)
    for tile in range(2):
        rows = slice(tile * 256, tile * 256 + 256)
        live = tile * 256 + lax.broadcasted_iota(jnp.int32, (1, 256), 1) < length
        scaled, factors = [], []
        for head in range(4):
            cols = slice(head * HD, (head + 1) * HD)
            s = jnp.minimum(scores_of(kv[:, :HD], q[rows, cols]), cap)
            own_top, own_sum = stats[head : head + 1, rows], stats[head + 8 : head + 9, rows]
            top = jnp.maximum(own_top, jnp.max(s, axis=0, keepdims=True))
            e = weights_of(s, top)
            factor = weights_of(own_top, top)
            total = own_sum * factor + jnp.sum(e, axis=0, keepdims=True)
            share = jnp.where(live, 1.0 / total, 0.0)
            scaled.append(dot_keys((e * share).astype(BF), kv[:, HD:]))
            factors.append(factor * share)
        across = jnp.concatenate(factors + factors, axis=0).T
        for head in range(4):
            cols = slice(head * HD, (head + 1) * HD)
            out[rows, cols] = (weighted[rows, cols] * across[:, head : head + 1] + scaled[head]).astype(BF)


def anchor_attention(lengths, q, kv_zero, kv_one, weighted, stats):
    return pl.pallas_call(
        anchor_kernel,
        out_shape=jax.ShapeDtypeStruct((512, 512), BF),
        in_specs=[SM, VM, VM, VM, VM, VM],
        out_specs=VM,
        scratch_shapes=[pltpu.VMEM((ROWS, 2 * HD), BF)],
        compiler_params=pltpu.CompilerParams(vmem_limit_bytes=VMEM_LIMIT),
        cost_estimate=pl.CostEstimate(flops=4 * 4 * 512 * 512 * 128, bytes_accessed=3 << 20, transcendentals=1 << 20),
    )(lengths, q, kv_zero, kv_one, weighted, stats)


def question_kernel(lengths_ref, q_own, q_other, kv_0, kv_1, kv_2, kv_3, out_own, out_other):
    kvs = (kv_0, kv_1, kv_2, kv_3)
    _, _, z, core = places()
    ctx = 2 * z + core
    blocks = [z, (z + 3) & 3, (z + 1) & 3, (z + 2) & 3]
    lengths = [lengths_ref[2 * block + core] for block in blocks]
    stacked = [q_own[:, h * HD : (h + 1) * HD] for h in range(4)]
    stacked += [q_other[:, h * HD : (h + 1) * HD] for h in range(4)]
    q = jnp.concatenate(stacked, axis=0)
    scores = []
    key = lax.broadcasted_iota(jnp.int32, (1, 512), 1)
    for kv, length in zip(kvs, lengths):
        scores.append(jnp.minimum(scores_of(q, kv[:ROWS, :HD]), jnp.where(key < length, -NEG, NEG)))
    row = lax.broadcasted_iota(jnp.int32, (256, 128), 0)
    lane = lax.broadcasted_iota(jnp.int32, (256, 128), 1)
    row_id = row % 32 + 32 * jnp.where(row < 128, ctx, ctx + 1 - 2 * core)
    block = jnp.where(lane < 64, jnp.where(lane < 32, blocks[0], blocks[1]), jnp.where(lane < 96, blocks[2], blocks[3]))
    key_id = lane % 32 + 32 * (2 * block + core)
    asked_keys = jnp.concatenate([kv[ROWS:, :HD] for kv in kvs], axis=0)
    asked_values = jnp.concatenate([kv[ROWS:, HD:] for kv in kvs], axis=0)
    scores.append(jnp.where(key_id <= row_id, scores_of(q, asked_keys), NEG))
    top = jnp.max(scores[-1], axis=1, keepdims=True)
    for s in scores[:-1]:
        top = jnp.maximum(top, jnp.max(s, axis=1, keepdims=True))
    values = [kv[:ROWS, HD:] for kv in kvs] + [asked_values]
    total = jnp.zeros((256, 1), F32)
    both = jnp.zeros((256, HD), F32)
    for s, value in zip(scores, values):
        e = weights_of(s, top)
        total = total + jnp.sum(e, axis=1, keepdims=True)
        both = both + jnp.dot(e.astype(BF), value, preferred_element_type=F32)
    for out, start in ((out_own, 0), (out_other, 128)):
        tops, totals = [], []
        for head in range(4):
            rows = slice(start + head * 32, start + head * 32 + 32)
            out[:, head * HD : (head + 1) * HD] = both[rows]
            tops.append(top[rows])
            totals.append(total[rows])
        out[:, 512:640] = columns_to_stats(tops + totals)


def question_attention(lengths, q_own, q_other, kvs):
    part = jax.ShapeDtypeStruct((32, 640), F32)
    return pl.pallas_call(
        question_kernel,
        out_shape=[part, part],
        in_specs=[SM] + [VM] * 6,
        out_specs=[VM, VM],
        compiler_params=pltpu.CompilerParams(vmem_limit_bytes=VMEM_LIMIT),
        cost_estimate=pl.CostEstimate(flops=4 * 256 * 2176 * 128, bytes_accessed=2 << 20, transcendentals=1 << 19),
    )(lengths, q_own, q_other, *kvs)


def merge_kernel(a, b, out):
    stat_a, stat_b = a[:, 512:640], b[:, 512:640]
    for head in range(4):
        cols = slice(head * HD, (head + 1) * HD)
        top_a, top_b = stat_a[:, head : head + 1], stat_b[:, head : head + 1]
        top = jnp.maximum(top_a, top_b)
        factor_a, factor_b = weights_of(top_a, top), weights_of(top_b, top)
        total = stat_a[:, head + 4 : head + 5] * factor_a + stat_b[:, head + 4 : head + 5] * factor_b
        out[:, cols] = ((a[:, cols] * factor_a + b[:, cols] * factor_b) / total).astype(BF)


def merge(a, b):
    return pl.pallas_call(
        merge_kernel,
        out_shape=jax.ShapeDtypeStruct((32, 512), BF),
        in_specs=[VM, VM],
        out_specs=VM,
        compiler_params=pltpu.CompilerParams(vmem_limit_bytes=VMEM_LIMIT),
    )(a, b)


PLAN_1 = [
    ((0, 0), 0, 512, [(0, 0, 512)]),
    ((-1, 0), 0, 512, [(1, 0, 512)]),
    ((1, 0), 0, 512, [(2, 0, 512)]),
    ((0, -1), 0, 512, [(3, 0, 512)]),
    ((0, 1), 0, 512, [(4, 0, 512)]),
    ((2, 0), 0, 256, [(5, 0, 256)]),
    ((0, 2), 256, 512, [(6, 0, 256)]),
]
PLAN_2 = [
    ((-1, -1), 0, 512, [(0, 0, 256), (2, 0, 256)]),
    ((1, -1), 0, 512, [(0, 256, 256), (3, 0, 256)]),
    ((-1, 1), 0, 512, [(1, 0, 256), (2, 256, 256)]),
    ((1, 1), 0, 512, [(1, 256, 256), (3, 256, 256)]),
    ((2, -1), 0, 256, [(0, 512, 256)]),
    ((2, 1), 0, 256, [(1, 512, 256)]),
    ((-1, 2), 256, 512, [(2, 512, 256)]),
    ((1, 2), 256, 512, [(3, 512, 256)]),
    ((0, 2), 0, 256, [(0, 768, 128), (1, 768, 128)]),
    ((2, 0), 256, 512, [(2, 768, 128), (3, 768, 128)]),
]
PLAN_3 = [
    ((2, 2), 0, 512, [(1, 128, 256), (3, 128, 256)]),
    ((-1, 2), 0, 256, [(0, 0, 256)]),
    ((1, 2), 0, 256, [(0, 256, 128), (1, 0, 128)]),
    ((2, -1), 256, 512, [(2, 0, 256)]),
    ((2, 1), 256, 512, [(2, 256, 128), (3, 0, 128)]),
]
NEAR_Y = [(0, 0, 256), (1, 0, 256), (4, 0, 256)]
NEAR_X = [(2, 256, 256), (3, 256, 256), (4, 0, 256)]
PACK_2 = [NEAR_Y + [(2, 0, 128)], NEAR_Y + [(3, 128, 128)], NEAR_X + [(0, 256, 128)], NEAR_X + [(1, 384, 128)]]
PACK_3 = [[(0, 0, 384)], [(1, 384, 384)]]


def tables_of(positions):
    inverse_freq = ROPE_BASE ** (-(jnp.arange(HD // 2, dtype=jnp.float32) * 2.0 / HD))
    inverse_freq = jnp.concatenate([inverse_freq, inverse_freq])
    phases = positions.astype(jnp.float32)[:, None] * inverse_freq[None, :]
    signs = jnp.where(jnp.arange(HD) < HD // 2, -1.0, 1.0).astype(jnp.float32)
    return jnp.cos(phases), jnp.sin(phases) * signs[None, :]


def shift_z(array, dz):
    pairs = [(i, ((i // 2 + dz) % 4) * 2 + i % 2) for i in range(8)]
    return lax.ppermute(array, "ctx", pairs)


def per_device(context, question, w_query, w_key, w_value, lengths, owner):
    ctx = lax.axis_index("ctx")
    ids = jnp.arange(8, dtype=jnp.int32)
    own_offset = jnp.sum(jnp.where(ids < ctx, lengths, 0))
    filled = jnp.sum(lengths)

    up = shift_heads(context, 1, 0)
    down = shift_heads(context, -1, 0)
    right = shift_heads(context, 0, 1)
    left = shift_heads(context, 0, -1)
    low, high = pack([[(0, 0, 256)], [(0, 256, 256)]], [context])
    low, high, cut = lax.optimization_barrier((low, high, owner))
    far_y = shift_heads(low, 2, 0)
    up, high = lax.optimization_barrier((up, high))
    far_x = shift_heads(high, 0, 2)

    share = lax.all_to_all(question[0].reshape(8, 32, 512), "ctx", 0, 0)
    share = lax.dynamic_index_in_dim(share, cut[0], 0, False)
    share = jnp.broadcast_to(share[None], (16, 32, 512))
    pieces = lax.all_to_all(share, "heads", 0, 0)
    up, pieces = lax.optimization_barrier((up, pieces))

    to_right, to_left = pack(PACK_2[:2], [up, down, right, left, far_y])
    to_up, to_down = pack(PACK_2[2:], [up, down, right, left, far_x])
    a_right, a_left = shift_heads(to_right, 0, 1), shift_heads(to_left, 0, -1)
    b_up, b_down = shift_heads(to_up, 1, 0), shift_heads(to_down, -1, 0)
    up, to_right = lax.optimization_barrier((up, to_right))
    tables = tables_of(
        jnp.concatenate(
            [own_offset + jnp.arange(ROWS, dtype=jnp.int32), filled + 32 * ctx + jnp.arange(ASKED, dtype=jnp.int32)]
        )
    )
    pieces, w_query, w_key, w_value, tables = lax.optimization_barrier(
        (pieces, w_query, w_key, w_value, tables)
    )
    weights = hold(w_query, w_key.T, w_value.T)
    accs = project([context, up, down, right, left, far_y, far_x], PLAN_1, weights, None, True, True)
    q_share = question_project(pieces, weights, tables)

    a_right, a_left, accs, q_share = lax.optimization_barrier((a_right, a_left, accs, q_share))
    to_right, to_left = pack(PACK_3, [a_right, a_left])
    to_up, to_down = pack(PACK_3, [b_up, b_down])
    last = [
        shift_heads(to_right, 0, 1),
        shift_heads(to_left, 0, -1),
        shift_heads(to_up, 1, 0),
        shift_heads(to_down, -1, 0),
    ]
    accs = project([a_right, a_left, b_up, b_down], PLAN_2, weights, accs, True, True)

    (halves,) = project(last, PLAN_3, weights, accs, False, True, True, asked=q_share)
    (queries,) = project(last, PLAN_3, weights, accs, True, False, True, tables)
    partner = swap_heads(halves, 0, 1)
    q_asked = q_share[:, :512]
    q_other = swap_ctx(q_asked, 0, 1)
    partner, queries, q_other = lax.optimization_barrier((partner, queries, q_other))
    kv = key_value(halves, partner, *tables)

    across = shift_z(kv, 2)
    above, below = shift_z(kv, -1), shift_z(kv, 1)
    weighted, stats = own_attention(lengths, queries, kv)
    above, below, across, weighted = lax.optimization_barrier((above, below, across, weighted))
    nearer = nearer_anchor(kv, below, across, above)
    from_zero = lax.ppermute(nearer, "ctx", [(0, 1), (2, 3), (4, 5), (6, 7)])
    part, part_other = question_attention(lengths, q_asked, q_other, [kv, below, above, across])
    from_zero, part = lax.optimization_barrier((from_zero, part))
    context_attn = anchor_attention(lengths, queries, nearer, from_zero, weighted, stats)
    question_attn = merge(part, swap_ctx(part_other, 0, 1))
    return (context_attn, question_attn)


def solution(mesh):
    in_specs = (
        P("ctx", "heads"),
        P("ctx", None, "heads"),
        P(None, "heads"),
        P(None, "heads"),
        P(None, "heads"),
        P(),
        P(),
    )
    out_specs = (P("ctx", "heads"), P("ctx", "heads"))
    return jax.shard_map(
        per_device, mesh=mesh, in_specs=in_specs, out_specs=out_specs, check_vma=False
    )
```

```python
import functools

import jax
import jax.numpy as jnp
from jax import lax
from jax.experimental import pallas as pl
from jax.experimental.pallas import tpu as pltpu
from jax.sharding import PartitionSpec as P

HD = 128
ROPE_BASE = 500000.0
BF = jnp.bfloat16
F32 = jnp.float32
VMEM_LIMIT = 8 * 1024 * 1024
HOLD_LIMIT = 37 * 1024 * 1024
NEG = -3.4e38
SCALE2 = HD ** (-0.5) * 1.4426950408889634
ROWS = 512
ASKED = 32
ALL = ROWS + ASKED

HBM = pl.BlockSpec(memory_space=pltpu.HBM)
VM = pl.BlockSpec(memory_space=pltpu.VMEM)
SM = pl.BlockSpec(memory_space=pltpu.SMEM)


def shift_heads(array, dy, dx):
    pairs = [(i, ((i // 4 + dy) % 4) * 4 + (i % 4 + dx) % 4) for i in range(16)]
    return lax.ppermute(array, "heads", pairs)


def swap_heads(array, my, mx):
    pairs = [(i, ((i // 4) ^ my) * 4 + ((i % 4) ^ mx)) for i in range(16)]
    return lax.ppermute(array, "heads", pairs)


def swap_ctx(array, mz, mc):
    pairs = [(i, ((i // 2) ^ mz) * 2 + ((i % 2) ^ mc)) for i in range(8)]
    return lax.ppermute(array, "ctx", pairs)


def places():
    heads, ctx = lax.axis_index("heads"), lax.axis_index("ctx")
    return lax.shift_right_logical(heads, 2), heads & 3, lax.shift_right_logical(ctx, 1), ctx & 1


def pack_kernel(plan, n_in, *refs):
    ins, outs = refs[:n_in], refs[n_in:]
    for out, pieces in zip(outs, plan):
        row = 0
        for operand, start, count in pieces:
            out[row : row + count, :] = ins[operand][start : start + count, :]
            row += count


def pack(plan, ins):
    return pl.pallas_call(
        functools.partial(pack_kernel, plan, len(ins)),
        out_shape=[jax.ShapeDtypeStruct((sum(p[2] for p in pieces), 512), BF) for pieces in plan],
        in_specs=[VM] * len(ins),
        out_specs=[VM] * len(plan),
        compiler_params=pltpu.CompilerParams(vmem_limit_bytes=VMEM_LIMIT),
        cost_estimate=pl.CostEstimate(flops=0, bytes_accessed=1 << 20, transcendentals=0),
    )(*ins)


def hold_kernel(wq, wk, wv, q_out, kv_out, sem):
    copies = []
    for part in range(8):
        rows = pl.ds(part * 1024, 1024)
        copies.append(pltpu.make_async_copy(wq.at[rows, :], q_out.at[rows, :], sem.at[part]))
    for part in range(4):
        cols = pl.ds(part * 2048, 2048)
        copies.append(pltpu.make_async_copy(wk.at[:, cols], kv_out.at[pl.ds(0, 64), cols], sem.at[8 + part]))
        copies.append(pltpu.make_async_copy(wv.at[:, cols], kv_out.at[pl.ds(64, 64), cols], sem.at[12 + part]))
    for copy in copies:
        copy.start()
    for copy in copies:
        copy.wait()


def hold(wq, wk, wv):
    return pl.pallas_call(
        hold_kernel,
        out_shape=[jax.ShapeDtypeStruct((8192, 512), BF), jax.ShapeDtypeStruct((128, 8192), BF)],
        in_specs=[HBM] * 3,
        out_specs=[VM, VM],
        scratch_shapes=[pltpu.SemaphoreType.DMA((16,))],
        compiler_params=pltpu.CompilerParams(vmem_limit_bytes=HOLD_LIMIT),
        cost_estimate=pl.CostEstimate(flops=0, bytes_accessed=20 << 20, transcendentals=0),
    )(wq, wk, wv)


def turn(part, cos, sin):
    return (part * cos + pltpu.roll(part, HD // 2, 1) * sin).astype(BF)


def project_kernel(plan, n_x, with_q, with_kv, has_acc, finish, *refs):
    refs = list(refs)
    take = lambda count: [refs.pop(0) for _ in range(count)]
    xs = take(n_x)
    wq = take(1)[0] if with_q else None
    wkv = take(1)[0] if with_kv else None
    acc_q = take(1)[0] if has_acc and with_q else None
    acc_kv = take(1)[0] if has_acc and with_kv else None
    cos, sin = take(2) if finish and with_q else (None, None)
    asked = take(1)[0] if finish and with_kv else None
    q_out = take(1)[0] if with_q else None
    kv_out = take(1)[0] if with_kv else None
    q_sum = take(1)[0] if finish and with_q else q_out
    kv_sum = take(1)[0] if finish and with_kv else kv_out
    y, x, _, _ = places()
    if has_acc:
        if with_q:
            q_sum[...] = acc_q[...]
        if with_kv:
            kv_sum[...] = acc_kv[...]
    for slot, ((dy, dx), low, high, uses) in enumerate(plan):
        base = pl.multiple_of((((y + dy) & 3) * 4 + ((x + dx) & 3)) * 512, 512)
        parts = [xs[operand][pl.ds(start, count), :] for operand, start, count in uses]
        piece = parts[0] if len(parts) == 1 else jnp.concatenate(parts, axis=0)
        fresh = slot == 0 and not has_acc
        if with_kv:
            both = wkv[:, pl.ds(base, 512)]
            term = lax.dot_general(piece, both, (((1,), (1,)), ((), ())), preferred_element_type=F32)
            kv_sum[low:high, :] = term if fresh else kv_sum[low:high, :] + term
        if with_q:
            term = jnp.dot(piece, wq[pl.ds(base, 512), :], preferred_element_type=F32)
            q_sum[low:high, :] = term if fresh else q_sum[low:high, :] + term
    if finish and with_kv:
        kv_out[:ROWS, :] = kv_sum[...].astype(BF)
        kv_out[ROWS:, :] = asked[:, 512:640]
    if finish and with_q:
        for head in range(4):
            cols = slice(head * HD, (head + 1) * HD)
            q_out[:, cols] = turn(q_sum[:, cols], cos[:ROWS, :], sin[:ROWS, :])


def project(xs, plan, weights, accs, with_q, with_kv, finish=False, tables=None, asked=None):
    wq, wkv = weights
    operands, specs = list(xs), [VM] * len(xs)
    if with_q:
        operands.append(wq)
        specs.append(VM)
    if with_kv:
        operands.append(wkv)
        specs.append(VM)
    has_acc = accs is not None
    if has_acc:
        if with_q:
            operands.append(accs[0])
            specs.append(VM)
        if with_kv:
            operands.append(accs[1])
            specs.append(VM)
    if finish and with_q:
        operands += list(tables)
        specs += [VM, VM]
    if finish and with_kv:
        operands.append(asked)
        specs.append(VM)
    outs, scratch = [], []
    if with_q:
        outs.append(jax.ShapeDtypeStruct((ROWS, 512), BF if finish else F32))
        if finish:
            scratch.append(pltpu.VMEM((ROWS, 512), F32))
    if with_kv:
        outs.append(jax.ShapeDtypeStruct((ALL, 128), BF) if finish else jax.ShapeDtypeStruct((ROWS, 128), F32))
        if finish:
            scratch.append(pltpu.VMEM((ROWS, 128), F32))
    columns = (512 if with_q else 0) + (128 if with_kv else 0)
    used = sum(high - low for _, low, high, _ in plan)
    return pl.pallas_call(
        functools.partial(project_kernel, plan, len(xs), with_q, with_kv, has_acc, finish),
        out_shape=outs,
        in_specs=specs,
        out_specs=[VM] * len(outs),
        scratch_shapes=scratch,
        compiler_params=pltpu.CompilerParams(vmem_limit_bytes=VMEM_LIMIT),
        cost_estimate=pl.CostEstimate(
            flops=2 * used * 512 * columns, bytes_accessed=len(plan) * 512 * columns * 2, transcendentals=0
        ),
    )(*operands)


def question_project_kernel(pieces, wq, wkv, cos, sin, out):
    q_sum, kv_sum = None, None
    for place in range(16):
        base = place * 512
        piece = pieces[place]
        both = wkv[:, pl.ds(base, 512)]
        kv_term = lax.dot_general(piece, both, (((1,), (1,)), ((), ())), preferred_element_type=F32)
        q_term = jnp.dot(piece, wq[pl.ds(base, 512), :], preferred_element_type=F32)
        q_sum = q_term if q_sum is None else q_sum + q_term
        kv_sum = kv_term if kv_sum is None else kv_sum + kv_term
    for head in range(4):
        cols = slice(head * HD, (head + 1) * HD)
        out[:, cols] = turn(q_sum[:, cols], cos[ROWS : ROWS + 32, :], sin[ROWS : ROWS + 32, :])
    out[:, 512:640] = kv_sum.astype(BF)


def question_project(pieces, weights, tables):
    return pl.pallas_call(
        question_project_kernel,
        out_shape=jax.ShapeDtypeStruct((32, 640), BF),
        in_specs=[VM] * 5,
        out_specs=VM,
        compiler_params=pltpu.CompilerParams(vmem_limit_bytes=VMEM_LIMIT),
        cost_estimate=pl.CostEstimate(flops=2 * 256 * 8192 * 640, bytes_accessed=8192 * 640 * 2, transcendentals=0),
    )(pieces, *weights, *tables)


def key_value_kernel(own, partner, cos, sin, out):
    is_lower = (places()[1] & 1) == 0
    mine, other = own[...].astype(F32), partner[...].astype(F32)
    low = jnp.where(is_lower, mine, other)
    high = jnp.where(is_lower, other, mine)
    lane = lax.broadcasted_iota(jnp.int32, low.shape, 1)
    keys = jnp.where(lane < 64, low, pltpu.roll(high, 64, 1))
    values = jnp.where(lane < 64, pltpu.roll(low, 64, 1), high)
    out[:, :HD] = (keys * cos[...] + pltpu.roll(keys, 64, 1) * sin[...]).astype(BF)
    out[:, HD:] = values.astype(BF)


def key_value(own, partner, cos, sin):
    return pl.pallas_call(
        key_value_kernel,
        out_shape=jax.ShapeDtypeStruct((ALL, 2 * HD), BF),
        in_specs=[VM, VM, VM, VM],
        out_specs=VM,
        compiler_params=pltpu.CompilerParams(vmem_limit_bytes=VMEM_LIMIT),
    )(own, partner, cos, sin)


def scores_of(queries, keys):
    return lax.dot_general(queries, keys, (((1,), (1,)), ((), ())), preferred_element_type=F32)


def weights_of(scores, top):
    return jnp.exp2(scores * SCALE2 - top * SCALE2)


def columns_to_stats(columns):
    rows = columns[0].shape[0]
    lane = lax.broadcasted_iota(jnp.int32, (rows, 128), 1)
    stats = jnp.zeros((rows, 128), F32)
    for index, column in enumerate(columns):
        stats = jnp.where(lane == index, column, stats)
    return stats


def dot_keys(weights, values):
    return lax.dot_general(weights, values, (((0,), (0,)), ((), ())), preferred_element_type=F32)


def own_kernel(lengths, q, kv, weighted, stats):
    _, _, z, core = places()
    length = lengths[2 * z + core]
    for tile in range(2):
        rows = slice(tile * 256, tile * 256 + 256)
        width = 256 * (tile + 1)
        key = lax.broadcasted_iota(jnp.int32, (width, 256), 0)
        row = tile * 256 + lax.broadcasted_iota(jnp.int32, (width, 256), 1)
        cap = jnp.where((key <= row) & (key < length), -NEG, NEG)
        for head in range(4):
            cols = slice(head * HD, (head + 1) * HD)
            s = jnp.minimum(scores_of(kv[:width, :HD], q[rows, cols]), cap)
            top = jnp.max(s, axis=0, keepdims=True)
            e = weights_of(s, top)
            stats[head : head + 1, rows] = top
            stats[head + 8 : head + 9, rows] = jnp.sum(e, axis=0, keepdims=True)
            weighted[rows, cols] = dot_keys(e.astype(BF), kv[:width, HD:])


def own_attention(lengths, q, kv):
    return pl.pallas_call(
        own_kernel,
        out_shape=[jax.ShapeDtypeStruct((512, 512), F32), jax.ShapeDtypeStruct((16, 512), F32)],
        in_specs=[SM, VM, VM],
        out_specs=[VM, VM],
        compiler_params=pltpu.CompilerParams(vmem_limit_bytes=VMEM_LIMIT),
        cost_estimate=pl.CostEstimate(flops=4 * 4 * 512 * 512 * 128, bytes_accessed=3 << 20, transcendentals=1 << 20),
    )(lengths, q, kv)


def nearer_kernel(own, below, across, above, out):
    _, _, z, _ = places()
    for plane, source in enumerate((own, below, across, above)):

        @pl.when(z == plane)
        def _(source=source):
            out[...] = source[:ROWS, :]


def nearer_anchor(own, below, across, above):
    return pl.pallas_call(
        nearer_kernel,
        out_shape=jax.ShapeDtypeStruct((ROWS, 2 * HD), BF),
        in_specs=[VM] * 4,
        out_specs=VM,
        compiler_params=pltpu.CompilerParams(vmem_limit_bytes=VMEM_LIMIT),
        cost_estimate=pl.CostEstimate(flops=0, bytes_accessed=1 << 19, transcendentals=0),
    )(own, below, across, above)


def anchor_kernel(lengths, q, kv_zero, kv_one, weighted, stats, out, kv):
    _, _, z, core = places()
    length = lengths[2 * z + core]
    anchor_length = jnp.where(2 * z + core > 0, lengths[0], 0)

    @pl.when(core == 0)
    def _():
        kv[...] = kv_zero[...]

    @pl.when(core != 0)
    def _():
        kv[...] = kv_one[...]

    key = lax.broadcasted_iota(jnp.int32, (512, 1), 0)
    cap = jnp.where(key < anchor_length, -NEG, NEG)
    for tile in range(2):
        rows = slice(tile * 256, tile * 256 + 256)
        live = tile * 256 + lax.broadcasted_iota(jnp.int32, (1, 256), 1) < length
        scaled, factors = [], []
        for head in range(4):
            cols = slice(head * HD, (head + 1) * HD)
            s = jnp.minimum(scores_of(kv[:, :HD], q[rows, cols]), cap)
            own_top, own_sum = stats[head : head + 1, rows], stats[head + 8 : head + 9, rows]
            top = jnp.maximum(own_top, jnp.max(s, axis=0, keepdims=True))
            e = weights_of(s, top)
            factor = weights_of(own_top, top)
            total = own_sum * factor + jnp.sum(e, axis=0, keepdims=True)
            share = jnp.where(live, 1.0 / total, 0.0)
            scaled.append(dot_keys((e * share).astype(BF), kv[:, HD:]))
            factors.append(factor * share)
        across = jnp.concatenate(factors + factors, axis=0).T
        for head in range(4):
            cols = slice(head * HD, (head + 1) * HD)
            out[rows, cols] = (weighted[rows, cols] * across[:, head : head + 1] + scaled[head]).astype(BF)


def anchor_attention(lengths, q, kv_zero, kv_one, weighted, stats):
    return pl.pallas_call(
        anchor_kernel,
        out_shape=jax.ShapeDtypeStruct((512, 512), BF),
        in_specs=[SM, VM, VM, VM, VM, VM],
        out_specs=VM,
        scratch_shapes=[pltpu.VMEM((ROWS, 2 * HD), BF)],
        compiler_params=pltpu.CompilerParams(vmem_limit_bytes=VMEM_LIMIT),
        cost_estimate=pl.CostEstimate(flops=4 * 4 * 512 * 512 * 128, bytes_accessed=3 << 20, transcendentals=1 << 20),
    )(lengths, q, kv_zero, kv_one, weighted, stats)


def question_kernel(lengths_ref, q_own, q_other, kv_0, kv_1, kv_2, kv_3, out_own, out_other):
    kvs = (kv_0, kv_1, kv_2, kv_3)
    _, _, z, core = places()
    ctx = 2 * z + core
    blocks = [z, (z + 3) & 3, (z + 1) & 3, (z + 2) & 3]
    lengths = [lengths_ref[2 * block + core] for block in blocks]
    stacked = [q_own[:, h * HD : (h + 1) * HD] for h in range(4)]
    stacked += [q_other[:, h * HD : (h + 1) * HD] for h in range(4)]
    q = jnp.concatenate(stacked, axis=0)
    scores = []
    key = lax.broadcasted_iota(jnp.int32, (1, 512), 1)
    for kv, length in zip(kvs, lengths):
        scores.append(jnp.minimum(scores_of(q, kv[:ROWS, :HD]), jnp.where(key < length, -NEG, NEG)))
    row = lax.broadcasted_iota(jnp.int32, (256, 128), 0)
    lane = lax.broadcasted_iota(jnp.int32, (256, 128), 1)
    row_id = row % 32 + 32 * jnp.where(row < 128, ctx, ctx + 1 - 2 * core)
    block = jnp.where(lane < 64, jnp.where(lane < 32, blocks[0], blocks[1]), jnp.where(lane < 96, blocks[2], blocks[3]))
    key_id = lane % 32 + 32 * (2 * block + core)
    asked_keys = jnp.concatenate([kv[ROWS:, :HD] for kv in kvs], axis=0)
    asked_values = jnp.concatenate([kv[ROWS:, HD:] for kv in kvs], axis=0)
    scores.append(jnp.where(key_id <= row_id, scores_of(q, asked_keys), NEG))
    top = jnp.max(scores[-1], axis=1, keepdims=True)
    for s in scores[:-1]:
        top = jnp.maximum(top, jnp.max(s, axis=1, keepdims=True))
    values = [kv[:ROWS, HD:] for kv in kvs] + [asked_values]
    total = jnp.zeros((256, 1), F32)
    both = jnp.zeros((256, HD), F32)
    for s, value in zip(scores, values):
        e = weights_of(s, top)
        total = total + jnp.sum(e, axis=1, keepdims=True)
        both = both + jnp.dot(e.astype(BF), value, preferred_element_type=F32)
    for out, start in ((out_own, 0), (out_other, 128)):
        tops, totals = [], []
        for head in range(4):
            rows = slice(start + head * 32, start + head * 32 + 32)
            out[:, head * HD : (head + 1) * HD] = both[rows]
            tops.append(top[rows])
            totals.append(total[rows])
        out[:, 512:640] = columns_to_stats(tops + totals)


def question_attention(lengths, q_own, q_other, kvs):
    part = jax.ShapeDtypeStruct((32, 640), F32)
    return pl.pallas_call(
        question_kernel,
        out_shape=[part, part],
        in_specs=[SM] + [VM] * 6,
        out_specs=[VM, VM],
        compiler_params=pltpu.CompilerParams(vmem_limit_bytes=VMEM_LIMIT),
        cost_estimate=pl.CostEstimate(flops=4 * 256 * 2176 * 128, bytes_accessed=2 << 20, transcendentals=1 << 19),
    )(lengths, q_own, q_other, *kvs)


def merge_kernel(a, b, out):
    stat_a, stat_b = a[:, 512:640], b[:, 512:640]
    for head in range(4):
        cols = slice(head * HD, (head + 1) * HD)
        top_a, top_b = stat_a[:, head : head + 1], stat_b[:, head : head + 1]
        top = jnp.maximum(top_a, top_b)
        factor_a, factor_b = weights_of(top_a, top), weights_of(top_b, top)
        total = stat_a[:, head + 4 : head + 5] * factor_a + stat_b[:, head + 4 : head + 5] * factor_b
        out[:, cols] = ((a[:, cols] * factor_a + b[:, cols] * factor_b) / total).astype(BF)


def merge(a, b):
    return pl.pallas_call(
        merge_kernel,
        out_shape=jax.ShapeDtypeStruct((32, 512), BF),
        in_specs=[VM, VM],
        out_specs=VM,
        compiler_params=pltpu.CompilerParams(vmem_limit_bytes=VMEM_LIMIT),
    )(a, b)


PLAN_1 = [
    ((0, 0), 0, 512, [(0, 0, 512)]),
    ((-1, 0), 0, 512, [(1, 0, 512)]),
    ((1, 0), 0, 512, [(2, 0, 512)]),
    ((0, -1), 0, 512, [(3, 0, 512)]),
    ((0, 1), 0, 512, [(4, 0, 512)]),
    ((2, 0), 0, 256, [(5, 0, 256)]),
    ((0, 2), 256, 512, [(6, 0, 256)]),
]
PLAN_2 = [
    ((-1, -1), 0, 512, [(0, 0, 256), (2, 0, 256)]),
    ((1, -1), 0, 512, [(0, 256, 256), (3, 0, 256)]),
    ((-1, 1), 0, 512, [(1, 0, 256), (2, 256, 256)]),
    ((1, 1), 0, 512, [(1, 256, 256), (3, 256, 256)]),
    ((2, -1), 0, 256, [(0, 512, 256)]),
    ((2, 1), 0, 256, [(1, 512, 256)]),
    ((-1, 2), 256, 512, [(2, 512, 256)]),
    ((1, 2), 256, 512, [(3, 512, 256)]),
    ((0, 2), 0, 256, [(0, 768, 128), (1, 768, 128)]),
    ((2, 0), 256, 512, [(2, 768, 160), (3, 768, 96)]),
]
PLAN_3 = [
    ((2, 2), 0, 512, [(1, 128, 256), (3, 96, 256)]),
    ((-1, 2), 0, 256, [(0, 0, 256)]),
    ((1, 2), 0, 256, [(0, 256, 128), (1, 0, 128)]),
    ((2, -1), 256, 512, [(2, 0, 256)]),
    ((2, 1), 256, 512, [(2, 256, 160), (3, 0, 96)]),
]
NEAR_Y = [(0, 0, 256), (1, 0, 256), (4, 0, 256)]
NEAR_X = [(2, 256, 256), (3, 256, 256), (4, 0, 256)]
PACK_2 = [NEAR_Y + [(2, 0, 128)], NEAR_Y + [(3, 128, 128)], NEAR_X + [(0, 256, 160)], NEAR_X + [(1, 416, 96)]]
PACK_3_X = [[(0, 0, 384)], [(1, 384, 384)]]
PACK_3_Y = [[(0, 0, 416)], [(1, 416, 352)]]


def tables_of(positions):
    inverse_freq = ROPE_BASE ** (-(jnp.arange(HD // 2, dtype=jnp.float32) * 2.0 / HD))
    inverse_freq = jnp.concatenate([inverse_freq, inverse_freq])
    phases = positions.astype(jnp.float32)[:, None] * inverse_freq[None, :]
    signs = jnp.where(jnp.arange(HD) < HD // 2, -1.0, 1.0).astype(jnp.float32)
    return jnp.cos(phases), jnp.sin(phases) * signs[None, :]


def shift_z(array, dz):
    pairs = [(i, ((i // 2 + dz) % 4) * 2 + i % 2) for i in range(8)]
    return lax.ppermute(array, "ctx", pairs)


def per_device(context, question, w_query, w_key, w_value, lengths, owner):
    ctx = lax.axis_index("ctx")
    ids = jnp.arange(8, dtype=jnp.int32)
    own_offset = jnp.sum(jnp.where(ids < ctx, lengths, 0))
    filled = jnp.sum(lengths)

    up = shift_heads(context, 1, 0)
    down = shift_heads(context, -1, 0)
    right = shift_heads(context, 0, 1)
    left = shift_heads(context, 0, -1)
    low, high = pack([[(0, 0, 256)], [(0, 256, 256)]], [context])
    low, high, cut = lax.optimization_barrier((low, high, owner))
    far_y = shift_heads(low, 2, 0)
    up, high = lax.optimization_barrier((up, high))
    far_x = shift_heads(high, 0, 2)

    share = lax.all_to_all(question[0].reshape(8, 32, 512), "ctx", 0, 0)
    share = lax.dynamic_index_in_dim(share, cut[0], 0, False)
    share = jnp.broadcast_to(share[None], (16, 32, 512))
    pieces = lax.all_to_all(share, "heads", 0, 0)
    up, pieces = lax.optimization_barrier((up, pieces))

    to_right, to_left = pack(PACK_2[:2], [up, down, right, left, far_y])
    to_up, to_down = pack(PACK_2[2:], [up, down, right, left, far_x])
    a_right, a_left = shift_heads(to_right, 0, 1), shift_heads(to_left, 0, -1)
    b_up, b_down = shift_heads(to_up, 1, 0), shift_heads(to_down, -1, 0)
    up, to_right = lax.optimization_barrier((up, to_right))
    tables = tables_of(
        jnp.concatenate(
            [own_offset + jnp.arange(ROWS, dtype=jnp.int32), filled + 32 * ctx + jnp.arange(ASKED, dtype=jnp.int32)]
        )
    )
    pieces, w_query, w_key, w_value, tables = lax.optimization_barrier(
        (pieces, w_query, w_key, w_value, tables)
    )
    weights = hold(w_query, w_key.T, w_value.T)
    accs = project([context, up, down, right, left, far_y, far_x], PLAN_1, weights, None, True, True)
    q_share = question_project(pieces, weights, tables)

    a_right, a_left, accs, q_share = lax.optimization_barrier((a_right, a_left, accs, q_share))
    to_right, to_left = pack(PACK_3_X, [a_right, a_left])
    to_up, to_down = pack(PACK_3_Y, [b_up, b_down])
    last = [
        shift_heads(to_right, 0, 1),
        shift_heads(to_left, 0, -1),
        shift_heads(to_up, 1, 0),
        shift_heads(to_down, -1, 0),
    ]
    accs = project([a_right, a_left, b_up, b_down], PLAN_2, weights, accs, True, True)

    (halves,) = project(last, PLAN_3, weights, accs, False, True, True, asked=q_share)
    (queries,) = project(last, PLAN_3, weights, accs, True, False, True, tables)
    partner = swap_heads(halves, 0, 1)
    q_asked = q_share[:, :512]
    q_other = swap_ctx(q_asked, 0, 1)
    partner, queries, q_other = lax.optimization_barrier((partner, queries, q_other))
    kv = key_value(halves, partner, *tables)

    below, above, across = shift_z(kv, 1), shift_z(kv, -1), shift_z(kv, 2)
    weighted, stats = own_attention(lengths, queries, kv)
    below, above, across, weighted = lax.optimization_barrier((below, above, across, weighted))
    nearer = nearer_anchor(kv, below, across, above)
    from_zero = lax.ppermute(nearer, "ctx", [(0, 1), (2, 3), (4, 5), (6, 7)])
    part, part_other = question_attention(lengths, q_asked, q_other, [kv, below, above, across])
    from_zero, part = lax.optimization_barrier((from_zero, part))
    context_attn = anchor_attention(lengths, queries, nearer, from_zero, weighted, stats)
    question_attn = merge(part, swap_ctx(part_other, 0, 1))
    return (context_attn, question_attn)


def solution(mesh):
    in_specs = (
        P("ctx", "heads"),
        P("ctx", None, "heads"),
        P(None, "heads"),
        P(None, "heads"),
        P(None, "heads"),
        P(),
        P(),
    )
    out_specs = (P("ctx", "heads"), P("ctx", "heads"))
    return jax.shard_map(
        per_device, mesh=mesh, in_specs=in_specs, out_specs=out_specs, check_vma=False
    )
```
